32 devices in a mesh: dp: 4 (over y, x), cp: 4 (over z), tp: 2 (over core).
Axes of the slice: x: 2, y: 2, z: 4, core: 2. Of those that a mesh axis runs over, the one named last changes fastest.
Arguments:
- activations: bfloat16 [4, 4, 2, 64, 2048], P('dp', 'cp'), may hold values from -6 to 6
- document_ids: int32 [4, 512], P('dp'), may hold values from 0 to 5, as said below
- attn_gain: bfloat16 [2048], P('cp'), may hold values from 0.099609375 to 1.8984375
- w_query: bfloat16 [2048, 2048], P('cp', 'tp'), may hold values from -0.1875 to 0.1875
- w_key: bfloat16 [2048, 2048], P('cp', 'tp'), may hold values from -0.1875 to 0.1875
- w_value: bfloat16 [2048, 2048], P('cp', 'tp'), may hold values from -0.125 to 0.125
- w_out: bfloat16 [2048, 2048], P('tp', 'cp'), may hold values from -0.25 to 0.25
- mlp_gain: bfloat16 [2048], P('cp'), may hold values from 0.099609375 to 1.8984375
- w_gate: bfloat16 [2048, 8192], P('cp', 'tp'), may hold values from -0.125 to 0.125
- w_up: bfloat16 [2048, 8192], P('cp', 'tp'), may hold values from -0.125 to 0.125
- w_down: bfloat16 [8192, 2048], P('tp', 'cp'), may hold values from -0.0625 to 0.0625
- cotangent: bfloat16 [4, 4, 2, 64, 2048], P('dp', 'cp'), may hold values from -6 to 6
Outputs:
- layer_out: bfloat16 [4, 4, 2, 64, 2048], P('dp', 'cp')
- input_grad: bfloat16 [4, 4, 2, 64, 2048], P('dp', 'cp')
- attn_gain_grad: float32 [2048], P('cp')
- w_query_grad: float32 [2048, 2048], P('cp', 'tp')
- w_key_grad: float32 [2048, 2048], P('cp', 'tp')
- w_value_grad: float32 [2048, 2048], P('cp', 'tp')
- w_out_grad: float32 [2048, 2048], P('tp', 'cp')
- mlp_gain_grad: float32 [2048], P('cp')
- w_gate_grad: float32 [2048, 8192], P('cp', 'tp')
- w_up_grad: float32 [2048, 8192], P('cp', 'tp')
- w_down_grad: float32 [8192, 2048], P('tp', 'cp')
The draws below stay inside these ranges and needn't reach their ends.
Inputs may be any that keep to these rules, and one draw needn't show every extreme that they name: `document_ids`: row b numbers the six documents of sequence b in the order of their tokens: 0 at the first token, never falling, rising by one at each new document. In every row the second document begins within the first 64 tokens and covers 512 / 2 tokens or more.
All inputs are finite; a program needn't handle non-finite values.
Results may differ from the reference program's by a relative error of at most 0.015.
Values may be sent and summed in bfloat16 or wider, within the bound.
A program may use at most 448 MiB of HBM per device.

```python
import math
import jax
import jax.numpy as jnp
from jax import lax

D = 2048
HEADS = 16
HEAD_DIM = 128
FF = 8192
CH = 64
SEQLEN = 512
N_DP = 4
N_CP = 4


def one_sequence(key):
    start_key, span_key = jax.random.split(key, 2)
    opening = jax.random.randint(start_key, (), 1, CH)
    closing = opening + jax.random.randint(span_key, (), SEQLEN // 2, SEQLEN // 2 + SEQLEN // 4 + 1)
    tail_gap = (SEQLEN - closing) // 4
    places = jnp.arange(SEQLEN, dtype=jnp.int32)
    fresh = (places == opening) | (places == closing)
    fresh = fresh | (places == closing + tail_gap) | (places == closing + 2 * tail_gap) | (places == closing + 3 * tail_gap)
    return jnp.cumsum(fresh.astype(jnp.int32)).astype(jnp.int32)


def draw_document_ids(key, part):
    key = jax.random.fold_in(key, 11)
    return jax.vmap(one_sequence)(jax.random.split(key, N_DP))


def shard_levels(key, dims, shards, smallest, largest):
    def one(axis_at, blocks):
        draws = jax.random.uniform(jax.random.fold_in(jax.random.fold_in(key, 6), axis_at), (blocks,), jnp.float32, smallest / len(shards), largest / len(shards))
        return jnp.repeat(jnp.exp(draws), dims[axis_at] // blocks).reshape((-1,) + (1,) * (len(dims) - axis_at - 1))

    level = one(*shards[0])
    for cut in shards[1:]:
        level = level * one(*cut)
    return level


def noise(own_key, shape, scale, limit, pieces=(), kind=jnp.bfloat16):
    values = scale * jax.random.normal(own_key, shape, jnp.float32)
    if pieces:
        values = values * shard_levels(own_key, shape, pieces, -0.22, 0.18)
    return jnp.clip(values, -limit, limit).astype(kind)


def setup_inputs(seed: int = 0) -> dict:
    arg_keys = jax.random.split(jax.random.key(seed), 13)
    return {
        "activations": noise(arg_keys[0], (N_DP, N_CP, 2, CH, D), 1.0, 6.0, ((0, 4), (1, 4))),
        "document_ids": draw_document_ids(jax.random.fold_in(arg_keys[12], 71), 0),
        "attn_gain": jnp.clip(1.0 + 0.18 * jax.random.normal(arg_keys[2], (D,), jnp.float32), 0.099609375, 1.8984375).astype(jnp.bfloat16),
        "w_query": noise(arg_keys[3], (D, HEADS * HEAD_DIM), (D // 2) ** -0.5, 0.1875, ((0, 4), (1, 2))),
        "w_key": noise(arg_keys[4], (D, HEADS * HEAD_DIM), (D // 2) ** -0.5, 0.1875, ((0, 4), (1, 2))),
        "w_value": noise(arg_keys[5], (D, HEADS * HEAD_DIM), D ** -0.5, 0.125, ((0, 4), (1, 2))),
        "w_out": noise(arg_keys[6], (HEADS * HEAD_DIM, D), (D // 4) ** -0.5, 0.25, ((0, 2), (1, 4))),
        "mlp_gain": jnp.clip(1.0 + 0.18 * jax.random.normal(arg_keys[7], (D,), jnp.float32), 0.099609375, 1.8984375).astype(jnp.bfloat16),
        "w_gate": noise(arg_keys[8], (D, FF), D ** -0.5, 0.125, ((0, 4), (1, 2))),
        "w_up": noise(arg_keys[9], (D, FF), D ** -0.5, 0.125, ((0, 4), (1, 2))),
        "w_down": noise(arg_keys[10], (FF, D), FF ** -0.5, 0.0625, ((0, 2), (1, 4))),
        "cotangent": noise(arg_keys[11], (N_DP, N_CP, 2, CH, D), 1.0, 6.0, ((0, 4), (1, 4))),
    }


@jax.custom_vjp
def low(v):
    return lax.optimization_barrier(v.astype(jnp.bfloat16)).astype(jnp.float32)

@jax.custom_vjp
def low_back(v):
    return v

def low_keep(v):
    return (low(v), None)

def low_pass(kept, grad):
    return (grad,)

def back_keep(v):
    return (v, None)

def back_low(kept, grad):
    return (low(grad),)
low.defvjp(low_keep, low_pass)
low_back.defvjp(back_keep, back_low)
EPS = 1e-05
SHIFT = math.log(4096.0)
ROPE_BASE = 10000.0
HIGHEST = lax.Precision.HIGHEST

def natural(mirrored):
    front = mirrored[:, :, 0]
    back = mirrored[:, ::-1, 1]
    joined = jnp.concatenate([front, back], axis=1)
    return joined.reshape((mirrored.shape[0], -1) + mirrored.shape[4:])

def mirror(flat):
    blocks = flat.reshape((flat.shape[0], 2 * N_CP, CH) + flat.shape[2:])
    return jnp.stack([blocks[:, :N_CP], blocks[:, N_CP:][:, ::-1]], axis=2)

def rotate(heads, positions):
    half_dim = HEAD_DIM // 2
    frequency = ROPE_BASE ** (-jnp.arange(half_dim, dtype=jnp.float32) / half_dim)
    angle = positions.astype(jnp.float32)[:, None] * frequency[None, :]
    cosine = jnp.cos(angle)[:, None, :]
    sine = jnp.sin(angle)[:, None, :]
    first = heads[..., :half_dim]
    second = heads[..., half_dim:]
    return jnp.concatenate([first * cosine - second * sine, second * cosine + first * sine], axis=-1)

def normalize(values):
    inverse = lax.rsqrt(lax.optimization_barrier(jnp.mean(values * values, axis=-1, keepdims=True)) + EPS)
    return values * inverse

def matmul(left, right):
    return jnp.dot(left, right, precision=HIGHEST, preferred_element_type=jnp.float32)

@jax.checkpoint
def attend_head(head_query, head_key, head_value, positions, documents):
    scores = low_back(jnp.dot(head_query, head_key.T, precision=HIGHEST, preferred_element_type=jnp.float32) * HEAD_DIM ** (-0.5))
    visible = ((documents[:, None] == documents[None, :]) & (positions[None, :] <= positions[:, None])).astype(jnp.float32)
    weights = low(jax.nn.sigmoid(scores - SHIFT) * visible)
    return low(low_back(matmul(weights, head_value)))

def sequence_forward(tokens, documents, attn_gain, w_query, w_key, w_value, w_out, mlp_gain, w_gate, w_up, w_down):
    positions = jnp.arange(SEQLEN, dtype=jnp.int32)
    hidden_one = low(normalize(tokens) * attn_gain)
    query_pre = low_back(matmul(hidden_one, w_query))
    key_pre = low_back(matmul(hidden_one, w_key))
    value_pre = low_back(matmul(hidden_one, w_value))
    queries = low(rotate(query_pre.reshape(SEQLEN, HEADS, HEAD_DIM), positions))
    key_rows = low(rotate(key_pre.reshape(SEQLEN, HEADS, HEAD_DIM), positions))
    value_rows = low(value_pre).reshape(SEQLEN, HEADS, HEAD_DIM)

    def one_head(operands):
        return attend_head(operands[0], operands[1], operands[2], positions, documents)
    stacked = lax.map(one_head, (jnp.transpose(queries, (1, 0, 2)), jnp.transpose(key_rows, (1, 0, 2)), jnp.transpose(value_rows, (1, 0, 2))))
    attended = jnp.transpose(stacked, (1, 0, 2)).reshape(SEQLEN, HEADS * HEAD_DIM)
    middle = tokens + low_back(matmul(attended, w_out))
    hidden_two = low(normalize(middle) * mlp_gain)
    gate = low_back(matmul(hidden_two, w_gate))
    upward = low_back(matmul(hidden_two, w_up))
    product = low(jax.nn.silu(gate) * upward)
    return middle + low_back(matmul(product, w_down))

def reference(activations, document_ids, attn_gain, w_query, w_key, w_value, w_out, mlp_gain, w_gate, w_up, w_down, cotangent):
    params = tuple((weight.astype(jnp.float32) for weight in (attn_gain, w_query, w_key, w_value, w_out, mlp_gain, w_gate, w_up, w_down)))
    tokens = natural(activations).astype(jnp.float32)

    def block_forward(token_rows, *weight_list):

        def per_sequence(element):
            return sequence_forward(element[0], element[1], *weight_list)
        return lax.map(jax.checkpoint(per_sequence), (token_rows, document_ids))
    result, pullback = jax.vjp(block_forward, tokens, *params)
    grads = pullback(natural(cotangent).astype(jnp.float32))
    layer_out = mirror(result).astype(jnp.bfloat16)
    input_grad = mirror(grads[0]).astype(jnp.bfloat16)
    return (layer_out, input_grad, grads[1], grads[2], grads[3], grads[4], grads[5], grads[6], grads[7], grads[8], grads[9])
```

```python
import functools
import math

import jax
import jax.numpy as jnp
from jax import lax
from jax.experimental import pallas as pl
from jax.experimental.pallas import tpu as pltpu
from jax.sharding import PartitionSpec as P

HEAD_DIM = 128
EPS = 1e-05
SHIFT = math.log(4096.0)
ROPE_BASE = 10000.0
BF = jnp.bfloat16
F32 = jnp.float32
MESH = pl.DeviceIdType.MESH
ANY = pl.ANY
VMEM = pltpu.VMEM
MIB = 2**20


class Net:
    def __init__(self, zs, send_sems, recv_sems):
        self.zs = zs
        self.dp, self.z, self.t = (lax.axis_index(a) for a in ("dp", "cp", "tp"))
        self.a, self.b = lax.div(self.dp, 2), lax.rem(self.dp, 2)
        self.send_sems, self.recv_sems = send_sems, recv_sems
        self.used = 0
        self.open = []

    def along_z(self, s):
        return (self.dp, lax.rem(self.z + s, self.zs), self.t)

    def source_z(self, s):
        return lax.rem(self.z + self.zs - s, self.zs)

    @property
    def over_x(self):
        return (2 * self.a + 1 - self.b, self.z, self.t)

    @property
    def over_y(self):
        return (2 * (1 - self.a) + self.b, self.z, self.t)

    @property
    def sibling(self):
        return (self.dp, self.z, 1 - self.t)

    def meet(self, y=True):
        ways = [self.along_z(s) for s in range(1, self.zs)] + [self.over_x, self.sibling]
        if y:
            ways.append(self.over_y)
        barrier = pltpu.get_barrier_semaphore()
        for way in ways:
            pl.semaphore_signal(barrier, inc=1, device_id=way, device_id_type=MESH)
        pl.semaphore_wait(barrier, len(ways))

    def send(self, src, dst, way):
        k = self.used
        self.used += 1
        copy = pltpu.make_async_remote_copy(
            src, dst, self.send_sems.at[k], self.recv_sems.at[k], device_id=way, device_id_type=MESH
        )
        copy.start()
        self.open.append(copy)
        return copy

    def keep(self, src, dst):
        k = self.used
        self.used += 1
        copy = pltpu.make_async_copy(src, dst, self.send_sems.at[k])
        copy.start()
        return copy

    def finish(self):
        for copy in self.open:
            copy.wait_send()
        self.open = []


def plane_start(net, place, halves):
    own = place(net.dp)
    return net.send(own, own, net.over_x), net.send(own, own, net.over_y)


def plane_relay(net, place, halves, over_x, over_y, sibling=None):
    dx, dy = 2 * net.a + 1 - net.b, 2 * (1 - net.a) + net.b
    dd = 2 * (1 - net.a) + 1 - net.b
    waits = []
    over_x.wait_recv()
    first = halves(place(dx), 0)
    up = net.send(first, first, net.over_y)
    if sibling:
        waits.append(sibling(dx))
    over_y.wait_recv()
    second = halves(place(dy), 1)
    side = net.send(second, second, net.over_x)
    if sibling:
        waits.append(sibling(dy))
    return up, side, dd, waits


def plane_end(net, place, halves, state, sibling=None):
    up, side, dd, waits = state
    up.wait_recv()
    side.wait_recv()
    if sibling:
        waits.append(sibling(dd))
    return waits


def rows_loop(count, step, body):
    def one(i, carry):
        body(pl.ds(pl.multiple_of(i * step, step), step))
        return carry

    lax.fori_loop(0, count // step, one, 0)


def add_rows(out, terms, rows):
    def body(at):
        total = terms[0][at, :].astype(F32)
        for term in terms[1:]:
            total += term[at, :].astype(F32)
        out[at, :] = total.astype(out.dtype)

    rows_loop(rows, 16, body)


class GatherAll:
    def __init__(self, net, src, dst):
        self.net, self.src, self.dst = net, src, dst
        rows = src.shape[0] // 2
        self.halves = lambda ref, k: ref.at[pl.ds(k * rows, rows)]

    def place(self, dp, z):
        return self.dst.at[dp, z, self.net.t]

    def start(self):
        net = self.net
        mine = self.place(net.dp, net.z)
        self.local = net.keep(self.src, mine)
        self.z_sends = [net.send(self.src, mine, net.along_z(s)) for s in range(1, net.zs)]
        self.plane = [(net.z, net.send(self.src, mine, net.over_x), net.send(self.src, mine, net.over_y))]
        self.twin = [net.send(self.src, mine, net.sibling)]

    def to_twin(self, dp, z):
        ref = self.place(dp, z)
        self.twin.append(self.net.send(ref, ref, self.net.sibling))

    def spread(self):
        net = self.net
        for s in range(1, net.zs):
            self.z_sends[s - 1].wait_recv()
            z = net.source_z(s)
            ref = self.place(net.dp, z)
            self.plane.append((z, net.send(ref, ref, net.over_x), net.send(ref, ref, net.over_y)))
            self.to_twin(net.dp, z)

    def relay(self):
        net = self.net
        self.states = []
        for z, over_x, over_y in self.plane:
            place = functools.partial(self.place, z=z)
            self.states.append(
                (z, plane_relay(net, place, self.halves, over_x, over_y, lambda dp, z=z: self.to_twin(dp, z)))
            )

    def end(self):
        for z, state in self.states:
            place = functools.partial(self.place, z=z)
            plane_end(self.net, place, self.halves, state, lambda dp, z=z: self.to_twin(dp, z))
        for copy in self.twin:
            copy.wait_recv()
        self.local.wait()


class GatherGroup:
    def __init__(self, net, src, dst):
        self.net, self.src, self.dst = net, src, dst

    def place(self, b, z):
        return self.dst.at[b, z, self.net.t]

    def start(self):
        net = self.net
        mine = self.place(net.b, net.z)
        self.local = net.keep(self.src, mine)
        self.z_sends = [net.send(self.src, mine, net.along_z(s)) for s in range(1, net.zs)]
        self.over = [(net.z, net.send(self.src, mine, net.over_x))]
        self.twin = [net.send(self.src, mine, net.sibling)]

    def to_twin(self, b, z):
        ref = self.place(b, z)
        self.twin.append(self.net.send(ref, ref, self.net.sibling))

    def spread(self):
        net = self.net
        for s in range(1, net.zs):
            self.z_sends[s - 1].wait_recv()
            z = net.source_z(s)
            ref = self.place(net.b, z)
            self.over.append((z, net.send(ref, ref, net.over_x)))
            self.to_twin(net.b, z)

    def end(self):
        net = self.net
        for z, copy in self.over:
            copy.wait_recv()
            self.to_twin(1 - net.b, z)
        for copy in self.twin:
            copy.wait_recv()
        self.local.wait()


class SumGroup:
    def __init__(self, net, part, own, sib, far, landed):
        self.net, self.part, self.own, self.sib, self.far, self.landed = net, part, own, sib, far, landed
        self.rows = part.shape[3]

    def start(self):
        net = self.net
        self.twin, self.mine = [], []
        for s in range(net.zs):
            z = lax.rem(net.z + s + 1, net.zs)
            for b in (1 - net.b, net.b):
                self.twin.append(net.send(self.part.at[b, z, 1 - net.t], self.sib.at[b, z], net.sibling))
                self.mine.append(net.keep(self.part.at[b, z, net.t], self.own.at[b, z]))

    def run(self):
        net = self.net
        over = []
        for s in range(net.zs):
            z = lax.rem(net.z + s + 1, net.zs)
            for j, b in enumerate((1 - net.b, net.b)):
                self.twin[2 * s + j].wait_recv()
                self.mine[2 * s + j].wait()
                add_rows(self.own.at[b, z], [self.own.at[b, z], self.sib.at[b, z]], self.rows)
                if j == 0:
                    over.append(net.send(self.own.at[b, z], self.far.at[z], net.over_x))
        self.z_sends = []
        for s in range(net.zs):
            z = lax.rem(net.z + s + 1, net.zs)
            over[s].wait_recv()
            out = self.landed.at[net.z] if s == net.zs - 1 else self.own.at[net.b, z]
            add_rows(out, [self.own.at[net.b, z], self.far.at[z]], self.rows)
            if s < net.zs - 1:
                self.z_sends.append(net.send(out, self.landed.at[net.z], net.along_z(s + 1)))

    def end(self):
        for copy in self.z_sends:
            copy.wait_recv()


class SumAll:
    def __init__(self, net, part, own, sib, one, two, landed):
        self.net, self.part, self.own, self.sib = net, part, own, sib
        self.one, self.two, self.landed = one, two, landed
        self.half = part.shape[3] // 2

    def order(self):
        net = self.net
        return [lax.rem(net.z + s + 1, net.zs) for s in range(net.zs)]

    def places(self):
        a, b = self.net.a, self.net.b
        return [2 * (1 - a) + 1 - b, 2 * a + 1 - b, 2 * (1 - a) + b, 2 * a + b]

    def start(self):
        net = self.net
        self.twin, self.mine = [], []
        for z in self.order():
            for dp in self.places():
                self.twin.append(net.send(self.part.at[dp, z, 1 - net.t], self.sib.at[dp, z], net.sibling))
                self.mine.append(net.keep(self.part.at[dp, z, net.t], self.own.at[dp, z]))

    def upper(self, ref):
        return ref.at[pl.ds(0, self.half)]

    def lower(self, ref):
        return ref.at[pl.ds(self.half, self.half)]

    def first(self, s):
        net = self.net
        z = self.order()[s]
        dd, dx, dy, me = self.places()
        for j, dp in enumerate((dd, dx, dy, me)):
            self.twin[4 * s + j].wait_recv()
            self.mine[4 * s + j].wait()
            add_rows(self.own.at[dp, z], [self.own.at[dp, z], self.sib.at[dp, z]], 2 * self.half)
        self.ones = getattr(self, "ones", [])
        self.ones.append(
            (
                net.send(self.upper(self.own.at[dd, z]), self.one.at[0, 0, z], net.over_x),
                net.send(self.upper(self.own.at[dx, z]), self.one.at[0, 1, z], net.over_x),
                net.send(self.lower(self.own.at[dd, z]), self.one.at[1, 0, z], net.over_y),
                net.send(self.lower(self.own.at[dy, z]), self.one.at[1, 1, z], net.over_y),
            )
        )

    def second(self, s):
        net = self.net
        z = self.order()[s]
        dd, dx, dy, me = self.places()
        x_dd, x_me, y_dd, y_me = self.ones[s]
        self.twos = getattr(self, "twos", [])
        x_dd.wait_recv()
        out = self.upper(self.own.at[dy, z])
        add_rows(out, [out, self.one.at[0, 0, z]], self.half)
        up = net.send(out, self.two.at[0, z], net.over_y)
        y_dd.wait_recv()
        out = self.lower(self.own.at[dx, z])
        add_rows(out, [out, self.one.at[1, 0, z]], self.half)
        side = net.send(out, self.two.at[1, z], net.over_x)
        self.twos.append((up, side))

    def third(self, s):
        net = self.net
        z = self.order()[s]
        dd, dx, dy, me = self.places()
        _, x_me, _, y_me = self.ones[s]
        up, side = self.twos[s]
        last = s == net.zs - 1
        out = self.landed.at[net.z] if last else self.own.at[me, z]
        x_me.wait_recv()
        up.wait_recv()
        mine = self.own.at[me, z]
        add_rows(self.upper(out), [self.upper(mine), self.one.at[0, 1, z], self.two.at[0, z]], self.half)
        y_me.wait_recv()
        side.wait_recv()
        add_rows(self.lower(out), [self.lower(mine), self.one.at[1, 1, z], self.two.at[1, z]], self.half)
        self.z_sends = getattr(self, "z_sends", [])
        if not last:
            self.z_sends.append(net.send(out, self.landed.at[net.z], net.along_z(s + 1)))

    def end(self):
        for copy in self.z_sends:
            copy.wait_recv()


class SpreadGrads:
    def __init__(self, net, src, dst, halves):
        self.net, self.src, self.dst, self.halves = net, src, dst, halves

    def start(self):
        net = self.net
        mine = self.dst(net.dp, net.z)
        self.local = net.keep(self.src(net.z), mine)
        self.z_sends = [
            net.send(self.src(lax.rem(net.z + s, net.zs)), mine, net.along_z(s)) for s in range(1, net.zs)
        ]
        self.plane = [
            (net.z, net.send(self.src(net.z), mine, net.over_x), net.send(self.src(net.z), mine, net.over_y))
        ]
        self.states = []

    def spread(self, s):
        net = self.net
        self.z_sends[s - 1].wait_recv()
        z = net.source_z(s)
        ref = self.dst(net.dp, z)
        self.plane.append((z, net.send(ref, ref, net.over_x), net.send(ref, ref, net.over_y)))

    def relay(self, s):
        z, over_x, over_y = self.plane[s]
        place = lambda dp: self.dst(dp, z)
        self.states.append(plane_relay(self.net, place, self.halves, over_x, over_y))

    def end(self):
        for state in self.states:
            plane_end(self.net, None, self.halves, state)
        self.local.wait()


def call(kernel, name, outs, scratch, count, args, spaces=None, vmem=40):
    spaces = spaces or [ANY] * len(args)
    return pl.pallas_call(
        kernel,
        out_shape=[jax.ShapeDtypeStruct(shape, kind) for shape, kind, _ in outs],
        in_specs=[pl.BlockSpec(memory_space=space) for space in spaces],
        out_specs=[pl.BlockSpec(memory_space=space) for _, _, space in outs],
        scratch_shapes=list(scratch) + [pltpu.SemaphoreType.DMA((count,)), pltpu.SemaphoreType.DMA((count,))],
        compiler_params=pltpu.CompilerParams(
            collective_id=name, has_side_effects=True, vmem_limit_bytes=vmem * MIB
        ),
    )(*args)


def open_kernel(zs, x, wq, wk, wv, wo, small, x_all, qkv_w, out_w, small_z, small_x, send_sems, recv_sems):
    net = Net(zs, send_sems, recv_sems)
    net.meet(y=False)
    deep = wq.shape[0]
    gather = GatherGroup(net, x.at[net.t], x_all)
    gather.start()
    waits, local = [], []

    def cols(w, z):
        return w.at[:, pl.ds(pl.multiple_of((net.b * zs + z) * HEAD_DIM, HEAD_DIM), HEAD_DIM)]

    def rows(z):
        return wo.at[pl.ds(pl.multiple_of((net.b * zs + z) * HEAD_DIM, HEAD_DIM), HEAD_DIM)]

    mine = pl.ds(pl.multiple_of(net.z * deep, deep), deep)
    for s in range(1, zs):
        waits.append(net.send(small, small_z.at[net.z], net.along_z(s)))
    waits.append(net.send(small, small_x.at[net.b], net.over_x))
    local.append(net.keep(small, small_z.at[net.z]))
    local.append(net.keep(small, small_x.at[net.b]))
    for m, w in enumerate((wq, wk, wv)):
        dst = qkv_w.at[mine, pl.ds(m * HEAD_DIM, HEAD_DIM)]
        local.append(net.keep(cols(w, net.z), dst))
        for s in range(1, zs):
            waits.append(net.send(cols(w, lax.rem(net.z + s, zs)), dst, net.along_z(s)))
    dst = out_w.at[:, mine]
    local.append(net.keep(rows(net.z), dst))
    for s in range(1, zs):
        waits.append(net.send(rows(lax.rem(net.z + s, zs)), dst, net.along_z(s)))
    gather.spread()
    gather.end()
    for copy in waits:
        copy.wait_recv()
    for copy in local:
        copy.wait()
    net.finish()


def middle_kernel(
    zs, part, x, gain, wg, wu, wd, cot, middle, h2_all, cot_all, gu_w, down_w,
    own, sib, far, landed, x_lane, h2, gain_v, mid_v, send_sems, recv_sems,
):
    net = Net(zs, send_sems, recv_sems)
    net.meet()
    deep, wide = wg.shape[0], gu_w.shape[1] // 2
    branch = SumGroup(net, part, own, sib, far, landed)
    branch.start()
    lane = net.keep(x.at[net.t], x_lane)
    gains = net.keep(gain, gain_v)
    waits, local = [], []
    mine = pl.ds(pl.multiple_of(net.z * deep, deep), deep)

    def block(z):
        return pl.ds(pl.multiple_of((net.dp * zs + z) * wide, wide), wide)

    def fetch(s, z):
        srcs = (wg.at[:, block(z)], wu.at[:, block(z)], wd.at[block(z)])
        dsts = (gu_w.at[mine, pl.ds(0, wide)], gu_w.at[mine, pl.ds(wide, wide)], down_w.at[:, mine])
        for src, dst in zip(srcs, dsts, strict=True):
            if s == 0:
                local.append(net.keep(src, dst))
            else:
                waits.append(net.send(src, dst, net.along_z(s)))

    fetch(0, net.z)
    branch.run()
    for s in range(1, zs):
        fetch(s, lax.rem(net.z + s, zs))
    lane.wait()
    gains.wait()
    branch.end()
    rows, width = x_lane.shape

    def body(at):
        total = x_lane[at, :].astype(F32)
        for z in range(zs):
            total += landed[z, at, :].astype(F32)
        mid_v[at, :] = total
        inverse = lax.rsqrt(jnp.mean(total * total, axis=-1, keepdims=True) + EPS)
        h2[at, :] = (total * inverse * gain_v[0:1, :]).astype(BF)

    rows_loop(rows, 16, body)
    out = net.keep(mid_v, middle)
    hidden = GatherAll(net, h2, h2_all)
    hidden.start()
    cotan = GatherAll(net, cot.at[net.t], cot_all)
    cotan.start()
    hidden.spread()
    hidden.relay()
    cotan.spread()
    cotan.relay()
    hidden.end()
    cotan.end()
    out.wait()
    for copy in waits:
        copy.wait_recv()
    for copy in local:
        copy.wait()
    net.finish()


def back_kernel(
    zs, gh_part, feed_part, gu_grad, down_grad, middle, cot, gain,
    gbr_all, grad_mid, layer_out, gain_part, gate_out, up_out, down_out,
    own, sib, one, two, landed, own_f, sib_f, one_f, two_f, landed_f, mid_v, cot_v, gain_v, gm_v, gbr_v, gsum_v, lo_v,
    send_sems, recv_sems,
):
    net = Net(zs, send_sems, recv_sems)
    net.meet()
    wide = gu_grad.shape[1] // 2
    deep = gate_out.shape[0]
    hidden = SumAll(net, gh_part, own, sib, one, two, landed)
    hidden.start()
    feed = SumAll(net, feed_part, own_f, sib_f, one_f, two_f, landed_f)
    feed.start()
    local = [net.keep(middle, mid_v), net.keep(cot.at[net.t], cot_v), net.keep(gain, gain_v)]

    def block(dp, z):
        return pl.ds(pl.multiple_of((dp * zs + z) * wide, wide), wide)

    def deep_rows(z):
        return pl.ds(pl.multiple_of(z * deep, deep), deep)

    def half_rows(ref, k):
        n = ref.shape[0] // 2
        return ref.at[pl.ds(k * n, n)]

    grads = [
        SpreadGrads(
            net,
            lambda z: gu_grad.at[deep_rows(z), pl.ds(0, wide)],
            lambda dp, z: gate_out.at[:, block(dp, z)],
            half_rows,
        ),
        SpreadGrads(
            net,
            lambda z: gu_grad.at[deep_rows(z), pl.ds(wide, wide)],
            lambda dp, z: up_out.at[:, block(dp, z)],
            half_rows,
        ),
        SpreadGrads(
            net,
            lambda z: down_grad.at[:, deep_rows(z)],
            lambda dp, z: down_out.at[block(dp, z)],
            half_rows,
        ),
    ]
    for s in range(zs):
        hidden.first(s)
    for s in range(zs):
        hidden.second(s)
    for s in range(zs):
        hidden.third(s)
    for grad in grads:
        grad.start()
    for s in range(zs):
        feed.first(s)
    for copy in local:
        copy.wait()
    hidden.end()
    rows = mid_v.shape[0]
    gsum_v[...] = jnp.zeros_like(gsum_v)

    def body(at):
        mid = mid_v[at, :]
        inverse = lax.rsqrt(jnp.mean(mid * mid, axis=-1, keepdims=True) + EPS)
        normed = mid * inverse
        total = landed[0, at, :].astype(F32)
        for z in range(1, zs):
            total += landed[z, at, :].astype(F32)
        prod = total * normed
        gsum_v[...] += prod[0:8, :] + prod[8:16, :]
        scaled = total * gain_v[0:1, :]
        grad = cot_v[at, :].astype(F32) + inverse * (
            scaled - normed * jnp.mean(scaled * normed, axis=-1, keepdims=True)
        )
        gm_v[at, :] = grad
        gbr_v[at, :] = grad.astype(BF)

    rows_loop(rows, 16, body)
    gather = GatherGroup(net, gbr_v, gbr_all)
    gather.start()
    outs = [net.keep(gm_v, grad_mid), net.keep(gsum_v, gain_part)]
    for s in range(zs):
        feed.second(s)
    gather.spread()
    for s in range(zs):
        feed.third(s)
    gather.end()
    for s in range(1, zs):
        for grad in grads:
            grad.spread(s)
    for grad in grads:
        grad.relay(0)
    feed.end()

    def close(at):
        total = mid_v[at, :]
        for z in range(zs):
            total += landed_f[z, at, :].astype(F32)
        lo_v[at, :] = total.astype(BF)

    rows_loop(rows, 16, close)
    outs.append(net.keep(lo_v, layer_out.at[net.t]))
    last = net.send(lo_v, layer_out.at[net.t], net.sibling)
    for s in range(1, zs):
        for grad in grads:
            grad.relay(s)
    for grad in grads:
        grad.end()
    last.wait_recv()
    for copy in outs:
        copy.wait()
    net.finish()


def close_kernel(
    zs, gh_part, qkv_grad, out_grad, grad_mid, x, gain, gain_part,
    input_grad, q_out, k_out, v_out, o_out, gains_out,
    own, sib, far, landed, x_v, gain_v, gm_v, gsum_v, gi_v, q_own, q_far, o_own, o_far, g_far, g_land,
    send_sems, recv_sems,
):
    net = Net(zs, send_sems, recv_sems)
    net.meet()
    deep = q_out.shape[0]
    half = deep // 2
    hidden = SumGroup(net, gh_part, own, sib, far, landed)
    local = [
        net.keep(grad_mid, gm_v), net.keep(x.at[net.t], x_v), net.keep(gain, gain_v),
        net.keep(gain_part, gsum_v.at[1]),
    ]
    sums = []
    for s in range(zs):
        z = lax.rem(net.z + s + 1, zs)
        at = lambda a: pl.ds(pl.multiple_of(z * deep + a * half, half), half)
        oc = pl.ds(pl.multiple_of(z * deep, deep), deep)
        oh = HEAD_DIM // 2
        orow = lambda a: pl.ds(pl.multiple_of(a * oh, oh), oh)
        sums.append(
            (
                z,
                net.send(qkv_grad.at[at(1 - net.a)], q_far.at[z], net.over_y),
                net.keep(qkv_grad.at[at(net.a)], q_own.at[z]),
                net.send(out_grad.at[orow(1 - net.a), oc], o_far.at[z], net.over_y),
                net.keep(out_grad.at[orow(net.a), oc], o_own.at[z]),
            )
        )
    hidden.start()
    hidden.run()

    def half_rows(ref, k):
        n = ref.shape[0] // 2
        return ref.at[pl.ds(k * n, n)]

    for z, q_in, q_mine, o_in, o_mine in sums:
        q_in.wait_recv()
        q_mine.wait()
        add_rows(q_own.at[z], [q_own.at[z], q_far.at[z]], half)
        o_in.wait_recv()
        o_mine.wait()
        add_rows(o_own.at[z], [o_own.at[z], o_far.at[z]], HEAD_DIM // 2)

    def q_place(ref):
        def place(dp, z):
            a, b = lax.div(dp, 2), lax.rem(dp, 2)
            return ref.at[
                pl.ds(pl.multiple_of(a * half, half), half),
                pl.ds(pl.multiple_of((b * zs + z) * HEAD_DIM, HEAD_DIM), HEAD_DIM),
            ]

        return place

    def o_place(dp, z):
        a, b = lax.div(dp, 2), lax.rem(dp, 2)
        oh = HEAD_DIM // 2
        return o_out.at[pl.ds(pl.multiple_of((b * zs + z) * HEAD_DIM + a * oh, oh), oh)]

    grads = [
        SpreadGrads(
            net, lambda z, m=m: q_own.at[z, :, pl.ds(m * HEAD_DIM, HEAD_DIM)], q_place(ref), half_rows
        )
        for m, ref in enumerate((q_out, k_out, v_out))
    ]
    grads.append(SpreadGrads(net, lambda z: o_own.at[z], o_place, half_rows))
    for grad in grads:
        grad.start()
    for copy in local:
        copy.wait()
    hidden.end()
    rows = x_v.shape[0]
    gsum_v[0] = jnp.zeros_like(gsum_v[0])

    def body(at):
        inputs = x_v[at, :].astype(F32)
        inverse = lax.rsqrt(jnp.mean(inputs * inputs, axis=-1, keepdims=True) + EPS)
        normed = inputs * inverse
        total = landed[0, at, :].astype(F32)
        for z in range(1, zs):
            total += landed[z, at, :].astype(F32)
        prod = total * normed
        gsum_v[0] += prod[0:8, :] + prod[8:16, :]
        scaled = total * gain_v[0:1, :]
        grad = gm_v[at, :] + inverse * (scaled - normed * jnp.mean(scaled * normed, axis=-1, keepdims=True))
        gi_v[at, :] = grad.astype(BF)

    rows_loop(rows, 16, body)
    out = net.keep(gi_v, input_grad.at[net.t])
    last = net.send(gi_v, input_grad.at[net.t], net.sibling)
    for k, way in enumerate((net.sibling, net.over_x, net.over_y)):
        swap = net.send(gsum_v, g_far.at[k], way)
        swap.wait()
        net.open = [c for c in net.open if c is not swap]
        gsum_v[...] = gsum_v[...] + g_far[k]
    cut = lambda z: gsum_v.at[:, :, pl.ds(pl.multiple_of(z * deep, deep), deep)]
    z_gain = [net.send(cut(lax.rem(net.z + s, zs)), g_land.at[net.z], net.along_z(s)) for s in range(1, zs)]
    keep = net.keep(cut(net.z), g_land.at[net.z])
    for s in range(1, zs):
        for grad in grads:
            grad.spread(s)
    for s in range(zs):
        for grad in grads:
            grad.relay(s)
    for grad in grads:
        grad.end()
    keep.wait()
    for copy in z_gain:
        copy.wait_recv()
    total = g_land[0]
    for z in range(1, zs):
        total += g_land[z]
    gains_out[...] = total
    last.wait_recv()
    out.wait()
    net.finish()


def rope_tables(positions):
    half_dim = HEAD_DIM // 2
    frequency = ROPE_BASE ** (-jnp.arange(half_dim, dtype=F32) / half_dim)
    angle = positions.astype(F32)[:, None] * frequency[None, :]
    return jnp.cos(angle), jnp.sin(angle)


def turn(u, cosine, sine):
    first, second = u[..., : HEAD_DIM // 2], u[..., HEAD_DIM // 2 :]
    return jnp.concatenate([first * cosine - second * sine, second * cosine + first * sine], axis=-1)


def dot(left, right, dims=((1,), (0,)), kind=F32):
    return lax.dot_general(left, right, (dims, ((), ())), preferred_element_type=F32).astype(kind)


def bdot(left, right, dims):
    return lax.dot_general(left, right, (dims, ((0,), (0,))), preferred_element_type=F32)


def heads_shards(
    zs, activations, document_ids, attn_gain, w_query, w_key, w_value, w_out, mlp_gain, w_gate, w_up, w_down, cotangent
):
    stretch, width = activations.shape[3:]
    deep = w_query.shape[0]
    seq = document_ids.shape[1]
    tokens = zs * 2 * stretch
    wide = w_gate.shape[1] // (4 * zs)
    x = activations.reshape(2, stretch, width)
    cot = cotangent.reshape(2, stretch, width)
    small = jnp.stack([attn_gain.astype(F32), mlp_gain.astype(F32)])
    docs_rows = document_ids.astype(F32).reshape(seq // deep, deep)
    small = jnp.concatenate([small, docs_rows, jnp.zeros((6 - seq // deep, deep), F32)])
    x_all, qkv_w, out_w, small_z, small_x = call(
        functools.partial(open_kernel, zs),
        1,
        [
            ((2, zs, 2, stretch, width), BF, ANY),
            ((width, 3 * HEAD_DIM), BF, ANY),
            ((HEAD_DIM, width), BF, ANY),
            ((zs, 8, deep), F32, ANY),
            ((2, 8, deep), F32, ANY),
        ],
        [],
        64,
        (x, w_query, w_key, w_value, w_out, small),
    )
    gain_one = small_z[:, 0].reshape(1, width)
    gain_two = small_z[:, 1].reshape(1, width)
    docs = small_x[:, 2 : 2 + seq // deep].reshape(2, seq)
    slots = jnp.arange(tokens, dtype=jnp.int32)
    owners = slots // (2 * stretch)
    halves = slots // stretch % 2
    places = jnp.where(halves == 0, owners, 2 * zs - 1 - owners) * stretch + slots % stretch
    cosine, sine = rope_tables(places)
    docs = jnp.take(docs, places, axis=1)
    visible = (docs[:, :, None] == docs[:, None, :]) & (places[None, None, :] <= places[None, :, None])

    flat = x_all.reshape(2 * tokens, width).astype(F32)
    inverse = lax.rsqrt(jnp.mean(flat * flat, axis=-1, keepdims=True) + EPS)
    hidden = (flat * inverse * gain_one).astype(BF)
    qkv = dot(hidden, qkv_w).reshape(2, tokens, 3, HEAD_DIM)
    queries = turn(qkv[:, :, 0], cosine, sine).astype(BF)
    keys = turn(qkv[:, :, 1], cosine, sine).astype(BF)
    values = qkv[:, :, 2].astype(BF)
    scale = HEAD_DIM**-0.5
    sigma = jax.nn.sigmoid(bdot(queries, keys, ((2,), (2,))) * scale - SHIFT)
    weights = jnp.where(visible, sigma, 0.0).astype(BF)
    attended = bdot(weights, values, ((2,), (1,))).astype(BF).reshape(2 * tokens, HEAD_DIM)
    part = dot(attended, out_w, kind=BF).reshape(2, zs, 2, stretch, width)

    middle, h2_all, cot_all, gu_w, down_w = call(
        functools.partial(middle_kernel, zs),
        2,
        [
            ((stretch, width), F32, ANY),
            ((4, zs, 2, stretch, width), BF, ANY),
            ((4, zs, 2, stretch, width), BF, ANY),
            ((width, 2 * wide), BF, ANY),
            ((wide, width), BF, ANY),
        ],
        [
            VMEM((2, zs, stretch, width), BF),
            VMEM((2, zs, stretch, width), BF),
            VMEM((zs, stretch, width), BF),
            VMEM((zs, stretch, width), BF),
            VMEM((stretch, width), BF),
            VMEM((stretch, width), BF),
            VMEM((8, width), F32),
            VMEM((stretch, width), F32),
        ],
        160,
        (part, x, jnp.broadcast_to(gain_two, (8, width)), w_gate, w_up, w_down, cot),
    )

    h2 = h2_all.reshape(4 * tokens, width)
    cots = cot_all.reshape(4 * tokens, width)
    gate_up = dot(h2, gu_w)
    gate, upward = gate_up[:, :wide], gate_up[:, wide:]
    grad_product = dot(cots, down_w, ((1,), (1,)))
    sigma_gate = jax.nn.sigmoid(gate)
    silu = gate * sigma_gate
    product = (silu * upward).astype(BF)
    grad_gate = (grad_product * upward * sigma_gate * (1.0 + gate * (1.0 - sigma_gate))).astype(BF)
    grad_up = (grad_product * silu).astype(BF)
    grad_gu = jnp.concatenate([grad_gate, grad_up], axis=1)
    gh_part = dot(grad_gu, gu_w, ((1,), (1,)), BF).reshape(4, zs, 2, stretch, width)
    feed_part = dot(product, down_w, kind=BF).reshape(4, zs, 2, stretch, width)
    gu_grad = dot(h2, grad_gu, ((0,), (0,)), BF)
    down_grad = dot(product, cots, ((0,), (0,)), BF)

    half = stretch // 2
    sum_scratch = [
        VMEM((4, zs, stretch, width), BF),
        VMEM((4, zs, stretch, width), BF),
        VMEM((2, 2, zs, half, width), BF),
        VMEM((2, zs, half, width), BF),
        VMEM((zs, stretch, width), BF),
    ]
    gbr_all, grad_mid, layer_out, gain_part, gate_g, up_g, down_g = call(
        functools.partial(back_kernel, zs),
        3,
        [
            ((2, zs, 2, stretch, width), BF, ANY),
            ((stretch, width), F32, ANY),
            ((2, stretch, width), BF, ANY),
            ((8, width), F32, ANY),
            (w_gate.shape, BF, ANY),
            (w_up.shape, BF, ANY),
            (w_down.shape, BF, ANY),
        ],
        sum_scratch
        + sum_scratch
        + [
            VMEM((stretch, width), F32),
            VMEM((stretch, width), BF),
            VMEM((8, width), F32),
            VMEM((stretch, width), F32),
            VMEM((stretch, width), BF),
            VMEM((8, width), F32),
            VMEM((stretch, width), BF),
        ],
        256,
        (gh_part, feed_part, gu_grad, down_grad, middle, cot, jnp.broadcast_to(gain_two, (8, width))),
        vmem=48,
    )

    grad_branch = gbr_all.reshape(2 * tokens, width)
    grad_attended = dot(grad_branch, out_w, ((1,), (1,)), BF)
    heads_grad = grad_attended.reshape(2, tokens, HEAD_DIM)
    grad_weights = bdot(heads_grad, values, ((2,), (2,)))
    grad_scores = jnp.where(visible, grad_weights * sigma * (1.0 - sigma), 0.0).astype(BF)
    grad_queries = bdot(grad_scores, keys, ((2,), (1,))) * scale
    grad_keys = bdot(grad_scores, queries, ((1,), (1,))) * scale
    grad_values = bdot(weights, heads_grad, ((1,), (1,)))
    grad_qkv = jnp.concatenate(
        [turn(grad_queries, cosine, -sine), turn(grad_keys, cosine, -sine), grad_values], axis=-1
    )
    grad_qkv = grad_qkv.astype(BF).reshape(2 * tokens, 3 * HEAD_DIM)
    gh_one = dot(grad_qkv, qkv_w, ((1,), (1,)), BF).reshape(2, zs, 2, stretch, width)
    qkv_grad = dot(hidden, grad_qkv, ((0,), (0,)), BF)
    out_grad = dot(attended, grad_branch, ((0,), (0,)), BF)

    input_grad, q_g, k_g, v_g, o_g, gains_g = call(
        functools.partial(close_kernel, zs),
        4,
        [
            ((2, stretch, width), BF, ANY),
            (w_query.shape, BF, ANY),
            (w_key.shape, BF, ANY),
            (w_value.shape, BF, ANY),
            (w_out.shape, BF, ANY),
            ((2, 8, deep), F32, VMEM),
        ],
        [
            VMEM((2, zs, stretch, width), BF),
            VMEM((2, zs, stretch, width), BF),
            VMEM((zs, stretch, width), BF),
            VMEM((zs, stretch, width), BF),
            VMEM((stretch, width), BF),
            VMEM((8, width), F32),
            VMEM((stretch, width), F32),
            VMEM((2, 8, width), F32),
            VMEM((stretch, width), BF),
            VMEM((zs, deep // 2, 3 * HEAD_DIM), BF),
            VMEM((zs, deep // 2, 3 * HEAD_DIM), BF),
            VMEM((zs, HEAD_DIM // 2, deep), BF),
            VMEM((zs, HEAD_DIM // 2, deep), BF),
            VMEM((3, 2, 8, width), F32),
            VMEM((zs, 2, 8, deep), F32),
        ],
        160,
        (gh_one, qkv_grad, out_grad, grad_mid, x, jnp.broadcast_to(gain_one, (8, width)), gain_part),
    )
    gain_grads = jnp.sum(gains_g, axis=1)
    return (
        layer_out.reshape(activations.shape),
        input_grad.reshape(activations.shape),
        gain_grads[0],
        q_g.astype(F32),
        k_g.astype(F32),
        v_g.astype(F32),
        o_g.astype(F32),
        gain_grads[1],
        gate_g.astype(F32),
        up_g.astype(F32),
        down_g.astype(F32),
    )


def angles(positions):
    half_dim = HEAD_DIM // 2
    frequency = ROPE_BASE ** (-jnp.arange(half_dim, dtype=jnp.float32) / half_dim)
    angle = positions.astype(jnp.float32)[:, None] * frequency[None, :]
    return (jnp.cos(angle)[:, None, :], jnp.sin(angle)[:, None, :])


def rotate(flat, positions):
    row_count = flat.shape[0]
    heads = flat.reshape(row_count, -1, HEAD_DIM)
    cosine, sine = angles(positions)
    first = heads[..., : HEAD_DIM // 2]
    second = heads[..., HEAD_DIM // 2 :]
    turned = jnp.concatenate(
        [first * cosine - second * sine, second * cosine + first * sine], axis=-1
    )
    return turned.reshape(row_count, -1)


def unrotate(flat, positions):
    row_count = flat.shape[0]
    heads = flat.reshape(row_count, -1, HEAD_DIM)
    cosine, sine = angles(positions)
    first = heads[..., : HEAD_DIM // 2]
    second = heads[..., HEAD_DIM // 2 :]
    turned = jnp.concatenate(
        [first * cosine + second * sine, second * cosine - first * sine], axis=-1
    )
    return turned.reshape(row_count, -1)


def normalize(values):
    inverse = lax.rsqrt(jnp.mean(values * values, axis=-1, keepdims=True) + EPS)
    return (values * inverse, inverse)


def norm_back(grad_normed_out, normed, inverse, gain):
    scaled = grad_normed_out * gain
    return inverse * (scaled - normed * jnp.mean(scaled * normed, axis=-1, keepdims=True))


def contract_rows(left, right):
    return lax.dot_general(
        left, right, (((1,), (1,)), ((), ())), preferred_element_type=jnp.float32
    )


def contract_cols(left, right):
    return lax.dot_general(
        left, right, (((0,), (0,)), ((), ())), preferred_element_type=jnp.float32
    )


def visibility(query_positions, query_docs, key_positions, key_docs):
    same_doc = query_docs[:, None] == key_docs[None, :]
    earlier = key_positions[None, :] <= query_positions[:, None]
    return jnp.where(same_doc & earlier, 1.0, 0.0).astype(jnp.float32)


def merge_heads(stacked):
    return jnp.transpose(stacked, (1, 0, 2)).reshape(stacked.shape[1], -1)


def head_slice(matrix, offset):
    return lax.dynamic_slice_in_dim(matrix, offset, HEAD_DIM, 1)


def attend_forward(queries, key_rows, value_rows, visible):
    score_scale = HEAD_DIM ** (-0.5)

    def one_head(head_index):
        offset = head_index * HEAD_DIM
        scores = (
            contract_rows(head_slice(queries, offset), head_slice(key_rows, offset)) * score_scale
        )
        weights = (jax.nn.sigmoid(scores - SHIFT) * visible).astype(jnp.bfloat16)
        return jnp.dot(weights, head_slice(value_rows, offset), preferred_element_type=jnp.float32)

    stacked = lax.map(one_head, jnp.arange(queries.shape[1] // HEAD_DIM))
    return merge_heads(stacked)


def attend_back(queries, key_rows, value_rows, grad_attended, visible):
    score_scale = HEAD_DIM ** (-0.5)

    def one_head(head_index):
        offset = head_index * HEAD_DIM
        head_query = head_slice(queries, offset)
        head_key = head_slice(key_rows, offset)
        head_grad = head_slice(grad_attended, offset)
        scores = contract_rows(head_query, head_key) * score_scale
        sigma = jax.nn.sigmoid(scores - SHIFT)
        grad_weights = contract_rows(head_grad, head_slice(value_rows, offset))
        grad_scores = (grad_weights * visible * sigma * (1.0 - sigma)).astype(jnp.bfloat16)
        pieces = []
        pieces.append(
            jnp.dot(grad_scores, head_key, preferred_element_type=jnp.float32) * score_scale
        )
        weights = (sigma * visible).astype(jnp.bfloat16)
        pieces.append(contract_cols(grad_scores, head_query) * score_scale)
        pieces.append(contract_cols(weights, head_grad))
        return tuple(pieces)

    stacked = lax.map(one_head, jnp.arange(queries.shape[1] // HEAD_DIM))
    return tuple((merge_heads(piece) for piece in stacked))


def rows_shards(
    activations,
    document_ids,
    attn_gain,
    w_query,
    w_key,
    w_value,
    w_out,
    mlp_gain,
    w_gate,
    w_up,
    w_down,
    cotangent,
):
    groups = lax.axis_size("cp")
    rank = lax.axis_index("cp")
    stretch_len = activations.shape[3]
    width = activations.shape[4]
    row_count = 2 * stretch_len
    offsets = jnp.arange(stretch_len, dtype=jnp.int32)
    my_positions = jnp.concatenate(
        [rank * stretch_len + offsets, (2 * groups - 1 - rank) * stretch_len + offsets]
    )
    all_docs = document_ids[0]
    my_docs = jnp.take(all_docs, my_positions)
    slots = jnp.arange(groups * row_count, dtype=jnp.int32)
    owners = slots // row_count
    halves = slots // stretch_len % 2
    key_positions = (
        jnp.where(halves == 0, owners, 2 * groups - 1 - owners) * stretch_len + slots % stretch_len
    )
    key_docs = jnp.take(all_docs, key_positions)
    visible = visibility(my_positions, my_docs, key_positions, key_docs)
    gathered = (
        lax.all_gather(w_query, "cp", axis=0, tiled=True),
        lax.all_gather(w_key, "cp", axis=0, tiled=True),
        lax.all_gather(w_value, "cp", axis=0, tiled=True),
        lax.all_gather(w_out, "cp", axis=1, tiled=True),
        lax.all_gather(w_gate, "cp", axis=0, tiled=True),
        lax.all_gather(w_up, "cp", axis=0, tiled=True),
        lax.all_gather(w_down, "cp", axis=1, tiled=True),
        lax.all_gather(attn_gain, "cp", axis=0, tiled=True),
        lax.all_gather(mlp_gain, "cp", axis=0, tiled=True),
    )
    (
        query_full,
        key_full,
        value_full,
        out_full,
        gate_full,
        up_full,
        down_full,
        gain_one,
        gain_two,
    ) = gathered
    gain_one = gain_one.astype(jnp.float32)
    gain_two = gain_two.astype(jnp.float32)
    inputs = activations.reshape(row_count, width).astype(jnp.float32)
    normed_one, inverse_one = normalize(inputs)
    hidden_one = (normed_one * gain_one).astype(jnp.bfloat16)
    queries = rotate(
        jnp.dot(hidden_one, query_full, preferred_element_type=jnp.float32), my_positions
    ).astype(jnp.bfloat16)
    keys_local = rotate(
        jnp.dot(hidden_one, key_full, preferred_element_type=jnp.float32), my_positions
    ).astype(jnp.bfloat16)
    values_local = jnp.dot(hidden_one, value_full, preferred_element_type=jnp.float32).astype(
        jnp.bfloat16
    )
    keys_all, values_all = (
        lax.all_gather(keys_local, "cp", axis=0, tiled=True),
        lax.all_gather(values_local, "cp", axis=0, tiled=True),
    )
    attended = attend_forward(queries, keys_all, values_all, visible).astype(jnp.bfloat16)
    branch = lax.psum(jnp.dot(attended, out_full, preferred_element_type=jnp.float32), "tp")
    middle = inputs + branch
    normed_two, inverse_two = normalize(middle)
    hidden_two = (normed_two * gain_two).astype(jnp.bfloat16)
    gate = jnp.dot(hidden_two, gate_full, preferred_element_type=jnp.float32)
    upward = jnp.dot(hidden_two, up_full, preferred_element_type=jnp.float32)
    sigma_gate = jax.nn.sigmoid(gate)
    silu_gate = gate * sigma_gate
    product = (silu_gate * upward).astype(jnp.bfloat16)
    feed = lax.psum(jnp.dot(product, down_full, preferred_element_type=jnp.float32), "tp")
    result = middle + feed
    layer_out = result.astype(jnp.bfloat16).reshape(activations.shape)
    grad_result = cotangent.reshape(row_count, width).astype(jnp.float32)
    grad_feed = grad_result.astype(jnp.bfloat16)
    grad_product = contract_rows(grad_feed, down_full)
    grad_gate = (grad_product * upward * sigma_gate * (1.0 + gate * (1.0 - sigma_gate))).astype(
        jnp.bfloat16
    )
    grad_up = (grad_product * silu_gate).astype(jnp.bfloat16)
    grad_hidden_two = lax.psum(
        contract_rows(grad_gate, gate_full) + contract_rows(grad_up, up_full), "tp"
    )
    grad_gain_two = jnp.sum(grad_hidden_two * normed_two, axis=0)
    grad_middle = grad_result + norm_back(grad_hidden_two, normed_two, inverse_two, gain_two)
    grad_down = contract_cols(product, grad_feed)
    grad_gate_w = contract_cols(hidden_two, grad_gate)
    grad_up_w = contract_cols(hidden_two, grad_up)
    share_gate, share_up, share_down, share_gain_two = (
        lax.psum_scatter(grad_gate_w, "cp", scatter_dimension=0, tiled=True),
        lax.psum_scatter(grad_up_w, "cp", scatter_dimension=0, tiled=True),
        lax.psum_scatter(grad_down, "cp", scatter_dimension=1, tiled=True),
        lax.psum_scatter(grad_gain_two, "cp", scatter_dimension=0, tiled=True),
    )
    grad_branch = grad_middle.astype(jnp.bfloat16)
    grad_attended = contract_rows(grad_branch, out_full).astype(jnp.bfloat16)
    grad_queries, key_terms, value_terms = attend_back(
        queries, keys_all, values_all, grad_attended, visible
    )
    grad_keys, grad_values = (
        lax.psum_scatter(key_terms, "cp", scatter_dimension=0, tiled=True),
        lax.psum_scatter(value_terms, "cp", scatter_dimension=0, tiled=True),
    )
    grad_query_pre = unrotate(grad_queries, my_positions).astype(jnp.bfloat16)
    grad_key_pre = unrotate(grad_keys, my_positions).astype(jnp.bfloat16)
    grad_value_pre = grad_values.astype(jnp.bfloat16)
    local_hidden = (
        contract_rows(grad_query_pre, query_full)
        + contract_rows(grad_key_pre, key_full)
        + contract_rows(grad_value_pre, value_full)
    )
    grad_hidden_one = lax.psum(local_hidden, "tp")
    grad_gain_one = jnp.sum(grad_hidden_one * normed_one, axis=0)
    grad_inputs = grad_middle + norm_back(grad_hidden_one, normed_one, inverse_one, gain_one)
    grad_query_w = contract_cols(hidden_one, grad_query_pre)
    grad_key_w = contract_cols(hidden_one, grad_key_pre)
    grad_value_w = contract_cols(hidden_one, grad_value_pre)
    grad_out_w = contract_cols(attended, grad_branch)
    share_query, share_key, share_value, share_out, share_gain_one = (
        lax.psum_scatter(grad_query_w, "cp", scatter_dimension=0, tiled=True),
        lax.psum_scatter(grad_key_w, "cp", scatter_dimension=0, tiled=True),
        lax.psum_scatter(grad_value_w, "cp", scatter_dimension=0, tiled=True),
        lax.psum_scatter(grad_out_w, "cp", scatter_dimension=1, tiled=True),
        lax.psum_scatter(grad_gain_one, "cp", scatter_dimension=0, tiled=True),
    )
    summed = lax.psum(
        (
            share_gain_one,
            share_query,
            share_key,
            share_value,
            share_out,
            share_gain_two,
            share_gate,
            share_up,
            share_down,
        ),
        "dp",
    )
    input_grad = grad_inputs.astype(jnp.bfloat16).reshape(activations.shape)
    return (
        layer_out,
        input_grad,
        summed[0],
        summed[1],
        summed[2],
        summed[3],
        summed[4],
        summed[5],
        summed[6],
        summed[7],
        summed[8],
    )


def layer(sizes, *args):
    heads = args[3].shape[1] // HEAD_DIM
    zs = sizes["cp"]
    fits = sizes["dp"] == 4 and sizes["tp"] == 2 and heads == 2 * zs
    fits = fits and args[0].shape[3] % 32 == 0 and args[8].shape[1] % (4 * zs * HEAD_DIM) == 0
    fits = fits and args[3].shape[0] % HEAD_DIM == 0 and args[1].shape[1] % args[3].shape[0] == 0
    fits = fits and args[1].shape[1] <= 6 * args[3].shape[0]
    if fits:
        return heads_shards(zs, *args)
    return rows_shards(*args)


def solution(mesh):
    return jax.shard_map(
        functools.partial(layer, dict(mesh.shape)),
        mesh=mesh,
        in_specs=(
            P("dp", "cp", None, None, None),
            P("dp", None),
            P("cp"),
            P("cp", "tp"),
            P("cp", "tp"),
            P("cp", "tp"),
            P("tp", "cp"),
            P("cp"),
            P("cp", "tp"),
            P("cp", "tp"),
            P("tp", "cp"),
            P("dp", "cp", None, None, None),
        ),
        out_specs=(
            P("dp", "cp", None, None, None),
            P("dp", "cp", None, None, None),
            P("cp"),
            P("cp", "tp"),
            P("cp", "tp"),
            P("cp", "tp"),
            P("tp", "cp"),
            P("cp"),
            P("cp", "tp"),
            P("cp", "tp"),
            P("tp", "cp"),
        ),
        check_vma=False,
    )
```

```python
import functools
import math

import jax
import jax.numpy as jnp
import numpy as np
from jax import lax
from jax.experimental import pallas as pl
from jax.experimental.pallas import tpu as pltpu
from jax.sharding import PartitionSpec as P

HEAD_DIM = 128
EPS = 1e-05
SHIFT = math.log(4096.0)
ROPE_BASE = 10000.0
BF = jnp.bfloat16
F32 = jnp.float32
MESH = pl.DeviceIdType.MESH
ANY = pl.ANY
VMEM = pltpu.VMEM
MIB = 2**20


class Net:
    def __init__(self, zs, send_sems, recv_sems):
        self.zs = zs
        self.dp, self.z, self.t = (lax.axis_index(a) for a in ("dp", "cp", "tp"))
        self.a, self.b = lax.div(self.dp, 2), lax.rem(self.dp, 2)
        self.send_sems, self.recv_sems = send_sems, recv_sems
        self.used = 0
        self.open = []

    def along_z(self, s):
        return (self.dp, lax.rem(self.z + s, self.zs), self.t)

    def source_z(self, s):
        return lax.rem(self.z + self.zs - s, self.zs)

    @property
    def over_x(self):
        return (2 * self.a + 1 - self.b, self.z, self.t)

    @property
    def over_y(self):
        return (2 * (1 - self.a) + self.b, self.z, self.t)

    @property
    def sibling(self):
        return (self.dp, self.z, 1 - self.t)

    def meet(self, y=True):
        ways = [self.along_z(s) for s in range(1, self.zs)] + [self.over_x, self.sibling]
        if y:
            ways.append(self.over_y)
        barrier = pltpu.get_barrier_semaphore()
        for way in ways:
            pl.semaphore_signal(barrier, inc=1, device_id=way, device_id_type=MESH)
        pl.semaphore_wait(barrier, len(ways))

    def send(self, src, dst, way):
        k = self.used
        self.used += 1
        copy = pltpu.make_async_remote_copy(
            src, dst, self.send_sems.at[k], self.recv_sems.at[k], device_id=way, device_id_type=MESH
        )
        copy.start()
        self.open.append(copy)
        return copy

    def keep(self, src, dst):
        k = self.used
        self.used += 1
        copy = pltpu.make_async_copy(src, dst, self.send_sems.at[k])
        copy.start()
        return copy

    def finish(self):
        for copy in self.open:
            copy.wait_send()
        self.open = []


def plane_start(net, place, halves):
    own = place(net.dp)
    return net.send(own, own, net.over_x), net.send(own, own, net.over_y)


def plane_relay(net, place, halves, over_x, over_y, sibling=None):
    dx, dy = 2 * net.a + 1 - net.b, 2 * (1 - net.a) + net.b
    dd = 2 * (1 - net.a) + 1 - net.b
    waits = []
    over_x.wait_recv()
    first = halves(place(dx), 0)
    up = net.send(first, first, net.over_y)
    if sibling:
        waits.append(sibling(dx))
    over_y.wait_recv()
    second = halves(place(dy), 1)
    side = net.send(second, second, net.over_x)
    if sibling:
        waits.append(sibling(dy))
    return up, side, dd, waits


def plane_end(net, place, halves, state, sibling=None):
    up, side, dd, waits = state
    up.wait_recv()
    side.wait_recv()
    if sibling:
        waits.append(sibling(dd))
    return waits


def rows_loop(count, step, body):
    def one(i, carry):
        body(pl.ds(pl.multiple_of(i * step, step), step))
        return carry

    lax.fori_loop(0, count // step, one, 0)


def add_rows(out, terms, rows):
    def body(at):
        total = terms[0][at, :].astype(F32)
        for term in terms[1:]:
            total += term[at, :].astype(F32)
        out[at, :] = total.astype(out.dtype)

    rows_loop(rows, 16, body)


class GatherAll:
    def __init__(self, net, src, dst):
        self.net, self.src, self.dst = net, src, dst
        rows = src.shape[0] // 2
        self.halves = lambda ref, k: ref.at[pl.ds(k * rows, rows)]

    def place(self, dp, z):
        return self.dst.at[dp, z, self.net.t]

    def start(self):
        net = self.net
        mine = self.place(net.dp, net.z)
        self.local = net.keep(self.src, mine)
        self.z_sends = [net.send(self.src, mine, net.along_z(s)) for s in range(1, net.zs)]
        self.plane = [(net.z, net.send(self.src, mine, net.over_x), net.send(self.src, mine, net.over_y))]
        self.twin = [net.send(self.src, mine, net.sibling)]

    def to_twin(self, dp, z):
        ref = self.place(dp, z)
        self.twin.append(self.net.send(ref, ref, self.net.sibling))

    def spread(self):
        net = self.net
        for s in range(1, net.zs):
            self.z_sends[s - 1].wait_recv()
            z = net.source_z(s)
            ref = self.place(net.dp, z)
            self.plane.append((z, net.send(ref, ref, net.over_x), net.send(ref, ref, net.over_y)))
            self.to_twin(net.dp, z)

    def relay(self):
        net = self.net
        self.states = []
        for z, over_x, over_y in self.plane:
            place = functools.partial(self.place, z=z)
            self.states.append(
                (z, plane_relay(net, place, self.halves, over_x, over_y, lambda dp, z=z: self.to_twin(dp, z)))
            )

    def end(self):
        for z, state in self.states:
            place = functools.partial(self.place, z=z)
            plane_end(self.net, place, self.halves, state, lambda dp, z=z: self.to_twin(dp, z))
        for copy in self.twin:
            copy.wait_recv()
        self.local.wait()


class GatherGroup:
    def __init__(self, net, src, dst, own_lanes=None):
        self.net, self.src, self.dst, self.own_lanes = net, src, dst, own_lanes
        self.rows = src.shape[0]

    def place(self, b, z, t=None):
        t = self.net.t if t is None else t
        last = 2 * self.net.zs - 1
        at = ((last + 1) * b + z + t * (last - 2 * z)) * self.rows
        return self.dst.at[pl.ds(pl.multiple_of(at, self.rows), self.rows)]

    def start(self):
        net = self.net
        mine = self.place(net.b, net.z)
        self.z_sends = [net.send(self.src, mine, net.along_z(s)) for s in range(1, net.zs)]
        self.over = [(net.z, net.send(self.src, mine, net.over_x))]
        self.twin, self.local = [], []
        if self.own_lanes is None:
            self.local.append(net.keep(self.src, mine))
            self.twin.append((net.b, net.z, net.send(self.src, mine, net.sibling)))
        else:
            for t in (0, 1):
                self.local.append(net.keep(self.own_lanes.at[t], self.place(net.b, net.z, t)))

    def to_twin(self, b, z):
        ref = self.place(b, z)
        self.twin.append((b, z, self.net.send(ref, ref, self.net.sibling)))

    def spread(self):
        net = self.net
        for s in range(1, net.zs):
            self.z_sends[s - 1].wait_recv()
            z = net.source_z(s)
            ref = self.place(net.b, z)
            self.over.append((z, net.send(ref, ref, net.over_x)))
            self.to_twin(net.b, z)

    def far(self):
        net = self.net
        for z, copy in self.over:
            copy.wait_recv()
            self.to_twin(1 - net.b, z)

    def end(self):
        for _, _, copy in self.twin:
            copy.wait_recv()
        for copy in self.local:
            copy.wait()


class SumGroup:
    def __init__(self, net, part, sib, far, landed):
        self.net, self.part, self.sib, self.far, self.landed = net, part, sib, far, landed
        self.rows = part.shape[3]
        self.twin, self.over, self.z_sends = {}, [], []

    def order(self):
        return [lax.rem(self.net.z + s + 1, self.net.zs) for s in range(self.net.zs)]

    def give(self, k):
        net = self.net
        b = net.b if k else 1 - net.b
        for s, z in enumerate(self.order()):
            self.twin[k, s] = net.send(self.part.at[b, 1 - net.t, z], self.sib.at[b, z], net.sibling)

    def take(self, k):
        net = self.net
        b = net.b if k else 1 - net.b
        for s, z in enumerate(self.order()):
            self.twin[k, s].wait_recv()
            own = self.part.at[b, net.t, z]
            add_rows(own, [own, self.sib.at[b, z]], self.rows)
            if k == 0:
                self.over.append(net.send(own, self.far.at[z], net.over_x))

    def along(self):
        net = self.net
        for s, z in enumerate(self.order()):
            self.over[s].wait_recv()
            last = s == net.zs - 1
            own = self.part.at[net.b, net.t, z]
            out = self.landed.at[net.z] if last else own
            add_rows(out, [own, self.far.at[z]], self.rows)
            if not last:
                self.z_sends.append(net.send(out, self.landed.at[net.z], net.along_z(s + 1)))

    def end(self):
        for copy in self.z_sends:
            copy.wait_recv()


class SumAll:
    def __init__(self, net, part, own, sib, one, two, landed):
        self.net, self.part, self.own, self.sib = net, part, own, sib
        self.one, self.two, self.landed = one, two, landed
        self.half = part.shape[3] // 2

    def order(self):
        net = self.net
        return [lax.rem(net.z + s + 1, net.zs) for s in range(net.zs)]

    def places(self):
        a, b = self.net.a, self.net.b
        return [2 * (1 - a) + 1 - b, 2 * a + 1 - b, 2 * (1 - a) + b, 2 * a + b]

    def start(self):
        net = self.net
        self.twin, self.mine = [], []
        for z in self.order():
            for dp in self.places():
                self.twin.append(net.send(self.part.at[dp, z, 1 - net.t], self.sib.at[dp, z], net.sibling))
                self.mine.append(net.keep(self.part.at[dp, z, net.t], self.own.at[dp, z]))

    def upper(self, ref):
        return ref.at[pl.ds(0, self.half)]

    def lower(self, ref):
        return ref.at[pl.ds(self.half, self.half)]

    def first(self, s):
        net = self.net
        z = self.order()[s]
        dd, dx, dy, me = self.places()
        for j, dp in enumerate((dd, dx, dy, me)):
            self.twin[4 * s + j].wait_recv()
            self.mine[4 * s + j].wait()
            add_rows(self.own.at[dp, z], [self.own.at[dp, z], self.sib.at[dp, z]], 2 * self.half)
        self.ones = getattr(self, "ones", [])
        self.ones.append(
            (
                net.send(self.upper(self.own.at[dd, z]), self.one.at[0, 0, z], net.over_x),
                net.send(self.upper(self.own.at[dx, z]), self.one.at[0, 1, z], net.over_x),
                net.send(self.lower(self.own.at[dd, z]), self.one.at[1, 0, z], net.over_y),
                net.send(self.lower(self.own.at[dy, z]), self.one.at[1, 1, z], net.over_y),
            )
        )

    def second(self, s):
        net = self.net
        z = self.order()[s]
        dd, dx, dy, me = self.places()
        x_dd, x_me, y_dd, y_me = self.ones[s]
        self.twos = getattr(self, "twos", [])
        x_dd.wait_recv()
        out = self.upper(self.own.at[dy, z])
        add_rows(out, [out, self.one.at[0, 0, z]], self.half)
        up = net.send(out, self.two.at[0, z], net.over_y)
        y_dd.wait_recv()
        out = self.lower(self.own.at[dx, z])
        add_rows(out, [out, self.one.at[1, 0, z]], self.half)
        side = net.send(out, self.two.at[1, z], net.over_x)
        self.twos.append((up, side))

    def third(self, s):
        net = self.net
        z = self.order()[s]
        dd, dx, dy, me = self.places()
        _, x_me, _, y_me = self.ones[s]
        up, side = self.twos[s]
        last = s == net.zs - 1
        out = self.landed.at[net.z] if last else self.own.at[me, z]
        x_me.wait_recv()
        up.wait_recv()
        mine = self.own.at[me, z]
        add_rows(self.upper(out), [self.upper(mine), self.one.at[0, 1, z], self.two.at[0, z]], self.half)
        y_me.wait_recv()
        side.wait_recv()
        add_rows(self.lower(out), [self.lower(mine), self.one.at[1, 1, z], self.two.at[1, z]], self.half)
        self.z_sends = getattr(self, "z_sends", [])
        if not last:
            self.z_sends.append(net.send(out, self.landed.at[net.z], net.along_z(s + 1)))

    def end(self):
        for copy in self.z_sends:
            copy.wait_recv()


class SpreadGrads:
    def __init__(self, net, src, dst, halves):
        self.net, self.src, self.dst, self.halves = net, src, dst, halves
        self.z_sends, self.plane, self.states = [], {}, []

    def mine(self):
        return self.dst(self.net.dp, self.net.z)

    def start(self):
        self.own()
        for s in range(1, self.net.zs):
            self.go(s)

    def own(self):
        self.local = self.net.keep(self.src(self.net.z), self.mine())

    def go(self, s):
        net = self.net
        self.z_sends.append(net.send(self.src(lax.rem(net.z + s, net.zs)), self.mine(), net.along_z(s)))

    def spread(self, s):
        net = self.net
        z = net.source_z(s)
        ref = self.dst(net.dp, z)
        if s:
            self.z_sends[s - 1].wait_recv()
            src = ref
        else:
            src = self.src(net.z)
        self.plane[s] = (z, net.send(src, ref, net.over_x), net.send(src, ref, net.over_y))

    def relay(self, s):
        z, over_x, over_y = self.plane[s]
        place = lambda dp: self.dst(dp, z)
        self.states.append(plane_relay(self.net, place, self.halves, over_x, over_y))

    def end(self):
        for state in self.states:
            plane_end(self.net, None, self.halves, state)
        self.local.wait()


def half_rows(ref, k):
    n = ref.shape[0] // 2
    return ref.at[pl.ds(k * n, n)]


def aligned(i, size):
    return pl.ds(pl.multiple_of(i * size, size), size)


def loop(count, body):
    def one(i, carry):
        body(i)
        return carry

    lax.fori_loop(0, count, one, 0)


def dot(left, right, dims=((1,), (0,)), kind=F32):
    return lax.dot_general(left, right, (dims, ((), ())), preferred_element_type=F32).astype(kind)


def turn(u, cosine, sine):
    return u * cosine + pltpu.roll(u, HEAD_DIM // 2, 1) * sine


def column(row, start, count):
    n = row.shape[1]
    here = lax.broadcasted_iota(jnp.int32, (count, n), 1) == start + lax.broadcasted_iota(jnp.int32, (count, n), 0)
    return jnp.sum(jnp.where(here, row, 0.0), axis=1, keepdims=True)


def seen(row, start, count, flip=False):
    n = row.shape[1]
    same = column(row, start, count) == row
    mine = start + lax.broadcasted_iota(jnp.int32, (count, n), 0)
    other = lax.broadcasted_iota(jnp.int32, (count, n), 1)
    return same & ((mine <= other) if flip else (other <= mine))


def sigma_of(left, right):
    return jax.nn.sigmoid(dot(left, right, ((1,), (1,))) * HEAD_DIM**-0.5 - SHIFT)


def call(kernel, name, outs, scratch, count, args, vmem):
    return pl.pallas_call(
        kernel,
        out_shape=[jax.ShapeDtypeStruct(shape, kind) for shape, kind, _ in outs],
        in_specs=[pl.BlockSpec(memory_space=ANY)] * len(args),
        out_specs=[pl.BlockSpec(memory_space=space) for _, _, space in outs],
        scratch_shapes=list(scratch) + [pltpu.SemaphoreType.DMA((count,)), pltpu.SemaphoreType.DMA((count,))],
        compiler_params=pltpu.CompilerParams(
            collective_id=name, has_side_effects=True, vmem_limit_bytes=vmem * MIB
        ),
    )(*args)


def forward_kernel(
    zs, x, wq, wk, wv, wo, small, cosine, sine, wg, wu, wd, cot,
    hidden_out, qkv_out, attended_out, qkv_w_out, out_w_out, gains_out, docs_out, middle, h2_all, cot_all, gu_w, down_w,
    x_all, h1, qkv_w, out_w, small_z, small_x, gains, docs, cos_v, sin_v, qkv, attended, part, sib, far, landed,
    x_lane, h2, mid_v, send_sems, recv_sems,
):
    net = Net(zs, send_sems, recv_sems)
    net.meet()
    deep, wide = wg.shape[0], gu_w.shape[1] // 2
    seq = docs.shape[1]
    half, side = deep // 2, HEAD_DIM // 2
    gather = GatherGroup(net, x.at[net.t], x_all, own_lanes=x)
    gather.start()
    small_waits = [net.send(small, small_z.at[net.z], net.along_z(s)) for s in range(1, zs)]
    small_waits.append(net.send(small, small_x.at[net.b], net.over_x))
    local = [net.keep(small, small_z.at[net.z]), net.keep(small, small_x.at[net.b])]
    local += [net.keep(cosine, cos_v), net.keep(sine, sin_v)]
    lane = net.keep(x.at[net.t], x_lane)

    def head(z):
        return aligned(net.b * zs + z, HEAD_DIM)

    mine = aligned(net.z, deep)
    my_half = pl.ds(pl.multiple_of(net.a * half, half), half)
    qkv_sends, out_sends, w_local = [], [], []
    for m, w in enumerate((wq, wk, wv)):
        col = pl.ds(m * HEAD_DIM, HEAD_DIM)
        w_local.append(net.keep(w.at[:, head(net.z)], qkv_w.at[mine, col]))
    for s in range(1, zs):
        z = lax.rem(net.z + s, zs)
        rows = pl.ds(pl.multiple_of(net.z * deep + net.a * half, half), half)
        qkv_sends.append(
            [
                net.send(w.at[my_half, head(z)], qkv_w.at[rows, pl.ds(m * HEAD_DIM, HEAD_DIM)], net.along_z(s))
                for m, w in enumerate((wq, wk, wv))
            ]
        )
    out_rows = pl.ds(pl.multiple_of(net.a * side, side), side)
    w_local.append(net.keep(wo.at[head(net.z)], out_w.at[:, mine]))
    for s in range(1, zs):
        z = lax.rem(net.z + s, zs)
        at = pl.ds(pl.multiple_of((net.b * zs + z) * HEAD_DIM + net.a * side, side), side)
        out_sends.append(net.send(wo.at[at], out_w.at[out_rows, mine], net.along_z(s)))

    cotan = GatherAll(net, cot.at[net.t], cot_all)
    cotan.start()
    mlp_waits, mlp_local = [], []

    def block(z):
        return aligned(net.dp * zs + z, wide)

    mlp = (
        (lambda z: wg.at[:, block(z)], gu_w.at[mine, pl.ds(0, wide)]),
        (lambda z: wu.at[:, block(z)], gu_w.at[mine, pl.ds(wide, wide)]),
        (lambda z: wd.at[block(z)], down_w.at[:, mine]),
    )
    for src, dst in mlp:
        mlp_local.append(net.keep(src(net.z), dst))

    def fetch(k):
        src, dst = mlp[k]
        for s in range(1, zs):
            mlp_waits.append(net.send(src(lax.rem(net.z + s, zs)), dst, net.along_z(s)))

    fetch(0)

    for copy in small_waits:
        copy.wait_recv()
    for copy in local:
        copy.wait()
    for z in range(zs):
        gains[0:1, z * deep : (z + 1) * deep] = small_z[z, 0:1, :]
        gains[1:2, z * deep : (z + 1) * deep] = small_z[z, 1:2, :]
    for b in range(2):
        for k in range(seq // deep):
            docs[b : b + 1, k * deep : (k + 1) * deep] = small_x[b, 2 + k : 3 + k, :]

    def norm_block(ref_at):
        def body(i):
            at = pl.ds(pl.multiple_of(ref_at + i * 16, 16), 16)
            rows = x_all[at, :].astype(F32)
            inverse = lax.rsqrt(jnp.mean(rows * rows, axis=-1, keepdims=True) + EPS)
            h1[at, :] = (rows * inverse * gains[0:1, :]).astype(BF)

        loop(x.shape[1] // 16, body)

    rows = x.shape[1]
    last = 2 * zs - 1

    def offset(b, z, t):
        return ((last + 1) * b + z + t * (last - 2 * z)) * rows

    gather.spread()
    for copy in gather.local:
        copy.wait()
    gather.local = []
    for t in (0, 1):
        norm_block(offset(net.b, net.z, t))
    for s in range(1, zs):
        norm_block(offset(net.b, net.source_z(s), net.t))
    qkv_y = []
    for s in range(1, zs):
        for copy in qkv_sends[s - 1]:
            copy.wait_recv()
        at = qkv_w.at[pl.ds(pl.multiple_of(net.source_z(s) * deep + net.a * half, half), half)]
        qkv_y.append(net.send(at, at, net.over_y))
    gather.far()
    for z, _ in gather.over:
        norm_block(offset(1 - net.b, z, net.t))
    out_y = []
    for s in range(1, zs):
        out_sends[s - 1].wait_recv()
        at = out_w.at[out_rows, aligned(net.source_z(s), deep)]
        out_y.append(net.send(at, at, net.over_y))
    for b, z, copy in gather.twin:
        copy.wait_recv()
        norm_block(offset(b, z, 1 - net.t))
    for copy in qkv_y:
        copy.wait_recv()
    for copy in w_local:
        copy.wait()
    cotan.spread()
    for copy in out_y:
        copy.wait_recv()

    branch = SumGroup(net, part, sib, far, landed)
    tile = 128
    for k in range(2):
        b = net.b if k else 1 - net.b
        base = b * seq

        def project(i):
            at = pl.ds(pl.multiple_of(base + i * 256, 256), 256)
            pos = aligned(i, 256)
            pre = dot(h1[at, :], qkv_w[...])
            c, s = cos_v[pos, :], sin_v[pos, :]
            qkv[at, 0:HEAD_DIM] = turn(pre[:, 0:HEAD_DIM], c, s).astype(BF)
            qkv[at, HEAD_DIM : 2 * HEAD_DIM] = turn(pre[:, HEAD_DIM : 2 * HEAD_DIM], c, s).astype(BF)
            qkv[at, 2 * HEAD_DIM : 3 * HEAD_DIM] = pre[:, 2 * HEAD_DIM : 3 * HEAD_DIM].astype(BF)

        loop(seq // 256, project)
        every = pl.ds(pl.multiple_of(base, seq), seq)
        row = docs[pl.ds(b, 1), :]

        def attend(i):
            at = pl.ds(pl.multiple_of(base + i * tile, tile), tile)
            sigma = sigma_of(qkv[at, 0:HEAD_DIM], qkv[every, HEAD_DIM : 2 * HEAD_DIM])
            weights = jnp.where(seen(row, i * tile, tile), sigma, 0.0).astype(BF)
            found = dot(weights, qkv[every, 2 * HEAD_DIM : 3 * HEAD_DIM], kind=BF)
            attended[at, :] = found
            out = dot(found, out_w[...], kind=BF)
            for j in range(tile // rows):
                blk = i * (tile // rows) + j
                t = lax.div(blk, zs)
                z = (1 - t) * blk + t * (last - blk)
                part[b, t, z] = out[j * rows : (j + 1) * rows, :]

        loop(seq // tile, attend)
        branch.give(k)
    saved = [
        net.keep(h1, hidden_out), net.keep(qkv, qkv_out), net.keep(attended, attended_out),
        net.keep(qkv_w, qkv_w_out), net.keep(out_w, out_w_out), net.keep(gains, gains_out), net.keep(docs, docs_out),
    ]
    branch.take(0)
    branch.take(1)
    branch.along()
    cotan.relay()
    lane.wait()
    branch.end()

    def body(i):
        at = aligned(i, 16)
        total = x_lane[at, :].astype(F32)
        for z in range(zs):
            total += landed[z, at, :].astype(F32)
        mid_v[at, :] = total
        inverse = lax.rsqrt(jnp.mean(total * total, axis=-1, keepdims=True) + EPS)
        h2[at, :] = (total * inverse * gains[1:2, :]).astype(BF)

    loop(rows // 16, body)
    saved.append(net.keep(mid_v, middle))
    hidden = GatherAll(net, h2, h2_all)
    hidden.start()
    fetch(1)
    fetch(2)
    hidden.spread()
    cotan.end()
    hidden.relay()
    hidden.end()
    for copy in saved:
        copy.wait()
    for copy in mlp_waits:
        copy.wait_recv()
    for copy in mlp_local:
        copy.wait()
    net.finish()


def backward_kernel(
    zs, gh_part, feed_part, gu_grad, down_grad, middle, cot, x, gains_in, docs_in, cosine, sine,
    hidden_in, qkv_in, attended_in, qkv_w_in, out_w_in,
    layer_out, input_grad, q_out, k_out, v_out, o_out, gate_out, up_out, down_out, gains_out,
    own, sib, one, two, landed, own_f, sib_f, one_f, two_f, landed_f, part, sib_1, far_1, landed_1,
    h1, qkv, attended, qkv_w, out_w, gbr_all, gqkv, gains, docs, cos_v, sin_v, hg, mid_v, cot_v, x_v, gm_v, gbr_v, out_v,
    lo_v, gsum, g_far, g_land, q_give, q_own, q_land, o_part, o_own, o_land, send_sems, recv_sems,
):
    net = Net(zs, send_sems, recv_sems)
    net.meet()
    deep, wide = gate_out.shape[0], gu_grad.shape[1] // 2
    seq = docs.shape[1]
    half, side = deep // 2, HEAD_DIM // 2
    rows = x.shape[1]
    last = 2 * zs - 1
    scale = HEAD_DIM**-0.5
    hidden = SumAll(net, gh_part, own, sib, one, two, landed)
    hidden.start()
    feed = SumAll(net, feed_part, own_f, sib_f, one_f, two_f, landed_f)
    local = [net.keep(middle, mid_v), net.keep(cot.at[net.t], cot_v), net.keep(gains_in, gains)]
    local += [net.keep(x.at[net.t], x_v), net.keep(docs_in, docs), net.keep(cosine, cos_v), net.keep(sine, sin_v)]
    local += [net.keep(qkv_in, qkv), net.keep(attended_in, attended), net.keep(qkv_w_in, qkv_w)]
    local += [net.keep(out_w_in, out_w), net.keep(hidden_in, h1)]

    def block(dp, z):
        return aligned(dp * zs + z, wide)

    grads = [
        SpreadGrads(
            net,
            lambda z: gu_grad.at[aligned(z, deep), pl.ds(0, wide)],
            lambda dp, z: gate_out.at[:, block(dp, z)],
            half_rows,
        ),
        SpreadGrads(
            net,
            lambda z: gu_grad.at[aligned(z, deep), pl.ds(wide, wide)],
            lambda dp, z: up_out.at[:, block(dp, z)],
            half_rows,
        ),
        SpreadGrads(
            net,
            lambda z: down_grad.at[:, aligned(z, deep)],
            lambda dp, z: down_out.at[block(dp, z)],
            half_rows,
        ),
    ]
    grads[0].start()
    grads[1].start()
    feed.start()
    for s in range(zs):
        hidden.first(s)
    for s in range(zs):
        hidden.second(s)
    for s in range(zs):
        hidden.third(s)
    for s in range(zs):
        feed.first(s)
    grads[2].start()
    for copy in local:
        copy.wait()
    hidden.end()
    gsum[...] = jnp.zeros_like(gsum)

    def total_of(ref, at):
        total = ref[0, at, :].astype(F32)
        for z in range(1, zs):
            total += ref[z, at, :].astype(F32)
        return total

    def norm_back(inputs, total, gain, k):
        inverse = lax.rsqrt(jnp.mean(inputs * inputs, axis=-1, keepdims=True) + EPS)
        normed = inputs * inverse
        prod = total * normed
        gsum[k] += prod[0:8, :] + prod[8:16, :]
        scaled = total * gain
        return inverse * (scaled - normed * jnp.mean(scaled * normed, axis=-1, keepdims=True))

    def back_two(i):
        at = aligned(i, 16)
        grad = cot_v[at, :].astype(F32) + norm_back(mid_v[at, :], total_of(landed, at), gains[1:2, :], 1)
        gm_v[at, :] = grad
        gbr_v[at, :] = grad.astype(BF)

    loop(rows // 16, back_two)
    gather = GatherGroup(net, gbr_v, gbr_all)
    gather.start()
    for s in range(zs):
        feed.second(s)
    gather.spread()
    for s in range(zs):
        feed.third(s)
    for s in range(zs):
        grads[0].spread(s)
    gather.far()
    gather.end()

    branch = SumGroup(net, part, sib_1, far_1, landed_1)
    tile = 128
    for k in range(2):
        b = net.b if k else 1 - net.b
        base = b * seq
        every = pl.ds(pl.multiple_of(base, seq), seq)
        row = docs[pl.ds(b, 1), :]

        def heads_grad(i):
            at = pl.ds(pl.multiple_of(base + i * 256, 256), 256)
            hg[aligned(i, 256), :] = dot(gbr_all[at, :], out_w[...], ((1,), (1,)), BF)

        loop(seq // 256, heads_grad)

        def by_query(i):
            at = pl.ds(pl.multiple_of(base + i * tile, tile), tile)
            pos = aligned(i, tile)
            keys = qkv[every, HEAD_DIM : 2 * HEAD_DIM]
            sigma = sigma_of(qkv[at, 0:HEAD_DIM], keys)
            gw = dot(hg[pos, :], qkv[every, 2 * HEAD_DIM : 3 * HEAD_DIM], ((1,), (1,)))
            gs = jnp.where(seen(row, i * tile, tile), gw * sigma * (1.0 - sigma), 0.0).astype(BF)
            gq = dot(gs, keys) * scale
            gqkv[at, 0:HEAD_DIM] = turn(gq, cos_v[pos, :], -sin_v[pos, :]).astype(BF)

        loop(seq // tile, by_query)

        def by_key(i):
            at = pl.ds(pl.multiple_of(base + i * tile, tile), tile)
            pos = aligned(i, tile)
            queries = qkv[every, 0:HEAD_DIM]
            sigma = sigma_of(qkv[at, HEAD_DIM : 2 * HEAD_DIM], queries)
            gw = dot(qkv[at, 2 * HEAD_DIM : 3 * HEAD_DIM], hg[...], ((1,), (1,)))
            mask = seen(row, i * tile, tile, flip=True)
            gs = jnp.where(mask, gw * sigma * (1.0 - sigma), 0.0).astype(BF)
            weights = jnp.where(mask, sigma, 0.0).astype(BF)
            gk = dot(gs, queries) * scale
            gqkv[at, HEAD_DIM : 2 * HEAD_DIM] = turn(gk, cos_v[pos, :], -sin_v[pos, :]).astype(BF)
            gqkv[at, 2 * HEAD_DIM : 3 * HEAD_DIM] = dot(weights, hg[...], kind=BF)

        loop(seq // tile, by_key)

        def back_one(i):
            at = pl.ds(pl.multiple_of(base + i * tile, tile), tile)
            out = dot(gqkv[at, :], qkv_w[...], ((1,), (1,)), BF)
            for j in range(tile // rows):
                blk = i * (tile // rows) + j
                t = lax.div(blk, zs)
                z = (1 - t) * blk + t * (last - blk)
                part[b, t, z] = out[j * rows : (j + 1) * rows, :]

        loop(seq // tile, back_one)
        branch.give(k)
    branch.take(0)
    branch.take(1)

    def qkv_grad(z, a):
        at = pl.ds(pl.multiple_of(z * deep + a * half, half), half)
        return dot(h1[:, at], gqkv[...], ((0,), (0,)), BF)

    def out_grad(z):
        o_part[z] = dot(attended[...], gbr_all[:, aligned(z, deep)], ((0,), (0,)), BF)

    def theirs(z):
        q_give[z] = qkv_grad(z, 1 - net.a)

    def ours(z):
        q_own[z] = qkv_grad(z, net.a)

    def side_rows(a):
        return pl.ds(pl.multiple_of(a * side, side), side)

    loop(zs, out_grad)
    loop(zs, theirs)
    swaps = []
    for s in range(zs):
        z = lax.rem(net.z + s + 1, zs)
        swaps.append(
            (
                z,
                net.send(q_give.at[z], q_land.at[z], net.over_y),
                net.send(o_part.at[z, side_rows(1 - net.a)], o_land.at[z], net.over_y),
            )
        )
    loop(zs, ours)
    branch.along()

    def q_place(ref):
        def place(dp, z):
            a, b = lax.div(dp, 2), lax.rem(dp, 2)
            return ref.at[pl.ds(pl.multiple_of(a * half, half), half), aligned(b * zs + z, HEAD_DIM)]

        return place

    def o_place(dp, z):
        a, b = lax.div(dp, 2), lax.rem(dp, 2)
        return o_out.at[pl.ds(pl.multiple_of((b * zs + z) * HEAD_DIM + a * side, side), side)]

    late = [
        SpreadGrads(net, lambda z, m=m: q_own.at[z, :, pl.ds(m * HEAD_DIM, HEAD_DIM)], q_place(ref), half_rows)
        for m, ref in enumerate((q_out, k_out, v_out))
    ]
    late.append(SpreadGrads(net, lambda z: o_own.at[z], o_place, half_rows))
    for s, (z, q_in, o_in) in enumerate(swaps):
        q_in.wait_recv()
        add_rows(q_own.at[z], [q_own.at[z], q_land.at[z]], half)
        o_in.wait_recv()
        add_rows(o_own.at[z], [o_part.at[z, side_rows(net.a)], o_land.at[z]], side)
        for grad in late:
            if s < zs - 1:
                grad.go(s + 1)
            else:
                grad.own()
    for s in range(zs):
        grads[1].spread(s)
    branch.end()

    def back_last(i):
        at = aligned(i, 16)
        grad = gm_v[at, :] + norm_back(x_v[at, :].astype(F32), total_of(landed_1, at), gains[0:1, :], 0)
        out_v[at, :] = grad.astype(BF)

    loop(rows // 16, back_last)
    outs = [net.keep(out_v, input_grad.at[net.t])]
    pairs = [net.send(out_v, input_grad.at[net.t], net.sibling)]
    for s in range(zs):
        grads[0].relay(s)
    feed.end()

    def close(i):
        at = aligned(i, 16)
        lo_v[at, :] = (mid_v[at, :] + total_of(landed_f, at)).astype(BF)

    loop(rows // 16, close)
    outs.append(net.keep(lo_v, layer_out.at[net.t]))
    pairs.append(net.send(lo_v, layer_out.at[net.t], net.sibling))
    for k, way in enumerate((net.sibling, net.over_x, net.over_y)):
        swap = net.send(gsum, g_far.at[k], way)
        swap.wait()
        net.open = [c for c in net.open if c is not swap]
        gsum[...] = gsum[...] + g_far[k]

    def cut(z):
        return gsum.at[:, :, aligned(z, deep)]

    z_gain = [net.send(cut(lax.rem(net.z + s, zs)), g_land.at[net.z], net.along_z(s)) for s in range(1, zs)]
    outs.append(net.keep(cut(net.z), g_land.at[net.z]))
    for s in range(zs):
        for grad in late:
            grad.spread(s)
    for s in range(zs):
        grads[2].spread(s)
    for s in range(zs):
        grads[1].relay(s)
    for s in range(zs):
        for grad in late:
            grad.relay(s)
    for s in range(zs):
        grads[2].relay(s)
    for grad in grads + late:
        grad.end()
    for copy in outs:
        copy.wait()
    for copy in z_gain + pairs:
        copy.wait_recv()
    total = g_land[0]
    for z in range(1, zs):
        total += g_land[z]
    gains_out[...] = total
    net.finish()


def rope_tables(seq):
    half_dim = HEAD_DIM // 2
    frequency = ROPE_BASE ** (-np.arange(half_dim, dtype=np.float32) / half_dim)
    angle = np.arange(seq, dtype=np.float32)[:, None] * frequency.astype(np.float32)[None, :]
    cosine, sine = np.cos(angle), np.sin(angle)
    return (
        np.concatenate([cosine, cosine], axis=1).astype(np.float32),
        np.concatenate([-sine, sine], axis=1).astype(np.float32),
    )


def heads_shards(
    zs, activations, document_ids, attn_gain, w_query, w_key, w_value, w_out, mlp_gain, w_gate, w_up, w_down, cotangent
):
    stretch, width = activations.shape[3:]
    deep = w_query.shape[0]
    seq = document_ids.shape[1]
    pair = 2 * seq
    wide = w_gate.shape[1] // (4 * zs)
    x = activations.reshape(2, stretch, width)
    cot = cotangent.reshape(2, stretch, width)
    small = jnp.stack([attn_gain.astype(F32), mlp_gain.astype(F32)])
    docs_rows = document_ids.astype(F32).reshape(seq // deep, deep)
    small = jnp.concatenate([small, docs_rows, jnp.zeros((6 - seq // deep, deep), F32)])
    cosine, sine = (jnp.asarray(table) for table in rope_tables(seq))
    half = stretch // 2
    hidden, qkv, attended, qkv_w, out_w, gains, docs, middle, h2_all, cot_all, gu_w, down_w = call(
        functools.partial(forward_kernel, zs),
        1,
        [
            ((pair, width), BF, ANY),
            ((pair, 3 * HEAD_DIM), BF, ANY),
            ((pair, HEAD_DIM), BF, ANY),
            ((width, 3 * HEAD_DIM), BF, ANY),
            ((HEAD_DIM, width), BF, ANY),
            ((8, width), F32, ANY),
            ((8, seq), F32, ANY),
            ((stretch, width), F32, ANY),
            ((4, zs, 2, stretch, width), BF, ANY),
            ((4, zs, 2, stretch, width), BF, ANY),
            ((width, 2 * wide), BF, ANY),
            ((wide, width), BF, ANY),
        ],
        [
            VMEM((pair, width), BF),
            VMEM((pair, width), BF),
            VMEM((width, 3 * HEAD_DIM), BF),
            VMEM((HEAD_DIM, width), BF),
            VMEM((zs, 8, deep), F32),
            VMEM((2, 8, deep), F32),
            VMEM((8, width), F32),
            VMEM((8, seq), F32),
            VMEM((seq, HEAD_DIM), F32),
            VMEM((seq, HEAD_DIM), F32),
            VMEM((pair, 3 * HEAD_DIM), BF),
            VMEM((pair, HEAD_DIM), BF),
            VMEM((2, 2, zs, stretch, width), BF),
            VMEM((2, zs, stretch, width), BF),
            VMEM((zs, stretch, width), BF),
            VMEM((zs, stretch, width), BF),
            VMEM((stretch, width), BF),
            VMEM((stretch, width), BF),
            VMEM((stretch, width), F32),
        ],
        240,
        (x, w_query, w_key, w_value, w_out, small, cosine, sine, w_gate, w_up, w_down, cot),
        52,
    )

    h2 = h2_all.reshape(4 * seq, width)
    cots = cot_all.reshape(4 * seq, width)
    gate_up = dot(h2, gu_w)
    gate, upward = gate_up[:, :wide], gate_up[:, wide:]
    grad_product = dot(cots, down_w, ((1,), (1,)))
    sigma_gate = jax.nn.sigmoid(gate)
    silu = gate * sigma_gate
    product = (silu * upward).astype(BF)
    grad_gate = (grad_product * upward * sigma_gate * (1.0 + gate * (1.0 - sigma_gate))).astype(BF)
    grad_up = (grad_product * silu).astype(BF)
    grad_gu = jnp.concatenate([grad_gate, grad_up], axis=1)
    gh_part = dot(grad_gu, gu_w, ((1,), (1,)), BF).reshape(4, zs, 2, stretch, width)
    feed_part = dot(product, down_w, kind=BF).reshape(4, zs, 2, stretch, width)
    gu_grad = dot(h2, grad_gu, ((0,), (0,)), BF)
    down_grad = dot(product, cots, ((0,), (0,)), BF)

    sum_scratch = [
        VMEM((4, zs, stretch, width), BF),
        VMEM((4, zs, stretch, width), BF),
        VMEM((2, 2, zs, half, width), BF),
        VMEM((2, zs, half, width), BF),
        VMEM((zs, stretch, width), BF),
    ]
    layer_out, input_grad, q_g, k_g, v_g, o_g, gate_g, up_g, down_g, gains_g = call(
        functools.partial(backward_kernel, zs),
        2,
        [
            ((2, stretch, width), BF, ANY),
            ((2, stretch, width), BF, ANY),
            (w_query.shape, BF, ANY),
            (w_key.shape, BF, ANY),
            (w_value.shape, BF, ANY),
            (w_out.shape, BF, ANY),
            (w_gate.shape, BF, ANY),
            (w_up.shape, BF, ANY),
            (w_down.shape, BF, ANY),
            ((2, 8, deep), F32, VMEM),
        ],
        sum_scratch
        + sum_scratch
        + [
            VMEM((2, 2, zs, stretch, width), BF),
            VMEM((2, zs, stretch, width), BF),
            VMEM((zs, stretch, width), BF),
            VMEM((zs, stretch, width), BF),
            VMEM((pair, width), BF),
            VMEM((pair, 3 * HEAD_DIM), BF),
            VMEM((pair, HEAD_DIM), BF),
            VMEM((width, 3 * HEAD_DIM), BF),
            VMEM((HEAD_DIM, width), BF),
            VMEM((pair, width), BF),
            VMEM((pair, 3 * HEAD_DIM), BF),
            VMEM((8, width), F32),
            VMEM((8, seq), F32),
            VMEM((seq, HEAD_DIM), F32),
            VMEM((seq, HEAD_DIM), F32),
            VMEM((seq, HEAD_DIM), BF),
            VMEM((stretch, width), F32),
            VMEM((stretch, width), BF),
            VMEM((stretch, width), BF),
            VMEM((stretch, width), F32),
            VMEM((stretch, width), BF),
            VMEM((stretch, width), BF),
            VMEM((stretch, width), BF),
            VMEM((2, 8, width), F32),
            VMEM((3, 2, 8, width), F32),
            VMEM((zs, 2, 8, deep), F32),
            VMEM((zs, deep // 2, 3 * HEAD_DIM), BF),
            VMEM((zs, deep // 2, 3 * HEAD_DIM), BF),
            VMEM((zs, deep // 2, 3 * HEAD_DIM), BF),
            VMEM((zs, HEAD_DIM, deep), BF),
            VMEM((zs, HEAD_DIM // 2, deep), BF),
            VMEM((zs, HEAD_DIM // 2, deep), BF),
        ],
        400,
        (
            gh_part, feed_part, gu_grad, down_grad, middle, cot, x, gains, docs, cosine, sine,
            hidden, qkv, attended, qkv_w, out_w,
        ),
        60,
    )
    gain_grads = jnp.sum(gains_g, axis=1)
    return (
        layer_out.reshape(activations.shape),
        input_grad.reshape(activations.shape),
        gain_grads[0],
        q_g.astype(F32),
        k_g.astype(F32),
        v_g.astype(F32),
        o_g.astype(F32),
        gain_grads[1],
        gate_g.astype(F32),
        up_g.astype(F32),
        down_g.astype(F32),
    )


def angles(positions):
    half_dim = HEAD_DIM // 2
    frequency = ROPE_BASE ** (-jnp.arange(half_dim, dtype=jnp.float32) / half_dim)
    angle = positions.astype(jnp.float32)[:, None] * frequency[None, :]
    return (jnp.cos(angle)[:, None, :], jnp.sin(angle)[:, None, :])


def rotate(flat, positions):
    row_count = flat.shape[0]
    heads = flat.reshape(row_count, -1, HEAD_DIM)
    cosine, sine = angles(positions)
    first = heads[..., : HEAD_DIM // 2]
    second = heads[..., HEAD_DIM // 2 :]
    turned = jnp.concatenate(
        [first * cosine - second * sine, second * cosine + first * sine], axis=-1
    )
    return turned.reshape(row_count, -1)


def unrotate(flat, positions):
    row_count = flat.shape[0]
    heads = flat.reshape(row_count, -1, HEAD_DIM)
    cosine, sine = angles(positions)
    first = heads[..., : HEAD_DIM // 2]
    second = heads[..., HEAD_DIM // 2 :]
    turned = jnp.concatenate(
        [first * cosine + second * sine, second * cosine - first * sine], axis=-1
    )
    return turned.reshape(row_count, -1)


def normalize(values):
    inverse = lax.rsqrt(jnp.mean(values * values, axis=-1, keepdims=True) + EPS)
    return (values * inverse, inverse)


def norm_back(grad_normed_out, normed, inverse, gain):
    scaled = grad_normed_out * gain
    return inverse * (scaled - normed * jnp.mean(scaled * normed, axis=-1, keepdims=True))


def contract_rows(left, right):
    return lax.dot_general(
        left, right, (((1,), (1,)), ((), ())), preferred_element_type=jnp.float32
    )


def contract_cols(left, right):
    return lax.dot_general(
        left, right, (((0,), (0,)), ((), ())), preferred_element_type=jnp.float32
    )


def visibility(query_positions, query_docs, key_positions, key_docs):
    same_doc = query_docs[:, None] == key_docs[None, :]
    earlier = key_positions[None, :] <= query_positions[:, None]
    return jnp.where(same_doc & earlier, 1.0, 0.0).astype(jnp.float32)


def merge_heads(stacked):
    return jnp.transpose(stacked, (1, 0, 2)).reshape(stacked.shape[1], -1)


def head_slice(matrix, offset):
    return lax.dynamic_slice_in_dim(matrix, offset, HEAD_DIM, 1)


def attend_forward(queries, key_rows, value_rows, visible):
    score_scale = HEAD_DIM ** (-0.5)

    def one_head(head_index):
        offset = head_index * HEAD_DIM
        scores = (
            contract_rows(head_slice(queries, offset), head_slice(key_rows, offset)) * score_scale
        )
        weights = (jax.nn.sigmoid(scores - SHIFT) * visible).astype(jnp.bfloat16)
        return jnp.dot(weights, head_slice(value_rows, offset), preferred_element_type=jnp.float32)

    stacked = lax.map(one_head, jnp.arange(queries.shape[1] // HEAD_DIM))
    return merge_heads(stacked)


def attend_back(queries, key_rows, value_rows, grad_attended, visible):
    score_scale = HEAD_DIM ** (-0.5)

    def one_head(head_index):
        offset = head_index * HEAD_DIM
        head_query = head_slice(queries, offset)
        head_key = head_slice(key_rows, offset)
        head_grad = head_slice(grad_attended, offset)
        scores = contract_rows(head_query, head_key) * score_scale
        sigma = jax.nn.sigmoid(scores - SHIFT)
        grad_weights = contract_rows(head_grad, head_slice(value_rows, offset))
        grad_scores = (grad_weights * visible * sigma * (1.0 - sigma)).astype(jnp.bfloat16)
        pieces = []
        pieces.append(
            jnp.dot(grad_scores, head_key, preferred_element_type=jnp.float32) * score_scale
        )
        weights = (sigma * visible).astype(jnp.bfloat16)
        pieces.append(contract_cols(grad_scores, head_query) * score_scale)
        pieces.append(contract_cols(weights, head_grad))
        return tuple(pieces)

    stacked = lax.map(one_head, jnp.arange(queries.shape[1] // HEAD_DIM))
    return tuple((merge_heads(piece) for piece in stacked))


def rows_shards(
    activations,
    document_ids,
    attn_gain,
    w_query,
    w_key,
    w_value,
    w_out,
    mlp_gain,
    w_gate,
    w_up,
    w_down,
    cotangent,
):
    groups = lax.axis_size("cp")
    rank = lax.axis_index("cp")
    stretch_len = activations.shape[3]
    width = activations.shape[4]
    row_count = 2 * stretch_len
    offsets = jnp.arange(stretch_len, dtype=jnp.int32)
    my_positions = jnp.concatenate(
        [rank * stretch_len + offsets, (2 * groups - 1 - rank) * stretch_len + offsets]
    )
    all_docs = document_ids[0]
    my_docs = jnp.take(all_docs, my_positions)
    slots = jnp.arange(groups * row_count, dtype=jnp.int32)
    owners = slots // row_count
    halves = slots // stretch_len % 2
    key_positions = (
        jnp.where(halves == 0, owners, 2 * groups - 1 - owners) * stretch_len + slots % stretch_len
    )
    key_docs = jnp.take(all_docs, key_positions)
    visible = visibility(my_positions, my_docs, key_positions, key_docs)
    gathered = (
        lax.all_gather(w_query, "cp", axis=0, tiled=True),
        lax.all_gather(w_key, "cp", axis=0, tiled=True),
        lax.all_gather(w_value, "cp", axis=0, tiled=True),
        lax.all_gather(w_out, "cp", axis=1, tiled=True),
        lax.all_gather(w_gate, "cp", axis=0, tiled=True),
        lax.all_gather(w_up, "cp", axis=0, tiled=True),
        lax.all_gather(w_down, "cp", axis=1, tiled=True),
        lax.all_gather(attn_gain, "cp", axis=0, tiled=True),
        lax.all_gather(mlp_gain, "cp", axis=0, tiled=True),
    )
    (
        query_full,
        key_full,
        value_full,
        out_full,
        gate_full,
        up_full,
        down_full,
        gain_one,
        gain_two,
    ) = gathered
    gain_one = gain_one.astype(jnp.float32)
    gain_two = gain_two.astype(jnp.float32)
    inputs = activations.reshape(row_count, width).astype(jnp.float32)
    normed_one, inverse_one = normalize(inputs)
    hidden_one = (normed_one * gain_one).astype(jnp.bfloat16)
    queries = rotate(
        jnp.dot(hidden_one, query_full, preferred_element_type=jnp.float32), my_positions
    ).astype(jnp.bfloat16)
    keys_local = rotate(
        jnp.dot(hidden_one, key_full, preferred_element_type=jnp.float32), my_positions
    ).astype(jnp.bfloat16)
    values_local = jnp.dot(hidden_one, value_full, preferred_element_type=jnp.float32).astype(
        jnp.bfloat16
    )
    keys_all, values_all = (
        lax.all_gather(keys_local, "cp", axis=0, tiled=True),
        lax.all_gather(values_local, "cp", axis=0, tiled=True),
    )
    attended = attend_forward(queries, keys_all, values_all, visible).astype(jnp.bfloat16)
    branch = lax.psum(jnp.dot(attended, out_full, preferred_element_type=jnp.float32), "tp")
    middle = inputs + branch
    normed_two, inverse_two = normalize(middle)
    hidden_two = (normed_two * gain_two).astype(jnp.bfloat16)
    gate = jnp.dot(hidden_two, gate_full, preferred_element_type=jnp.float32)
    upward = jnp.dot(hidden_two, up_full, preferred_element_type=jnp.float32)
    sigma_gate = jax.nn.sigmoid(gate)
    silu_gate = gate * sigma_gate
    product = (silu_gate * upward).astype(jnp.bfloat16)
    feed = lax.psum(jnp.dot(product, down_full, preferred_element_type=jnp.float32), "tp")
    result = middle + feed
    layer_out = result.astype(jnp.bfloat16).reshape(activations.shape)
    grad_result = cotangent.reshape(row_count, width).astype(jnp.float32)
    grad_feed = grad_result.astype(jnp.bfloat16)
    grad_product = contract_rows(grad_feed, down_full)
    grad_gate = (grad_product * upward * sigma_gate * (1.0 + gate * (1.0 - sigma_gate))).astype(
        jnp.bfloat16
    )
    grad_up = (grad_product * silu_gate).astype(jnp.bfloat16)
    grad_hidden_two = lax.psum(
        contract_rows(grad_gate, gate_full) + contract_rows(grad_up, up_full), "tp"
    )
    grad_gain_two = jnp.sum(grad_hidden_two * normed_two, axis=0)
    grad_middle = grad_result + norm_back(grad_hidden_two, normed_two, inverse_two, gain_two)
    grad_down = contract_cols(product, grad_feed)
    grad_gate_w = contract_cols(hidden_two, grad_gate)
    grad_up_w = contract_cols(hidden_two, grad_up)
    share_gate, share_up, share_down, share_gain_two = (
        lax.psum_scatter(grad_gate_w, "cp", scatter_dimension=0, tiled=True),
        lax.psum_scatter(grad_up_w, "cp", scatter_dimension=0, tiled=True),
        lax.psum_scatter(grad_down, "cp", scatter_dimension=1, tiled=True),
        lax.psum_scatter(grad_gain_two, "cp", scatter_dimension=0, tiled=True),
    )
    grad_branch = grad_middle.astype(jnp.bfloat16)
    grad_attended = contract_rows(grad_branch, out_full).astype(jnp.bfloat16)
    grad_queries, key_terms, value_terms = attend_back(
        queries, keys_all, values_all, grad_attended, visible
    )
    grad_keys, grad_values = (
        lax.psum_scatter(key_terms, "cp", scatter_dimension=0, tiled=True),
        lax.psum_scatter(value_terms, "cp", scatter_dimension=0, tiled=True),
    )
    grad_query_pre = unrotate(grad_queries, my_positions).astype(jnp.bfloat16)
    grad_key_pre = unrotate(grad_keys, my_positions).astype(jnp.bfloat16)
    grad_value_pre = grad_values.astype(jnp.bfloat16)
    local_hidden = (
        contract_rows(grad_query_pre, query_full)
        + contract_rows(grad_key_pre, key_full)
        + contract_rows(grad_value_pre, value_full)
    )
    grad_hidden_one = lax.psum(local_hidden, "tp")
    grad_gain_one = jnp.sum(grad_hidden_one * normed_one, axis=0)
    grad_inputs = grad_middle + norm_back(grad_hidden_one, normed_one, inverse_one, gain_one)
    grad_query_w = contract_cols(hidden_one, grad_query_pre)
    grad_key_w = contract_cols(hidden_one, grad_key_pre)
    grad_value_w = contract_cols(hidden_one, grad_value_pre)
    grad_out_w = contract_cols(attended, grad_branch)
    share_query, share_key, share_value, share_out, share_gain_one = (
        lax.psum_scatter(grad_query_w, "cp", scatter_dimension=0, tiled=True),
        lax.psum_scatter(grad_key_w, "cp", scatter_dimension=0, tiled=True),
        lax.psum_scatter(grad_value_w, "cp", scatter_dimension=0, tiled=True),
        lax.psum_scatter(grad_out_w, "cp", scatter_dimension=1, tiled=True),
        lax.psum_scatter(grad_gain_one, "cp", scatter_dimension=0, tiled=True),
    )
    summed = lax.psum(
        (
            share_gain_one,
            share_query,
            share_key,
            share_value,
            share_out,
            share_gain_two,
            share_gate,
            share_up,
            share_down,
        ),
        "dp",
    )
    input_grad = grad_inputs.astype(jnp.bfloat16).reshape(activations.shape)
    return (
        layer_out,
        input_grad,
        summed[0],
        summed[1],
        summed[2],
        summed[3],
        summed[4],
        summed[5],
        summed[6],
        summed[7],
        summed[8],
    )


def layer(sizes, *args):
    heads = args[3].shape[1] // HEAD_DIM
    zs = sizes["cp"]
    fits = sizes["dp"] == 4 and sizes["tp"] == 2 and heads == 2 * zs
    fits = fits and args[0].shape[3] % 32 == 0 and args[8].shape[1] % (4 * zs * HEAD_DIM) == 0
    fits = fits and args[3].shape[0] % HEAD_DIM == 0 and args[1].shape[1] % args[3].shape[0] == 0
    fits = fits and args[1].shape[1] <= 6 * args[3].shape[0]
    if fits:
        return heads_shards(zs, *args)
    return rows_shards(*args)


def solution(mesh):
    return jax.shard_map(
        functools.partial(layer, dict(mesh.shape)),
        mesh=mesh,
        in_specs=(
            P("dp", "cp", None, None, None),
            P("dp", None),
            P("cp"),
            P("cp", "tp"),
            P("cp", "tp"),
            P("cp", "tp"),
            P("tp", "cp"),
            P("cp"),
            P("cp", "tp"),
            P("cp", "tp"),
            P("tp", "cp"),
            P("dp", "cp", None, None, None),
        ),
        out_specs=(
            P("dp", "cp", None, None, None),
            P("dp", "cp", None, None, None),
            P("cp"),
            P("cp", "tp"),
            P("cp", "tp"),
            P("cp", "tp"),
            P("tp", "cp"),
            P("cp"),
            P("cp", "tp"),
            P("cp", "tp"),
            P("tp", "cp"),
        ),
        check_vma=False,
    )
```

```python
import functools
import math

import jax
import jax.numpy as jnp
import numpy as np
from jax import lax
from jax.experimental import pallas as pl
from jax.experimental.pallas import tpu as pltpu
from jax.sharding import PartitionSpec as P

HEAD_DIM = 128
EPS = 1e-05
SHIFT = math.log(4096.0)
ROPE_BASE = 10000.0
BF = jnp.bfloat16
F32 = jnp.float32
MESH = pl.DeviceIdType.MESH
ANY = pl.ANY
VMEM = pltpu.VMEM
MIB = 2**20


class Net:
    def __init__(self, zs, send_sems, recv_sems):
        self.zs = zs
        self.dp, self.z, self.t = (lax.axis_index(a) for a in ("dp", "cp", "tp"))
        self.a, self.b = lax.div(self.dp, 2), lax.rem(self.dp, 2)
        self.send_sems, self.recv_sems = send_sems, recv_sems
        self.used = 0
        self.open = []

    def along_z(self, s):
        return (self.dp, lax.rem(self.z + s, self.zs), self.t)

    def source_z(self, s):
        return lax.rem(self.z + self.zs - s, self.zs)

    @property
    def over_x(self):
        return (2 * self.a + 1 - self.b, self.z, self.t)

    @property
    def over_y(self):
        return (2 * (1 - self.a) + self.b, self.z, self.t)

    @property
    def sibling(self):
        return (self.dp, self.z, 1 - self.t)

    def meet(self, y=True):
        ways = [self.along_z(s) for s in range(1, self.zs)] + [self.over_x, self.sibling]
        if y:
            ways.append(self.over_y)
        barrier = pltpu.get_barrier_semaphore()
        for way in ways:
            pl.semaphore_signal(barrier, inc=1, device_id=way, device_id_type=MESH)
        pl.semaphore_wait(barrier, len(ways))

    def slot(self):
        self.used += 1
        return self.used - 1

    def send(self, src, dst, way, arrive=None, when=None):
        k = self.slot()
        arrive = k if arrive is None else arrive
        copy = pltpu.make_async_remote_copy(
            src, dst, self.send_sems.at[k], self.recv_sems.at[arrive], device_id=way, device_id_type=MESH
        )
        if when is None:
            copy.start()
        else:
            pl.when(when)(copy.start)
        self.open.append((copy, when))
        return copy

    def arrival(self, ref, slot):
        return pltpu.make_async_remote_copy(
            ref, ref, self.send_sems.at[0], self.recv_sems.at[slot], device_id=self.sibling, device_id_type=MESH
        )

    def keep(self, src, dst):
        k = self.used
        self.used += 1
        copy = pltpu.make_async_copy(src, dst, self.send_sems.at[k])
        copy.start()
        return copy

    def finish(self):
        for copy, when in self.open:
            if when is None:
                copy.wait_send()
            else:
                pl.when(when)(copy.wait_send)
        self.open = []


class LineGather:
    def __init__(self, net, src, place):
        self.net, self.src, self.place = net, src, place
        self.h, self.low = lax.div(net.z, 2), lax.rem(net.z, 2)
        self.mate = (net.dp, net.z + 1 - 2 * self.low, net.t)
        self.gate = (net.dp, 2 - self.h, net.t)
        self.hands_on = self.h != self.low

    def start(self):
        net = self.net
        mine = self.place(net.z)
        self.near = net.send(self.src, mine, self.mate)
        self.slots = [net.slot(), net.slot()]
        net.send(self.src, mine, self.gate, arrive=self.slots[0] + self.low)

    def take(self, s):
        net = self.net
        if s == 1:
            self.near.wait_recv()
            return net.z + 1 - 2 * self.low
        z = 2 * (1 - self.h) + s - 2
        ref = self.place(z)
        net.arrival(ref, self.slots[s - 2]).wait_recv()
        net.send(ref, ref, self.mate, arrive=self.slots[s - 2], when=self.hands_on)
        return z


def plane_relay(net, place, halves, over_x, over_y, sibling=None):
    dx, dy = 2 * net.a + 1 - net.b, 2 * (1 - net.a) + net.b
    relays = []
    over_x.wait_recv()
    first = halves(place(dx), 0) if halves else place(dx)
    relays.append(net.send(first, first, net.over_y))
    if sibling:
        sibling(dx)
    over_y.wait_recv()
    if halves:
        second = halves(place(dy), 1)
        relays.append(net.send(second, second, net.over_x))
    if sibling:
        sibling(dy)
    return relays


def plane_end(net, relays, sibling=None):
    for copy in relays:
        copy.wait_recv()
    if sibling:
        sibling(2 * (1 - net.a) + 1 - net.b)


def rows_loop(count, step, body):
    def one(i, carry):
        body(pl.ds(pl.multiple_of(i * step, step), step))
        return carry

    lax.fori_loop(0, count // step, one, 0)


def add_rows(out, terms, rows):
    def body(at):
        total = terms[0][at, :].astype(F32)
        for term in terms[1:]:
            total += term[at, :].astype(F32)
        out[at, :] = total.astype(out.dtype)

    rows_loop(rows, 16, body)


class GatherAll:
    def __init__(self, net, src, dst):
        self.net, self.src, self.dst = net, src, dst
        rows = src.shape[0] // 2
        self.halves = lambda ref, k: ref.at[pl.ds(k * rows, rows)]

    def place(self, dp, z):
        return self.dst.at[dp, z, self.net.t]

    def start(self):
        net = self.net
        mine = self.place(net.dp, net.z)
        self.line = LineGather(net, self.src, lambda z: self.place(net.dp, z))
        self.line.start()
        self.local = net.keep(self.src, mine)
        self.plane = [(net.z, net.send(self.src, mine, net.over_x), net.send(self.src, mine, net.over_y))]
        self.twin = [net.send(self.src, mine, net.sibling)]
        self.states = []

    def to_twin(self, dp, z):
        ref = self.place(dp, z)
        self.twin.append(self.net.send(ref, ref, self.net.sibling))

    def spread(self, s):
        net = self.net
        z = self.line.take(s)
        ref = self.place(net.dp, z)
        self.plane.append((z, net.send(ref, ref, net.over_x), net.send(ref, ref, net.over_y)))
        self.to_twin(net.dp, z)

    def relay(self, s):
        z, over_x, over_y = self.plane[s]
        place = functools.partial(self.place, z=z)
        self.states.append((z, plane_relay(self.net, place, self.halves, over_x, over_y, lambda dp: self.to_twin(dp, z))))

    def end(self):
        for z, relays in self.states:
            plane_end(self.net, relays, lambda dp, z=z: self.to_twin(dp, z))
        for copy in self.twin:
            copy.wait_recv()
        self.local.wait()


class GatherGroup:
    def __init__(self, net, src, dst, own_lanes=None):
        self.net, self.src, self.dst, self.own_lanes = net, src, dst, own_lanes
        self.rows = src.shape[0]

    def place(self, b, z, t=None):
        t = self.net.t if t is None else t
        last = 2 * self.net.zs - 1
        at = ((last + 1) * b + z + t * (last - 2 * z)) * self.rows
        return self.dst.at[pl.ds(pl.multiple_of(at, self.rows), self.rows)]

    def start(self):
        net = self.net
        mine = self.place(net.b, net.z)
        self.line = LineGather(net, self.src, lambda z: self.place(net.b, z))
        self.line.start()
        self.over = [(net.z, net.send(self.src, mine, net.over_x))]
        self.twin, self.local = [], []
        if self.own_lanes is None:
            self.local.append(net.keep(self.src, mine))
            self.twin.append((net.b, net.z, net.send(self.src, mine, net.sibling)))
        else:
            for t in (0, 1):
                self.local.append(net.keep(self.own_lanes.at[t], self.place(net.b, net.z, t)))

    def to_twin(self, b, z):
        ref = self.place(b, z)
        self.twin.append((b, z, self.net.send(ref, ref, self.net.sibling)))

    def spread(self, s):
        net = self.net
        z = self.line.take(s)
        ref = self.place(net.b, z)
        self.over.append((z, net.send(ref, ref, net.over_x)))
        self.to_twin(net.b, z)
        return z

    def far(self, s):
        z, copy = self.over[s]
        copy.wait_recv()
        self.to_twin(1 - self.net.b, z)
        return z

    def end(self):
        for _, _, copy in self.twin:
            copy.wait_recv()
        for copy in self.local:
            copy.wait()


class SumGroup:
    def __init__(self, net, part, sib, far, landed):
        self.net, self.part, self.sib, self.far, self.landed = net, part, sib, far, landed
        self.rows = part.shape[3]
        self.twin, self.over, self.z_sends = {}, [], []

    def order(self):
        return [lax.rem(self.net.z + s + 1, self.net.zs) for s in range(self.net.zs)]

    def give(self, k):
        net = self.net
        b = net.b if k else 1 - net.b
        for s, z in enumerate(self.order()):
            self.twin[k, s] = net.send(self.part.at[b, 1 - net.t, z], self.sib.at[b, z], net.sibling)

    def take(self, k):
        net = self.net
        b = net.b if k else 1 - net.b
        for s, z in enumerate(self.order()):
            self.twin[k, s].wait_recv()
            own = self.part.at[b, net.t, z]
            add_rows(own, [own, self.sib.at[b, z]], self.rows)
            if k == 0:
                self.over.append(net.send(own, self.far.at[z], net.over_x))

    def along(self):
        net = self.net
        for s, z in enumerate(self.order()):
            self.over[s].wait_recv()
            last = s == net.zs - 1
            own = self.part.at[net.b, net.t, z]
            out = self.landed.at[net.z] if last else own
            add_rows(out, [own, self.far.at[z]], self.rows)
            if not last:
                self.z_sends.append(net.send(out, self.landed.at[net.z], net.along_z(s + 1)))

    def end(self):
        for copy in self.z_sends:
            copy.wait_recv()


class SumAll:
    def __init__(self, net, part, own, sib, one, two, landed):
        self.net, self.part, self.own, self.sib = net, part, own, sib
        self.one, self.two, self.landed = one, two, landed
        self.half = part.shape[3] // 2

    def order(self):
        net = self.net
        return [lax.rem(net.z + s + 1, net.zs) for s in range(net.zs)]

    def places(self):
        a, b = self.net.a, self.net.b
        return [2 * (1 - a) + 1 - b, 2 * a + 1 - b, 2 * (1 - a) + b, 2 * a + b]

    def start(self):
        net = self.net
        self.twin, self.mine = [], []
        for z in self.order():
            for dp in self.places():
                self.twin.append(net.send(self.part.at[dp, z, 1 - net.t], self.sib.at[dp, z], net.sibling))
                self.mine.append(net.keep(self.part.at[dp, z, net.t], self.own.at[dp, z]))

    def upper(self, ref):
        return ref.at[pl.ds(0, self.half)]

    def lower(self, ref):
        return ref.at[pl.ds(self.half, self.half)]

    def first(self, s):
        net = self.net
        z = self.order()[s]
        dd, dx, dy, me = self.places()
        for j, dp in enumerate((dd, dx, dy, me)):
            self.twin[4 * s + j].wait_recv()
            self.mine[4 * s + j].wait()
            add_rows(self.own.at[dp, z], [self.own.at[dp, z], self.sib.at[dp, z]], 2 * self.half)
        self.ones = getattr(self, "ones", [])
        self.ones.append(
            (
                net.send(self.upper(self.own.at[dd, z]), self.one.at[0, 0, z], net.over_x),
                net.send(self.upper(self.own.at[dx, z]), self.one.at[0, 1, z], net.over_x),
                net.send(self.lower(self.own.at[dd, z]), self.one.at[1, 0, z], net.over_y),
                net.send(self.lower(self.own.at[dy, z]), self.one.at[1, 1, z], net.over_y),
            )
        )

    def second(self, s):
        net = self.net
        z = self.order()[s]
        dd, dx, dy, me = self.places()
        x_dd, x_me, y_dd, y_me = self.ones[s]
        self.twos = getattr(self, "twos", [])
        x_dd.wait_recv()
        out = self.upper(self.own.at[dy, z])
        add_rows(out, [out, self.one.at[0, 0, z]], self.half)
        up = net.send(out, self.two.at[0, z], net.over_y)
        y_dd.wait_recv()
        out = self.lower(self.own.at[dx, z])
        add_rows(out, [out, self.one.at[1, 0, z]], self.half)
        side = net.send(out, self.two.at[1, z], net.over_x)
        self.twos.append((up, side))

    def third(self, s):
        net = self.net
        z = self.order()[s]
        dd, dx, dy, me = self.places()
        _, x_me, _, y_me = self.ones[s]
        up, side = self.twos[s]
        last = s == net.zs - 1
        out = self.landed.at[net.z] if last else self.own.at[me, z]
        x_me.wait_recv()
        up.wait_recv()
        mine = self.own.at[me, z]
        add_rows(self.upper(out), [self.upper(mine), self.one.at[0, 1, z], self.two.at[0, z]], self.half)
        y_me.wait_recv()
        side.wait_recv()
        add_rows(self.lower(out), [self.lower(mine), self.one.at[1, 1, z], self.two.at[1, z]], self.half)
        self.z_sends = getattr(self, "z_sends", [])
        if not last:
            self.z_sends.append(net.send(out, self.landed.at[net.z], net.along_z(s + 1)))

    def end(self):
        for copy in self.z_sends:
            copy.wait_recv()


class SpreadGrads:
    def __init__(self, net, src, dst, halves):
        self.net, self.src, self.dst, self.halves = net, src, dst, halves
        self.z_sends, self.plane, self.states = [], {}, []

    def mine(self):
        return self.dst(self.net.dp, self.net.z)

    def start(self):
        self.own()
        for s in range(1, self.net.zs):
            self.go(s)

    def own(self):
        self.local = self.net.keep(self.src(self.net.z), self.mine())

    def go(self, s):
        net = self.net
        self.z_sends.append(net.send(self.src(lax.rem(net.z + s, net.zs)), self.mine(), net.along_z(s)))

    def spread(self, s):
        net = self.net
        z = net.source_z(s)
        ref = self.dst(net.dp, z)
        if s:
            self.z_sends[s - 1].wait_recv()
            src = ref
        else:
            src = self.src(net.z)
        self.plane[s] = (z, net.send(src, ref, net.over_x), net.send(src, ref, net.over_y))

    def relay(self, s):
        z, over_x, over_y = self.plane[s]
        self.states.append(plane_relay(self.net, lambda dp: self.dst(dp, z), self.halves, over_x, over_y))

    def end(self):
        for relays in self.states:
            plane_end(self.net, relays)
        self.local.wait()


def half_rows(ref, k):
    n = ref.shape[0] // 2
    return ref.at[pl.ds(k * n, n)]


def aligned(i, size):
    return pl.ds(pl.multiple_of(i * size, size), size)


def loop(count, body):
    def one(i, carry):
        body(i)
        return carry

    lax.fori_loop(0, count, one, 0)


def dot(left, right, dims=((1,), (0,)), kind=F32):
    return lax.dot_general(left, right, (dims, ((), ())), preferred_element_type=F32).astype(kind)


def turn(u, cosine, sine):
    return u * cosine + pltpu.roll(u, HEAD_DIM // 2, 1) * sine


def column(row, start, count):
    n = row.shape[1]
    here = lax.broadcasted_iota(jnp.int32, (count, n), 1) == start + lax.broadcasted_iota(jnp.int32, (count, n), 0)
    return jnp.sum(jnp.where(here, row, 0.0), axis=1, keepdims=True)


def seen(row, start, count, flip=False):
    n = row.shape[1]
    same = column(row, start, count) == row
    mine = start + lax.broadcasted_iota(jnp.int32, (count, n), 0)
    other = lax.broadcasted_iota(jnp.int32, (count, n), 1)
    return same & ((mine <= other) if flip else (other <= mine))


def sigma_of(left, right):
    return jax.nn.sigmoid(dot(left, right, ((1,), (1,))) * HEAD_DIM**-0.5 - SHIFT)


def call(kernel, name, outs, scratch, count, args, vmem):
    return pl.pallas_call(
        kernel,
        out_shape=[jax.ShapeDtypeStruct(shape, kind) for shape, kind, _ in outs],
        in_specs=[pl.BlockSpec(memory_space=ANY)] * len(args),
        out_specs=[pl.BlockSpec(memory_space=space) for _, _, space in outs],
        scratch_shapes=list(scratch) + [pltpu.SemaphoreType.DMA((count,)), pltpu.SemaphoreType.DMA((count,))],
        compiler_params=pltpu.CompilerParams(
            collective_id=name, has_side_effects=True, vmem_limit_bytes=vmem * MIB
        ),
    )(*args)


def forward_kernel(
    zs, x, wq, wk, wv, wo, small, cosine, sine, wg, wu, wd, cot,
    hidden_out, qkv_out, attended_out, qkv_w_out, out_w_out, gains_out, docs_out, middle, h2_all, cot_all, gu_w, down_w,
    x_all, h1, qkv_w, out_w, small_z, small_x, gains, docs, cos_v, sin_v, qkv, attended, part, sib, far, landed,
    x_lane, h2, mid_v, send_sems, recv_sems,
):
    net = Net(zs, send_sems, recv_sems)
    net.meet()
    deep, wide = wg.shape[0], gu_w.shape[1] // 2
    seq = docs.shape[1]
    half, side = deep // 2, HEAD_DIM // 2
    gather = GatherGroup(net, x.at[net.t], x_all, own_lanes=x)
    gather.start()
    small_waits = [net.send(small, small_z.at[net.z], net.along_z(s)) for s in range(1, zs)]
    small_waits.append(net.send(small, small_x.at[net.b], net.over_x))
    local = [net.keep(small, small_z.at[net.z]), net.keep(small, small_x.at[net.b])]
    local += [net.keep(cosine, cos_v), net.keep(sine, sin_v)]
    lane = net.keep(x.at[net.t], x_lane)

    def head(z):
        return aligned(net.b * zs + z, HEAD_DIM)

    mine = aligned(net.z, deep)
    my_half = pl.ds(pl.multiple_of(net.a * half, half), half)
    qkv_sends, out_sends, w_local = [], [], []
    for m, w in enumerate((wq, wk, wv)):
        col = pl.ds(m * HEAD_DIM, HEAD_DIM)
        w_local.append(net.keep(w.at[:, head(net.z)], qkv_w.at[mine, col]))
    for s in range(1, zs):
        z = lax.rem(net.z + s, zs)
        rows = pl.ds(pl.multiple_of(net.z * deep + net.a * half, half), half)
        qkv_sends.append(
            [
                net.send(w.at[my_half, head(z)], qkv_w.at[rows, pl.ds(m * HEAD_DIM, HEAD_DIM)], net.along_z(s))
                for m, w in enumerate((wq, wk, wv))
            ]
        )
    out_rows = pl.ds(pl.multiple_of(net.a * side, side), side)
    w_local.append(net.keep(wo.at[head(net.z)], out_w.at[:, mine]))
    for s in range(1, zs):
        z = lax.rem(net.z + s, zs)
        at = pl.ds(pl.multiple_of((net.b * zs + z) * HEAD_DIM + net.a * side, side), side)
        out_sends.append(net.send(wo.at[at], out_w.at[out_rows, mine], net.along_z(s)))

    cotan = GatherAll(net, cot.at[net.t], cot_all)
    mlp_waits, mlp_local = [], []

    def block(z):
        return aligned(net.dp * zs + z, wide)

    mlp = (
        (lambda z: wg.at[:, block(z)], gu_w.at[mine, pl.ds(0, wide)]),
        (lambda z: wu.at[:, block(z)], gu_w.at[mine, pl.ds(wide, wide)]),
        (lambda z: wd.at[block(z)], down_w.at[:, mine]),
    )
    for src, dst in mlp:
        mlp_local.append(net.keep(src(net.z), dst))

    def fetch(k):
        src, dst = mlp[k]
        for s in range(1, zs):
            mlp_waits.append(net.send(src(lax.rem(net.z + s, zs)), dst, net.along_z(s)))

    for copy in small_waits:
        copy.wait_recv()
    for copy in local:
        copy.wait()
    for z in range(zs):
        gains[0:1, z * deep : (z + 1) * deep] = small_z[z, 0:1, :]
        gains[1:2, z * deep : (z + 1) * deep] = small_z[z, 1:2, :]
    for b in range(2):
        for k in range(seq // deep):
            docs[b : b + 1, k * deep : (k + 1) * deep] = small_x[b, 2 + k : 3 + k, :]

    def norm_block(ref_at):
        def body(i):
            at = pl.ds(pl.multiple_of(ref_at + i * 16, 16), 16)
            rows = x_all[at, :].astype(F32)
            inverse = lax.rsqrt(jnp.mean(rows * rows, axis=-1, keepdims=True) + EPS)
            h1[at, :] = (rows * inverse * gains[0:1, :]).astype(BF)

        loop(x.shape[1] // 16, body)

    rows = x.shape[1]
    last = 2 * zs - 1

    def offset(b, z, t):
        return ((last + 1) * b + z + t * (last - 2 * z)) * rows

    for copy in gather.local:
        copy.wait()
    gather.local = []
    for t in (0, 1):
        norm_block(offset(net.b, net.z, t))
    for s in range(1, zs):
        norm_block(offset(net.b, gather.spread(s), net.t))
    cotan.start()
    fetch(0)
    qkv_y = []
    for s in range(1, zs):
        norm_block(offset(1 - net.b, gather.far(s - 1), net.t))
        for copy in qkv_sends[s - 1]:
            copy.wait_recv()
        at = qkv_w.at[pl.ds(pl.multiple_of(net.source_z(s) * deep + net.a * half, half), half)]
        qkv_y.append(net.send(at, at, net.over_y))
    norm_block(offset(1 - net.b, gather.far(zs - 1), net.t))
    out_y = []
    for s in range(1, zs):
        out_sends[s - 1].wait_recv()
        at = out_w.at[out_rows, aligned(net.source_z(s), deep)]
        out_y.append(net.send(at, at, net.over_y))
    for b, z, copy in gather.twin:
        copy.wait_recv()
        norm_block(offset(b, z, 1 - net.t))
    for copy in qkv_y:
        copy.wait_recv()
    for copy in w_local:
        copy.wait()
    for s in range(1, zs):
        cotan.spread(s)
    for copy in out_y:
        copy.wait_recv()

    branch = SumGroup(net, part, sib, far, landed)
    tile = 128
    for k in range(2):
        b = net.b if k else 1 - net.b
        base = b * seq

        def project(i):
            at = pl.ds(pl.multiple_of(base + i * 256, 256), 256)
            pos = aligned(i, 256)
            pre = dot(h1[at, :], qkv_w[...])
            c, s = cos_v[pos, :], sin_v[pos, :]
            qkv[at, 0:HEAD_DIM] = turn(pre[:, 0:HEAD_DIM], c, s).astype(BF)
            qkv[at, HEAD_DIM : 2 * HEAD_DIM] = turn(pre[:, HEAD_DIM : 2 * HEAD_DIM], c, s).astype(BF)
            qkv[at, 2 * HEAD_DIM : 3 * HEAD_DIM] = pre[:, 2 * HEAD_DIM : 3 * HEAD_DIM].astype(BF)

        loop(seq // 256, project)
        every = pl.ds(pl.multiple_of(base, seq), seq)
        row = docs[pl.ds(b, 1), :]

        def attend(i):
            at = pl.ds(pl.multiple_of(base + i * tile, tile), tile)
            sigma = sigma_of(qkv[at, 0:HEAD_DIM], qkv[every, HEAD_DIM : 2 * HEAD_DIM])
            weights = jnp.where(seen(row, i * tile, tile), sigma, 0.0).astype(BF)
            found = dot(weights, qkv[every, 2 * HEAD_DIM : 3 * HEAD_DIM], kind=BF)
            attended[at, :] = found
            out = dot(found, out_w[...], kind=BF)
            for j in range(tile // rows):
                blk = i * (tile // rows) + j
                t = lax.div(blk, zs)
                z = (1 - t) * blk + t * (last - blk)
                part[b, t, z] = out[j * rows : (j + 1) * rows, :]

        loop(seq // tile, attend)
        branch.give(k)
    saved = [
        net.keep(h1, hidden_out), net.keep(qkv, qkv_out), net.keep(attended, attended_out),
        net.keep(qkv_w, qkv_w_out), net.keep(out_w, out_w_out), net.keep(gains, gains_out), net.keep(docs, docs_out),
    ]
    branch.take(0)
    branch.take(1)
    branch.along()
    for s in range(zs):
        cotan.relay(s)
    lane.wait()
    branch.end()

    def body(i):
        at = aligned(i, 16)
        total = x_lane[at, :].astype(F32)
        for z in range(zs):
            total += landed[z, at, :].astype(F32)
        mid_v[at, :] = total
        inverse = lax.rsqrt(jnp.mean(total * total, axis=-1, keepdims=True) + EPS)
        h2[at, :] = (total * inverse * gains[1:2, :]).astype(BF)

    loop(rows // 16, body)
    saved.append(net.keep(mid_v, middle))
    hidden = GatherAll(net, h2, h2_all)
    hidden.start()
    hidden.spread(1)
    hidden.spread(2)
    hidden.spread(3)
    fetch(1)
    fetch(2)
    cotan.end()
    for s in range(zs):
        hidden.relay(s)
    hidden.end()
    for copy in saved:
        copy.wait()
    for copy in mlp_waits:
        copy.wait_recv()
    for copy in mlp_local:
        copy.wait()
    net.finish()


def backward_kernel(
    zs, gh_part, feed_part, gu_grad, down_grad, middle, cot, x, gains_in, docs_in, cosine, sine,
    hidden_in, qkv_in, attended_in, qkv_w_in, out_w_in,
    layer_out, input_grad, q_out, k_out, v_out, o_out, gate_out, up_out, down_out, gains_out,
    own, sib, one, two, landed, own_f, sib_f, one_f, two_f, landed_f, part, sib_1, far_1, landed_1,
    h1, qkv, attended, qkv_w, out_w, gbr_all, gqkv, gains, docs, cos_v, sin_v, hg, mid_v, cot_v, x_v, gm_v, gbr_v, out_v,
    lo_v, gsum, g_far, g_land, q_give, q_own, q_land, o_part, o_own, o_land, send_sems, recv_sems,
):
    net = Net(zs, send_sems, recv_sems)
    net.meet()
    deep, wide = gate_out.shape[0], gu_grad.shape[1] // 2
    seq = docs.shape[1]
    half, side = deep // 2, HEAD_DIM // 2
    rows = x.shape[1]
    last = 2 * zs - 1
    scale = HEAD_DIM**-0.5
    hidden = SumAll(net, gh_part, own, sib, one, two, landed)
    hidden.start()
    feed = SumAll(net, feed_part, own_f, sib_f, one_f, two_f, landed_f)
    local = [net.keep(middle, mid_v), net.keep(cot.at[net.t], cot_v), net.keep(gains_in, gains)]
    local += [net.keep(x.at[net.t], x_v), net.keep(docs_in, docs), net.keep(cosine, cos_v), net.keep(sine, sin_v)]
    local += [net.keep(qkv_in, qkv), net.keep(attended_in, attended), net.keep(qkv_w_in, qkv_w)]
    local += [net.keep(out_w_in, out_w), net.keep(hidden_in, h1)]

    def block(dp, z):
        return aligned(dp * zs + z, wide)

    grads = [
        SpreadGrads(
            net,
            lambda z: gu_grad.at[aligned(z, deep), pl.ds(0, wide)],
            lambda dp, z: gate_out.at[:, block(dp, z)],
            half_rows,
        ),
        SpreadGrads(
            net,
            lambda z: gu_grad.at[aligned(z, deep), pl.ds(wide, wide)],
            lambda dp, z: up_out.at[:, block(dp, z)],
            half_rows,
        ),
        SpreadGrads(
            net,
            lambda z: down_grad.at[:, aligned(z, deep)],
            lambda dp, z: down_out.at[block(dp, z)],
            half_rows,
        ),
    ]
    grads[0].start()
    grads[0].spread(0)
    feed.start()
    for step, s in (
        (hidden.first, 0), (hidden.first, 1), (hidden.first, 2), (hidden.second, 0), (hidden.first, 3),
        (hidden.second, 1), (hidden.third, 0), (hidden.second, 2), (hidden.third, 1), (hidden.second, 3),
        (hidden.third, 2), (hidden.third, 3),
    ):
        step(s)
    for s in range(1, zs):
        grads[0].spread(s)
    feed.first(0)
    feed.first(1)
    for copy in local:
        copy.wait()
    hidden.end()
    gsum[...] = jnp.zeros_like(gsum)

    def total_of(ref, at):
        total = ref[0, at, :].astype(F32)
        for z in range(1, zs):
            total += ref[z, at, :].astype(F32)
        return total

    def norm_back(inputs, total, gain, k):
        inverse = lax.rsqrt(jnp.mean(inputs * inputs, axis=-1, keepdims=True) + EPS)
        normed = inputs * inverse
        prod = total * normed
        gsum[k] += prod[0:8, :] + prod[8:16, :]
        scaled = total * gain
        return inverse * (scaled - normed * jnp.mean(scaled * normed, axis=-1, keepdims=True))

    def back_two(i):
        at = aligned(i, 16)
        grad = cot_v[at, :].astype(F32) + norm_back(mid_v[at, :], total_of(landed, at), gains[1:2, :], 1)
        gm_v[at, :] = grad
        gbr_v[at, :] = grad.astype(BF)

    loop(rows // 16, back_two)
    gather = GatherGroup(net, gbr_v, gbr_all)
    gather.start()
    for s in range(1, zs):
        gather.spread(s)
    grads[1].start()
    for s in range(zs):
        grads[0].relay(s)
    for s in range(zs):
        gather.far(s)
    gather.end()

    branch = SumGroup(net, part, sib_1, far_1, landed_1)
    tile = 128
    for k in range(2):
        b = net.b if k else 1 - net.b
        base = b * seq
        every = pl.ds(pl.multiple_of(base, seq), seq)
        row = docs[pl.ds(b, 1), :]

        def heads_grad(i):
            at = pl.ds(pl.multiple_of(base + i * 256, 256), 256)
            hg[aligned(i, 256), :] = dot(gbr_all[at, :], out_w[...], ((1,), (1,)), BF)

        loop(seq // 256, heads_grad)

        def by_query(i):
            at = pl.ds(pl.multiple_of(base + i * tile, tile), tile)
            pos = aligned(i, tile)
            keys = qkv[every, HEAD_DIM : 2 * HEAD_DIM]
            sigma = sigma_of(qkv[at, 0:HEAD_DIM], keys)
            gw = dot(hg[pos, :], qkv[every, 2 * HEAD_DIM : 3 * HEAD_DIM], ((1,), (1,)))
            gs = jnp.where(seen(row, i * tile, tile), gw * sigma * (1.0 - sigma), 0.0).astype(BF)
            gq = dot(gs, keys) * scale
            gqkv[at, 0:HEAD_DIM] = turn(gq, cos_v[pos, :], -sin_v[pos, :]).astype(BF)

        loop(seq // tile, by_query)

        def by_key(i):
            at = pl.ds(pl.multiple_of(base + i * tile, tile), tile)
            pos = aligned(i, tile)
            queries = qkv[every, 0:HEAD_DIM]
            sigma = sigma_of(qkv[at, HEAD_DIM : 2 * HEAD_DIM], queries)
            gw = dot(qkv[at, 2 * HEAD_DIM : 3 * HEAD_DIM], hg[...], ((1,), (1,)))
            mask = seen(row, i * tile, tile, flip=True)
            gs = jnp.where(mask, gw * sigma * (1.0 - sigma), 0.0).astype(BF)
            weights = jnp.where(mask, sigma, 0.0).astype(BF)
            gk = dot(gs, queries) * scale
            gqkv[at, HEAD_DIM : 2 * HEAD_DIM] = turn(gk, cos_v[pos, :], -sin_v[pos, :]).astype(BF)
            gqkv[at, 2 * HEAD_DIM : 3 * HEAD_DIM] = dot(weights, hg[...], kind=BF)

        loop(seq // tile, by_key)

        def back_one(i):
            at = pl.ds(pl.multiple_of(base + i * tile, tile), tile)
            out = dot(gqkv[at, :], qkv_w[...], ((1,), (1,)), BF)
            for j in range(tile // rows):
                blk = i * (tile // rows) + j
                t = lax.div(blk, zs)
                z = (1 - t) * blk + t * (last - blk)
                part[b, t, z] = out[j * rows : (j + 1) * rows, :]

        loop(seq // tile, back_one)
        branch.give(k)
        if k == 0:
            feed.first(2)
            feed.first(3)
            branch.take(0)
            for s in range(zs):
                feed.second(s)
    branch.take(1)
    for s in range(zs):
        grads[1].spread(s)

    def qkv_grad(z, a):
        at = pl.ds(pl.multiple_of(z * deep + a * half, half), half)
        return dot(h1[:, at], gqkv[...], ((0,), (0,)), BF)

    def out_grad(z):
        o_part[z] = dot(attended[...], gbr_all[:, aligned(z, deep)], ((0,), (0,)), BF)

    def theirs(z):
        q_give[z] = qkv_grad(z, 1 - net.a)

    def ours(z):
        q_own[z] = qkv_grad(z, net.a)

    def side_rows(a):
        return pl.ds(pl.multiple_of(a * side, side), side)

    loop(zs, out_grad)
    loop(zs, theirs)
    swaps = []
    for s in range(zs):
        z = lax.rem(net.z + s + 1, zs)
        swaps.append(
            (
                z,
                net.send(q_give.at[z], q_land.at[z], net.over_y),
                net.send(o_part.at[z, side_rows(1 - net.a)], o_land.at[z], net.over_y),
            )
        )
    loop(zs, ours)
    branch.along()
    grads[2].start()
    for s in range(zs):
        feed.third(s)

    def q_place(ref):
        def place(dp, z):
            a, b = lax.div(dp, 2), lax.rem(dp, 2)
            return ref.at[pl.ds(pl.multiple_of(a * half, half), half), aligned(b * zs + z, HEAD_DIM)]

        return place

    def o_place(dp, z):
        a, b = lax.div(dp, 2), lax.rem(dp, 2)
        return o_out.at[pl.ds(pl.multiple_of((b * zs + z) * HEAD_DIM + a * side, side), side)]

    late = [
        SpreadGrads(net, lambda z, m=m: q_own.at[z, :, pl.ds(m * HEAD_DIM, HEAD_DIM)], q_place(ref), None)
        for m, ref in enumerate((q_out, k_out, v_out))
    ]
    late.append(SpreadGrads(net, lambda z: o_own.at[z], o_place, None))
    for s, (z, q_in, o_in) in enumerate(swaps):
        q_in.wait_recv()
        add_rows(q_own.at[z], [q_own.at[z], q_land.at[z]], half)
        o_in.wait_recv()
        add_rows(o_own.at[z], [o_part.at[z, side_rows(net.a)], o_land.at[z]], side)
        for grad in late:
            if s < zs - 1:
                grad.go(s + 1)
            else:
                grad.own()
    branch.end()

    def back_last(i):
        at = aligned(i, 16)
        grad = gm_v[at, :] + norm_back(x_v[at, :].astype(F32), total_of(landed_1, at), gains[0:1, :], 0)
        out_v[at, :] = grad.astype(BF)

    loop(rows // 16, back_last)
    outs = [net.keep(out_v, input_grad.at[net.t])]
    pairs = [net.send(out_v, input_grad.at[net.t], net.sibling)]
    for s in range(zs):
        grads[1].relay(s)
    for s in range(zs):
        grads[2].spread(s)
    feed.end()

    def close(i):
        at = aligned(i, 16)
        lo_v[at, :] = (mid_v[at, :] + total_of(landed_f, at)).astype(BF)

    loop(rows // 16, close)
    outs.append(net.keep(lo_v, layer_out.at[net.t]))
    pairs.append(net.send(lo_v, layer_out.at[net.t], net.sibling))
    for k, way in enumerate((net.sibling, net.over_x, net.over_y)):
        swap = net.send(gsum, g_far.at[k], way)
        swap.wait()
        net.open = [c for c in net.open if c[0] is not swap]
        gsum[...] = gsum[...] + g_far[k]

    def cut(z):
        return gsum.at[:, :, aligned(z, deep)]

    z_gain = [net.send(cut(lax.rem(net.z + s, zs)), g_land.at[net.z], net.along_z(s)) for s in range(1, zs)]
    outs.append(net.keep(cut(net.z), g_land.at[net.z]))
    for s in range(zs):
        for grad in late:
            grad.spread(s)
    for s in range(zs):
        grads[2].relay(s)
    for s in range(zs):
        for grad in late:
            grad.relay(s)
    for grad in grads + late:
        grad.end()
    for copy in outs:
        copy.wait()
    for copy in z_gain + pairs:
        copy.wait_recv()
    total = g_land[0]
    for z in range(1, zs):
        total += g_land[z]
    gains_out[...] = total
    net.finish()


def rope_tables(seq):
    half_dim = HEAD_DIM // 2
    frequency = ROPE_BASE ** (-np.arange(half_dim, dtype=np.float32) / half_dim)
    angle = np.arange(seq, dtype=np.float32)[:, None] * frequency.astype(np.float32)[None, :]
    cosine, sine = np.cos(angle), np.sin(angle)
    return (
        np.concatenate([cosine, cosine], axis=1).astype(np.float32),
        np.concatenate([-sine, sine], axis=1).astype(np.float32),
    )


def heads_shards(
    zs, activations, document_ids, attn_gain, w_query, w_key, w_value, w_out, mlp_gain, w_gate, w_up, w_down, cotangent
):
    stretch, width = activations.shape[3:]
    deep = w_query.shape[0]
    seq = document_ids.shape[1]
    pair = 2 * seq
    wide = w_gate.shape[1] // (4 * zs)
    x = activations.reshape(2, stretch, width)
    cot = cotangent.reshape(2, stretch, width)
    small = jnp.stack([attn_gain.astype(F32), mlp_gain.astype(F32)])
    docs_rows = document_ids.astype(F32).reshape(seq // deep, deep)
    small = jnp.concatenate([small, docs_rows, jnp.zeros((6 - seq // deep, deep), F32)])
    cosine, sine = (jnp.asarray(table) for table in rope_tables(seq))
    half = stretch // 2
    hidden, qkv, attended, qkv_w, out_w, gains, docs, middle, h2_all, cot_all, gu_w, down_w = call(
        functools.partial(forward_kernel, zs),
        1,
        [
            ((pair, width), BF, ANY),
            ((pair, 3 * HEAD_DIM), BF, ANY),
            ((pair, HEAD_DIM), BF, ANY),
            ((width, 3 * HEAD_DIM), BF, ANY),
            ((HEAD_DIM, width), BF, ANY),
            ((8, width), F32, ANY),
            ((8, seq), F32, ANY),
            ((stretch, width), F32, ANY),
            ((4, zs, 2, stretch, width), BF, ANY),
            ((4, zs, 2, stretch, width), BF, ANY),
            ((width, 2 * wide), BF, ANY),
            ((wide, width), BF, ANY),
        ],
        [
            VMEM((pair, width), BF),
            VMEM((pair, width), BF),
            VMEM((width, 3 * HEAD_DIM), BF),
            VMEM((HEAD_DIM, width), BF),
            VMEM((zs, 8, deep), F32),
            VMEM((2, 8, deep), F32),
            VMEM((8, width), F32),
            VMEM((8, seq), F32),
            VMEM((seq, HEAD_DIM), F32),
            VMEM((seq, HEAD_DIM), F32),
            VMEM((pair, 3 * HEAD_DIM), BF),
            VMEM((pair, HEAD_DIM), BF),
            VMEM((2, 2, zs, stretch, width), BF),
            VMEM((2, zs, stretch, width), BF),
            VMEM((zs, stretch, width), BF),
            VMEM((zs, stretch, width), BF),
            VMEM((stretch, width), BF),
            VMEM((stretch, width), BF),
            VMEM((stretch, width), F32),
        ],
        240,
        (x, w_query, w_key, w_value, w_out, small, cosine, sine, w_gate, w_up, w_down, cot),
        52,
    )

    h2 = h2_all.reshape(4 * seq, width)
    cots = cot_all.reshape(4 * seq, width)
    gate_up = dot(h2, gu_w)
    gate, upward = gate_up[:, :wide], gate_up[:, wide:]
    grad_product = dot(cots, down_w, ((1,), (1,)))
    sigma_gate = jax.nn.sigmoid(gate)
    silu = gate * sigma_gate
    product = (silu * upward).astype(BF)
    grad_gate = (grad_product * upward * sigma_gate * (1.0 + gate * (1.0 - sigma_gate))).astype(BF)
    grad_up = (grad_product * silu).astype(BF)
    grad_gu = jnp.concatenate([grad_gate, grad_up], axis=1)
    gh_part = dot(grad_gu, gu_w, ((1,), (1,)), BF).reshape(4, zs, 2, stretch, width)
    feed_part = dot(product, down_w, kind=BF).reshape(4, zs, 2, stretch, width)
    gu_grad = dot(h2, grad_gu, ((0,), (0,)), BF)
    down_grad = dot(product, cots, ((0,), (0,)), BF)

    sum_scratch = [
        VMEM((4, zs, stretch, width), BF),
        VMEM((4, zs, stretch, width), BF),
        VMEM((2, 2, zs, half, width), BF),
        VMEM((2, zs, half, width), BF),
        VMEM((zs, stretch, width), BF),
    ]
    layer_out, input_grad, q_g, k_g, v_g, o_g, gate_g, up_g, down_g, gains_g = call(
        functools.partial(backward_kernel, zs),
        2,
        [
            ((2, stretch, width), BF, ANY),
            ((2, stretch, width), BF, ANY),
            (w_query.shape, BF, ANY),
            (w_key.shape, BF, ANY),
            (w_value.shape, BF, ANY),
            (w_out.shape, BF, ANY),
            (w_gate.shape, BF, ANY),
            (w_up.shape, BF, ANY),
            (w_down.shape, BF, ANY),
            ((2, 8, deep), F32, VMEM),
        ],
        sum_scratch
        + sum_scratch
        + [
            VMEM((2, 2, zs, stretch, width), BF),
            VMEM((2, zs, stretch, width), BF),
            VMEM((zs, stretch, width), BF),
            VMEM((zs, stretch, width), BF),
            VMEM((pair, width), BF),
            VMEM((pair, 3 * HEAD_DIM), BF),
            VMEM((pair, HEAD_DIM), BF),
            VMEM((width, 3 * HEAD_DIM), BF),
            VMEM((HEAD_DIM, width), BF),
            VMEM((pair, width), BF),
            VMEM((pair, 3 * HEAD_DIM), BF),
            VMEM((8, width), F32),
            VMEM((8, seq), F32),
            VMEM((seq, HEAD_DIM), F32),
            VMEM((seq, HEAD_DIM), F32),
            VMEM((seq, HEAD_DIM), BF),
            VMEM((stretch, width), F32),
            VMEM((stretch, width), BF),
            VMEM((stretch, width), BF),
            VMEM((stretch, width), F32),
            VMEM((stretch, width), BF),
            VMEM((stretch, width), BF),
            VMEM((stretch, width), BF),
            VMEM((2, 8, width), F32),
            VMEM((3, 2, 8, width), F32),
            VMEM((zs, 2, 8, deep), F32),
            VMEM((zs, deep // 2, 3 * HEAD_DIM), BF),
            VMEM((zs, deep // 2, 3 * HEAD_DIM), BF),
            VMEM((zs, deep // 2, 3 * HEAD_DIM), BF),
            VMEM((zs, HEAD_DIM, deep), BF),
            VMEM((zs, HEAD_DIM // 2, deep), BF),
            VMEM((zs, HEAD_DIM // 2, deep), BF),
        ],
        400,
        (
            gh_part, feed_part, gu_grad, down_grad, middle, cot, x, gains, docs, cosine, sine,
            hidden, qkv, attended, qkv_w, out_w,
        ),
        60,
    )
    gain_grads = jnp.sum(gains_g, axis=1)
    return (
        layer_out.reshape(activations.shape),
        input_grad.reshape(activations.shape),
        gain_grads[0],
        q_g.astype(F32),
        k_g.astype(F32),
        v_g.astype(F32),
        o_g.astype(F32),
        gain_grads[1],
        gate_g.astype(F32),
        up_g.astype(F32),
        down_g.astype(F32),
    )


def angles(positions):
    half_dim = HEAD_DIM // 2
    frequency = ROPE_BASE ** (-jnp.arange(half_dim, dtype=jnp.float32) / half_dim)
    angle = positions.astype(jnp.float32)[:, None] * frequency[None, :]
    return (jnp.cos(angle)[:, None, :], jnp.sin(angle)[:, None, :])


def rotate(flat, positions):
    row_count = flat.shape[0]
    heads = flat.reshape(row_count, -1, HEAD_DIM)
    cosine, sine = angles(positions)
    first = heads[..., : HEAD_DIM // 2]
    second = heads[..., HEAD_DIM // 2 :]
    turned = jnp.concatenate(
        [first * cosine - second * sine, second * cosine + first * sine], axis=-1
    )
    return turned.reshape(row_count, -1)


def unrotate(flat, positions):
    row_count = flat.shape[0]
    heads = flat.reshape(row_count, -1, HEAD_DIM)
    cosine, sine = angles(positions)
    first = heads[..., : HEAD_DIM // 2]
    second = heads[..., HEAD_DIM // 2 :]
    turned = jnp.concatenate(
        [first * cosine + second * sine, second * cosine - first * sine], axis=-1
    )
    return turned.reshape(row_count, -1)


def normalize(values):
    inverse = lax.rsqrt(jnp.mean(values * values, axis=-1, keepdims=True) + EPS)
    return (values * inverse, inverse)


def norm_back(grad_normed_out, normed, inverse, gain):
    scaled = grad_normed_out * gain
    return inverse * (scaled - normed * jnp.mean(scaled * normed, axis=-1, keepdims=True))


def contract_rows(left, right):
    return lax.dot_general(
        left, right, (((1,), (1,)), ((), ())), preferred_element_type=jnp.float32
    )


def contract_cols(left, right):
    return lax.dot_general(
        left, right, (((0,), (0,)), ((), ())), preferred_element_type=jnp.float32
    )


def visibility(query_positions, query_docs, key_positions, key_docs):
    same_doc = query_docs[:, None] == key_docs[None, :]
    earlier = key_positions[None, :] <= query_positions[:, None]
    return jnp.where(same_doc & earlier, 1.0, 0.0).astype(jnp.float32)


def merge_heads(stacked):
    return jnp.transpose(stacked, (1, 0, 2)).reshape(stacked.shape[1], -1)


def head_slice(matrix, offset):
    return lax.dynamic_slice_in_dim(matrix, offset, HEAD_DIM, 1)


def attend_forward(queries, key_rows, value_rows, visible):
    score_scale = HEAD_DIM ** (-0.5)

    def one_head(head_index):
        offset = head_index * HEAD_DIM
        scores = (
            contract_rows(head_slice(queries, offset), head_slice(key_rows, offset)) * score_scale
        )
        weights = (jax.nn.sigmoid(scores - SHIFT) * visible).astype(jnp.bfloat16)
        return jnp.dot(weights, head_slice(value_rows, offset), preferred_element_type=jnp.float32)

    stacked = lax.map(one_head, jnp.arange(queries.shape[1] // HEAD_DIM))
    return merge_heads(stacked)


def attend_back(queries, key_rows, value_rows, grad_attended, visible):
    score_scale = HEAD_DIM ** (-0.5)

    def one_head(head_index):
        offset = head_index * HEAD_DIM
        head_query = head_slice(queries, offset)
        head_key = head_slice(key_rows, offset)
        head_grad = head_slice(grad_attended, offset)
        scores = contract_rows(head_query, head_key) * score_scale
        sigma = jax.nn.sigmoid(scores - SHIFT)
        grad_weights = contract_rows(head_grad, head_slice(value_rows, offset))
        grad_scores = (grad_weights * visible * sigma * (1.0 - sigma)).astype(jnp.bfloat16)
        pieces = []
        pieces.append(
            jnp.dot(grad_scores, head_key, preferred_element_type=jnp.float32) * score_scale
        )
        weights = (sigma * visible).astype(jnp.bfloat16)
        pieces.append(contract_cols(grad_scores, head_query) * score_scale)
        pieces.append(contract_cols(weights, head_grad))
        return tuple(pieces)

    stacked = lax.map(one_head, jnp.arange(queries.shape[1] // HEAD_DIM))
    return tuple((merge_heads(piece) for piece in stacked))


def rows_shards(
    activations,
    document_ids,
    attn_gain,
    w_query,
    w_key,
    w_value,
    w_out,
    mlp_gain,
    w_gate,
    w_up,
    w_down,
    cotangent,
):
    groups = lax.axis_size("cp")
    rank = lax.axis_index("cp")
    stretch_len = activations.shape[3]
    width = activations.shape[4]
    row_count = 2 * stretch_len
    offsets = jnp.arange(stretch_len, dtype=jnp.int32)
    my_positions = jnp.concatenate(
        [rank * stretch_len + offsets, (2 * groups - 1 - rank) * stretch_len + offsets]
    )
    all_docs = document_ids[0]
    my_docs = jnp.take(all_docs, my_positions)
    slots = jnp.arange(groups * row_count, dtype=jnp.int32)
    owners = slots // row_count
    halves = slots // stretch_len % 2
    key_positions = (
        jnp.where(halves == 0, owners, 2 * groups - 1 - owners) * stretch_len + slots % stretch_len
    )
    key_docs = jnp.take(all_docs, key_positions)
    visible = visibility(my_positions, my_docs, key_positions, key_docs)
    gathered = (
        lax.all_gather(w_query, "cp", axis=0, tiled=True),
        lax.all_gather(w_key, "cp", axis=0, tiled=True),
        lax.all_gather(w_value, "cp", axis=0, tiled=True),
        lax.all_gather(w_out, "cp", axis=1, tiled=True),
        lax.all_gather(w_gate, "cp", axis=0, tiled=True),
        lax.all_gather(w_up, "cp", axis=0, tiled=True),
        lax.all_gather(w_down, "cp", axis=1, tiled=True),
        lax.all_gather(attn_gain, "cp", axis=0, tiled=True),
        lax.all_gather(mlp_gain, "cp", axis=0, tiled=True),
    )
    (
        query_full,
        key_full,
        value_full,
        out_full,
        gate_full,
        up_full,
        down_full,
        gain_one,
        gain_two,
    ) = gathered
    gain_one = gain_one.astype(jnp.float32)
    gain_two = gain_two.astype(jnp.float32)
    inputs = activations.reshape(row_count, width).astype(jnp.float32)
    normed_one, inverse_one = normalize(inputs)
    hidden_one = (normed_one * gain_one).astype(jnp.bfloat16)
    queries = rotate(
        jnp.dot(hidden_one, query_full, preferred_element_type=jnp.float32), my_positions
    ).astype(jnp.bfloat16)
    keys_local = rotate(
        jnp.dot(hidden_one, key_full, preferred_element_type=jnp.float32), my_positions
    ).astype(jnp.bfloat16)
    values_local = jnp.dot(hidden_one, value_full, preferred_element_type=jnp.float32).astype(
        jnp.bfloat16
    )
    keys_all, values_all = (
        lax.all_gather(keys_local, "cp", axis=0, tiled=True),
        lax.all_gather(values_local, "cp", axis=0, tiled=True),
    )
    attended = attend_forward(queries, keys_all, values_all, visible).astype(jnp.bfloat16)
    branch = lax.psum(jnp.dot(attended, out_full, preferred_element_type=jnp.float32), "tp")
    middle = inputs + branch
    normed_two, inverse_two = normalize(middle)
    hidden_two = (normed_two * gain_two).astype(jnp.bfloat16)
    gate = jnp.dot(hidden_two, gate_full, preferred_element_type=jnp.float32)
    upward = jnp.dot(hidden_two, up_full, preferred_element_type=jnp.float32)
    sigma_gate = jax.nn.sigmoid(gate)
    silu_gate = gate * sigma_gate
    product = (silu_gate * upward).astype(jnp.bfloat16)
    feed = lax.psum(jnp.dot(product, down_full, preferred_element_type=jnp.float32), "tp")
    result = middle + feed
    layer_out = result.astype(jnp.bfloat16).reshape(activations.shape)
    grad_result = cotangent.reshape(row_count, width).astype(jnp.float32)
    grad_feed = grad_result.astype(jnp.bfloat16)
    grad_product = contract_rows(grad_feed, down_full)
    grad_gate = (grad_product * upward * sigma_gate * (1.0 + gate * (1.0 - sigma_gate))).astype(
        jnp.bfloat16
    )
    grad_up = (grad_product * silu_gate).astype(jnp.bfloat16)
    grad_hidden_two = lax.psum(
        contract_rows(grad_gate, gate_full) + contract_rows(grad_up, up_full), "tp"
    )
    grad_gain_two = jnp.sum(grad_hidden_two * normed_two, axis=0)
    grad_middle = grad_result + norm_back(grad_hidden_two, normed_two, inverse_two, gain_two)
    grad_down = contract_cols(product, grad_feed)
    grad_gate_w = contract_cols(hidden_two, grad_gate)
    grad_up_w = contract_cols(hidden_two, grad_up)
    share_gate, share_up, share_down, share_gain_two = (
        lax.psum_scatter(grad_gate_w, "cp", scatter_dimension=0, tiled=True),
        lax.psum_scatter(grad_up_w, "cp", scatter_dimension=0, tiled=True),
        lax.psum_scatter(grad_down, "cp", scatter_dimension=1, tiled=True),
        lax.psum_scatter(grad_gain_two, "cp", scatter_dimension=0, tiled=True),
    )
    grad_branch = grad_middle.astype(jnp.bfloat16)
    grad_attended = contract_rows(grad_branch, out_full).astype(jnp.bfloat16)
    grad_queries, key_terms, value_terms = attend_back(
        queries, keys_all, values_all, grad_attended, visible
    )
    grad_keys, grad_values = (
        lax.psum_scatter(key_terms, "cp", scatter_dimension=0, tiled=True),
        lax.psum_scatter(value_terms, "cp", scatter_dimension=0, tiled=True),
    )
    grad_query_pre = unrotate(grad_queries, my_positions).astype(jnp.bfloat16)
    grad_key_pre = unrotate(grad_keys, my_positions).astype(jnp.bfloat16)
    grad_value_pre = grad_values.astype(jnp.bfloat16)
    local_hidden = (
        contract_rows(grad_query_pre, query_full)
        + contract_rows(grad_key_pre, key_full)
        + contract_rows(grad_value_pre, value_full)
    )
    grad_hidden_one = lax.psum(local_hidden, "tp")
    grad_gain_one = jnp.sum(grad_hidden_one * normed_one, axis=0)
    grad_inputs = grad_middle + norm_back(grad_hidden_one, normed_one, inverse_one, gain_one)
    grad_query_w = contract_cols(hidden_one, grad_query_pre)
    grad_key_w = contract_cols(hidden_one, grad_key_pre)
    grad_value_w = contract_cols(hidden_one, grad_value_pre)
    grad_out_w = contract_cols(attended, grad_branch)
    share_query, share_key, share_value, share_out, share_gain_one = (
        lax.psum_scatter(grad_query_w, "cp", scatter_dimension=0, tiled=True),
        lax.psum_scatter(grad_key_w, "cp", scatter_dimension=0, tiled=True),
        lax.psum_scatter(grad_value_w, "cp", scatter_dimension=0, tiled=True),
        lax.psum_scatter(grad_out_w, "cp", scatter_dimension=1, tiled=True),
        lax.psum_scatter(grad_gain_one, "cp", scatter_dimension=0, tiled=True),
    )
    summed = lax.psum(
        (
            share_gain_one,
            share_query,
            share_key,
            share_value,
            share_out,
            share_gain_two,
            share_gate,
            share_up,
            share_down,
        ),
        "dp",
    )
    input_grad = grad_inputs.astype(jnp.bfloat16).reshape(activations.shape)
    return (
        layer_out,
        input_grad,
        summed[0],
        summed[1],
        summed[2],
        summed[3],
        summed[4],
        summed[5],
        summed[6],
        summed[7],
        summed[8],
    )


def layer(sizes, *args):
    heads = args[3].shape[1] // HEAD_DIM
    zs = sizes["cp"]
    fits = sizes["dp"] == 4 and sizes["tp"] == 2 and zs == 4 and heads == 2 * zs
    fits = fits and args[0].shape[3] % 32 == 0 and args[8].shape[1] % (4 * zs * HEAD_DIM) == 0
    fits = fits and args[3].shape[0] % HEAD_DIM == 0 and args[1].shape[1] % args[3].shape[0] == 0
    fits = fits and args[1].shape[1] <= 6 * args[3].shape[0]
    if fits:
        return heads_shards(zs, *args)
    return rows_shards(*args)


def solution(mesh):
    return jax.shard_map(
        functools.partial(layer, dict(mesh.shape)),
        mesh=mesh,
        in_specs=(
            P("dp", "cp", None, None, None),
            P("dp", None),
            P("cp"),
            P("cp", "tp"),
            P("cp", "tp"),
            P("cp", "tp"),
            P("tp", "cp"),
            P("cp"),
            P("cp", "tp"),
            P("cp", "tp"),
            P("tp", "cp"),
            P("dp", "cp", None, None, None),
        ),
        out_specs=(
            P("dp", "cp", None, None, None),
            P("dp", "cp", None, None, None),
            P("cp"),
            P("cp", "tp"),
            P("cp", "tp"),
            P("cp", "tp"),
            P("tp", "cp"),
            P("cp"),
            P("cp", "tp"),
            P("cp", "tp"),
            P("tp", "cp"),
        ),
        check_vma=False,
    )
```

```python
import functools
import math

import jax
import jax.numpy as jnp
import numpy as np
from jax import lax
from jax.experimental import pallas as pl
from jax.experimental.pallas import tpu as pltpu
from jax.sharding import PartitionSpec as P

HEAD_DIM = 128
EPS = 1e-05
SHIFT = math.log(4096.0)
ROPE_BASE = 10000.0
BF = jnp.bfloat16
F32 = jnp.float32
MESH = pl.DeviceIdType.MESH
ANY = pl.ANY
VMEM = pltpu.VMEM
MIB = 2**20


class Net:
    def __init__(self, zs, send_sems, recv_sems, local_sems):
        self.zs = zs
        self.dp, self.z, self.t = (lax.axis_index(a) for a in ("dp", "cp", "tp"))
        self.a, self.b = lax.div(self.dp, 2), lax.rem(self.dp, 2)
        self.send_sems, self.recv_sems, self.local_sems = send_sems, recv_sems, local_sems
        self.arrivals = 0
        self.free_locals = list(range(local_sems.shape[0]))
        self.open = []

    def along_z(self, s):
        return (self.dp, lax.rem(self.z + s, self.zs), self.t)

    def source_z(self, s):
        return lax.rem(self.z + self.zs - s, self.zs)

    @property
    def over_x(self):
        return (2 * self.a + 1 - self.b, self.z, self.t)

    @property
    def over_y(self):
        return (2 * (1 - self.a) + self.b, self.z, self.t)

    @property
    def sibling(self):
        return (self.dp, self.z, 1 - self.t)

    @property
    def across(self):
        return (2 * (1 - self.a) + 1 - self.b, self.z, self.t)

    def meet(self):
        ways = [self.along_z(s) for s in range(1, self.zs)] + [self.over_x, self.over_y, self.across, self.sibling]
        barrier = pltpu.get_barrier_semaphore()
        for way in ways:
            pl.semaphore_signal(barrier, inc=1, device_id=way, device_id_type=MESH)
        pl.semaphore_wait(barrier, len(ways))

    def slot(self):
        self.arrivals += 1
        return self.arrivals - 1

    def send(self, src, dst, way, arrive=None, when=None):
        arrive = self.slot() if arrive is None else arrive
        sem = self.send_sems.at[len(self.open)]
        copy = pltpu.make_async_remote_copy(
            src, dst, sem, self.recv_sems.at[arrive], device_id=way, device_id_type=MESH
        )
        if when is None:
            copy.start()
        else:
            pl.when(when)(copy.start)
        self.open.append((copy, when))
        return copy

    def arrival(self, ref, slot):
        return pltpu.make_async_remote_copy(
            ref, ref, self.send_sems.at[0], self.recv_sems.at[slot], device_id=self.sibling, device_id_type=MESH
        )

    def keep(self, src, dst):
        return Kept(self, src, dst)

    def finish(self):
        for copy, when in self.open:
            if when is None:
                copy.wait_send()
            else:
                pl.when(when)(copy.wait_send)


class Kept:
    def __init__(self, net, src, dst):
        self.net, self.slot = net, net.free_locals.pop(0)
        self.copy = pltpu.make_async_copy(src, dst, net.local_sems.at[self.slot])
        self.copy.start()

    def wait(self):
        self.copy.wait()
        self.net.free_locals.append(self.slot)


class LineGather:
    def __init__(self, net, src, place):
        self.net, self.src, self.place = net, src, place
        self.h, self.low = lax.div(net.z, 2), lax.rem(net.z, 2)
        self.mate = (net.dp, net.z + 1 - 2 * self.low, net.t)
        self.gate = (net.dp, 2 - self.h, net.t)
        self.hands_on = self.h != self.low

    def start(self):
        net = self.net
        mine = self.place(net.z)
        self.near = net.send(self.src, mine, self.mate)
        self.slots = [net.slot(), net.slot()]
        net.send(self.src, mine, self.gate, arrive=self.slots[0] + self.low)

    def take(self, s):
        net = self.net
        if s == 1:
            self.near.wait_recv()
            return net.z + 1 - 2 * self.low
        z = 2 * (1 - self.h) + s - 2
        ref = self.place(z)
        net.arrival(ref, self.slots[s - 2]).wait_recv()
        net.send(ref, ref, self.mate, arrive=self.slots[s - 2], when=self.hands_on)
        return z


def plane_relay(net, place, halves, over_x, over_y, ways="xy", sibling=None):
    dx, dy = 2 * net.a + 1 - net.b, 2 * (1 - net.a) + net.b
    relays = []

    def by_y():
        over_x.wait_recv()
        piece = halves(place(dx), 0) if "x" in ways else place(dx)
        if "y" in ways:
            relays.append(net.send(piece, piece, net.over_y))
        if sibling:
            sibling(dx)

    def by_x():
        over_y.wait_recv()
        piece = halves(place(dy), 1) if "y" in ways else place(dy)
        if "x" in ways:
            relays.append(net.send(piece, piece, net.over_x))
        if sibling:
            sibling(dy)

    for step in (by_x, by_y) if ways == "x" else (by_y, by_x):
        step()
    return relays


def plane_end(net, relays, sibling=None):
    for copy in relays:
        copy.wait_recv()
    if sibling:
        sibling(2 * (1 - net.a) + 1 - net.b)


def rows_loop(count, step, body):
    def one(i, carry):
        body(pl.ds(pl.multiple_of(i * step, step), step))
        return carry

    lax.fori_loop(0, count // step, one, 0)


def add_rows(out, terms, rows):
    def body(at):
        total = terms[0][at, :].astype(F32)
        for term in terms[1:]:
            total += term[at, :].astype(F32)
        out[at, :] = total.astype(out.dtype)

    rows_loop(rows, 16, body)


class GatherAll:
    def __init__(self, net, src, dst):
        self.net, self.src, self.dst = net, src, dst
        rows = src.shape[0] // 2
        self.halves = lambda ref, k: ref.at[pl.ds(k * rows, rows)]

    def place(self, dp, z):
        return self.dst.at[dp, z, self.net.t]

    def start(self):
        net = self.net
        mine = self.place(net.dp, net.z)
        self.line = LineGather(net, self.src, lambda z: self.place(net.dp, z))
        self.line.start()
        self.local = net.keep(self.src, mine)
        self.plane = [(net.z, net.send(self.src, mine, net.over_x), net.send(self.src, mine, net.over_y))]
        self.twin = [net.send(self.src, mine, net.sibling)]
        self.states = []

    def to_twin(self, dp, z):
        ref = self.place(dp, z)
        self.twin.append(self.net.send(ref, ref, self.net.sibling))

    def spread(self, s):
        net = self.net
        z = self.line.take(s)
        ref = self.place(net.dp, z)
        self.plane.append((z, net.send(ref, ref, net.over_x), net.send(ref, ref, net.over_y)))
        self.to_twin(net.dp, z)

    def relay(self, s):
        z, over_x, over_y = self.plane[s]
        place = functools.partial(self.place, z=z)
        self.states.append((z, plane_relay(self.net, place, self.halves, over_x, over_y, sibling=lambda dp: self.to_twin(dp, z))))

    def end(self):
        for z, relays in self.states:
            plane_end(self.net, relays, lambda dp, z=z: self.to_twin(dp, z))
        for copy in self.twin:
            copy.wait_recv()
        self.local.wait()


class GatherGroup:
    def __init__(self, net, src, dst, own_lanes=None):
        self.net, self.src, self.dst, self.own_lanes = net, src, dst, own_lanes
        self.rows = src.shape[0]

    def place(self, b, z, t=None):
        t = self.net.t if t is None else t
        last = 2 * self.net.zs - 1
        at = ((last + 1) * b + z + t * (last - 2 * z)) * self.rows
        return self.dst.at[pl.ds(pl.multiple_of(at, self.rows), self.rows)]

    def start(self):
        net = self.net
        mine = self.place(net.b, net.z)
        self.line = LineGather(net, self.src, lambda z: self.place(net.b, z))
        self.line.start()
        self.over = [(net.z, net.send(self.src, mine, net.over_x))]
        self.twin, self.local = [], []
        if self.own_lanes is None:
            self.local.append(net.keep(self.src, mine))
            self.twin.append((net.b, net.z, net.send(self.src, mine, net.sibling)))
        else:
            for t in (0, 1):
                self.local.append(net.keep(self.own_lanes.at[t], self.place(net.b, net.z, t)))

    def to_twin(self, b, z):
        ref = self.place(b, z)
        self.twin.append((b, z, self.net.send(ref, ref, self.net.sibling)))

    def spread(self, s):
        net = self.net
        z = self.line.take(s)
        ref = self.place(net.b, z)
        self.over.append((z, net.send(ref, ref, net.over_x)))
        self.to_twin(net.b, z)
        return z

    def far(self, s):
        z, copy = self.over[s]
        copy.wait_recv()
        self.to_twin(1 - self.net.b, z)
        return z

    def end(self):
        for _, _, copy in self.twin:
            copy.wait_recv()
        for copy in self.local:
            copy.wait()


class SumGroup:
    def __init__(self, net, part, sib, far, landed):
        self.net, self.part, self.sib, self.far, self.landed = net, part, sib, far, landed
        self.rows = part.shape[3]
        self.twin, self.over, self.z_sends = {}, [], []

    def order(self):
        return [lax.rem(self.net.z + s + 1, self.net.zs) for s in range(self.net.zs)]

    def give(self, k):
        net = self.net
        b = net.b if k else 1 - net.b
        for s, z in enumerate(self.order()):
            self.twin[k, s] = net.send(self.part.at[b, 1 - net.t, z], self.sib.at[b, z], net.sibling)

    def take(self, k):
        net = self.net
        b = net.b if k else 1 - net.b
        for s, z in enumerate(self.order()):
            self.twin[k, s].wait_recv()
            own = self.part.at[b, net.t, z]
            add_rows(own, [own, self.sib.at[b, z]], self.rows)
            if k == 0:
                self.over.append(net.send(own, self.far.at[z], net.over_x))

    def along(self):
        net = self.net
        for s, z in enumerate(self.order()):
            self.over[s].wait_recv()
            last = s == net.zs - 1
            own = self.part.at[net.b, net.t, z]
            out = self.landed.at[net.z] if last else own
            add_rows(out, [own, self.far.at[z]], self.rows)
            if not last:
                self.z_sends.append(net.send(out, self.landed.at[net.z], net.along_z(s + 1)))

    def end(self):
        for copy in self.z_sends:
            copy.wait_recv()


class SumLine(SumGroup):
    def take(self, k):
        net = self.net
        b = net.b if k else 1 - net.b
        for s, z in enumerate(self.order()):
            self.twin[k, s].wait_recv()
            own, last = self.part.at[b, net.t, z], s == net.zs - 1
            out = self.landed.at[b, net.z] if last else own
            add_rows(out, [own, self.sib.at[b, z]], self.rows)
            if not last:
                self.z_sends.append(net.send(own, self.landed.at[b, net.z], net.along_z(s + 1)))

    def across(self):
        net = self.net
        b = 1 - net.b
        for copy in self.z_sends[: net.zs - 1]:
            copy.wait_recv()
        out = self.part.at[b, net.t, net.z]
        add_rows(out, [self.landed.at[b, z] for z in range(net.zs)], self.rows)
        self.over = net.send(out, self.far, net.over_x)

    def end(self):
        for copy in self.z_sends[self.net.zs - 1 :]:
            copy.wait_recv()
        self.over.wait_recv()


class SumAll:
    def __init__(self, net, part, own, sib, one, two, landed):
        self.net, self.part, self.own, self.sib = net, part, own, sib
        self.one, self.two, self.landed = one, two, landed
        self.half = part.shape[3] // 2

    def order(self):
        net = self.net
        return [lax.rem(net.z + s + 1, net.zs) for s in range(net.zs)]

    def places(self):
        a, b = self.net.a, self.net.b
        return [2 * (1 - a) + 1 - b, 2 * a + 1 - b, 2 * (1 - a) + b, 2 * a + b]

    def start(self):
        net = self.net
        self.twin, self.mine = [], []
        for z in self.order():
            self.twin.append(net.send(self.part.at[:, z, 1 - net.t], self.sib.at[:, z], net.sibling))
            self.mine.append(net.keep(self.part.at[:, z, net.t], self.own.at[:, z]))

    def upper(self, ref):
        return ref.at[pl.ds(0, self.half)]

    def lower(self, ref):
        return ref.at[pl.ds(self.half, self.half)]

    def first(self, s):
        net = self.net
        z = self.order()[s]
        dd, dx, dy, me = self.places()
        self.twin[s].wait_recv()
        self.mine[s].wait()
        for dp in (dd, dx, dy, me):
            add_rows(self.own.at[dp, z], [self.own.at[dp, z], self.sib.at[dp, z]], 2 * self.half)
        self.ones = getattr(self, "ones", [])
        self.ones.append(
            (
                net.send(self.upper(self.own.at[dd, z]), self.one.at[0, 0, z], net.over_x),
                net.send(self.upper(self.own.at[dx, z]), self.one.at[0, 1, z], net.over_x),
                net.send(self.lower(self.own.at[dd, z]), self.one.at[1, 0, z], net.over_y),
                net.send(self.lower(self.own.at[dy, z]), self.one.at[1, 1, z], net.over_y),
            )
        )

    def second(self, s):
        net = self.net
        z = self.order()[s]
        dd, dx, dy, me = self.places()
        x_dd, x_me, y_dd, y_me = self.ones[s]
        self.twos = getattr(self, "twos", [])
        x_dd.wait_recv()
        out = self.upper(self.own.at[dy, z])
        add_rows(out, [out, self.one.at[0, 0, z]], self.half)
        up = net.send(out, self.two.at[0, z], net.over_y)
        y_dd.wait_recv()
        out = self.lower(self.own.at[dx, z])
        add_rows(out, [out, self.one.at[1, 0, z]], self.half)
        side = net.send(out, self.two.at[1, z], net.over_x)
        self.twos.append((up, side))

    def third(self, s):
        net = self.net
        z = self.order()[s]
        dd, dx, dy, me = self.places()
        _, x_me, _, y_me = self.ones[s]
        up, side = self.twos[s]
        last = s == net.zs - 1
        out = self.landed.at[net.z] if last else self.own.at[me, z]
        x_me.wait_recv()
        up.wait_recv()
        mine = self.own.at[me, z]
        add_rows(self.upper(out), [self.upper(mine), self.one.at[0, 1, z], self.two.at[0, z]], self.half)
        y_me.wait_recv()
        side.wait_recv()
        add_rows(self.lower(out), [self.lower(mine), self.one.at[1, 1, z], self.two.at[1, z]], self.half)
        self.z_sends = getattr(self, "z_sends", [])
        if not last:
            self.z_sends.append(net.send(out, self.landed.at[net.z], net.along_z(s + 1)))

    def end(self):
        for copy in self.z_sends:
            copy.wait_recv()


class SpreadGrads:
    def __init__(self, net, src, dst, ways):
        self.net, self.src, self.dst, self.ways = net, src, dst, ways
        self.z_sends, self.plane, self.states = {}, {}, []

    def mine(self):
        return self.dst(self.net.dp, self.net.z)

    def start(self):
        self.own()
        for s in range(1, self.net.zs):
            self.go(s)

    def own(self):
        self.local = self.net.keep(self.src(self.net.z), self.mine())

    def go(self, s):
        net = self.net
        self.z_sends[s] = net.send(self.src(lax.rem(net.z + s, net.zs)), self.mine(), net.along_z(s))

    def spread(self, s):
        net = self.net
        z = net.source_z(s)
        ref = self.dst(net.dp, z)
        if s:
            self.z_sends[s].wait_recv()
            src = ref
        else:
            src = self.src(net.z)
        self.plane[s] = (z, net.send(src, ref, net.over_x), net.send(src, ref, net.over_y))

    def relay(self, s):
        z, over_x, over_y = self.plane[s]
        self.states.append(plane_relay(self.net, lambda dp: self.dst(dp, z), half_rows, over_x, over_y, self.ways))

    def end(self):
        for relays in self.states:
            plane_end(self.net, relays)
        self.local.wait()


def half_rows(ref, k):
    n = ref.shape[0] // 2
    return ref.at[pl.ds(k * n, n)]


def aligned(i, size):
    return pl.ds(pl.multiple_of(i * size, size), size)


def loop(count, body):
    def one(i, carry):
        body(i)
        return carry

    lax.fori_loop(0, count, one, 0)


def dot(left, right, dims=((1,), (0,)), kind=F32):
    return lax.dot_general(left, right, (dims, ((), ())), preferred_element_type=F32).astype(kind)


def turn(u, cosine, sine):
    return u * cosine + pltpu.roll(u, HEAD_DIM // 2, 1) * sine


def column(row, start, count):
    n = row.shape[1]
    here = lax.broadcasted_iota(jnp.int32, (count, n), 1) == start + lax.broadcasted_iota(jnp.int32, (count, n), 0)
    return jnp.sum(jnp.where(here, row, 0.0), axis=1, keepdims=True)


def seen(row, start, count, flip=False):
    n = row.shape[1]
    same = column(row, start, count) == row
    mine = start + lax.broadcasted_iota(jnp.int32, (count, n), 0)
    other = lax.broadcasted_iota(jnp.int32, (count, n), 1)
    return same & ((mine <= other) if flip else (other <= mine))


def sigma_of(left, right):
    return jax.nn.sigmoid(dot(left, right, ((1,), (1,))) * HEAD_DIM**-0.5 - SHIFT)


def call(kernel, name, outs, scratch, counts, args, vmem):
    return pl.pallas_call(
        kernel,
        out_shape=[jax.ShapeDtypeStruct(shape, kind) for shape, kind, _ in outs],
        in_specs=[pl.BlockSpec(memory_space=ANY)] * len(args),
        out_specs=[pl.BlockSpec(memory_space=space) for _, _, space in outs],
        scratch_shapes=list(scratch) + [pltpu.SemaphoreType.DMA((count,)) for count in counts],
        compiler_params=pltpu.CompilerParams(
            collective_id=name, has_side_effects=True, vmem_limit_bytes=vmem * MIB
        ),
    )(*args)


def forward_kernel(
    zs, x, wq, wk, wv, wo, small, cosine, sine, wg, wu, wd, cot,
    hidden_out, qkv_out, attended_out, qkv_w_out, out_w_out, gains_out, docs_out, middle, h2_all, cot_all, gu_w, down_w,
    x_all, h1, qkv_w, out_w, small_z, small_x, gains, docs, cos_v, sin_v, qkv, attended, part, sib, far, landed,
    x_lane, h2, mid_v, send_sems, recv_sems, local_sems,
):
    net = Net(zs, send_sems, recv_sems, local_sems)
    net.meet()
    deep, wide = wg.shape[0], gu_w.shape[1] // 2
    seq = docs.shape[1]
    half, side = deep // 2, HEAD_DIM // 2
    gather = GatherGroup(net, x.at[net.t], x_all, own_lanes=x)
    gather.start()
    small_waits = [net.send(small, small_z.at[net.z], net.along_z(s)) for s in range(1, zs)]
    small_waits.append(net.send(small, small_x.at[net.b], net.over_x))
    local = [net.keep(small, small_z.at[net.z]), net.keep(small, small_x.at[net.b])]
    local += [net.keep(cosine, cos_v), net.keep(sine, sin_v)]
    lane = net.keep(x.at[net.t], x_lane)

    def head(z):
        return aligned(net.b * zs + z, HEAD_DIM)

    mine = aligned(net.z, deep)
    my_half = pl.ds(pl.multiple_of(net.a * half, half), half)
    qkv_sends, out_sends, w_local = [], [], []
    for m, w in enumerate((wq, wk, wv)):
        col = pl.ds(m * HEAD_DIM, HEAD_DIM)
        w_local.append(net.keep(w.at[:, head(net.z)], qkv_w.at[mine, col]))
    for s in range(1, zs):
        z = lax.rem(net.z + s, zs)
        rows = pl.ds(pl.multiple_of(net.z * deep + net.a * half, half), half)
        qkv_sends.append(
            [
                net.send(w.at[my_half, head(z)], qkv_w.at[rows, pl.ds(m * HEAD_DIM, HEAD_DIM)], net.along_z(s))
                for m, w in enumerate((wq, wk, wv))
            ]
        )
    out_rows = pl.ds(pl.multiple_of(net.a * side, side), side)
    w_local.append(net.keep(wo.at[head(net.z)], out_w.at[:, mine]))
    for s in range(1, zs):
        z = lax.rem(net.z + s, zs)
        at = pl.ds(pl.multiple_of((net.b * zs + z) * HEAD_DIM + net.a * side, side), side)
        out_sends.append(net.send(wo.at[at], out_w.at[out_rows, mine], net.along_z(s)))

    cotan = GatherAll(net, cot.at[net.t], cot_all)
    mlp_waits, mlp_local = [], []

    def block(z):
        return aligned(net.dp * zs + z, wide)

    mlp = (
        (lambda z: wg.at[:, block(z)], gu_w.at[mine, pl.ds(0, wide)]),
        (lambda z: wu.at[:, block(z)], gu_w.at[mine, pl.ds(wide, wide)]),
        (lambda z: wd.at[block(z)], down_w.at[:, mine]),
    )
    for src, dst in mlp:
        mlp_local.append(net.keep(src(net.z), dst))

    def fetch(k):
        src, dst = mlp[k]
        for s in range(1, zs):
            mlp_waits.append(net.send(src(lax.rem(net.z + s, zs)), dst, net.along_z(s)))

    for copy in small_waits:
        copy.wait_recv()
    for copy in local:
        copy.wait()
    for z in range(zs):
        gains[0:1, z * deep : (z + 1) * deep] = small_z[z, 0:1, :]
        gains[1:2, z * deep : (z + 1) * deep] = small_z[z, 1:2, :]
    for b in range(2):
        for k in range(seq // deep):
            docs[b : b + 1, k * deep : (k + 1) * deep] = small_x[b, 2 + k : 3 + k, :]

    def norm_block(ref_at):
        def body(i):
            at = pl.ds(pl.multiple_of(ref_at + i * 16, 16), 16)
            rows = x_all[at, :].astype(F32)
            inverse = lax.rsqrt(jnp.mean(rows * rows, axis=-1, keepdims=True) + EPS)
            h1[at, :] = (rows * inverse * gains[0:1, :]).astype(BF)

        loop(x.shape[1] // 16, body)

    rows = x.shape[1]
    last = 2 * zs - 1

    def offset(b, z, t):
        return ((last + 1) * b + z + t * (last - 2 * z)) * rows

    for copy in gather.local:
        copy.wait()
    gather.local = []
    for t in (0, 1):
        norm_block(offset(net.b, net.z, t))
    for s in range(1, zs):
        norm_block(offset(net.b, gather.spread(s), net.t))
    cotan.start()
    fetch(0)
    qkv_y = []
    for s in range(1, zs):
        norm_block(offset(1 - net.b, gather.far(s - 1), net.t))
        for copy in qkv_sends[s - 1]:
            copy.wait_recv()
        at = qkv_w.at[pl.ds(pl.multiple_of(net.source_z(s) * deep + net.a * half, half), half)]
        qkv_y.append(net.send(at, at, net.over_y))
    norm_block(offset(1 - net.b, gather.far(zs - 1), net.t))
    out_y = []
    for s in range(1, zs):
        out_sends[s - 1].wait_recv()
        at = out_w.at[out_rows, aligned(net.source_z(s), deep)]
        out_y.append(net.send(at, at, net.over_y))
    for b, z, copy in gather.twin:
        copy.wait_recv()
        norm_block(offset(b, z, 1 - net.t))
    for copy in qkv_y:
        copy.wait_recv()
    for copy in w_local:
        copy.wait()
    for s in range(1, zs):
        cotan.spread(s)
    for copy in out_y:
        copy.wait_recv()

    branch = SumGroup(net, part, sib, far, landed)
    tile = 128
    for k in range(2):
        b = net.b if k else 1 - net.b
        base = b * seq

        def project(i):
            at = pl.ds(pl.multiple_of(base + i * 256, 256), 256)
            pos = aligned(i, 256)
            pre = dot(h1[at, :], qkv_w[...])
            c, s = cos_v[pos, :], sin_v[pos, :]
            qkv[at, 0:HEAD_DIM] = turn(pre[:, 0:HEAD_DIM], c, s).astype(BF)
            qkv[at, HEAD_DIM : 2 * HEAD_DIM] = turn(pre[:, HEAD_DIM : 2 * HEAD_DIM], c, s).astype(BF)
            qkv[at, 2 * HEAD_DIM : 3 * HEAD_DIM] = pre[:, 2 * HEAD_DIM : 3 * HEAD_DIM].astype(BF)

        loop(seq // 256, project)
        every = pl.ds(pl.multiple_of(base, seq), seq)
        row = docs[pl.ds(b, 1), :]

        def attend(i):
            at = pl.ds(pl.multiple_of(base + i * tile, tile), tile)
            sigma = sigma_of(qkv[at, 0:HEAD_DIM], qkv[every, HEAD_DIM : 2 * HEAD_DIM])
            weights = jnp.where(seen(row, i * tile, tile), sigma, 0.0).astype(BF)
            found = dot(weights, qkv[every, 2 * HEAD_DIM : 3 * HEAD_DIM], kind=BF)
            attended[at, :] = found
            out = dot(found, out_w[...], kind=BF)
            for j in range(tile // rows):
                blk = i * (tile // rows) + j
                t = lax.div(blk, zs)
                z = (1 - t) * blk + t * (last - blk)
                part[b, t, z] = out[j * rows : (j + 1) * rows, :]

        loop(seq // tile, attend)
        branch.give(k)
    saved = [
        net.keep(h1, hidden_out), net.keep(qkv, qkv_out), net.keep(attended, attended_out),
        net.keep(qkv_w, qkv_w_out), net.keep(out_w, out_w_out), net.keep(gains, gains_out), net.keep(docs, docs_out),
    ]
    branch.take(0)
    branch.take(1)
    branch.along()
    for s in range(zs):
        cotan.relay(s)
    lane.wait()
    branch.end()

    def body(i):
        at = aligned(i, 16)
        total = x_lane[at, :].astype(F32)
        for z in range(zs):
            total += landed[z, at, :].astype(F32)
        mid_v[at, :] = total
        inverse = lax.rsqrt(jnp.mean(total * total, axis=-1, keepdims=True) + EPS)
        h2[at, :] = (total * inverse * gains[1:2, :]).astype(BF)

    loop(rows // 16, body)
    saved.append(net.keep(mid_v, middle))
    hidden = GatherAll(net, h2, h2_all)
    hidden.start()
    hidden.spread(1)
    hidden.spread(2)
    hidden.spread(3)
    fetch(1)
    fetch(2)
    cotan.end()
    for s in range(zs):
        hidden.relay(s)
    hidden.end()
    for copy in saved:
        copy.wait()
    for copy in mlp_waits:
        copy.wait_recv()
    for copy in mlp_local:
        copy.wait()
    net.finish()


ORDER = (
    "g2s0", "hstart", "F0", "g0z", "F1", "F2", "S0", "F3", "S1", "fstart", "T0", "g0s0", "S2", "g0r0",
    "T1", "S3", "fF0", "T2", "g0s1", "fF1", "T3", "g1s0", "hend", "gstart", "fF2", "gs1", "g2z", "g0s2",
    "g0r1", "g0s3", "fF3", "fS0", "gs2", "gs3", "g2s1", "gf0", "fS1", "gf1", "g1z", "g1s1", "gf2", "gf3",
    "gend", "g2s2", "fT0", "A0", "fS2", "g2r0", "B0", "A1", "g1s2", "g1s3", "B1", "W1", "bt0", "W2",
    "sw0", "g2s3", "g2r1", "sw1", "sw2", "g1r0", "sw3", "Ls0", "Ls1", "bt1", "fS3", "Lr0", "g1r1", "fT1",
    "Ls2", "fT2", "g1r2", "bx", "g1r3", "Lr1", "Ls3", "g0r2", "g2r2", "Lr2", "fT3", "bend", "gain2", "Lr3",
    "g0r3", "fend", "gain3", "g2r3",
)
RELAY_WAYS = ("y", "x", "xy", "y", "xy", "xy", "xy")


def backward_kernel(
    zs, gh_part, feed_part, gu_grad, down_grad, middle, cot, x, gains_in, docs_in, cosine, sine,
    hidden_in, qkv_in, attended_in, qkv_w_in, out_w_in,
    layer_out, input_grad, q_out, k_out, v_out, o_out, gate_out, up_out, down_out, gains_out,
    own, sib, one, two, landed, own_f, sib_f, one_f, two_f, landed_f, part, sib_1, far_1, landed_1,
    h1, qkv, attended, qkv_w, out_w, gbr_all, gqkv, gains, docs, cos_v, sin_v, hg, mid_v, cot_v, x_v, gm_v, gbr_v, out_v,
    lo_v, gsum, gall, gsum_z, g_far, g_land, q_give, q_own, q_land, o_part, o_own, o_land, send_sems, recv_sems, local_sems,
):
    net = Net(zs, send_sems, recv_sems, local_sems)
    net.meet()
    deep, wide = gate_out.shape[0], gu_grad.shape[1] // 2
    seq = docs.shape[1]
    half, side = deep // 2, HEAD_DIM // 2
    rows = x.shape[1]
    last = 2 * zs - 1
    scale = HEAD_DIM**-0.5
    hidden = SumAll(net, gh_part, own, sib, one, two, landed)
    feed = SumAll(net, feed_part, own_f, sib_f, one_f, two_f, landed_f)
    local = [net.keep(middle, mid_v), net.keep(cot.at[net.t], cot_v), net.keep(gains_in, gains)]
    local += [net.keep(x.at[net.t], x_v), net.keep(docs_in, docs), net.keep(cosine, cos_v), net.keep(sine, sin_v)]
    local += [net.keep(qkv_in, qkv), net.keep(attended_in, attended), net.keep(qkv_w_in, qkv_w)]
    local += [net.keep(out_w_in, out_w), net.keep(hidden_in, h1)]

    def block(dp, z):
        return aligned(dp * zs + z, wide)

    ways = iter(RELAY_WAYS)
    grads = [
        SpreadGrads(
            net,
            lambda z: gu_grad.at[aligned(z, deep), pl.ds(0, wide)],
            lambda dp, z: gate_out.at[:, block(dp, z)],
            next(ways),
        ),
        SpreadGrads(
            net,
            lambda z: gu_grad.at[aligned(z, deep), pl.ds(wide, wide)],
            lambda dp, z: up_out.at[:, block(dp, z)],
            next(ways),
        ),
        SpreadGrads(
            net,
            lambda z: down_grad.at[:, aligned(z, deep)],
            lambda dp, z: down_out.at[block(dp, z)],
            next(ways),
        ),
    ]

    def q_place(ref):
        def place(dp, z):
            a, b = lax.div(dp, 2), lax.rem(dp, 2)
            return ref.at[pl.ds(pl.multiple_of(a * half, half), half), aligned(b * zs + z, HEAD_DIM)]

        return place

    def o_place(dp, z):
        a, b = lax.div(dp, 2), lax.rem(dp, 2)
        return o_out.at[pl.ds(pl.multiple_of((b * zs + z) * HEAD_DIM + a * side, side), side)]

    late = [
        SpreadGrads(net, lambda z, m=m: q_own.at[z, :, pl.ds(m * HEAD_DIM, HEAD_DIM)], q_place(ref), next(ways))
        for m, ref in enumerate((q_out, k_out, v_out))
    ]
    late.append(SpreadGrads(net, lambda z: o_own.at[z], o_place, next(ways)))
    branch = SumLine(net, part, sib_1, far_1, landed_1)
    gather = GatherGroup(net, gbr_v, gbr_all)
    tile = 128
    outs, pairs, swaps, plane, z_gain = [], [], [], [], []

    def total_of(ref, at):
        total = ref[0, at, :].astype(F32)
        for z in range(1, zs):
            total += ref[z, at, :].astype(F32)
        return total

    def norm_back(inputs, total, gain, k):
        inverse = lax.rsqrt(jnp.mean(inputs * inputs, axis=-1, keepdims=True) + EPS)
        normed = inputs * inverse
        prod = total * normed
        gsum[k] += prod[0:8, :] + prod[8:16, :]
        scaled = total * gain
        return inverse * (scaled - normed * jnp.mean(scaled * normed, axis=-1, keepdims=True))

    def hidden_end():
        for copy in local:
            copy.wait()
        hidden.end()
        gsum[...] = jnp.zeros_like(gsum)

        def back_two(i):
            at = aligned(i, 16)
            grad = cot_v[at, :].astype(F32) + norm_back(mid_v[at, :], total_of(landed, at), gains[1:2, :], 1)
            gm_v[at, :] = grad
            gbr_v[at, :] = grad.astype(BF)

        loop(rows // 16, back_two)

    def place_of(k):
        b = net.b if k else 1 - net.b
        return b, b * seq, pl.ds(pl.multiple_of(b * seq, seq), seq), docs[pl.ds(b, 1), :]

    def queries_back(k):
        b, base, every, row = place_of(k)

        def heads_grad(i):
            at = pl.ds(pl.multiple_of(base + i * 256, 256), 256)
            hg[aligned(i, 256), :] = dot(gbr_all[at, :], out_w[...], ((1,), (1,)), BF)

        loop(seq // 256, heads_grad)

        def by_query(i):
            at = pl.ds(pl.multiple_of(base + i * tile, tile), tile)
            pos = aligned(i, tile)
            keys = qkv[every, HEAD_DIM : 2 * HEAD_DIM]
            sigma = sigma_of(qkv[at, 0:HEAD_DIM], keys)
            gw = dot(hg[pos, :], qkv[every, 2 * HEAD_DIM : 3 * HEAD_DIM], ((1,), (1,)))
            gs = jnp.where(seen(row, i * tile, tile), gw * sigma * (1.0 - sigma), 0.0).astype(BF)
            gq = dot(gs, keys) * scale
            gqkv[at, 0:HEAD_DIM] = turn(gq, cos_v[pos, :], -sin_v[pos, :]).astype(BF)

        loop(seq // tile, by_query)

    def keys_back(k):
        b, base, every, row = place_of(k)

        def by_key(i):
            at = pl.ds(pl.multiple_of(base + i * tile, tile), tile)
            pos = aligned(i, tile)
            queries = qkv[every, 0:HEAD_DIM]
            sigma = sigma_of(qkv[at, HEAD_DIM : 2 * HEAD_DIM], queries)
            gw = dot(qkv[at, 2 * HEAD_DIM : 3 * HEAD_DIM], hg[...], ((1,), (1,)))
            mask = seen(row, i * tile, tile, flip=True)
            gs = jnp.where(mask, gw * sigma * (1.0 - sigma), 0.0).astype(BF)
            weights = jnp.where(mask, sigma, 0.0).astype(BF)
            gk = dot(gs, queries) * scale
            gqkv[at, HEAD_DIM : 2 * HEAD_DIM] = turn(gk, cos_v[pos, :], -sin_v[pos, :]).astype(BF)
            gqkv[at, 2 * HEAD_DIM : 3 * HEAD_DIM] = dot(weights, hg[...], kind=BF)

        loop(seq // tile, by_key)

        def back_one(i):
            at = pl.ds(pl.multiple_of(base + i * tile, tile), tile)
            out = dot(gqkv[at, :], qkv_w[...], ((1,), (1,)), BF)
            for j in range(tile // rows):
                blk = i * (tile // rows) + j
                t = lax.div(blk, zs)
                z = (1 - t) * blk + t * (last - blk)
                part[b, t, z] = out[j * rows : (j + 1) * rows, :]

        loop(seq // tile, back_one)
        branch.give(k)

    def qkv_grad(z, a):
        at = pl.ds(pl.multiple_of(z * deep + a * half, half), half)
        return dot(h1[:, at], gqkv[...], ((0,), (0,)), BF)

    def side_rows(a):
        return pl.ds(pl.multiple_of(a * side, side), side)

    def weights_give():
        def out_grad(z):
            o_part[z] = dot(attended[...], gbr_all[:, aligned(z, deep)], ((0,), (0,)), BF)

        def theirs(z):
            q_give[z] = qkv_grad(z, 1 - net.a)

        loop(zs, out_grad)
        loop(zs, theirs)
        for s in range(zs):
            z = lax.rem(net.z + s + 1, zs)
            swaps.append(
                (
                    z,
                    net.send(q_give.at[z], q_land.at[z], net.over_y),
                    net.send(o_part.at[z, side_rows(1 - net.a)], o_land.at[z], net.over_y),
                )
            )

    def weights_own():
        def ours(z):
            q_own[z] = qkv_grad(z, net.a)

        loop(zs, ours)

    def weights_sum(s):
        z, q_in, o_in = swaps[s]
        q_in.wait_recv()
        add_rows(q_own.at[z], [q_own.at[z], q_land.at[z]], half)
        o_in.wait_recv()
        add_rows(o_own.at[z], [o_part.at[z, side_rows(net.a)], o_land.at[z]], side)
        for grad in late:
            grad.go(s + 1) if s < zs - 1 else grad.own()

    def branch_end():
        branch.end()

        def back_last(i):
            at = aligned(i, 16)
            total = total_of(landed_1.at[net.b], at) + far_1[at, :].astype(F32)
            grad = gm_v[at, :] + norm_back(x_v[at, :].astype(F32), total, gains[0:1, :], 0)
            out_v[at, :] = grad.astype(BF)

        loop(rows // 16, back_last)
        outs.append(net.keep(out_v, input_grad.at[net.t]))
        pairs.append(net.send(out_v, input_grad.at[net.t], net.sibling))
        plane.append(net.send(gsum, g_far.at[0], net.sibling))

    def gains_plane():
        plane[0].wait_recv()
        gall[...] = gsum[...] + g_far[0]
        for k, way in ((1, net.over_x), (2, net.over_y), (3, net.across)):
            plane.append(net.send(gall, g_far.at[k], way))

    def gains_line():
        for copy in plane[1:]:
            copy.wait_recv()
        gsum_z[...] = gall[...] + g_far[1] + g_far[2] + g_far[3]

        def cut(z):
            return gsum_z.at[:, :, aligned(z, deep)]

        z_gain.extend(net.send(cut(lax.rem(net.z + s, zs)), g_land.at[net.z], net.along_z(s)) for s in range(1, zs))
        outs.append(net.keep(cut(net.z), g_land.at[net.z]))

    def feed_end():
        feed.end()

        def close(i):
            at = aligned(i, 16)
            lo_v[at, :] = (mid_v[at, :] + total_of(landed_f, at)).astype(BF)

        loop(rows // 16, close)
        outs.append(net.keep(lo_v, layer_out.at[net.t]))
        pairs.append(net.send(lo_v, layer_out.at[net.t], net.sibling))

    def each(method):
        def step(s):
            for grad in late:
                getattr(grad, method)(s)

        return step

    steps = {
        "hstart": hidden.start, "hend": hidden_end, "gstart": gather.start, "gend": gather.end, "fstart": feed.start,
        "fend": feed_end, "W1": weights_give, "W2": weights_own, "bx": branch.across, "bend": branch_end,
        "gain2": gains_plane, "gain3": gains_line,
    }
    counted = {
        "F": hidden.first, "S": hidden.second, "T": hidden.third, "fF": feed.first, "fS": feed.second,
        "fT": feed.third, "gs": gather.spread, "gf": gather.far, "A": queries_back, "B": keys_back, "sw": weights_sum,
        "bt": branch.take, "Ls": each("spread"), "Lr": each("relay"),
    }
    for k, grad in enumerate(grads):
        steps["g%dz" % k] = grad.start
        counted["g%ds" % k], counted["g%dr" % k] = grad.spread, grad.relay
    for name in ORDER:
        if name in steps:
            steps[name]()
        else:
            counted[name[:-1]](int(name[-1]))
    for grad in grads + late:
        grad.end()
    for copy in outs:
        copy.wait()
    for copy in z_gain + pairs:
        copy.wait_recv()
    total = g_land[0]
    for z in range(1, zs):
        total += g_land[z]
    gains_out[...] = total
    net.finish()


def rope_tables(seq):
    half_dim = HEAD_DIM // 2
    frequency = ROPE_BASE ** (-np.arange(half_dim, dtype=np.float32) / half_dim)
    angle = np.arange(seq, dtype=np.float32)[:, None] * frequency.astype(np.float32)[None, :]
    cosine, sine = np.cos(angle), np.sin(angle)
    return (
        np.concatenate([cosine, cosine], axis=1).astype(np.float32),
        np.concatenate([-sine, sine], axis=1).astype(np.float32),
    )


def heads_shards(
    zs, activations, document_ids, attn_gain, w_query, w_key, w_value, w_out, mlp_gain, w_gate, w_up, w_down, cotangent
):
    stretch, width = activations.shape[3:]
    deep = w_query.shape[0]
    seq = document_ids.shape[1]
    pair = 2 * seq
    wide = w_gate.shape[1] // (4 * zs)
    x = activations.reshape(2, stretch, width)
    cot = cotangent.reshape(2, stretch, width)
    small = jnp.stack([attn_gain.astype(F32), mlp_gain.astype(F32)])
    docs_rows = document_ids.astype(F32).reshape(seq // deep, deep)
    small = jnp.concatenate([small, docs_rows, jnp.zeros((6 - seq // deep, deep), F32)])
    cosine, sine = (jnp.asarray(table) for table in rope_tables(seq))
    half = stretch // 2
    hidden, qkv, attended, qkv_w, out_w, gains, docs, middle, h2_all, cot_all, gu_w, down_w = call(
        functools.partial(forward_kernel, zs),
        1,
        [
            ((pair, width), BF, ANY),
            ((pair, 3 * HEAD_DIM), BF, ANY),
            ((pair, HEAD_DIM), BF, ANY),
            ((width, 3 * HEAD_DIM), BF, ANY),
            ((HEAD_DIM, width), BF, ANY),
            ((8, width), F32, ANY),
            ((8, seq), F32, ANY),
            ((stretch, width), F32, ANY),
            ((4, zs, 2, stretch, width), BF, ANY),
            ((4, zs, 2, stretch, width), BF, ANY),
            ((width, 2 * wide), BF, ANY),
            ((wide, width), BF, ANY),
        ],
        [
            VMEM((pair, width), BF),
            VMEM((pair, width), BF),
            VMEM((width, 3 * HEAD_DIM), BF),
            VMEM((HEAD_DIM, width), BF),
            VMEM((zs, 8, deep), F32),
            VMEM((2, 8, deep), F32),
            VMEM((8, width), F32),
            VMEM((8, seq), F32),
            VMEM((seq, HEAD_DIM), F32),
            VMEM((seq, HEAD_DIM), F32),
            VMEM((pair, 3 * HEAD_DIM), BF),
            VMEM((pair, HEAD_DIM), BF),
            VMEM((2, 2, zs, stretch, width), BF),
            VMEM((2, zs, stretch, width), BF),
            VMEM((zs, stretch, width), BF),
            VMEM((zs, stretch, width), BF),
            VMEM((stretch, width), BF),
            VMEM((stretch, width), BF),
            VMEM((stretch, width), F32),
        ],
        (134, 131, 34),
        (x, w_query, w_key, w_value, w_out, small, cosine, sine, w_gate, w_up, w_down, cot),
        52,
    )

    h2 = h2_all.reshape(4 * seq, width)
    cots = cot_all.reshape(4 * seq, width)
    gate_up = dot(h2, gu_w)
    gate, upward = gate_up[:, :wide], gate_up[:, wide:]
    grad_product = dot(cots, down_w, ((1,), (1,)))
    sigma_gate = jax.nn.sigmoid(gate)
    silu = gate * sigma_gate
    product = (silu * upward).astype(BF)
    grad_gate = (grad_product * upward * sigma_gate * (1.0 + gate * (1.0 - sigma_gate))).astype(BF)
    grad_up = (grad_product * silu).astype(BF)
    grad_gu = jnp.concatenate([grad_gate, grad_up], axis=1)
    gh_part = dot(grad_gu, gu_w, ((1,), (1,)), BF).reshape(4, zs, 2, stretch, width)
    feed_part = dot(product, down_w, kind=BF).reshape(4, zs, 2, stretch, width)
    gu_grad = dot(h2, grad_gu, ((0,), (0,)), BF)
    down_grad = dot(product, cots, ((0,), (0,)), BF)

    sum_scratch = [
        VMEM((4, zs, stretch, width), BF),
        VMEM((4, zs, stretch, width), BF),
        VMEM((2, 2, zs, half, width), BF),
        VMEM((2, zs, half, width), BF),
        VMEM((zs, stretch, width), BF),
    ]
    layer_out, input_grad, q_g, k_g, v_g, o_g, gate_g, up_g, down_g, gains_g = call(
        functools.partial(backward_kernel, zs),
        2,
        [
            ((2, stretch, width), BF, ANY),
            ((2, stretch, width), BF, ANY),
            (w_query.shape, BF, ANY),
            (w_key.shape, BF, ANY),
            (w_value.shape, BF, ANY),
            (w_out.shape, BF, ANY),
            (w_gate.shape, BF, ANY),
            (w_up.shape, BF, ANY),
            (w_down.shape, BF, ANY),
            ((2, 8, deep), F32, VMEM),
        ],
        sum_scratch
        + sum_scratch
        + [
            VMEM((2, 2, zs, stretch, width), BF),
            VMEM((2, zs, stretch, width), BF),
            VMEM((stretch, width), BF),
            VMEM((2, zs, stretch, width), BF),
            VMEM((pair, width), BF),
            VMEM((pair, 3 * HEAD_DIM), BF),
            VMEM((pair, HEAD_DIM), BF),
            VMEM((width, 3 * HEAD_DIM), BF),
            VMEM((HEAD_DIM, width), BF),
            VMEM((pair, width), BF),
            VMEM((pair, 3 * HEAD_DIM), BF),
            VMEM((8, width), F32),
            VMEM((8, seq), F32),
            VMEM((seq, HEAD_DIM), F32),
            VMEM((seq, HEAD_DIM), F32),
            VMEM((seq, HEAD_DIM), BF),
            VMEM((stretch, width), F32),
            VMEM((stretch, width), BF),
            VMEM((stretch, width), BF),
            VMEM((stretch, width), F32),
            VMEM((stretch, width), BF),
            VMEM((stretch, width), BF),
            VMEM((stretch, width), BF),
            VMEM((2, 8, width), F32),
            VMEM((2, 8, width), F32),
            VMEM((2, 8, width), F32),
            VMEM((4, 2, 8, width), F32),
            VMEM((zs, 2, 8, deep), F32),
            VMEM((zs, deep // 2, 3 * HEAD_DIM), BF),
            VMEM((zs, deep // 2, 3 * HEAD_DIM), BF),
            VMEM((zs, deep // 2, 3 * HEAD_DIM), BF),
            VMEM((zs, HEAD_DIM, deep), BF),
            VMEM((zs, HEAD_DIM // 2, deep), BF),
            VMEM((zs, HEAD_DIM // 2, deep), BF),
        ],
        (232, 231, 34),
        (
            gh_part, feed_part, gu_grad, down_grad, middle, cot, x, gains, docs, cosine, sine,
            hidden, qkv, attended, qkv_w, out_w,
        ),
        60,
    )
    gain_grads = jnp.sum(gains_g, axis=1)
    return (
        layer_out.reshape(activations.shape),
        input_grad.reshape(activations.shape),
        gain_grads[0],
        q_g.astype(F32),
        k_g.astype(F32),
        v_g.astype(F32),
        o_g.astype(F32),
        gain_grads[1],
        gate_g.astype(F32),
        up_g.astype(F32),
        down_g.astype(F32),
    )


def angles(positions):
    half_dim = HEAD_DIM // 2
    frequency = ROPE_BASE ** (-jnp.arange(half_dim, dtype=jnp.float32) / half_dim)
    angle = positions.astype(jnp.float32)[:, None] * frequency[None, :]
    return (jnp.cos(angle)[:, None, :], jnp.sin(angle)[:, None, :])


def rotate(flat, positions):
    row_count = flat.shape[0]
    heads = flat.reshape(row_count, -1, HEAD_DIM)
    cosine, sine = angles(positions)
    first = heads[..., : HEAD_DIM // 2]
    second = heads[..., HEAD_DIM // 2 :]
    turned = jnp.concatenate(
        [first * cosine - second * sine, second * cosine + first * sine], axis=-1
    )
    return turned.reshape(row_count, -1)


def unrotate(flat, positions):
    row_count = flat.shape[0]
    heads = flat.reshape(row_count, -1, HEAD_DIM)
    cosine, sine = angles(positions)
    first = heads[..., : HEAD_DIM // 2]
    second = heads[..., HEAD_DIM // 2 :]
    turned = jnp.concatenate(
        [first * cosine + second * sine, second * cosine - first * sine], axis=-1
    )
    return turned.reshape(row_count, -1)


def normalize(values):
    inverse = lax.rsqrt(jnp.mean(values * values, axis=-1, keepdims=True) + EPS)
    return (values * inverse, inverse)


def norm_back(grad_normed_out, normed, inverse, gain):
    scaled = grad_normed_out * gain
    return inverse * (scaled - normed * jnp.mean(scaled * normed, axis=-1, keepdims=True))


def contract_rows(left, right):
    return lax.dot_general(
        left, right, (((1,), (1,)), ((), ())), preferred_element_type=jnp.float32
    )


def contract_cols(left, right):
    return lax.dot_general(
        left, right, (((0,), (0,)), ((), ())), preferred_element_type=jnp.float32
    )


def visibility(query_positions, query_docs, key_positions, key_docs):
    same_doc = query_docs[:, None] == key_docs[None, :]
    earlier = key_positions[None, :] <= query_positions[:, None]
    return jnp.where(same_doc & earlier, 1.0, 0.0).astype(jnp.float32)


def merge_heads(stacked):
    return jnp.transpose(stacked, (1, 0, 2)).reshape(stacked.shape[1], -1)


def head_slice(matrix, offset):
    return lax.dynamic_slice_in_dim(matrix, offset, HEAD_DIM, 1)


def attend_forward(queries, key_rows, value_rows, visible):
    score_scale = HEAD_DIM ** (-0.5)

    def one_head(head_index):
        offset = head_index * HEAD_DIM
        scores = (
            contract_rows(head_slice(queries, offset), head_slice(key_rows, offset)) * score_scale
        )
        weights = (jax.nn.sigmoid(scores - SHIFT) * visible).astype(jnp.bfloat16)
        return jnp.dot(weights, head_slice(value_rows, offset), preferred_element_type=jnp.float32)

    stacked = lax.map(one_head, jnp.arange(queries.shape[1] // HEAD_DIM))
    return merge_heads(stacked)


def attend_back(queries, key_rows, value_rows, grad_attended, visible):
    score_scale = HEAD_DIM ** (-0.5)

    def one_head(head_index):
        offset = head_index * HEAD_DIM
        head_query = head_slice(queries, offset)
        head_key = head_slice(key_rows, offset)
        head_grad = head_slice(grad_attended, offset)
        scores = contract_rows(head_query, head_key) * score_scale
        sigma = jax.nn.sigmoid(scores - SHIFT)
        grad_weights = contract_rows(head_grad, head_slice(value_rows, offset))
        grad_scores = (grad_weights * visible * sigma * (1.0 - sigma)).astype(jnp.bfloat16)
        pieces = []
        pieces.append(
            jnp.dot(grad_scores, head_key, preferred_element_type=jnp.float32) * score_scale
        )
        weights = (sigma * visible).astype(jnp.bfloat16)
        pieces.append(contract_cols(grad_scores, head_query) * score_scale)
        pieces.append(contract_cols(weights, head_grad))
        return tuple(pieces)

    stacked = lax.map(one_head, jnp.arange(queries.shape[1] // HEAD_DIM))
    return tuple((merge_heads(piece) for piece in stacked))


def rows_shards(
    activations,
    document_ids,
    attn_gain,
    w_query,
    w_key,
    w_value,
    w_out,
    mlp_gain,
    w_gate,
    w_up,
    w_down,
    cotangent,
):
    groups = lax.axis_size("cp")
    rank = lax.axis_index("cp")
    stretch_len = activations.shape[3]
    width = activations.shape[4]
    row_count = 2 * stretch_len
    offsets = jnp.arange(stretch_len, dtype=jnp.int32)
    my_positions = jnp.concatenate(
        [rank * stretch_len + offsets, (2 * groups - 1 - rank) * stretch_len + offsets]
    )
    all_docs = document_ids[0]
    my_docs = jnp.take(all_docs, my_positions)
    slots = jnp.arange(groups * row_count, dtype=jnp.int32)
    owners = slots // row_count
    halves = slots // stretch_len % 2
    key_positions = (
        jnp.where(halves == 0, owners, 2 * groups - 1 - owners) * stretch_len + slots % stretch_len
    )
    key_docs = jnp.take(all_docs, key_positions)
    visible = visibility(my_positions, my_docs, key_positions, key_docs)
    gathered = (
        lax.all_gather(w_query, "cp", axis=0, tiled=True),
        lax.all_gather(w_key, "cp", axis=0, tiled=True),
        lax.all_gather(w_value, "cp", axis=0, tiled=True),
        lax.all_gather(w_out, "cp", axis=1, tiled=True),
        lax.all_gather(w_gate, "cp", axis=0, tiled=True),
        lax.all_gather(w_up, "cp", axis=0, tiled=True),
        lax.all_gather(w_down, "cp", axis=1, tiled=True),
        lax.all_gather(attn_gain, "cp", axis=0, tiled=True),
        lax.all_gather(mlp_gain, "cp", axis=0, tiled=True),
    )
    (
        query_full,
        key_full,
        value_full,
        out_full,
        gate_full,
        up_full,
        down_full,
        gain_one,
        gain_two,
    ) = gathered
    gain_one = gain_one.astype(jnp.float32)
    gain_two = gain_two.astype(jnp.float32)
    inputs = activations.reshape(row_count, width).astype(jnp.float32)
    normed_one, inverse_one = normalize(inputs)
    hidden_one = (normed_one * gain_one).astype(jnp.bfloat16)
    queries = rotate(
        jnp.dot(hidden_one, query_full, preferred_element_type=jnp.float32), my_positions
    ).astype(jnp.bfloat16)
    keys_local = rotate(
        jnp.dot(hidden_one, key_full, preferred_element_type=jnp.float32), my_positions
    ).astype(jnp.bfloat16)
    values_local = jnp.dot(hidden_one, value_full, preferred_element_type=jnp.float32).astype(
        jnp.bfloat16
    )
    keys_all, values_all = (
        lax.all_gather(keys_local, "cp", axis=0, tiled=True),
        lax.all_gather(values_local, "cp", axis=0, tiled=True),
    )
    attended = attend_forward(queries, keys_all, values_all, visible).astype(jnp.bfloat16)
    branch = lax.psum(jnp.dot(attended, out_full, preferred_element_type=jnp.float32), "tp")
    middle = inputs + branch
    normed_two, inverse_two = normalize(middle)
    hidden_two = (normed_two * gain_two).astype(jnp.bfloat16)
    gate = jnp.dot(hidden_two, gate_full, preferred_element_type=jnp.float32)
    upward = jnp.dot(hidden_two, up_full, preferred_element_type=jnp.float32)
    sigma_gate = jax.nn.sigmoid(gate)
    silu_gate = gate * sigma_gate
    product = (silu_gate * upward).astype(jnp.bfloat16)
    feed = lax.psum(jnp.dot(product, down_full, preferred_element_type=jnp.float32), "tp")
    result = middle + feed
    layer_out = result.astype(jnp.bfloat16).reshape(activations.shape)
    grad_result = cotangent.reshape(row_count, width).astype(jnp.float32)
    grad_feed = grad_result.astype(jnp.bfloat16)
    grad_product = contract_rows(grad_feed, down_full)
    grad_gate = (grad_product * upward * sigma_gate * (1.0 + gate * (1.0 - sigma_gate))).astype(
        jnp.bfloat16
    )
    grad_up = (grad_product * silu_gate).astype(jnp.bfloat16)
    grad_hidden_two = lax.psum(
        contract_rows(grad_gate, gate_full) + contract_rows(grad_up, up_full), "tp"
    )
    grad_gain_two = jnp.sum(grad_hidden_two * normed_two, axis=0)
    grad_middle = grad_result + norm_back(grad_hidden_two, normed_two, inverse_two, gain_two)
    grad_down = contract_cols(product, grad_feed)
    grad_gate_w = contract_cols(hidden_two, grad_gate)
    grad_up_w = contract_cols(hidden_two, grad_up)
    share_gate, share_up, share_down, share_gain_two = (
        lax.psum_scatter(grad_gate_w, "cp", scatter_dimension=0, tiled=True),
        lax.psum_scatter(grad_up_w, "cp", scatter_dimension=0, tiled=True),
        lax.psum_scatter(grad_down, "cp", scatter_dimension=1, tiled=True),
        lax.psum_scatter(grad_gain_two, "cp", scatter_dimension=0, tiled=True),
    )
    grad_branch = grad_middle.astype(jnp.bfloat16)
    grad_attended = contract_rows(grad_branch, out_full).astype(jnp.bfloat16)
    grad_queries, key_terms, value_terms = attend_back(
        queries, keys_all, values_all, grad_attended, visible
    )
    grad_keys, grad_values = (
        lax.psum_scatter(key_terms, "cp", scatter_dimension=0, tiled=True),
        lax.psum_scatter(value_terms, "cp", scatter_dimension=0, tiled=True),
    )
    grad_query_pre = unrotate(grad_queries, my_positions).astype(jnp.bfloat16)
    grad_key_pre = unrotate(grad_keys, my_positions).astype(jnp.bfloat16)
    grad_value_pre = grad_values.astype(jnp.bfloat16)
    local_hidden = (
        contract_rows(grad_query_pre, query_full)
        + contract_rows(grad_key_pre, key_full)
        + contract_rows(grad_value_pre, value_full)
    )
    grad_hidden_one = lax.psum(local_hidden, "tp")
    grad_gain_one = jnp.sum(grad_hidden_one * normed_one, axis=0)
    grad_inputs = grad_middle + norm_back(grad_hidden_one, normed_one, inverse_one, gain_one)
    grad_query_w = contract_cols(hidden_one, grad_query_pre)
    grad_key_w = contract_cols(hidden_one, grad_key_pre)
    grad_value_w = contract_cols(hidden_one, grad_value_pre)
    grad_out_w = contract_cols(attended, grad_branch)
    share_query, share_key, share_value, share_out, share_gain_one = (
        lax.psum_scatter(grad_query_w, "cp", scatter_dimension=0, tiled=True),
        lax.psum_scatter(grad_key_w, "cp", scatter_dimension=0, tiled=True),
        lax.psum_scatter(grad_value_w, "cp", scatter_dimension=0, tiled=True),
        lax.psum_scatter(grad_out_w, "cp", scatter_dimension=1, tiled=True),
        lax.psum_scatter(grad_gain_one, "cp", scatter_dimension=0, tiled=True),
    )
    summed = lax.psum(
        (
            share_gain_one,
            share_query,
            share_key,
            share_value,
            share_out,
            share_gain_two,
            share_gate,
            share_up,
            share_down,
        ),
        "dp",
    )
    input_grad = grad_inputs.astype(jnp.bfloat16).reshape(activations.shape)
    return (
        layer_out,
        input_grad,
        summed[0],
        summed[1],
        summed[2],
        summed[3],
        summed[4],
        summed[5],
        summed[6],
        summed[7],
        summed[8],
    )


def layer(sizes, *args):
    heads = args[3].shape[1] // HEAD_DIM
    zs = sizes["cp"]
    fits = sizes["dp"] == 4 and sizes["tp"] == 2 and zs == 4 and heads == 2 * zs
    fits = fits and args[0].shape[3] % 32 == 0 and args[8].shape[1] % (2 * zs * HEAD_DIM) == 0
    fits = fits and args[3].shape[0] % HEAD_DIM == 0 and args[1].shape[1] % args[3].shape[0] == 0
    fits = fits and args[1].shape[1] <= 6 * args[3].shape[0]
    if fits:
        return heads_shards(zs, *args)
    return rows_shards(*args)


def solution(mesh):
    return jax.shard_map(
        functools.partial(layer, dict(mesh.shape)),
        mesh=mesh,
        in_specs=(
            P("dp", "cp", None, None, None),
            P("dp", None),
            P("cp"),
            P("cp", "tp"),
            P("cp", "tp"),
            P("cp", "tp"),
            P("tp", "cp"),
            P("cp"),
            P("cp", "tp"),
            P("cp", "tp"),
            P("tp", "cp"),
            P("dp", "cp", None, None, None),
        ),
        out_specs=(
            P("dp", "cp", None, None, None),
            P("dp", "cp", None, None, None),
            P("cp"),
            P("cp", "tp"),
            P("cp", "tp"),
            P("cp", "tp"),
            P("tp", "cp"),
            P("cp"),
            P("cp", "tp"),
            P("cp", "tp"),
            P("tp", "cp"),
        ),
        check_vma=False,
    )
```

```python
import functools
import math

import jax
import jax.numpy as jnp
import numpy as np
from jax import lax
from jax.experimental import pallas as pl
from jax.experimental.pallas import tpu as pltpu
from jax.sharding import PartitionSpec as P

HEAD_DIM = 128
EPS = 1e-05
SHIFT = math.log(4096.0)
ROPE_BASE = 10000.0
BF = jnp.bfloat16
F32 = jnp.float32
MESH = pl.DeviceIdType.MESH
ANY = pl.ANY
VMEM = pltpu.VMEM
MIB = 2**20


class Net:
    def __init__(self, zs, send_sems, recv_sems, local_sems):
        self.zs = zs
        self.dp, self.z, self.t = (lax.axis_index(a) for a in ("dp", "cp", "tp"))
        self.a, self.b = lax.div(self.dp, 2), lax.rem(self.dp, 2)
        self.send_sems, self.recv_sems, self.local_sems = send_sems, recv_sems, local_sems
        self.arrivals = 0
        self.free_locals = list(range(local_sems.shape[0]))
        self.open = []

    def along_z(self, s):
        return (self.dp, lax.rem(self.z + s, self.zs), self.t)

    def source_z(self, s):
        return lax.rem(self.z + self.zs - s, self.zs)

    @property
    def over_x(self):
        return (2 * self.a + 1 - self.b, self.z, self.t)

    @property
    def over_y(self):
        return (2 * (1 - self.a) + self.b, self.z, self.t)

    @property
    def sibling(self):
        return (self.dp, self.z, 1 - self.t)

    @property
    def across(self):
        return (2 * (1 - self.a) + 1 - self.b, self.z, self.t)

    def meet(self):
        ways = [self.along_z(s) for s in range(1, self.zs)] + [self.over_x, self.over_y, self.across, self.sibling]
        barrier = pltpu.get_barrier_semaphore()
        for way in ways:
            pl.semaphore_signal(barrier, inc=1, device_id=way, device_id_type=MESH)
        pl.semaphore_wait(barrier, len(ways))

    def slot(self):
        self.arrivals += 1
        return self.arrivals - 1

    def send(self, src, dst, way, arrive=None, when=None):
        arrive = self.slot() if arrive is None else arrive
        sem = self.send_sems.at[len(self.open)]
        copy = pltpu.make_async_remote_copy(
            src, dst, sem, self.recv_sems.at[arrive], device_id=way, device_id_type=MESH
        )
        if when is None:
            copy.start()
        else:
            pl.when(when)(copy.start)
        self.open.append((copy, when))
        return copy

    def arrival(self, ref, slot):
        return pltpu.make_async_remote_copy(
            ref, ref, self.send_sems.at[0], self.recv_sems.at[slot], device_id=self.sibling, device_id_type=MESH
        )

    def keep(self, src, dst):
        return Kept(self, src, dst)

    def finish(self):
        for copy, when in self.open:
            if when is None:
                copy.wait_send()
            else:
                pl.when(when)(copy.wait_send)


class Kept:
    def __init__(self, net, src, dst):
        self.net, self.slot = net, net.free_locals.pop(0)
        self.copy = pltpu.make_async_copy(src, dst, net.local_sems.at[self.slot])
        self.copy.start()

    def wait(self):
        self.copy.wait()
        self.net.free_locals.append(self.slot)


class LineGather:
    def __init__(self, net, src, place):
        self.net, self.src, self.place = net, src, place
        self.h, self.low = lax.div(net.z, 2), lax.rem(net.z, 2)
        self.mate = (net.dp, net.z + 1 - 2 * self.low, net.t)
        self.gate = (net.dp, 2 - self.h, net.t)
        self.hands_on = self.h != self.low

    def start(self):
        net = self.net
        mine = self.place(net.z)
        self.near = net.send(self.src, mine, self.mate)
        self.slots = [net.slot(), net.slot()]
        net.send(self.src, mine, self.gate, arrive=self.slots[0] + self.low)

    def take(self, s):
        net = self.net
        if s == 1:
            self.near.wait_recv()
            return net.z + 1 - 2 * self.low
        z = 2 * (1 - self.h) + s - 2
        ref = self.place(z)
        net.arrival(ref, self.slots[s - 2]).wait_recv()
        net.send(ref, ref, self.mate, arrive=self.slots[s - 2], when=self.hands_on)
        return z


def plane_relay(net, place, halves, over_x, over_y, ways="xy", sibling=None):
    dx, dy = 2 * net.a + 1 - net.b, 2 * (1 - net.a) + net.b
    relays = []

    def by_y():
        over_x.wait_recv()
        piece = halves(place(dx), 0) if "x" in ways else place(dx)
        if "y" in ways:
            relays.append(net.send(piece, piece, net.over_y))
        if sibling:
            sibling(dx)

    def by_x():
        over_y.wait_recv()
        piece = halves(place(dy), 1) if "y" in ways else place(dy)
        if "x" in ways:
            relays.append(net.send(piece, piece, net.over_x))
        if sibling:
            sibling(dy)

    for step in (by_x, by_y) if ways == "x" else (by_y, by_x):
        step()
    return relays


def plane_end(net, relays, sibling=None):
    for copy in relays:
        copy.wait_recv()
    if sibling:
        sibling(2 * (1 - net.a) + 1 - net.b)


def rows_loop(count, step, body):
    def one(i, carry):
        body(pl.ds(pl.multiple_of(i * step, step), step))
        return carry

    lax.fori_loop(0, count // step, one, 0)


def add_rows(out, terms, rows):
    def body(at):
        total = terms[0][at, :].astype(F32)
        for term in terms[1:]:
            total += term[at, :].astype(F32)
        out[at, :] = total.astype(out.dtype)

    rows_loop(rows, 16, body)


class GatherAll:
    def __init__(self, net, src, dst):
        self.net, self.src, self.dst = net, src, dst
        rows = src.shape[0] // 2
        self.halves = lambda ref, k: ref.at[pl.ds(k * rows, rows)]

    def place(self, dp, z):
        return self.dst.at[dp, z, self.net.t]

    def start(self):
        net = self.net
        mine = self.place(net.dp, net.z)
        self.line = LineGather(net, self.src, lambda z: self.place(net.dp, z))
        self.line.start()
        self.local = net.keep(self.src, mine)
        self.plane = [(net.z, net.send(self.src, mine, net.over_x), net.send(self.src, mine, net.over_y))]
        self.twin = [net.send(self.src, mine, net.sibling)]
        self.states = []

    def to_twin(self, dp, z):
        ref = self.place(dp, z)
        self.twin.append(self.net.send(ref, ref, self.net.sibling))

    def spread(self, s):
        net = self.net
        z = self.line.take(s)
        ref = self.place(net.dp, z)
        self.plane.append((z, net.send(ref, ref, net.over_x), net.send(ref, ref, net.over_y)))
        self.to_twin(net.dp, z)

    def relay(self, s):
        z, over_x, over_y = self.plane[s]
        place = functools.partial(self.place, z=z)
        self.states.append((z, plane_relay(self.net, place, self.halves, over_x, over_y, sibling=lambda dp: self.to_twin(dp, z))))

    def end(self):
        for z, relays in self.states:
            plane_end(self.net, relays, lambda dp, z=z: self.to_twin(dp, z))
        for copy in self.twin:
            copy.wait_recv()
        self.local.wait()


class GatherGroup:
    def __init__(self, net, src, dst, own_lanes=None):
        self.net, self.src, self.dst, self.own_lanes = net, src, dst, own_lanes
        self.rows = src.shape[0]

    def place(self, b, z, t=None):
        t = self.net.t if t is None else t
        last = 2 * self.net.zs - 1
        at = ((last + 1) * b + z + t * (last - 2 * z)) * self.rows
        return self.dst.at[pl.ds(pl.multiple_of(at, self.rows), self.rows)]

    def start(self):
        net = self.net
        mine = self.place(net.b, net.z)
        self.line = LineGather(net, self.src, lambda z: self.place(net.b, z))
        self.line.start()
        self.over = [(net.z, net.send(self.src, mine, net.over_x))]
        self.twin, self.local = [], []
        if self.own_lanes is None:
            self.local.append(net.keep(self.src, mine))
            self.twin.append((net.b, net.z, net.send(self.src, mine, net.sibling)))
        else:
            for t in (0, 1):
                self.local.append(net.keep(self.own_lanes.at[t], self.place(net.b, net.z, t)))

    def to_twin(self, b, z):
        ref = self.place(b, z)
        self.twin.append((b, z, self.net.send(ref, ref, self.net.sibling)))

    def spread(self, s):
        net = self.net
        z = self.line.take(s)
        ref = self.place(net.b, z)
        self.over.append((z, net.send(ref, ref, net.over_x)))
        self.to_twin(net.b, z)
        return z

    def far(self, s):
        z, copy = self.over[s]
        copy.wait_recv()
        self.to_twin(1 - self.net.b, z)
        return z

    def end(self):
        for _, _, copy in self.twin:
            copy.wait_recv()
        for copy in self.local:
            copy.wait()


class SumGroup:
    def __init__(self, net, part, sib, far, landed):
        self.net, self.part, self.sib, self.far, self.landed = net, part, sib, far, landed
        self.rows = part.shape[3]
        self.twin, self.over, self.z_sends = {}, [], []

    def order(self):
        return [lax.rem(self.net.z + s + 1, self.net.zs) for s in range(self.net.zs)]

    def give(self, k):
        net = self.net
        b = net.b if k else 1 - net.b
        for s, z in enumerate(self.order()):
            self.twin[k, s] = net.send(self.part.at[b, 1 - net.t, z], self.sib.at[b, z], net.sibling)

    def take(self, k):
        net = self.net
        b = net.b if k else 1 - net.b
        for s, z in enumerate(self.order()):
            self.twin[k, s].wait_recv()
            own = self.part.at[b, net.t, z]
            add_rows(own, [own, self.sib.at[b, z]], self.rows)
            if k == 0:
                self.over.append(net.send(own, self.far.at[z], net.over_x))

    def along(self):
        net = self.net
        for s, z in enumerate(self.order()):
            self.over[s].wait_recv()
            last = s == net.zs - 1
            own = self.part.at[net.b, net.t, z]
            out = self.landed.at[net.z] if last else own
            add_rows(out, [own, self.far.at[z]], self.rows)
            if not last:
                self.z_sends.append(net.send(out, self.landed.at[net.z], net.along_z(s + 1)))

    def end(self):
        for copy in self.z_sends:
            copy.wait_recv()


class SumLine(SumGroup):
    def take(self, k):
        net = self.net
        b = net.b if k else 1 - net.b
        for s, z in enumerate(self.order()):
            self.twin[k, s].wait_recv()
            own, last = self.part.at[b, net.t, z], s == net.zs - 1
            out = self.landed.at[b, net.z] if last else own
            add_rows(out, [own, self.sib.at[b, z]], self.rows)
            if not last:
                self.z_sends.append(net.send(own, self.landed.at[b, net.z], net.along_z(s + 1)))

    def across(self):
        net = self.net
        b = 1 - net.b
        for copy in self.z_sends[: net.zs - 1]:
            copy.wait_recv()
        out = self.part.at[b, net.t, net.z]
        add_rows(out, [self.landed.at[b, z] for z in range(net.zs)], self.rows)
        self.over = net.send(out, self.far, net.over_x)

    def end(self):
        for copy in self.z_sends[self.net.zs - 1 :]:
            copy.wait_recv()
        self.over.wait_recv()


class SumAll:
    def __init__(self, net, part, own, sib, one, two, landed):
        self.net, self.part, self.own, self.sib = net, part, own, sib
        self.one, self.two, self.landed = one, two, landed
        self.half = part.shape[3] // 2

    def order(self):
        net = self.net
        return [lax.rem(net.z + s + 1, net.zs) for s in range(net.zs)]

    def places(self):
        a, b = self.net.a, self.net.b
        return [2 * (1 - a) + 1 - b, 2 * a + 1 - b, 2 * (1 - a) + b, 2 * a + b]

    def start(self):
        net = self.net
        self.twin, self.mine = [], []
        for z in self.order():
            self.twin.append(net.send(self.part.at[:, z, 1 - net.t], self.sib.at[:, z], net.sibling))
            self.mine.append(net.keep(self.part.at[:, z, net.t], self.own.at[:, z]))

    def upper(self, ref):
        return ref.at[pl.ds(0, self.half)]

    def lower(self, ref):
        return ref.at[pl.ds(self.half, self.half)]

    def first(self, s):
        net = self.net
        z = self.order()[s]
        dd, dx, dy, me = self.places()
        self.twin[s].wait_recv()
        self.mine[s].wait()
        for dp in (dd, dx, dy, me):
            add_rows(self.own.at[dp, z], [self.own.at[dp, z], self.sib.at[dp, z]], 2 * self.half)
        self.ones = getattr(self, "ones", [])
        self.ones.append(
            (
                net.send(self.upper(self.own.at[dd, z]), self.one.at[0, 0, z], net.over_x),
                net.send(self.upper(self.own.at[dx, z]), self.one.at[0, 1, z], net.over_x),
                net.send(self.lower(self.own.at[dd, z]), self.one.at[1, 0, z], net.over_y),
                net.send(self.lower(self.own.at[dy, z]), self.one.at[1, 1, z], net.over_y),
            )
        )

    def second(self, s):
        net = self.net
        z = self.order()[s]
        dd, dx, dy, me = self.places()
        x_dd, x_me, y_dd, y_me = self.ones[s]
        self.twos = getattr(self, "twos", [])
        x_dd.wait_recv()
        out = self.upper(self.own.at[dy, z])
        add_rows(out, [out, self.one.at[0, 0, z]], self.half)
        up = net.send(out, self.two.at[0, z], net.over_y)
        y_dd.wait_recv()
        out = self.lower(self.own.at[dx, z])
        add_rows(out, [out, self.one.at[1, 0, z]], self.half)
        side = net.send(out, self.two.at[1, z], net.over_x)
        self.twos.append((up, side))

    def third(self, s):
        net = self.net
        z = self.order()[s]
        dd, dx, dy, me = self.places()
        _, x_me, _, y_me = self.ones[s]
        up, side = self.twos[s]
        last = s == net.zs - 1
        out = self.landed.at[net.z] if last else self.own.at[me, z]
        x_me.wait_recv()
        up.wait_recv()
        mine = self.own.at[me, z]
        add_rows(self.upper(out), [self.upper(mine), self.one.at[0, 1, z], self.two.at[0, z]], self.half)
        y_me.wait_recv()
        side.wait_recv()
        add_rows(self.lower(out), [self.lower(mine), self.one.at[1, 1, z], self.two.at[1, z]], self.half)
        self.z_sends = getattr(self, "z_sends", [])
        if not last:
            self.z_sends.append(net.send(out, self.landed.at[net.z], net.along_z(s + 1)))

    def end(self):
        for copy in self.z_sends:
            copy.wait_recv()


class SpreadGrads:
    def __init__(self, net, src, dst, ways):
        self.net, self.src, self.dst, self.ways = net, src, dst, ways
        self.z_sends, self.plane, self.states = {}, {}, []

    def mine(self):
        return self.dst(self.net.dp, self.net.z)

    def start(self):
        self.own()
        for s in range(1, self.net.zs):
            self.go(s)

    def own(self):
        self.local = self.net.keep(self.src(self.net.z), self.mine())

    def go(self, s):
        net = self.net
        self.z_sends[s] = net.send(self.src(lax.rem(net.z + s, net.zs)), self.mine(), net.along_z(s))

    def spread(self, s):
        net = self.net
        z = net.source_z(s)
        ref = self.dst(net.dp, z)
        if s:
            self.z_sends[s].wait_recv()
            src = ref
        else:
            src = self.src(net.z)
        self.plane[s] = (z, net.send(src, ref, net.over_x), net.send(src, ref, net.over_y))

    def relay(self, s):
        z, over_x, over_y = self.plane[s]
        self.states.append(plane_relay(self.net, lambda dp: self.dst(dp, z), half_rows, over_x, over_y, self.ways))

    def end(self):
        for relays in self.states:
            plane_end(self.net, relays)
        self.local.wait()


def half_rows(ref, k):
    n = ref.shape[0] // 2
    return ref.at[pl.ds(k * n, n)]


def aligned(i, size):
    return pl.ds(pl.multiple_of(i * size, size), size)


def loop(count, body):
    def one(i, carry):
        body(i)
        return carry

    lax.fori_loop(0, count, one, 0)


def dot(left, right, dims=((1,), (0,)), kind=F32):
    return lax.dot_general(left, right, (dims, ((), ())), preferred_element_type=F32).astype(kind)


def turn(u, cosine, sine):
    return u * cosine + pltpu.roll(u, HEAD_DIM // 2, 1) * sine


def column(row, start, count):
    n = row.shape[1]
    here = lax.broadcasted_iota(jnp.int32, (count, n), 1) == start + lax.broadcasted_iota(jnp.int32, (count, n), 0)
    return jnp.sum(jnp.where(here, row, 0.0), axis=1, keepdims=True)


def seen(row, start, count, flip=False):
    n = row.shape[1]
    same = column(row, start, count) == row
    mine = start + lax.broadcasted_iota(jnp.int32, (count, n), 0)
    other = lax.broadcasted_iota(jnp.int32, (count, n), 1)
    return same & ((mine <= other) if flip else (other <= mine))


def sigma_of(left, right):
    return jax.nn.sigmoid(dot(left, right, ((1,), (1,))) * HEAD_DIM**-0.5 - SHIFT)


def call(kernel, name, outs, scratch, counts, args, vmem):
    return pl.pallas_call(
        kernel,
        out_shape=[jax.ShapeDtypeStruct(shape, kind) for shape, kind, _ in outs],
        in_specs=[pl.BlockSpec(memory_space=ANY)] * len(args),
        out_specs=[pl.BlockSpec(memory_space=space) for _, _, space in outs],
        scratch_shapes=list(scratch) + [pltpu.SemaphoreType.DMA((count,)) for count in counts],
        compiler_params=pltpu.CompilerParams(
            collective_id=name, has_side_effects=True, vmem_limit_bytes=vmem * MIB
        ),
    )(*args)


def forward_kernel(
    zs, x, wq, wk, wv, wo, small, cosine, sine, wg, wu, wd, cot,
    hidden_out, qkv_out, attended_out, qkv_w_out, out_w_out, gains_out, docs_out, middle, h2_out, cot_out, gu_w_out, down_w_out, gate_out, gp_out,
    x_all, h1, qkv_w, out_w, small_z, small_x, gains, docs, cos_v, sin_v, qkv, attended, part, sib, far, landed,
    x_lane, h2, mid_v, h2_all, cot_all, gu_w, down_w, gate_v, gp_v, send_sems, recv_sems, local_sems,
):
    net = Net(zs, send_sems, recv_sems, local_sems)
    net.meet()
    deep, wide = wg.shape[0], gu_w.shape[1] // 2
    seq = docs.shape[1]
    half, side = deep // 2, HEAD_DIM // 2
    gather = GatherGroup(net, x.at[net.t], x_all, own_lanes=x)
    gather.start()
    small_waits = [net.send(small, small_z.at[net.z], net.along_z(s)) for s in range(1, zs)]
    small_waits.append(net.send(small, small_x.at[net.b], net.over_x))
    local = [net.keep(small, small_z.at[net.z]), net.keep(small, small_x.at[net.b])]
    local += [net.keep(cosine, cos_v), net.keep(sine, sin_v)]
    lane = net.keep(x.at[net.t], x_lane)

    def head(z):
        return aligned(net.b * zs + z, HEAD_DIM)

    mine = aligned(net.z, deep)
    my_half = pl.ds(pl.multiple_of(net.a * half, half), half)
    qkv_sends, out_sends, w_local = [], [], []
    for m, w in enumerate((wq, wk, wv)):
        col = pl.ds(m * HEAD_DIM, HEAD_DIM)
        w_local.append(net.keep(w.at[:, head(net.z)], qkv_w.at[mine, col]))
    for s in range(1, zs):
        z = lax.rem(net.z + s, zs)
        rows = pl.ds(pl.multiple_of(net.z * deep + net.a * half, half), half)
        qkv_sends.append(
            [
                net.send(w.at[my_half, head(z)], qkv_w.at[rows, pl.ds(m * HEAD_DIM, HEAD_DIM)], net.along_z(s))
                for m, w in enumerate((wq, wk, wv))
            ]
        )
    out_rows = pl.ds(pl.multiple_of(net.a * side, side), side)
    w_local.append(net.keep(wo.at[head(net.z)], out_w.at[:, mine]))
    for s in range(1, zs):
        z = lax.rem(net.z + s, zs)
        at = pl.ds(pl.multiple_of((net.b * zs + z) * HEAD_DIM + net.a * side, side), side)
        out_sends.append(net.send(wo.at[at], out_w.at[out_rows, mine], net.along_z(s)))

    cotan = GatherAll(net, cot.at[net.t], cot_all)
    mlp_waits, mlp_local = {}, {}

    def block(z):
        return aligned(net.dp * zs + z, wide)

    mlp = (
        (lambda z: wg.at[:, block(z)], gu_w.at[mine, pl.ds(0, wide)]),
        (lambda z: wu.at[:, block(z)], gu_w.at[mine, pl.ds(wide, wide)]),
        (lambda z: wd.at[block(z)], down_w.at[:, mine]),
    )
    for k, (src, dst) in enumerate(mlp):
        mlp_local[k] = net.keep(src(net.z), dst)

    def fetch(k):
        src, dst = mlp[k]
        mlp_waits[k] = [net.send(src(lax.rem(net.z + s, zs)), dst, net.along_z(s)) for s in range(1, zs)]

    def fetched(k):
        for copy in mlp_waits[k]:
            copy.wait_recv()
        mlp_local[k].wait()

    for copy in small_waits:
        copy.wait_recv()
    for copy in local:
        copy.wait()
    for z in range(zs):
        gains[0:1, z * deep : (z + 1) * deep] = small_z[z, 0:1, :]
        gains[1:2, z * deep : (z + 1) * deep] = small_z[z, 1:2, :]
    for b in range(2):
        for k in range(seq // deep):
            docs[b : b + 1, k * deep : (k + 1) * deep] = small_x[b, 2 + k : 3 + k, :]

    def norm_block(ref_at):
        def body(i):
            at = pl.ds(pl.multiple_of(ref_at + i * 16, 16), 16)
            rows = x_all[at, :].astype(F32)
            inverse = lax.rsqrt(jnp.mean(rows * rows, axis=-1, keepdims=True) + EPS)
            h1[at, :] = (rows * inverse * gains[0:1, :]).astype(BF)

        loop(x.shape[1] // 16, body)

    rows = x.shape[1]
    last = 2 * zs - 1

    def offset(b, z, t):
        return ((last + 1) * b + z + t * (last - 2 * z)) * rows

    for copy in gather.local:
        copy.wait()
    gather.local = []
    for t in (0, 1):
        norm_block(offset(net.b, net.z, t))
    for s in range(1, zs):
        norm_block(offset(net.b, gather.spread(s), net.t))
    cotan.start()
    fetch(2)
    qkv_y = []
    for s in range(1, zs):
        norm_block(offset(1 - net.b, gather.far(s - 1), net.t))
        for copy in qkv_sends[s - 1]:
            copy.wait_recv()
        at = qkv_w.at[pl.ds(pl.multiple_of(net.source_z(s) * deep + net.a * half, half), half)]
        qkv_y.append(net.send(at, at, net.over_y))
    norm_block(offset(1 - net.b, gather.far(zs - 1), net.t))
    out_y = []
    for s in range(1, zs):
        out_sends[s - 1].wait_recv()
        at = out_w.at[out_rows, aligned(net.source_z(s), deep)]
        out_y.append(net.send(at, at, net.over_y))
    for b, z, copy in gather.twin:
        copy.wait_recv()
        norm_block(offset(b, z, 1 - net.t))
    for copy in qkv_y:
        copy.wait_recv()
    for copy in w_local:
        copy.wait()
    for s in range(1, zs):
        cotan.spread(s)
    for copy in out_y:
        copy.wait_recv()

    branch = SumGroup(net, part, sib, far, landed)
    tile = 128
    for k in range(2):
        b = net.b if k else 1 - net.b
        base = b * seq

        def project(i):
            at = pl.ds(pl.multiple_of(base + i * 256, 256), 256)
            pos = aligned(i, 256)
            pre = dot(h1[at, :], qkv_w[...])
            c, s = cos_v[pos, :], sin_v[pos, :]
            qkv[at, 0:HEAD_DIM] = turn(pre[:, 0:HEAD_DIM], c, s).astype(BF)
            qkv[at, HEAD_DIM : 2 * HEAD_DIM] = turn(pre[:, HEAD_DIM : 2 * HEAD_DIM], c, s).astype(BF)
            qkv[at, 2 * HEAD_DIM : 3 * HEAD_DIM] = pre[:, 2 * HEAD_DIM : 3 * HEAD_DIM].astype(BF)

        loop(seq // 256, project)
        every = pl.ds(pl.multiple_of(base, seq), seq)
        row = docs[pl.ds(b, 1), :]

        def attend(i):
            at = pl.ds(pl.multiple_of(base + i * tile, tile), tile)
            sigma = sigma_of(qkv[at, 0:HEAD_DIM], qkv[every, HEAD_DIM : 2 * HEAD_DIM])
            weights = jnp.where(seen(row, i * tile, tile), sigma, 0.0).astype(BF)
            found = dot(weights, qkv[every, 2 * HEAD_DIM : 3 * HEAD_DIM], kind=BF)
            attended[at, :] = found
            out = dot(found, out_w[...], kind=BF)
            for j in range(tile // rows):
                blk = i * (tile // rows) + j
                t = lax.div(blk, zs)
                z = (1 - t) * blk + t * (last - blk)
                part[b, t, z] = out[j * rows : (j + 1) * rows, :]

        loop(seq // tile, attend)
        branch.give(k)
    saved = [
        net.keep(h1, hidden_out), net.keep(qkv, qkv_out), net.keep(attended, attended_out),
        net.keep(qkv_w, qkv_w_out), net.keep(out_w, out_w_out), net.keep(gains, gains_out), net.keep(docs, docs_out),
    ]
    branch.take(0)
    branch.take(1)
    branch.along()
    for s in range(zs):
        cotan.relay(s)
    lane.wait()
    branch.end()

    def body(i):
        at = aligned(i, 16)
        total = x_lane[at, :].astype(F32)
        for z in range(zs):
            total += landed[z, at, :].astype(F32)
        mid_v[at, :] = total
        inverse = lax.rsqrt(jnp.mean(total * total, axis=-1, keepdims=True) + EPS)
        h2[at, :] = (total * inverse * gains[1:2, :]).astype(BF)

    loop(rows // 16, body)
    saved.append(net.keep(mid_v, middle))
    hidden = GatherAll(net, h2, h2_all)
    hidden.start()
    hidden.spread(1)
    hidden.spread(2)
    hidden.spread(3)
    fetch(0)
    fetch(1)
    cotan.end()
    saved.append(net.keep(cot_all, cot_out))

    few = 256 // (2 * rows)

    def tiles(body):
        def one(i):
            dp, z = lax.div(i, zs // few), pl.ds(lax.rem(i, zs // few) * few, few)
            body(dp, z, aligned(i, 256))

        loop(4 * zs // few, one)

    def gates(dp, z, at):
        gate_v[at, :] = dot(h2_all[dp, z].reshape(256, -1), gu_w[:, 0:wide])

    def products(dp, z, at):
        gp_v[at, :] = dot(cot_all[dp, z].reshape(256, -1), down_w[...], ((1,), (1,)))

    hidden.relay(0)
    fetched(2)
    tiles(products)
    saved += [net.keep(down_w, down_w_out), net.keep(gp_v, gp_out)]
    for s in range(1, zs):
        hidden.relay(s)
    hidden.end()
    saved.append(net.keep(h2_all, h2_out))
    fetched(0)
    tiles(gates)
    saved.append(net.keep(gate_v, gate_out))
    fetched(1)
    saved.append(net.keep(gu_w, gu_w_out))
    for copy in saved:
        copy.wait()
    net.finish()


ORDER = (
    "g0s0", "g0z", "g2s0", "g2z", "hstart", "F0", "g0s1", "F1", "F2", "S0", "F3", "S1", "T0", "fstart",
    "g0r0", "S2", "fF0", "T1", "S3", "T2", "g2s1", "g2s2", "g2r0", "fS0", "T3", "g2r1", "hend", "gstart",
    "g2s3", "fF1", "g2r2", "gs1", "gs2", "gs3", "gf0", "gf1", "g1z", "g1s0", "fF2", "g0s2", "g1s1", "gf2",
    "gf3", "gend", "g0s3", "A0", "B0", "bt0", "g0r1", "fF3", "g1s2", "A1", "B1", "fS1", "g1r0", "W1",
    "W2", "fT0", "sw0", "g1r1", "sw1", "fS2", "g1s3", "sw2", "g0r2", "bt1", "bx", "sw3", "fT1", "Ls0",
    "g1r2", "Ls1", "Ls2", "Lr0", "fS3", "Ls3", "g0r3", "fT2", "fT3", "Lr1", "bend", "gain2", "Lr2", "g2r3",
    "Lr3", "g1r3", "gain3", "fend",
)
RELAY_WAYS = ("xy", "x", "y", "y", "x", "y", "xy")


def backward_kernel(
    zs, gh_part, feed_part, gu_grad, down_grad, middle, cot, x, gains_in, docs_in, cosine, sine,
    hidden_in, qkv_in, attended_in, qkv_w_in, out_w_in,
    layer_out, input_grad, q_out, k_out, v_out, o_out, gate_out, up_out, down_out, gains_out,
    own, sib, one, two, landed, own_f, sib_f, one_f, two_f, landed_f, part, sib_1, far_1, landed_1,
    h1, qkv, attended, qkv_w, out_w, gbr_all, gqkv, gains, docs, cos_v, sin_v, hg, mid_v, cot_v, x_v, gm_v, gbr_v, out_v,
    lo_v, gsum, gall, gsum_z, g_far, g_land, q_give, q_own, q_land, o_part, o_own, o_land, send_sems, recv_sems, local_sems,
):
    net = Net(zs, send_sems, recv_sems, local_sems)
    net.meet()
    deep, wide = gate_out.shape[0], gu_grad.shape[1] // 2
    seq = docs.shape[1]
    half, side = deep // 2, HEAD_DIM // 2
    rows = x.shape[1]
    last = 2 * zs - 1
    scale = HEAD_DIM**-0.5
    hidden = SumAll(net, gh_part, own, sib, one, two, landed)
    feed = SumAll(net, feed_part, own_f, sib_f, one_f, two_f, landed_f)
    local = [net.keep(middle, mid_v), net.keep(cot.at[net.t], cot_v), net.keep(gains_in, gains)]
    local += [net.keep(x.at[net.t], x_v), net.keep(docs_in, docs), net.keep(cosine, cos_v), net.keep(sine, sin_v)]
    local += [net.keep(qkv_in, qkv), net.keep(attended_in, attended), net.keep(qkv_w_in, qkv_w)]
    local += [net.keep(out_w_in, out_w), net.keep(hidden_in, h1)]

    def block(dp, z):
        return aligned(dp * zs + z, wide)

    ways = iter(RELAY_WAYS)
    grads = [
        SpreadGrads(
            net,
            lambda z: gu_grad.at[aligned(z, deep), pl.ds(0, wide)],
            lambda dp, z: gate_out.at[:, block(dp, z)],
            next(ways),
        ),
        SpreadGrads(
            net,
            lambda z: gu_grad.at[aligned(z, deep), pl.ds(wide, wide)],
            lambda dp, z: up_out.at[:, block(dp, z)],
            next(ways),
        ),
        SpreadGrads(
            net,
            lambda z: down_grad.at[:, aligned(z, deep)],
            lambda dp, z: down_out.at[block(dp, z)],
            next(ways),
        ),
    ]

    def q_place(ref):
        def place(dp, z):
            a, b = lax.div(dp, 2), lax.rem(dp, 2)
            return ref.at[pl.ds(pl.multiple_of(a * half, half), half), aligned(b * zs + z, HEAD_DIM)]

        return place

    def o_place(dp, z):
        a, b = lax.div(dp, 2), lax.rem(dp, 2)
        return o_out.at[pl.ds(pl.multiple_of((b * zs + z) * HEAD_DIM + a * side, side), side)]

    late = [
        SpreadGrads(net, lambda z, m=m: q_own.at[z, :, pl.ds(m * HEAD_DIM, HEAD_DIM)], q_place(ref), next(ways))
        for m, ref in enumerate((q_out, k_out, v_out))
    ]
    late.append(SpreadGrads(net, lambda z: o_own.at[z], o_place, next(ways)))
    branch = SumLine(net, part, sib_1, far_1, landed_1)
    gather = GatherGroup(net, gbr_v, gbr_all)
    tile = 128
    outs, pairs, swaps, plane, z_gain = [], [], [], [], []

    def total_of(ref, at):
        total = ref[0, at, :].astype(F32)
        for z in range(1, zs):
            total += ref[z, at, :].astype(F32)
        return total

    def norm_back(inputs, total, gain, k):
        inverse = lax.rsqrt(jnp.mean(inputs * inputs, axis=-1, keepdims=True) + EPS)
        normed = inputs * inverse
        prod = total * normed
        gsum[k] += prod[0:8, :] + prod[8:16, :]
        scaled = total * gain
        return inverse * (scaled - normed * jnp.mean(scaled * normed, axis=-1, keepdims=True))

    def hidden_end():
        for copy in local:
            copy.wait()
        hidden.end()
        gsum[...] = jnp.zeros_like(gsum)

        def back_two(i):
            at = aligned(i, 16)
            grad = cot_v[at, :].astype(F32) + norm_back(mid_v[at, :], total_of(landed, at), gains[1:2, :], 1)
            gm_v[at, :] = grad
            gbr_v[at, :] = grad.astype(BF)

        loop(rows // 16, back_two)

    def place_of(k):
        b = net.b if k else 1 - net.b
        return b, b * seq, pl.ds(pl.multiple_of(b * seq, seq), seq), docs[pl.ds(b, 1), :]

    def queries_back(k):
        b, base, every, row = place_of(k)

        def heads_grad(i):
            at = pl.ds(pl.multiple_of(base + i * 256, 256), 256)
            hg[aligned(i, 256), :] = dot(gbr_all[at, :], out_w[...], ((1,), (1,)), BF)

        loop(seq // 256, heads_grad)

        def by_query(i):
            at = pl.ds(pl.multiple_of(base + i * tile, tile), tile)
            pos = aligned(i, tile)
            keys = qkv[every, HEAD_DIM : 2 * HEAD_DIM]
            sigma = sigma_of(qkv[at, 0:HEAD_DIM], keys)
            gw = dot(hg[pos, :], qkv[every, 2 * HEAD_DIM : 3 * HEAD_DIM], ((1,), (1,)))
            gs = jnp.where(seen(row, i * tile, tile), gw * sigma * (1.0 - sigma), 0.0).astype(BF)
            gq = dot(gs, keys) * scale
            gqkv[at, 0:HEAD_DIM] = turn(gq, cos_v[pos, :], -sin_v[pos, :]).astype(BF)

        loop(seq // tile, by_query)

    def keys_back(k):
        b, base, every, row = place_of(k)

        def by_key(i):
            at = pl.ds(pl.multiple_of(base + i * tile, tile), tile)
            pos = aligned(i, tile)
            queries = qkv[every, 0:HEAD_DIM]
            sigma = sigma_of(qkv[at, HEAD_DIM : 2 * HEAD_DIM], queries)
            gw = dot(qkv[at, 2 * HEAD_DIM : 3 * HEAD_DIM], hg[...], ((1,), (1,)))
            mask = seen(row, i * tile, tile, flip=True)
            gs = jnp.where(mask, gw * sigma * (1.0 - sigma), 0.0).astype(BF)
            weights = jnp.where(mask, sigma, 0.0).astype(BF)
            gk = dot(gs, queries) * scale
            gqkv[at, HEAD_DIM : 2 * HEAD_DIM] = turn(gk, cos_v[pos, :], -sin_v[pos, :]).astype(BF)
            gqkv[at, 2 * HEAD_DIM : 3 * HEAD_DIM] = dot(weights, hg[...], kind=BF)

        loop(seq // tile, by_key)

        def back_one(i):
            at = pl.ds(pl.multiple_of(base + i * tile, tile), tile)
            out = dot(gqkv[at, :], qkv_w[...], ((1,), (1,)), BF)
            for j in range(tile // rows):
                blk = i * (tile // rows) + j
                t = lax.div(blk, zs)
                z = (1 - t) * blk + t * (last - blk)
                part[b, t, z] = out[j * rows : (j + 1) * rows, :]

        loop(seq // tile, back_one)
        branch.give(k)

    def qkv_grad(z, a):
        at = pl.ds(pl.multiple_of(z * deep + a * half, half), half)
        return dot(h1[:, at], gqkv[...], ((0,), (0,)), BF)

    def side_rows(a):
        return pl.ds(pl.multiple_of(a * side, side), side)

    def weights_give():
        def out_grad(z):
            o_part[z] = dot(attended[...], gbr_all[:, aligned(z, deep)], ((0,), (0,)), BF)

        def theirs(z):
            q_give[z] = qkv_grad(z, 1 - net.a)

        loop(zs, out_grad)
        loop(zs, theirs)
        for s in range(zs):
            z = lax.rem(net.z + s + 1, zs)
            swaps.append(
                (
                    z,
                    net.send(q_give.at[z], q_land.at[z], net.over_y),
                    net.send(o_part.at[z, side_rows(1 - net.a)], o_land.at[z], net.over_y),
                )
            )

    def weights_own():
        def ours(z):
            q_own[z] = qkv_grad(z, net.a)

        loop(zs, ours)

    def weights_sum(s):
        z, q_in, o_in = swaps[s]
        q_in.wait_recv()
        add_rows(q_own.at[z], [q_own.at[z], q_land.at[z]], half)
        o_in.wait_recv()
        add_rows(o_own.at[z], [o_part.at[z, side_rows(net.a)], o_land.at[z]], side)
        for grad in late:
            grad.go(s + 1) if s < zs - 1 else grad.own()

    def branch_end():
        branch.end()

        def back_last(i):
            at = aligned(i, 16)
            total = total_of(landed_1.at[net.b], at) + far_1[at, :].astype(F32)
            grad = gm_v[at, :] + norm_back(x_v[at, :].astype(F32), total, gains[0:1, :], 0)
            out_v[at, :] = grad.astype(BF)

        loop(rows // 16, back_last)
        outs.append(net.keep(out_v, input_grad.at[net.t]))
        pairs.append(net.send(out_v, input_grad.at[net.t], net.sibling))
        plane.append(net.send(gsum, g_far.at[0], net.sibling))

    def gains_plane():
        plane[0].wait_recv()
        gall[...] = gsum[...] + g_far[0]
        for k, way in ((1, net.over_x), (2, net.over_y), (3, net.across)):
            plane.append(net.send(gall, g_far.at[k], way))

    def gains_line():
        for copy in plane[1:]:
            copy.wait_recv()
        gsum_z[...] = gall[...] + g_far[1] + g_far[2] + g_far[3]

        def cut(z):
            return gsum_z.at[:, :, aligned(z, deep)]

        z_gain.extend(net.send(cut(lax.rem(net.z + s, zs)), g_land.at[net.z], net.along_z(s)) for s in range(1, zs))
        outs.append(net.keep(cut(net.z), g_land.at[net.z]))

    def feed_end():
        feed.end()

        def close(i):
            at = aligned(i, 16)
            lo_v[at, :] = (mid_v[at, :] + total_of(landed_f, at)).astype(BF)

        loop(rows // 16, close)
        outs.append(net.keep(lo_v, layer_out.at[net.t]))
        pairs.append(net.send(lo_v, layer_out.at[net.t], net.sibling))

    def each(method):
        def step(s):
            for grad in late:
                getattr(grad, method)(s)

        return step

    steps = {
        "hstart": hidden.start, "hend": hidden_end, "gstart": gather.start, "gend": gather.end, "fstart": feed.start,
        "fend": feed_end, "W1": weights_give, "W2": weights_own, "bx": branch.across, "bend": branch_end,
        "gain2": gains_plane, "gain3": gains_line,
    }
    counted = {
        "F": hidden.first, "S": hidden.second, "T": hidden.third, "fF": feed.first, "fS": feed.second,
        "fT": feed.third, "gs": gather.spread, "gf": gather.far, "A": queries_back, "B": keys_back, "sw": weights_sum,
        "bt": branch.take, "Ls": each("spread"), "Lr": each("relay"),
    }
    for k, grad in enumerate(grads):
        steps["g%dz" % k] = grad.start
        counted["g%ds" % k], counted["g%dr" % k] = grad.spread, grad.relay
    for name in ORDER:
        if name in steps:
            steps[name]()
        else:
            counted[name[:-1]](int(name[-1]))
    for grad in grads + late:
        grad.end()
    for copy in outs:
        copy.wait()
    for copy in z_gain + pairs:
        copy.wait_recv()
    total = g_land[0]
    for z in range(1, zs):
        total += g_land[z]
    gains_out[...] = total
    net.finish()


def widen(*arrays):
    steps = 16

    def kernel(*refs):
        for src, dst in zip(refs[: len(arrays)], refs[len(arrays) :], strict=True):
            dst[...] = src[...].astype(F32)

    specs = [pl.BlockSpec((a.shape[0] // steps, a.shape[1]), lambda i: (i, 0)) for a in arrays]
    return pl.pallas_call(
        kernel,
        grid=(steps,),
        in_specs=specs,
        out_specs=specs,
        out_shape=[jax.ShapeDtypeStruct(a.shape, F32) for a in arrays],
        compiler_params=pltpu.CompilerParams(vmem_limit_bytes=60 * MIB),
    )(*arrays)


def rope_tables(seq):
    half_dim = HEAD_DIM // 2
    frequency = ROPE_BASE ** (-np.arange(half_dim, dtype=np.float32) / half_dim)
    angle = np.arange(seq, dtype=np.float32)[:, None] * frequency.astype(np.float32)[None, :]
    cosine, sine = np.cos(angle), np.sin(angle)
    return (
        np.concatenate([cosine, cosine], axis=1).astype(np.float32),
        np.concatenate([-sine, sine], axis=1).astype(np.float32),
    )


def heads_shards(
    zs, activations, document_ids, attn_gain, w_query, w_key, w_value, w_out, mlp_gain, w_gate, w_up, w_down, cotangent
):
    stretch, width = activations.shape[3:]
    deep = w_query.shape[0]
    seq = document_ids.shape[1]
    pair = 2 * seq
    wide = w_gate.shape[1] // (4 * zs)
    x = activations.reshape(2, stretch, width)
    cot = cotangent.reshape(2, stretch, width)
    small = jnp.stack([attn_gain.astype(F32), mlp_gain.astype(F32)])
    docs_rows = document_ids.astype(F32).reshape(seq // deep, deep)
    small = jnp.concatenate([small, docs_rows, jnp.zeros((6 - seq // deep, deep), F32)])
    cosine, sine = (jnp.asarray(table) for table in rope_tables(seq))
    half = stretch // 2
    hidden, qkv, attended, qkv_w, out_w, gains, docs, middle, h2_all, cot_all, gu_w, down_w, gate, grad_product = call(
        functools.partial(forward_kernel, zs),
        1,
        [
            ((pair, width), BF, ANY),
            ((pair, 3 * HEAD_DIM), BF, ANY),
            ((pair, HEAD_DIM), BF, ANY),
            ((width, 3 * HEAD_DIM), BF, ANY),
            ((HEAD_DIM, width), BF, ANY),
            ((8, width), F32, ANY),
            ((8, seq), F32, ANY),
            ((stretch, width), F32, ANY),
            ((4, zs, 2, stretch, width), BF, ANY),
            ((4, zs, 2, stretch, width), BF, ANY),
            ((width, 2 * wide), BF, ANY),
            ((wide, width), BF, ANY),
            ((4 * seq, wide), F32, ANY),
            ((4 * seq, wide), F32, ANY),
        ],
        [
            VMEM((pair, width), BF),
            VMEM((pair, width), BF),
            VMEM((width, 3 * HEAD_DIM), BF),
            VMEM((HEAD_DIM, width), BF),
            VMEM((zs, 8, deep), F32),
            VMEM((2, 8, deep), F32),
            VMEM((8, width), F32),
            VMEM((8, seq), F32),
            VMEM((seq, HEAD_DIM), F32),
            VMEM((seq, HEAD_DIM), F32),
            VMEM((pair, 3 * HEAD_DIM), BF),
            VMEM((pair, HEAD_DIM), BF),
            VMEM((2, 2, zs, stretch, width), BF),
            VMEM((2, zs, stretch, width), BF),
            VMEM((zs, stretch, width), BF),
            VMEM((zs, stretch, width), BF),
            VMEM((stretch, width), BF),
            VMEM((stretch, width), BF),
            VMEM((stretch, width), F32),
            VMEM((4, zs, 2, stretch, width), BF),
            VMEM((4, zs, 2, stretch, width), BF),
            VMEM((width, 2 * wide), BF),
            VMEM((wide, width), BF),
            VMEM((4 * seq, wide), F32),
            VMEM((4 * seq, wide), F32),
        ],
        (134, 131, 34),
        (x, w_query, w_key, w_value, w_out, small, cosine, sine, w_gate, w_up, w_down, cot),
        58,
    )

    h2 = h2_all.reshape(4 * seq, width)
    cots = cot_all.reshape(4 * seq, width)
    upward = dot(h2, gu_w[:, wide:])
    sigma_gate = jax.nn.sigmoid(gate)
    silu = gate * sigma_gate
    product = (silu * upward).astype(BF)
    grad_gate = (grad_product * upward * sigma_gate * (1.0 + gate * (1.0 - sigma_gate))).astype(BF)
    grad_up = (grad_product * silu).astype(BF)
    grad_gu = jnp.concatenate([grad_gate, grad_up], axis=1)
    gh_part = dot(grad_gu, gu_w, ((1,), (1,)), BF).reshape(4, zs, 2, stretch, width)
    feed_part = dot(product, down_w, kind=BF).reshape(4, zs, 2, stretch, width)
    gu_grad = dot(h2, grad_gu, ((0,), (0,)), BF)
    down_grad = dot(product, cots, ((0,), (0,)), BF)

    sum_scratch = [
        VMEM((4, zs, stretch, width), BF),
        VMEM((4, zs, stretch, width), BF),
        VMEM((2, 2, zs, half, width), BF),
        VMEM((2, zs, half, width), BF),
        VMEM((zs, stretch, width), BF),
    ]
    layer_out, input_grad, q_g, k_g, v_g, o_g, gate_g, up_g, down_g, gains_g = call(
        functools.partial(backward_kernel, zs),
        2,
        [
            ((2, stretch, width), BF, ANY),
            ((2, stretch, width), BF, ANY),
            (w_query.shape, BF, ANY),
            (w_key.shape, BF, ANY),
            (w_value.shape, BF, ANY),
            (w_out.shape, BF, ANY),
            (w_gate.shape, BF, ANY),
            (w_up.shape, BF, ANY),
            (w_down.shape, BF, ANY),
            ((2, 8, deep), F32, VMEM),
        ],
        sum_scratch
        + sum_scratch
        + [
            VMEM((2, 2, zs, stretch, width), BF),
            VMEM((2, zs, stretch, width), BF),
            VMEM((stretch, width), BF),
            VMEM((2, zs, stretch, width), BF),
            VMEM((pair, width), BF),
            VMEM((pair, 3 * HEAD_DIM), BF),
            VMEM((pair, HEAD_DIM), BF),
            VMEM((width, 3 * HEAD_DIM), BF),
            VMEM((HEAD_DIM, width), BF),
            VMEM((pair, width), BF),
            VMEM((pair, 3 * HEAD_DIM), BF),
            VMEM((8, width), F32),
            VMEM((8, seq), F32),
            VMEM((seq, HEAD_DIM), F32),
            VMEM((seq, HEAD_DIM), F32),
            VMEM((seq, HEAD_DIM), BF),
            VMEM((stretch, width), F32),
            VMEM((stretch, width), BF),
            VMEM((stretch, width), BF),
            VMEM((stretch, width), F32),
            VMEM((stretch, width), BF),
            VMEM((stretch, width), BF),
            VMEM((stretch, width), BF),
            VMEM((2, 8, width), F32),
            VMEM((2, 8, width), F32),
            VMEM((2, 8, width), F32),
            VMEM((4, 2, 8, width), F32),
            VMEM((zs, 2, 8, deep), F32),
            VMEM((zs, deep // 2, 3 * HEAD_DIM), BF),
            VMEM((zs, deep // 2, 3 * HEAD_DIM), BF),
            VMEM((zs, deep // 2, 3 * HEAD_DIM), BF),
            VMEM((zs, HEAD_DIM, deep), BF),
            VMEM((zs, HEAD_DIM // 2, deep), BF),
            VMEM((zs, HEAD_DIM // 2, deep), BF),
        ],
        (232, 231, 34),
        (
            gh_part, feed_part, gu_grad, down_grad, middle, cot, x, gains, docs, cosine, sine,
            hidden, qkv, attended, qkv_w, out_w,
        ),
        60,
    )
    gain_grads = jnp.sum(gains_g, axis=1)
    q_g, k_g, v_g, o_g, gate_g, up_g, down_g = widen(q_g, k_g, v_g, o_g, gate_g, up_g, down_g)
    return (
        layer_out.reshape(activations.shape),
        input_grad.reshape(activations.shape),
        gain_grads[0],
        q_g,
        k_g,
        v_g,
        o_g,
        gain_grads[1],
        gate_g,
        up_g,
        down_g,
    )


def angles(positions):
    half_dim = HEAD_DIM // 2
    frequency = ROPE_BASE ** (-jnp.arange(half_dim, dtype=jnp.float32) / half_dim)
    angle = positions.astype(jnp.float32)[:, None] * frequency[None, :]
    return (jnp.cos(angle)[:, None, :], jnp.sin(angle)[:, None, :])


def rotate(flat, positions):
    row_count = flat.shape[0]
    heads = flat.reshape(row_count, -1, HEAD_DIM)
    cosine, sine = angles(positions)
    first = heads[..., : HEAD_DIM // 2]
    second = heads[..., HEAD_DIM // 2 :]
    turned = jnp.concatenate(
        [first * cosine - second * sine, second * cosine + first * sine], axis=-1
    )
    return turned.reshape(row_count, -1)


def unrotate(flat, positions):
    row_count = flat.shape[0]
    heads = flat.reshape(row_count, -1, HEAD_DIM)
    cosine, sine = angles(positions)
    first = heads[..., : HEAD_DIM // 2]
    second = heads[..., HEAD_DIM // 2 :]
    turned = jnp.concatenate(
        [first * cosine + second * sine, second * cosine - first * sine], axis=-1
    )
    return turned.reshape(row_count, -1)


def normalize(values):
    inverse = lax.rsqrt(jnp.mean(values * values, axis=-1, keepdims=True) + EPS)
    return (values * inverse, inverse)


def norm_back(grad_normed_out, normed, inverse, gain):
    scaled = grad_normed_out * gain
    return inverse * (scaled - normed * jnp.mean(scaled * normed, axis=-1, keepdims=True))


def contract_rows(left, right):
    return lax.dot_general(
        left, right, (((1,), (1,)), ((), ())), preferred_element_type=jnp.float32
    )


def contract_cols(left, right):
    return lax.dot_general(
        left, right, (((0,), (0,)), ((), ())), preferred_element_type=jnp.float32
    )


def visibility(query_positions, query_docs, key_positions, key_docs):
    same_doc = query_docs[:, None] == key_docs[None, :]
    earlier = key_positions[None, :] <= query_positions[:, None]
    return jnp.where(same_doc & earlier, 1.0, 0.0).astype(jnp.float32)


def merge_heads(stacked):
    return jnp.transpose(stacked, (1, 0, 2)).reshape(stacked.shape[1], -1)


def head_slice(matrix, offset):
    return lax.dynamic_slice_in_dim(matrix, offset, HEAD_DIM, 1)


def attend_forward(queries, key_rows, value_rows, visible):
    score_scale = HEAD_DIM ** (-0.5)

    def one_head(head_index):
        offset = head_index * HEAD_DIM
        scores = (
            contract_rows(head_slice(queries, offset), head_slice(key_rows, offset)) * score_scale
        )
        weights = (jax.nn.sigmoid(scores - SHIFT) * visible).astype(jnp.bfloat16)
        return jnp.dot(weights, head_slice(value_rows, offset), preferred_element_type=jnp.float32)

    stacked = lax.map(one_head, jnp.arange(queries.shape[1] // HEAD_DIM))
    return merge_heads(stacked)


def attend_back(queries, key_rows, value_rows, grad_attended, visible):
    score_scale = HEAD_DIM ** (-0.5)

    def one_head(head_index):
        offset = head_index * HEAD_DIM
        head_query = head_slice(queries, offset)
        head_key = head_slice(key_rows, offset)
        head_grad = head_slice(grad_attended, offset)
        scores = contract_rows(head_query, head_key) * score_scale
        sigma = jax.nn.sigmoid(scores - SHIFT)
        grad_weights = contract_rows(head_grad, head_slice(value_rows, offset))
        grad_scores = (grad_weights * visible * sigma * (1.0 - sigma)).astype(jnp.bfloat16)
        pieces = []
        pieces.append(
            jnp.dot(grad_scores, head_key, preferred_element_type=jnp.float32) * score_scale
        )
        weights = (sigma * visible).astype(jnp.bfloat16)
        pieces.append(contract_cols(grad_scores, head_query) * score_scale)
        pieces.append(contract_cols(weights, head_grad))
        return tuple(pieces)

    stacked = lax.map(one_head, jnp.arange(queries.shape[1] // HEAD_DIM))
    return tuple((merge_heads(piece) for piece in stacked))


def rows_shards(
    activations,
    document_ids,
    attn_gain,
    w_query,
    w_key,
    w_value,
    w_out,
    mlp_gain,
    w_gate,
    w_up,
    w_down,
    cotangent,
):
    groups = lax.axis_size("cp")
    rank = lax.axis_index("cp")
    stretch_len = activations.shape[3]
    width = activations.shape[4]
    row_count = 2 * stretch_len
    offsets = jnp.arange(stretch_len, dtype=jnp.int32)
    my_positions = jnp.concatenate(
        [rank * stretch_len + offsets, (2 * groups - 1 - rank) * stretch_len + offsets]
    )
    all_docs = document_ids[0]
    my_docs = jnp.take(all_docs, my_positions)
    slots = jnp.arange(groups * row_count, dtype=jnp.int32)
    owners = slots // row_count
    halves = slots // stretch_len % 2
    key_positions = (
        jnp.where(halves == 0, owners, 2 * groups - 1 - owners) * stretch_len + slots % stretch_len
    )
    key_docs = jnp.take(all_docs, key_positions)
    visible = visibility(my_positions, my_docs, key_positions, key_docs)
    gathered = (
        lax.all_gather(w_query, "cp", axis=0, tiled=True),
        lax.all_gather(w_key, "cp", axis=0, tiled=True),
        lax.all_gather(w_value, "cp", axis=0, tiled=True),
        lax.all_gather(w_out, "cp", axis=1, tiled=True),
        lax.all_gather(w_gate, "cp", axis=0, tiled=True),
        lax.all_gather(w_up, "cp", axis=0, tiled=True),
        lax.all_gather(w_down, "cp", axis=1, tiled=True),
        lax.all_gather(attn_gain, "cp", axis=0, tiled=True),
        lax.all_gather(mlp_gain, "cp", axis=0, tiled=True),
    )
    (
        query_full,
        key_full,
        value_full,
        out_full,
        gate_full,
        up_full,
        down_full,
        gain_one,
        gain_two,
    ) = gathered
    gain_one = gain_one.astype(jnp.float32)
    gain_two = gain_two.astype(jnp.float32)
    inputs = activations.reshape(row_count, width).astype(jnp.float32)
    normed_one, inverse_one = normalize(inputs)
    hidden_one = (normed_one * gain_one).astype(jnp.bfloat16)
    queries = rotate(
        jnp.dot(hidden_one, query_full, preferred_element_type=jnp.float32), my_positions
    ).astype(jnp.bfloat16)
    keys_local = rotate(
        jnp.dot(hidden_one, key_full, preferred_element_type=jnp.float32), my_positions
    ).astype(jnp.bfloat16)
    values_local = jnp.dot(hidden_one, value_full, preferred_element_type=jnp.float32).astype(
        jnp.bfloat16
    )
    keys_all, values_all = (
        lax.all_gather(keys_local, "cp", axis=0, tiled=True),
        lax.all_gather(values_local, "cp", axis=0, tiled=True),
    )
    attended = attend_forward(queries, keys_all, values_all, visible).astype(jnp.bfloat16)
    branch = lax.psum(jnp.dot(attended, out_full, preferred_element_type=jnp.float32), "tp")
    middle = inputs + branch
    normed_two, inverse_two = normalize(middle)
    hidden_two = (normed_two * gain_two).astype(jnp.bfloat16)
    gate = jnp.dot(hidden_two, gate_full, preferred_element_type=jnp.float32)
    upward = jnp.dot(hidden_two, up_full, preferred_element_type=jnp.float32)
    sigma_gate = jax.nn.sigmoid(gate)
    silu_gate = gate * sigma_gate
    product = (silu_gate * upward).astype(jnp.bfloat16)
    feed = lax.psum(jnp.dot(product, down_full, preferred_element_type=jnp.float32), "tp")
    result = middle + feed
    layer_out = result.astype(jnp.bfloat16).reshape(activations.shape)
    grad_result = cotangent.reshape(row_count, width).astype(jnp.float32)
    grad_feed = grad_result.astype(jnp.bfloat16)
    grad_product = contract_rows(grad_feed, down_full)
    grad_gate = (grad_product * upward * sigma_gate * (1.0 + gate * (1.0 - sigma_gate))).astype(
        jnp.bfloat16
    )
    grad_up = (grad_product * silu_gate).astype(jnp.bfloat16)
    grad_hidden_two = lax.psum(
        contract_rows(grad_gate, gate_full) + contract_rows(grad_up, up_full), "tp"
    )
    grad_gain_two = jnp.sum(grad_hidden_two * normed_two, axis=0)
    grad_middle = grad_result + norm_back(grad_hidden_two, normed_two, inverse_two, gain_two)
    grad_down = contract_cols(product, grad_feed)
    grad_gate_w = contract_cols(hidden_two, grad_gate)
    grad_up_w = contract_cols(hidden_two, grad_up)
    share_gate, share_up, share_down, share_gain_two = (
        lax.psum_scatter(grad_gate_w, "cp", scatter_dimension=0, tiled=True),
        lax.psum_scatter(grad_up_w, "cp", scatter_dimension=0, tiled=True),
        lax.psum_scatter(grad_down, "cp", scatter_dimension=1, tiled=True),
        lax.psum_scatter(grad_gain_two, "cp", scatter_dimension=0, tiled=True),
    )
    grad_branch = grad_middle.astype(jnp.bfloat16)
    grad_attended = contract_rows(grad_branch, out_full).astype(jnp.bfloat16)
    grad_queries, key_terms, value_terms = attend_back(
        queries, keys_all, values_all, grad_attended, visible
    )
    grad_keys, grad_values = (
        lax.psum_scatter(key_terms, "cp", scatter_dimension=0, tiled=True),
        lax.psum_scatter(value_terms, "cp", scatter_dimension=0, tiled=True),
    )
    grad_query_pre = unrotate(grad_queries, my_positions).astype(jnp.bfloat16)
    grad_key_pre = unrotate(grad_keys, my_positions).astype(jnp.bfloat16)
    grad_value_pre = grad_values.astype(jnp.bfloat16)
    local_hidden = (
        contract_rows(grad_query_pre, query_full)
        + contract_rows(grad_key_pre, key_full)
        + contract_rows(grad_value_pre, value_full)
    )
    grad_hidden_one = lax.psum(local_hidden, "tp")
    grad_gain_one = jnp.sum(grad_hidden_one * normed_one, axis=0)
    grad_inputs = grad_middle + norm_back(grad_hidden_one, normed_one, inverse_one, gain_one)
    grad_query_w = contract_cols(hidden_one, grad_query_pre)
    grad_key_w = contract_cols(hidden_one, grad_key_pre)
    grad_value_w = contract_cols(hidden_one, grad_value_pre)
    grad_out_w = contract_cols(attended, grad_branch)
    share_query, share_key, share_value, share_out, share_gain_one = (
        lax.psum_scatter(grad_query_w, "cp", scatter_dimension=0, tiled=True),
        lax.psum_scatter(grad_key_w, "cp", scatter_dimension=0, tiled=True),
        lax.psum_scatter(grad_value_w, "cp", scatter_dimension=0, tiled=True),
        lax.psum_scatter(grad_out_w, "cp", scatter_dimension=1, tiled=True),
        lax.psum_scatter(grad_gain_one, "cp", scatter_dimension=0, tiled=True),
    )
    summed = lax.psum(
        (
            share_gain_one,
            share_query,
            share_key,
            share_value,
            share_out,
            share_gain_two,
            share_gate,
            share_up,
            share_down,
        ),
        "dp",
    )
    input_grad = grad_inputs.astype(jnp.bfloat16).reshape(activations.shape)
    return (
        layer_out,
        input_grad,
        summed[0],
        summed[1],
        summed[2],
        summed[3],
        summed[4],
        summed[5],
        summed[6],
        summed[7],
        summed[8],
    )


def layer(sizes, *args):
    heads = args[3].shape[1] // HEAD_DIM
    zs = sizes["cp"]
    fits = sizes["dp"] == 4 and sizes["tp"] == 2 and zs == 4 and heads == 2 * zs
    fits = fits and args[0].shape[3] % 32 == 0 and args[8].shape[1] % (2 * zs * HEAD_DIM) == 0
    fits = fits and args[3].shape[0] % HEAD_DIM == 0 and args[1].shape[1] % args[3].shape[0] == 0
    fits = fits and args[1].shape[1] <= 6 * args[3].shape[0]
    if fits:
        return heads_shards(zs, *args)
    return rows_shards(*args)


def solution(mesh):
    return jax.shard_map(
        functools.partial(layer, dict(mesh.shape)),
        mesh=mesh,
        in_specs=(
            P("dp", "cp", None, None, None),
            P("dp", None),
            P("cp"),
            P("cp", "tp"),
            P("cp", "tp"),
            P("cp", "tp"),
            P("tp", "cp"),
            P("cp"),
            P("cp", "tp"),
            P("cp", "tp"),
            P("tp", "cp"),
            P("dp", "cp", None, None, None),
        ),
        out_specs=(
            P("dp", "cp", None, None, None),
            P("dp", "cp", None, None, None),
            P("cp"),
            P("cp", "tp"),
            P("cp", "tp"),
            P("cp", "tp"),
            P("tp", "cp"),
            P("cp"),
            P("cp", "tp"),
            P("cp", "tp"),
            P("tp", "cp"),
        ),
        check_vma=False,
    )
```

```python
import functools
import math

import jax
import jax.numpy as jnp
import numpy as np
from jax import lax
from jax.experimental import pallas as pl
from jax.experimental.pallas import tpu as pltpu
from jax.sharding import PartitionSpec as P

HEAD_DIM = 128
EPS = 1e-05
SHIFT = math.log(4096.0)
ROPE_BASE = 10000.0
BF = jnp.bfloat16
F32 = jnp.float32
MESH = pl.DeviceIdType.MESH
ANY = pl.ANY
VMEM = pltpu.VMEM
MIB = 2**20


class Net:
    def __init__(self, zs, send_sems, recv_sems, local_sems):
        self.zs = zs
        self.dp, self.z, self.t = (lax.axis_index(a) for a in ("dp", "cp", "tp"))
        self.a, self.b = lax.div(self.dp, 2), lax.rem(self.dp, 2)
        self.send_sems, self.recv_sems, self.local_sems = send_sems, recv_sems, local_sems
        self.arrivals = 0
        self.free_locals = list(range(local_sems.shape[0]))
        self.open = []

    def along_z(self, s):
        return (self.dp, lax.rem(self.z + s, self.zs), self.t)

    def source_z(self, s):
        return lax.rem(self.z + self.zs - s, self.zs)

    @property
    def over_x(self):
        return (2 * self.a + 1 - self.b, self.z, self.t)

    @property
    def over_y(self):
        return (2 * (1 - self.a) + self.b, self.z, self.t)

    @property
    def sibling(self):
        return (self.dp, self.z, 1 - self.t)

    @property
    def across(self):
        return (2 * (1 - self.a) + 1 - self.b, self.z, self.t)

    def meet(self):
        ways = [self.along_z(s) for s in range(1, self.zs)] + [self.over_x, self.over_y, self.across, self.sibling]
        barrier = pltpu.get_barrier_semaphore()
        for way in ways:
            pl.semaphore_signal(barrier, inc=1, device_id=way, device_id_type=MESH)
        pl.semaphore_wait(barrier, len(ways))

    def slot(self):
        self.arrivals += 1
        return self.arrivals - 1

    def send(self, src, dst, way, arrive=None, when=None):
        arrive = self.slot() if arrive is None else arrive
        sem = self.send_sems.at[len(self.open)]
        copy = pltpu.make_async_remote_copy(
            src, dst, sem, self.recv_sems.at[arrive], device_id=way, device_id_type=MESH
        )
        if when is None:
            copy.start()
        else:
            pl.when(when)(copy.start)
        self.open.append((copy, when))
        return copy

    def arrival(self, ref, slot):
        return pltpu.make_async_remote_copy(
            ref, ref, self.send_sems.at[0], self.recv_sems.at[slot], device_id=self.sibling, device_id_type=MESH
        )

    def keep(self, src, dst):
        return Kept(self, src, dst)

    def finish(self):
        for copy, when in self.open:
            if when is None:
                copy.wait_send()
            else:
                pl.when(when)(copy.wait_send)


class Kept:
    def __init__(self, net, src, dst):
        self.net, self.slot = net, net.free_locals.pop(0)
        self.copy = pltpu.make_async_copy(src, dst, net.local_sems.at[self.slot])
        self.copy.start()

    def wait(self):
        self.copy.wait()
        self.net.free_locals.append(self.slot)


class LineGather:
    def __init__(self, net, src, place):
        self.net, self.src, self.place = net, src, place
        self.h, self.low = lax.div(net.z, 2), lax.rem(net.z, 2)
        self.mate = (net.dp, net.z + 1 - 2 * self.low, net.t)
        self.gate = (net.dp, 2 - self.h, net.t)
        self.hands_on = self.h != self.low

    def start(self):
        net = self.net
        mine = self.place(net.z)
        self.near = net.send(self.src, mine, self.mate)
        self.slots = [net.slot(), net.slot()]
        net.send(self.src, mine, self.gate, arrive=self.slots[0] + self.low)

    def take(self, s):
        net = self.net
        if s == 1:
            self.near.wait_recv()
            return net.z + 1 - 2 * self.low
        z = 2 * (1 - self.h) + s - 2
        ref = self.place(z)
        net.arrival(ref, self.slots[s - 2]).wait_recv()
        net.send(ref, ref, self.mate, arrive=self.slots[s - 2], when=self.hands_on)
        return z


def plane_relay(net, place, halves, over_x, over_y, ways="xy", sibling=None):
    dx, dy = 2 * net.a + 1 - net.b, 2 * (1 - net.a) + net.b
    relays = []

    def by_y():
        over_x.wait_recv()
        piece = halves(place(dx), 0) if "x" in ways else place(dx)
        if "y" in ways:
            relays.append(net.send(piece, piece, net.over_y))
        if sibling:
            sibling(dx)

    def by_x():
        over_y.wait_recv()
        piece = halves(place(dy), 1) if "y" in ways else place(dy)
        if "x" in ways:
            relays.append(net.send(piece, piece, net.over_x))
        if sibling:
            sibling(dy)

    for step in (by_x, by_y) if ways == "x" else (by_y, by_x):
        step()
    return relays


def plane_end(net, relays, sibling=None):
    for copy in relays:
        copy.wait_recv()
    if sibling:
        sibling(2 * (1 - net.a) + 1 - net.b)


def rows_loop(count, step, body):
    def one(i, carry):
        body(pl.ds(pl.multiple_of(i * step, step), step))
        return carry

    lax.fori_loop(0, count // step, one, 0)


def add_rows(out, terms, rows):
    def body(at):
        total = terms[0][at, :].astype(F32)
        for term in terms[1:]:
            total += term[at, :].astype(F32)
        out[at, :] = total.astype(out.dtype)

    rows_loop(rows, 16, body)


class GatherAll:
    def __init__(self, net, src, dst):
        self.net, self.src, self.dst = net, src, dst
        rows = src.shape[0] // 2
        self.halves = lambda ref, k: ref.at[pl.ds(k * rows, rows)]

    def place(self, dp, z):
        return self.dst.at[dp, z, self.net.t]

    def start(self):
        net = self.net
        mine = self.place(net.dp, net.z)
        self.line = LineGather(net, self.src, lambda z: self.place(net.dp, z))
        self.line.start()
        self.local = net.keep(self.src, mine)
        self.plane = [(net.z, net.send(self.src, mine, net.over_x), net.send(self.src, mine, net.over_y))]
        self.twin = [net.send(self.src, mine, net.sibling)]
        self.states = []

    def to_twin(self, dp, z):
        ref = self.place(dp, z)
        self.twin.append(self.net.send(ref, ref, self.net.sibling))

    def spread(self, s):
        net = self.net
        z = self.line.take(s)
        ref = self.place(net.dp, z)
        self.plane.append((z, net.send(ref, ref, net.over_x), net.send(ref, ref, net.over_y)))
        self.to_twin(net.dp, z)

    def relay(self, s):
        z, over_x, over_y = self.plane[s]
        place = functools.partial(self.place, z=z)
        self.states.append((z, plane_relay(self.net, place, self.halves, over_x, over_y, sibling=lambda dp: self.to_twin(dp, z))))

    def end(self):
        for z, relays in self.states:
            plane_end(self.net, relays, lambda dp, z=z: self.to_twin(dp, z))
        for copy in self.twin:
            copy.wait_recv()
        self.local.wait()


class GatherGroup:
    def __init__(self, net, src, dst, own_lanes=None):
        self.net, self.src, self.dst, self.own_lanes = net, src, dst, own_lanes
        self.rows = src.shape[0]

    def place(self, b, z, t=None):
        t = self.net.t if t is None else t
        last = 2 * self.net.zs - 1
        at = ((last + 1) * b + z + t * (last - 2 * z)) * self.rows
        return self.dst.at[pl.ds(pl.multiple_of(at, self.rows), self.rows)]

    def start(self):
        net = self.net
        mine = self.place(net.b, net.z)
        self.line = LineGather(net, self.src, lambda z: self.place(net.b, z))
        self.line.start()
        self.over = [(net.z, net.send(self.src, mine, net.over_x))]
        self.twin, self.local = [], []
        if self.own_lanes is None:
            self.local.append(net.keep(self.src, mine))
            self.twin.append((net.b, net.z, net.send(self.src, mine, net.sibling)))
        else:
            for t in (0, 1):
                self.local.append(net.keep(self.own_lanes.at[t], self.place(net.b, net.z, t)))

    def to_twin(self, b, z):
        ref = self.place(b, z)
        self.twin.append((b, z, self.net.send(ref, ref, self.net.sibling)))

    def spread(self, s):
        net = self.net
        z = self.line.take(s)
        ref = self.place(net.b, z)
        self.over.append((z, net.send(ref, ref, net.over_x)))
        self.to_twin(net.b, z)
        return z

    def far(self, s):
        z, copy = self.over[s]
        copy.wait_recv()
        self.to_twin(1 - self.net.b, z)
        return z

    def end(self):
        for _, _, copy in self.twin:
            copy.wait_recv()
        for copy in self.local:
            copy.wait()


class SumGroup:
    def __init__(self, net, part, sib, far, landed):
        self.net, self.part, self.sib, self.far, self.landed = net, part, sib, far, landed
        self.rows = part.shape[3]
        self.twin, self.over, self.z_sends = {}, [], []

    def order(self):
        return [lax.rem(self.net.z + s + 1, self.net.zs) for s in range(self.net.zs)]

    def give(self, k):
        net = self.net
        b = net.b if k else 1 - net.b
        for s, z in enumerate(self.order()):
            self.twin[k, s] = net.send(self.part.at[b, 1 - net.t, z], self.sib.at[b, z], net.sibling)

    def take(self, k):
        net = self.net
        b = net.b if k else 1 - net.b
        for s, z in enumerate(self.order()):
            self.twin[k, s].wait_recv()
            own = self.part.at[b, net.t, z]
            add_rows(own, [own, self.sib.at[b, z]], self.rows)
            if k == 0:
                self.over.append(net.send(own, self.far.at[z], net.over_x))

    def along(self):
        net = self.net
        for s, z in enumerate(self.order()):
            self.over[s].wait_recv()
            last = s == net.zs - 1
            own = self.part.at[net.b, net.t, z]
            out = self.landed.at[net.z] if last else own
            add_rows(out, [own, self.far.at[z]], self.rows)
            if not last:
                self.z_sends.append(net.send(out, self.landed.at[net.z], net.along_z(s + 1)))

    def end(self):
        for copy in self.z_sends:
            copy.wait_recv()


class SumLine(SumGroup):
    def take(self, k):
        net = self.net
        b = net.b if k else 1 - net.b
        for s, z in enumerate(self.order()):
            self.twin[k, s].wait_recv()
            own, last = self.part.at[b, net.t, z], s == net.zs - 1
            out = self.landed.at[b, net.z] if last else own
            add_rows(out, [own, self.sib.at[b, z]], self.rows)
            if not last:
                self.z_sends.append(net.send(own, self.landed.at[b, net.z], net.along_z(s + 1)))

    def across(self):
        net = self.net
        b = 1 - net.b
        for copy in self.z_sends[: net.zs - 1]:
            copy.wait_recv()
        out = self.part.at[b, net.t, net.z]
        add_rows(out, [self.landed.at[b, z] for z in range(net.zs)], self.rows)
        self.over = net.send(out, self.far, net.over_x)

    def end(self):
        for copy in self.z_sends[self.net.zs - 1 :]:
            copy.wait_recv()
        self.over.wait_recv()


class SumAll:
    def __init__(self, net, part, own, sib, one, two, landed):
        self.net, self.part, self.own, self.sib = net, part, own, sib
        self.one, self.two, self.landed = one, two, landed
        self.half = part.shape[3] // 2

    def order(self):
        net = self.net
        return [lax.rem(net.z + s + 1, net.zs) for s in range(net.zs)]

    def places(self):
        a, b = self.net.a, self.net.b
        return [2 * (1 - a) + 1 - b, 2 * a + 1 - b, 2 * (1 - a) + b, 2 * a + b]

    def start(self):
        net = self.net
        self.twin, self.mine = [], []
        for z in self.order():
            self.twin.append(net.send(self.part.at[:, z, 1 - net.t], self.sib.at[:, z], net.sibling))
            self.mine.append(net.keep(self.part.at[:, z, net.t], self.own.at[:, z]))

    def upper(self, ref):
        return ref.at[pl.ds(0, self.half)]

    def lower(self, ref):
        return ref.at[pl.ds(self.half, self.half)]

    def first(self, s):
        net = self.net
        z = self.order()[s]
        dd, dx, dy, me = self.places()
        self.twin[s].wait_recv()
        self.mine[s].wait()
        for dp in (dd, dx, dy, me):
            add_rows(self.own.at[dp, z], [self.own.at[dp, z], self.sib.at[dp, z]], 2 * self.half)
        self.ones = getattr(self, "ones", [])
        self.ones.append(
            (
                net.send(self.upper(self.own.at[dd, z]), self.one.at[0, 0, z], net.over_x),
                net.send(self.upper(self.own.at[dx, z]), self.one.at[0, 1, z], net.over_x),
                net.send(self.lower(self.own.at[dd, z]), self.one.at[1, 0, z], net.over_y),
                net.send(self.lower(self.own.at[dy, z]), self.one.at[1, 1, z], net.over_y),
            )
        )

    def second(self, s):
        net = self.net
        z = self.order()[s]
        dd, dx, dy, me = self.places()
        x_dd, x_me, y_dd, y_me = self.ones[s]
        self.twos = getattr(self, "twos", [])
        x_dd.wait_recv()
        out = self.upper(self.own.at[dy, z])
        add_rows(out, [out, self.one.at[0, 0, z]], self.half)
        up = net.send(out, self.two.at[0, z], net.over_y)
        y_dd.wait_recv()
        out = self.lower(self.own.at[dx, z])
        add_rows(out, [out, self.one.at[1, 0, z]], self.half)
        side = net.send(out, self.two.at[1, z], net.over_x)
        self.twos.append((up, side))

    def third(self, s):
        net = self.net
        z = self.order()[s]
        dd, dx, dy, me = self.places()
        _, x_me, _, y_me = self.ones[s]
        up, side = self.twos[s]
        last = s == net.zs - 1
        out = self.landed.at[net.z] if last else self.own.at[me, z]
        x_me.wait_recv()
        up.wait_recv()
        mine = self.own.at[me, z]
        add_rows(self.upper(out), [self.upper(mine), self.one.at[0, 1, z], self.two.at[0, z]], self.half)
        y_me.wait_recv()
        side.wait_recv()
        add_rows(self.lower(out), [self.lower(mine), self.one.at[1, 1, z], self.two.at[1, z]], self.half)
        self.z_sends = getattr(self, "z_sends", [])
        if not last:
            self.z_sends.append(net.send(out, self.landed.at[net.z], net.along_z(s + 1)))

    def end(self):
        for copy in self.z_sends:
            copy.wait_recv()


class SpreadGrads:
    def __init__(self, net, src, dst, ways):
        self.net, self.src, self.dst, self.ways = net, src, dst, ways
        self.z_sends, self.plane, self.states = {}, {}, []

    def mine(self):
        return self.dst(self.net.dp, self.net.z)

    def start(self):
        self.own()
        for s in range(1, self.net.zs):
            self.go(s)

    def own(self):
        self.local = self.net.keep(self.src(self.net.z), self.mine())

    def go(self, s):
        net = self.net
        self.z_sends[s] = net.send(self.src(lax.rem(net.z + s, net.zs)), self.mine(), net.along_z(s))

    def spread(self, s):
        net = self.net
        z = net.source_z(s)
        ref = self.dst(net.dp, z)
        if s:
            self.z_sends[s].wait_recv()
            src = ref
        else:
            src = self.src(net.z)
        self.plane[s] = (z, net.send(src, ref, net.over_x), net.send(src, ref, net.over_y))

    def relay(self, s):
        z, over_x, over_y = self.plane[s]
        self.states.append(plane_relay(self.net, lambda dp: self.dst(dp, z), half_rows, over_x, over_y, self.ways))

    def end(self):
        for relays in self.states:
            plane_end(self.net, relays)
        self.local.wait()


def half_rows(ref, k):
    n = ref.shape[0] // 2
    return ref.at[pl.ds(k * n, n)]


def aligned(i, size):
    return pl.ds(pl.multiple_of(i * size, size), size)


def loop(count, body):
    def one(i, carry):
        body(i)
        return carry

    lax.fori_loop(0, count, one, 0)


def dot(left, right, dims=((1,), (0,)), kind=F32):
    return lax.dot_general(left, right, (dims, ((), ())), preferred_element_type=F32).astype(kind)


def turn(u, cosine, sine):
    return u * cosine + pltpu.roll(u, HEAD_DIM // 2, 1) * sine


def column(row, start, count):
    n = row.shape[1]
    here = lax.broadcasted_iota(jnp.int32, (count, n), 1) == start + lax.broadcasted_iota(jnp.int32, (count, n), 0)
    return jnp.sum(jnp.where(here, row, 0.0), axis=1, keepdims=True)


def seen(row, start, count, flip=False):
    n = row.shape[1]
    same = column(row, start, count) == row
    mine = start + lax.broadcasted_iota(jnp.int32, (count, n), 0)
    other = lax.broadcasted_iota(jnp.int32, (count, n), 1)
    return same & ((mine <= other) if flip else (other <= mine))


def sigma_of(left, right):
    return jax.nn.sigmoid(dot(left, right, ((1,), (1,))) * HEAD_DIM**-0.5 - SHIFT)


def call(kernel, name, outs, scratch, counts, args, vmem):
    return pl.pallas_call(
        kernel,
        out_shape=[jax.ShapeDtypeStruct(shape, kind) for shape, kind, _ in outs],
        in_specs=[pl.BlockSpec(memory_space=ANY)] * len(args),
        out_specs=[pl.BlockSpec(memory_space=space) for _, _, space in outs],
        scratch_shapes=list(scratch) + [pltpu.SemaphoreType.DMA(shape) for shape in counts],
        compiler_params=pltpu.CompilerParams(
            collective_id=name, has_side_effects=True, vmem_limit_bytes=vmem * MIB
        ),
    )(*args)


def forward_kernel(
    zs, x, wq, wk, wv, wo, small, cosine, sine, wg, wu, wd, cot,
    hidden_out, qkv_out, attended_out, qkv_w_out, out_w_out, gains_out, docs_out, middle, h2_out, cot_out, gh_out, feed_out, grad_gu_out, product_out,
    x_all, h1, qkv_w, out_w, small_z, small_x, gains, docs, cos_v, sin_v, qkv, attended, part, sib, far, landed,
    x_lane, h2, mid_v, h2_all, cot_all, gu_w, down_w, gate_v, gp_v,
    grad_gu, product, gh_v, feed_v, send_sems, recv_sems, local_sems, stage_sems,
):
    net = Net(zs, send_sems, recv_sems, local_sems)
    net.meet()
    deep, wide = wg.shape[0], gu_w.shape[1] // 2
    seq = docs.shape[1]
    half, side = deep // 2, HEAD_DIM // 2
    gather = GatherGroup(net, x.at[net.t], x_all, own_lanes=x)
    gather.start()
    small_waits = [net.send(small, small_z.at[net.z], net.along_z(s)) for s in range(1, zs)]
    small_waits.append(net.send(small, small_x.at[net.b], net.over_x))
    local = [net.keep(small, small_z.at[net.z]), net.keep(small, small_x.at[net.b])]
    local += [net.keep(cosine, cos_v), net.keep(sine, sin_v)]
    lane = net.keep(x.at[net.t], x_lane)

    def head(z):
        return aligned(net.b * zs + z, HEAD_DIM)

    mine = aligned(net.z, deep)
    my_half = pl.ds(pl.multiple_of(net.a * half, half), half)
    qkv_sends, out_sends, w_local = [], [], []
    for m, w in enumerate((wq, wk, wv)):
        col = pl.ds(m * HEAD_DIM, HEAD_DIM)
        w_local.append(net.keep(w.at[:, head(net.z)], qkv_w.at[mine, col]))
    for s in range(1, zs):
        z = lax.rem(net.z + s, zs)
        rows = pl.ds(pl.multiple_of(net.z * deep + net.a * half, half), half)
        qkv_sends.append(
            [
                net.send(w.at[my_half, head(z)], qkv_w.at[rows, pl.ds(m * HEAD_DIM, HEAD_DIM)], net.along_z(s))
                for m, w in enumerate((wq, wk, wv))
            ]
        )
    out_rows = pl.ds(pl.multiple_of(net.a * side, side), side)
    w_local.append(net.keep(wo.at[head(net.z)], out_w.at[:, mine]))
    for s in range(1, zs):
        z = lax.rem(net.z + s, zs)
        at = pl.ds(pl.multiple_of((net.b * zs + z) * HEAD_DIM + net.a * side, side), side)
        out_sends.append(net.send(wo.at[at], out_w.at[out_rows, mine], net.along_z(s)))

    cotan = GatherAll(net, cot.at[net.t], cot_all)
    mlp_waits, mlp_local = {}, {}

    def block(z):
        return aligned(net.dp * zs + z, wide)

    mlp = (
        (lambda z: wg.at[:, block(z)], gu_w.at[mine, pl.ds(0, wide)]),
        (lambda z: wu.at[:, block(z)], gu_w.at[mine, pl.ds(wide, wide)]),
        (lambda z: wd.at[block(z)], down_w.at[:, mine]),
    )
    for k, (src, dst) in enumerate(mlp):
        mlp_local[k] = net.keep(src(net.z), dst)

    def fetch(k):
        src, dst = mlp[k]
        mlp_waits[k] = [net.send(src(lax.rem(net.z + s, zs)), dst, net.along_z(s)) for s in range(1, zs)]

    def fetched(k):
        for copy in mlp_waits[k]:
            copy.wait_recv()
        mlp_local[k].wait()

    for copy in small_waits:
        copy.wait_recv()
    for copy in local:
        copy.wait()
    for z in range(zs):
        gains[0:1, z * deep : (z + 1) * deep] = small_z[z, 0:1, :]
        gains[1:2, z * deep : (z + 1) * deep] = small_z[z, 1:2, :]
    for b in range(2):
        for k in range(seq // deep):
            docs[b : b + 1, k * deep : (k + 1) * deep] = small_x[b, 2 + k : 3 + k, :]

    def norm_block(ref_at):
        def body(i):
            at = pl.ds(pl.multiple_of(ref_at + i * 16, 16), 16)
            rows = x_all[at, :].astype(F32)
            inverse = lax.rsqrt(jnp.mean(rows * rows, axis=-1, keepdims=True) + EPS)
            h1[at, :] = (rows * inverse * gains[0:1, :]).astype(BF)

        loop(x.shape[1] // 16, body)

    rows = x.shape[1]
    last = 2 * zs - 1

    def offset(b, z, t):
        return ((last + 1) * b + z + t * (last - 2 * z)) * rows

    for copy in gather.local:
        copy.wait()
    gather.local = []
    for t in (0, 1):
        norm_block(offset(net.b, net.z, t))
    for s in range(1, zs):
        norm_block(offset(net.b, gather.spread(s), net.t))
    cotan.start()
    fetch(2)
    qkv_y = []
    for s in range(1, zs):
        norm_block(offset(1 - net.b, gather.far(s - 1), net.t))
        for copy in qkv_sends[s - 1]:
            copy.wait_recv()
        at = qkv_w.at[pl.ds(pl.multiple_of(net.source_z(s) * deep + net.a * half, half), half)]
        qkv_y.append(net.send(at, at, net.over_y))
    norm_block(offset(1 - net.b, gather.far(zs - 1), net.t))
    out_y = []
    for s in range(1, zs):
        out_sends[s - 1].wait_recv()
        at = out_w.at[out_rows, aligned(net.source_z(s), deep)]
        out_y.append(net.send(at, at, net.over_y))
    for b, z, copy in gather.twin:
        copy.wait_recv()
        norm_block(offset(b, z, 1 - net.t))
    for copy in qkv_y:
        copy.wait_recv()
    for copy in w_local:
        copy.wait()
    for s in range(1, zs):
        cotan.spread(s)
    for copy in out_y:
        copy.wait_recv()

    branch = SumGroup(net, part, sib, far, landed)
    tile = 128
    for k in range(2):
        b = net.b if k else 1 - net.b
        base = b * seq

        def project(i):
            at = pl.ds(pl.multiple_of(base + i * 256, 256), 256)
            pos = aligned(i, 256)
            pre = dot(h1[at, :], qkv_w[...])
            c, s = cos_v[pos, :], sin_v[pos, :]
            qkv[at, 0:HEAD_DIM] = turn(pre[:, 0:HEAD_DIM], c, s).astype(BF)
            qkv[at, HEAD_DIM : 2 * HEAD_DIM] = turn(pre[:, HEAD_DIM : 2 * HEAD_DIM], c, s).astype(BF)
            qkv[at, 2 * HEAD_DIM : 3 * HEAD_DIM] = pre[:, 2 * HEAD_DIM : 3 * HEAD_DIM].astype(BF)

        loop(seq // 256, project)
        every = pl.ds(pl.multiple_of(base, seq), seq)
        row = docs[pl.ds(b, 1), :]

        def attend(i):
            at = pl.ds(pl.multiple_of(base + i * tile, tile), tile)
            sigma = sigma_of(qkv[at, 0:HEAD_DIM], qkv[every, HEAD_DIM : 2 * HEAD_DIM])
            weights = jnp.where(seen(row, i * tile, tile), sigma, 0.0).astype(BF)
            found = dot(weights, qkv[every, 2 * HEAD_DIM : 3 * HEAD_DIM], kind=BF)
            attended[at, :] = found
            out = dot(found, out_w[...], kind=BF)
            for j in range(tile // rows):
                blk = i * (tile // rows) + j
                t = lax.div(blk, zs)
                z = (1 - t) * blk + t * (last - blk)
                part[b, t, z] = out[j * rows : (j + 1) * rows, :]

        loop(seq // tile, attend)
        branch.give(k)
    saved = [
        net.keep(h1, hidden_out), net.keep(qkv, qkv_out), net.keep(attended, attended_out),
        net.keep(qkv_w, qkv_w_out), net.keep(out_w, out_w_out), net.keep(gains, gains_out), net.keep(docs, docs_out),
    ]
    branch.take(0)
    branch.take(1)
    branch.along()
    for s in range(zs):
        cotan.relay(s)
    lane.wait()
    branch.end()

    def body(i):
        at = aligned(i, 16)
        total = x_lane[at, :].astype(F32)
        for z in range(zs):
            total += landed[z, at, :].astype(F32)
        mid_v[at, :] = total
        inverse = lax.rsqrt(jnp.mean(total * total, axis=-1, keepdims=True) + EPS)
        h2[at, :] = (total * inverse * gains[1:2, :]).astype(BF)

    loop(rows // 16, body)
    saved.append(net.keep(mid_v, middle))
    hidden = GatherAll(net, h2, h2_all)
    hidden.start()
    hidden.spread(1)
    hidden.spread(2)
    hidden.spread(3)
    fetch(0)
    fetch(1)
    cotan.end()
    saved.append(net.keep(cot_all, cot_out))

    few = 256 // (2 * rows)

    def tiles(body):
        def one(i):
            dp, z = lax.div(i, zs // few), pl.ds(lax.rem(i, zs // few) * few, few)
            body(dp, z, aligned(i, 256))

        loop(4 * zs // few, one)

    def gates(dp, z, at):
        gate_v[at, :] = dot(h2_all[dp, z].reshape(256, -1), gu_w[:, 0:wide])

    def products(dp, z, at):
        gp_v[at, :] = dot(cot_all[dp, z].reshape(256, -1), down_w[...], ((1,), (1,)))

    hidden.relay(0)
    fetched(2)
    tiles(products)
    for s in range(1, zs):
        hidden.relay(s)
    hidden.end()
    saved.append(net.keep(h2_all, h2_out))
    fetched(0)
    tiles(gates)
    fetched(1)

    def leave(slot, at):
        return (
            pltpu.make_async_copy(gh_v.at[slot], gh_out.at[at], stage_sems.at[0, slot]),
            pltpu.make_async_copy(feed_v.at[slot], feed_out.at[at], stage_sems.at[1, slot]),
        )

    def both(pair):
        for slot in range(2):
            i = 2 * pair + slot
            dp, z = lax.div(i, zs // few), pl.ds(lax.rem(i, zs // few) * few, few)
            at = aligned(i, 256)
            upward = dot(h2_all[dp, z].reshape(256, -1), gu_w[:, wide:])
            gate, grad_product = gate_v[at, :], gp_v[at, :]
            sigma = jax.nn.sigmoid(gate)
            silu = gate * sigma
            product[at, :] = (silu * upward).astype(BF)
            grad_gu[at, 0:wide] = (grad_product * upward * sigma * (1.0 + gate * (1.0 - sigma))).astype(BF)
            grad_gu[at, wide:] = (grad_product * silu).astype(BF)

            @pl.when(pair > 0)
            def _():
                for copy in leave(slot, at):
                    copy.wait()

            gh_v[slot] = dot(grad_gu[at, :], gu_w[...], ((1,), (1,)), BF)
            feed_v[slot] = dot(product[at, :], down_w[...], kind=BF)
            for copy in leave(slot, at):
                copy.start()

    loop(2 * zs // few, both)
    saved += [net.keep(grad_gu, grad_gu_out), net.keep(product, product_out)]
    for slot in range(2):
        for copy in leave(slot, aligned(slot, 256)):
            copy.wait()
    for copy in saved:
        copy.wait()
    net.finish()


ORDER = (
    "hstart", "F0", "F1", "MG", "g0s0", "F2", "g0z", "S0", "F3", "S1", "T0", "g1s0", "fstart", "S2",
    "T1", "S3", "g0r0", "T2", "g0s1", "T3", "g0s2", "fF0", "g0r1", "hend", "gstart", "MD", "fF1", "gs1",
    "fF2", "gs2", "g0r2", "g2s0", "gs3", "g2z", "gf0", "g2s1", "fS0", "g1z", "gf1", "g2r0", "g0s3", "gf2",
    "gf3", "fS1", "gend", "fS2", "A0", "g2s2", "fF3", "B0", "A1", "g1s1", "g1s2", "bt0", "g1r0", "B1",
    "g2r1", "W1", "g2r2", "bt1", "g1s3", "g0r3", "bx", "W2", "sw0", "sw1", "fT0", "sw2", "fT1", "fS3",
    "sw3", "g2s3", "g1r1", "Ls0", "bend", "g1r2", "Ls1", "Lr0", "gain2", "Lr1", "fT2", "Ls2", "Ls3", "fT3",
    "g2r3", "Lr2", "g1r3", "Lr3", "gain3", "fend",
)
RELAY_WAYS = ("y", "xy", "x", "xy", "y", "xy", "xy")


def backward_kernel(
    zs, gh_part, feed_part, h2_in, cots_in, grad_gu_in, product_in, middle, cot, x, gains_in, docs_in, cosine, sine,
    hidden_in, qkv_in, attended_in, qkv_w_in, out_w_in,
    layer_out, input_grad, q_out, k_out, v_out, o_out, gate_out, up_out, down_out, gains_out,
    own, sib, one, two, landed, own_f, sib_f, one_f, two_f, landed_f, part, sib_1, far_1, landed_1,
    h1, qkv, attended, qkv_w, out_w, gbr_all, gqkv, gains, docs, cos_v, sin_v, hg, mid_v, cot_v, x_v, gm_v, gbr_v, out_v,
    lo_v, gsum, gall, gsum_z, g_far, g_land, q_give, q_own, q_land, o_part, o_own, o_land,
    grad_gu, product_t, strip, gu_grad, down_grad, send_sems, recv_sems, local_sems, strip_sems,
):
    net = Net(zs, send_sems, recv_sems, local_sems)
    net.meet()
    deep, wide = gate_out.shape[0], gu_grad.shape[1] // 2
    seq = docs.shape[1]
    half, side = deep // 2, HEAD_DIM // 2
    rows = x.shape[1]
    last = 2 * zs - 1
    scale = HEAD_DIM**-0.5
    hidden = SumAll(net, gh_part, own, sib, one, two, landed)
    feed = SumAll(net, feed_part, own_f, sib_f, one_f, two_f, landed_f)
    mlp_local = [net.keep(grad_gu_in, grad_gu)]
    local = [net.keep(middle, mid_v), net.keep(cot.at[net.t], cot_v), net.keep(gains_in, gains)]
    local += [net.keep(x.at[net.t], x_v), net.keep(docs_in, docs), net.keep(cosine, cos_v), net.keep(sine, sin_v)]
    local += [net.keep(qkv_in, qkv), net.keep(attended_in, attended), net.keep(qkv_w_in, qkv_w)]
    local += [net.keep(out_w_in, out_w), net.keep(hidden_in, h1)]

    def block(dp, z):
        return aligned(dp * zs + z, wide)

    ways = iter(RELAY_WAYS)
    grads = [
        SpreadGrads(
            net,
            lambda z: gu_grad.at[aligned(z, deep), pl.ds(0, wide)],
            lambda dp, z: gate_out.at[:, block(dp, z)],
            next(ways),
        ),
        SpreadGrads(
            net,
            lambda z: gu_grad.at[aligned(z, deep), pl.ds(wide, wide)],
            lambda dp, z: up_out.at[:, block(dp, z)],
            next(ways),
        ),
        SpreadGrads(
            net,
            lambda z: down_grad.at[:, aligned(z, deep)],
            lambda dp, z: down_out.at[block(dp, z)],
            next(ways),
        ),
    ]

    def q_place(ref):
        def place(dp, z):
            a, b = lax.div(dp, 2), lax.rem(dp, 2)
            return ref.at[pl.ds(pl.multiple_of(a * half, half), half), aligned(b * zs + z, HEAD_DIM)]

        return place

    def o_place(dp, z):
        a, b = lax.div(dp, 2), lax.rem(dp, 2)
        return o_out.at[pl.ds(pl.multiple_of((b * zs + z) * HEAD_DIM + a * side, side), side)]

    late = [
        SpreadGrads(net, lambda z, m=m: q_own.at[z, :, pl.ds(m * HEAD_DIM, HEAD_DIM)], q_place(ref), next(ways))
        for m, ref in enumerate((q_out, k_out, v_out))
    ]
    late.append(SpreadGrads(net, lambda z: o_own.at[z], o_place, next(ways)))
    branch = SumLine(net, part, sib_1, far_1, landed_1)
    gather = GatherGroup(net, gbr_v, gbr_all)
    tile = 128
    outs, pairs, swaps, plane, z_gain = [], [], [], [], []

    def total_of(ref, at):
        total = ref[0, at, :].astype(F32)
        for z in range(1, zs):
            total += ref[z, at, :].astype(F32)
        return total

    def norm_back(inputs, total, gain, k):
        inverse = lax.rsqrt(jnp.mean(inputs * inputs, axis=-1, keepdims=True) + EPS)
        normed = inputs * inverse
        prod = total * normed
        gsum[k] += prod[0:8, :] + prod[8:16, :]
        scaled = total * gain
        return inverse * (scaled - normed * jnp.mean(scaled * normed, axis=-1, keepdims=True))

    def hidden_end():
        for copy in local:
            copy.wait()
        hidden.end()
        gsum[...] = jnp.zeros_like(gsum)

        def back_two(i):
            at = aligned(i, 16)
            grad = cot_v[at, :].astype(F32) + norm_back(mid_v[at, :], total_of(landed, at), gains[1:2, :], 1)
            gm_v[at, :] = grad
            gbr_v[at, :] = grad.astype(BF)

        loop(rows // 16, back_two)

    def place_of(k):
        b = net.b if k else 1 - net.b
        return b, b * seq, pl.ds(pl.multiple_of(b * seq, seq), seq), docs[pl.ds(b, 1), :]

    def queries_back(k):
        b, base, every, row = place_of(k)

        def heads_grad(i):
            at = pl.ds(pl.multiple_of(base + i * 256, 256), 256)
            hg[aligned(i, 256), :] = dot(gbr_all[at, :], out_w[...], ((1,), (1,)), BF)

        loop(seq // 256, heads_grad)

        def by_query(i):
            at = pl.ds(pl.multiple_of(base + i * tile, tile), tile)
            pos = aligned(i, tile)
            keys = qkv[every, HEAD_DIM : 2 * HEAD_DIM]
            sigma = sigma_of(qkv[at, 0:HEAD_DIM], keys)
            gw = dot(hg[pos, :], qkv[every, 2 * HEAD_DIM : 3 * HEAD_DIM], ((1,), (1,)))
            gs = jnp.where(seen(row, i * tile, tile), gw * sigma * (1.0 - sigma), 0.0).astype(BF)
            gq = dot(gs, keys) * scale
            gqkv[at, 0:HEAD_DIM] = turn(gq, cos_v[pos, :], -sin_v[pos, :]).astype(BF)

        loop(seq // tile, by_query)

    def keys_back(k):
        b, base, every, row = place_of(k)

        def by_key(i):
            at = pl.ds(pl.multiple_of(base + i * tile, tile), tile)
            pos = aligned(i, tile)
            queries = qkv[every, 0:HEAD_DIM]
            sigma = sigma_of(qkv[at, HEAD_DIM : 2 * HEAD_DIM], queries)
            gw = dot(qkv[at, 2 * HEAD_DIM : 3 * HEAD_DIM], hg[...], ((1,), (1,)))
            mask = seen(row, i * tile, tile, flip=True)
            gs = jnp.where(mask, gw * sigma * (1.0 - sigma), 0.0).astype(BF)
            weights = jnp.where(mask, sigma, 0.0).astype(BF)
            gk = dot(gs, queries) * scale
            gqkv[at, HEAD_DIM : 2 * HEAD_DIM] = turn(gk, cos_v[pos, :], -sin_v[pos, :]).astype(BF)
            gqkv[at, 2 * HEAD_DIM : 3 * HEAD_DIM] = dot(weights, hg[...], kind=BF)

        loop(seq // tile, by_key)

        def back_one(i):
            at = pl.ds(pl.multiple_of(base + i * tile, tile), tile)
            out = dot(gqkv[at, :], qkv_w[...], ((1,), (1,)), BF)
            for j in range(tile // rows):
                blk = i * (tile // rows) + j
                t = lax.div(blk, zs)
                z = (1 - t) * blk + t * (last - blk)
                part[b, t, z] = out[j * rows : (j + 1) * rows, :]

        loop(seq // tile, back_one)
        branch.give(k)

    def qkv_grad(z, a):
        at = pl.ds(pl.multiple_of(z * deep + a * half, half), half)
        return dot(h1[:, at], gqkv[...], ((0,), (0,)), BF)

    def side_rows(a):
        return pl.ds(pl.multiple_of(a * side, side), side)

    def weights_give():
        def out_grad(z):
            o_part[z] = dot(attended[...], gbr_all[:, aligned(z, deep)], ((0,), (0,)), BF)

        def theirs(z):
            q_give[z] = qkv_grad(z, 1 - net.a)

        loop(zs, out_grad)
        loop(zs, theirs)
        for s in range(zs):
            z = lax.rem(net.z + s + 1, zs)
            swaps.append(
                (
                    z,
                    net.send(q_give.at[z], q_land.at[z], net.over_y),
                    net.send(o_part.at[z, side_rows(1 - net.a)], o_land.at[z], net.over_y),
                )
            )

    def weights_own():
        def ours(z):
            q_own[z] = qkv_grad(z, net.a)

        loop(zs, ours)

    def weights_sum(s):
        z, q_in, o_in = swaps[s]
        q_in.wait_recv()
        add_rows(q_own.at[z], [q_own.at[z], q_land.at[z]], half)
        o_in.wait_recv()
        add_rows(o_own.at[z], [o_part.at[z, side_rows(net.a)], o_land.at[z]], side)
        for grad in late:
            grad.go(s + 1) if s < zs - 1 else grad.own()

    def branch_end():
        branch.end()

        def back_last(i):
            at = aligned(i, 16)
            total = total_of(landed_1.at[net.b], at) + far_1[at, :].astype(F32)
            grad = gm_v[at, :] + norm_back(x_v[at, :].astype(F32), total, gains[0:1, :], 0)
            out_v[at, :] = grad.astype(BF)

        loop(rows // 16, back_last)
        outs.append(net.keep(out_v, input_grad.at[net.t]))
        pairs.append(net.send(out_v, input_grad.at[net.t], net.sibling))
        plane.append(net.send(gsum, g_far.at[0], net.sibling))

    def gains_plane():
        plane[0].wait_recv()
        gall[...] = gsum[...] + g_far[0]
        for k, way in ((1, net.over_x), (2, net.over_y), (3, net.across)):
            plane.append(net.send(gall, g_far.at[k], way))

    def gains_line():
        for copy in plane[1:]:
            copy.wait_recv()
        gsum_z[...] = gall[...] + g_far[1] + g_far[2] + g_far[3]

        def cut(z):
            return gsum_z.at[:, :, aligned(z, deep)]

        z_gain.extend(net.send(cut(lax.rem(net.z + s, zs)), g_land.at[net.z], net.along_z(s)) for s in range(1, zs))
        outs.append(net.keep(cut(net.z), g_land.at[net.z]))

    def feed_end():
        feed.end()

        def close(i):
            at = aligned(i, 16)
            lo_v[at, :] = (mid_v[at, :] + total_of(landed_f, at)).astype(BF)

        loop(rows // 16, close)
        outs.append(net.keep(lo_v, layer_out.at[net.t]))
        pairs.append(net.send(lo_v, layer_out.at[net.t], net.sibling))

    def each(method):
        def step(s):
            for grad in late:
                getattr(grad, method)(s)

        return step

    thin = strip.shape[2]

    def strips(ref, body, first=None):
        def load(i):
            return pltpu.make_async_copy(ref.at[:, aligned(i, thin)], strip.at[lax.rem(i, 2)], strip_sems.at[lax.rem(i, 2)])

        count = ref.shape[1] // thin
        load(0).start()
        if first:
            first()

        def one(i):
            @pl.when(i + 1 < count)
            def _():
                load(i + 1).start()

            load(i).wait()
            body(i, strip.at[lax.rem(i, 2)])

        loop(count, one)

    def gate_up_grads():
        mlp_local[0].wait()

        def one(i, part):
            gu_grad[aligned(i, thin), :] = dot(part[...], grad_gu[...], ((0,), (0,)), BF)

        strips(h2_in, one)

    def down_grads():
        def turn_product():
            net.keep(product_in, strip.at[1]).wait()
            product_t[...] = strip[1].T

        def one(i, part):
            down_grad[:, aligned(i, thin)] = dot(product_t[...], part[...], kind=BF)

        strips(cots_in, one, turn_product)

    steps = {
        "MG": gate_up_grads, "MD": down_grads, "hstart": hidden.start, "hend": hidden_end, "gstart": gather.start, "gend": gather.end, "fstart": feed.start,
        "fend": feed_end, "W1": weights_give, "W2": weights_own, "bx": branch.across, "bend": branch_end,
        "gain2": gains_plane, "gain3": gains_line,
    }
    counted = {
        "F": hidden.first, "S": hidden.second, "T": hidden.third, "fF": feed.first, "fS": feed.second,
        "fT": feed.third, "gs": gather.spread, "gf": gather.far, "A": queries_back, "B": keys_back, "sw": weights_sum,
        "bt": branch.take, "Ls": each("spread"), "Lr": each("relay"),
    }
    for k, grad in enumerate(grads):
        steps["g%dz" % k] = grad.start
        counted["g%ds" % k], counted["g%dr" % k] = grad.spread, grad.relay
    for name in ORDER:
        if name in steps:
            steps[name]()
        else:
            counted[name[:-1]](int(name[-1]))
    for grad in grads + late:
        grad.end()
    for copy in outs:
        copy.wait()
    for copy in z_gain + pairs:
        copy.wait_recv()
    total = g_land[0]
    for z in range(1, zs):
        total += g_land[z]
    gains_out[...] = jnp.sum(total, axis=1)
    net.finish()


def widen(*arrays):
    steps = 16

    def kernel(*refs):
        for src, dst in zip(refs[: len(arrays)], refs[len(arrays) :], strict=True):
            dst[...] = src[...].astype(F32)

    specs = [pl.BlockSpec((a.shape[0] // steps, a.shape[1]), lambda i: (i, 0)) for a in arrays]
    return pl.pallas_call(
        kernel,
        grid=(steps,),
        in_specs=specs,
        out_specs=specs,
        out_shape=[jax.ShapeDtypeStruct(a.shape, F32) for a in arrays],
        compiler_params=pltpu.CompilerParams(vmem_limit_bytes=60 * MIB),
    )(*arrays)


def rope_tables(seq):
    half_dim = HEAD_DIM // 2
    frequency = ROPE_BASE ** (-np.arange(half_dim, dtype=np.float32) / half_dim)
    angle = np.arange(seq, dtype=np.float32)[:, None] * frequency.astype(np.float32)[None, :]
    cosine, sine = np.cos(angle), np.sin(angle)
    return (
        np.concatenate([cosine, cosine], axis=1).astype(np.float32),
        np.concatenate([-sine, sine], axis=1).astype(np.float32),
    )


def heads_shards(
    zs, activations, document_ids, attn_gain, w_query, w_key, w_value, w_out, mlp_gain, w_gate, w_up, w_down, cotangent
):
    stretch, width = activations.shape[3:]
    deep = w_query.shape[0]
    seq = document_ids.shape[1]
    pair = 2 * seq
    wide = w_gate.shape[1] // (4 * zs)
    x = activations.reshape(2, stretch, width)
    cot = cotangent.reshape(2, stretch, width)
    small = jnp.stack([attn_gain.astype(F32), mlp_gain.astype(F32)])
    docs_rows = document_ids.astype(F32).reshape(seq // deep, deep)
    small = jnp.concatenate([small, docs_rows, jnp.zeros((6 - seq // deep, deep), F32)])
    cosine, sine = (jnp.asarray(table) for table in rope_tables(seq))
    half = stretch // 2
    hidden, qkv, attended, qkv_w, out_w, gains, docs, middle, h2_all, cot_all, gh_part, feed_part, grad_gu, product = call(
        functools.partial(forward_kernel, zs),
        1,
        [
            ((pair, width), BF, ANY),
            ((pair, 3 * HEAD_DIM), BF, ANY),
            ((pair, HEAD_DIM), BF, ANY),
            ((width, 3 * HEAD_DIM), BF, ANY),
            ((HEAD_DIM, width), BF, ANY),
            ((8, width), F32, ANY),
            ((8, seq), F32, ANY),
            ((stretch, width), F32, ANY),
            ((4, zs, 2, stretch, width), BF, ANY),
            ((4, zs, 2, stretch, width), BF, ANY),
            ((4 * seq, width), BF, ANY),
            ((4 * seq, width), BF, ANY),
            ((4 * seq, 2 * wide), BF, ANY),
            ((4 * seq, wide), BF, ANY),
        ],
        [
            VMEM((pair, width), BF),
            VMEM((pair, width), BF),
            VMEM((width, 3 * HEAD_DIM), BF),
            VMEM((HEAD_DIM, width), BF),
            VMEM((zs, 8, deep), F32),
            VMEM((2, 8, deep), F32),
            VMEM((8, width), F32),
            VMEM((8, seq), F32),
            VMEM((seq, HEAD_DIM), F32),
            VMEM((seq, HEAD_DIM), F32),
            VMEM((pair, 3 * HEAD_DIM), BF),
            VMEM((pair, HEAD_DIM), BF),
            VMEM((2, 2, zs, stretch, width), BF),
            VMEM((2, zs, stretch, width), BF),
            VMEM((zs, stretch, width), BF),
            VMEM((zs, stretch, width), BF),
            VMEM((stretch, width), BF),
            VMEM((stretch, width), BF),
            VMEM((stretch, width), F32),
            VMEM((4, zs, 2, stretch, width), BF),
            VMEM((4, zs, 2, stretch, width), BF),
            VMEM((width, 2 * wide), BF),
            VMEM((wide, width), BF),
            VMEM((4 * seq, wide), F32),
            VMEM((4 * seq, wide), F32),
            VMEM((4 * seq, 2 * wide), BF),
            VMEM((4 * seq, wide), BF),
            VMEM((2, 256, width), BF),
            VMEM((2, 256, width), BF),
        ],
        ((134,), (131,), (34,), (2, 2)),
        (x, w_query, w_key, w_value, w_out, small, cosine, sine, w_gate, w_up, w_down, cot),
        60,
    )

    h2 = h2_all.reshape(4 * seq, width)
    cots = cot_all.reshape(4 * seq, width)
    gh_part = gh_part.reshape(4, zs, 2, stretch, width)
    feed_part = feed_part.reshape(4, zs, 2, stretch, width)

    sum_scratch = [
        VMEM((4, zs, stretch, width), BF),
        VMEM((4, zs, stretch, width), BF),
        VMEM((2, 2, zs, half, width), BF),
        VMEM((2, zs, half, width), BF),
        VMEM((zs, stretch, width), BF),
    ]
    layer_out, input_grad, q_g, k_g, v_g, o_g, gate_g, up_g, down_g, gains_g = call(
        functools.partial(backward_kernel, zs),
        2,
        [
            ((2, stretch, width), BF, ANY),
            ((2, stretch, width), BF, ANY),
            (w_query.shape, BF, ANY),
            (w_key.shape, BF, ANY),
            (w_value.shape, BF, ANY),
            (w_out.shape, BF, ANY),
            (w_gate.shape, BF, ANY),
            (w_up.shape, BF, ANY),
            (w_down.shape, BF, ANY),
            ((2, deep), F32, VMEM),
        ],
        sum_scratch
        + sum_scratch
        + [
            VMEM((2, 2, zs, stretch, width), BF),
            VMEM((2, zs, stretch, width), BF),
            VMEM((stretch, width), BF),
            VMEM((2, zs, stretch, width), BF),
            VMEM((pair, width), BF),
            VMEM((pair, 3 * HEAD_DIM), BF),
            VMEM((pair, HEAD_DIM), BF),
            VMEM((width, 3 * HEAD_DIM), BF),
            VMEM((HEAD_DIM, width), BF),
            VMEM((pair, width), BF),
            VMEM((pair, 3 * HEAD_DIM), BF),
            VMEM((8, width), F32),
            VMEM((8, seq), F32),
            VMEM((seq, HEAD_DIM), F32),
            VMEM((seq, HEAD_DIM), F32),
            VMEM((seq, HEAD_DIM), BF),
            VMEM((stretch, width), F32),
            VMEM((stretch, width), BF),
            VMEM((stretch, width), BF),
            VMEM((stretch, width), F32),
            VMEM((stretch, width), BF),
            VMEM((stretch, width), BF),
            VMEM((stretch, width), BF),
            VMEM((2, 8, width), F32),
            VMEM((2, 8, width), F32),
            VMEM((2, 8, width), F32),
            VMEM((4, 2, 8, width), F32),
            VMEM((zs, 2, 8, deep), F32),
            VMEM((zs, deep // 2, 3 * HEAD_DIM), BF),
            VMEM((zs, deep // 2, 3 * HEAD_DIM), BF),
            VMEM((zs, deep // 2, 3 * HEAD_DIM), BF),
            VMEM((zs, HEAD_DIM, deep), BF),
            VMEM((zs, HEAD_DIM // 2, deep), BF),
            VMEM((zs, HEAD_DIM // 2, deep), BF),
            VMEM((4 * seq, 2 * wide), BF),
            VMEM((wide, 4 * seq), BF),
            VMEM((2, 4 * seq, 256), BF),
            VMEM((width, 2 * wide), BF),
            VMEM((wide, width), BF),
        ],
        ((232,), (231,), (36,), (2,)),
        (
            gh_part, feed_part, h2, cots, grad_gu, product, middle, cot, x, gains, docs, cosine, sine,
            hidden, qkv, attended, qkv_w, out_w,
        ),
        60,
    )
    q_g, k_g, v_g, o_g, gate_g, up_g, down_g = widen(q_g, k_g, v_g, o_g, gate_g, up_g, down_g)
    return (
        layer_out.reshape(activations.shape),
        input_grad.reshape(activations.shape),
        gains_g[0],
        q_g,
        k_g,
        v_g,
        o_g,
        gains_g[1],
        gate_g,
        up_g,
        down_g,
    )


def angles(positions):
    half_dim = HEAD_DIM // 2
    frequency = ROPE_BASE ** (-jnp.arange(half_dim, dtype=jnp.float32) / half_dim)
    angle = positions.astype(jnp.float32)[:, None] * frequency[None, :]
    return (jnp.cos(angle)[:, None, :], jnp.sin(angle)[:, None, :])


def rotate(flat, positions):
    row_count = flat.shape[0]
    heads = flat.reshape(row_count, -1, HEAD_DIM)
    cosine, sine = angles(positions)
    first = heads[..., : HEAD_DIM // 2]
    second = heads[..., HEAD_DIM // 2 :]
    turned = jnp.concatenate(
        [first * cosine - second * sine, second * cosine + first * sine], axis=-1
    )
    return turned.reshape(row_count, -1)


def unrotate(flat, positions):
    row_count = flat.shape[0]
    heads = flat.reshape(row_count, -1, HEAD_DIM)
    cosine, sine = angles(positions)
    first = heads[..., : HEAD_DIM // 2]
    second = heads[..., HEAD_DIM // 2 :]
    turned = jnp.concatenate(
        [first * cosine + second * sine, second * cosine - first * sine], axis=-1
    )
    return turned.reshape(row_count, -1)


def normalize(values):
    inverse = lax.rsqrt(jnp.mean(values * values, axis=-1, keepdims=True) + EPS)
    return (values * inverse, inverse)


def norm_back(grad_normed_out, normed, inverse, gain):
    scaled = grad_normed_out * gain
    return inverse * (scaled - normed * jnp.mean(scaled * normed, axis=-1, keepdims=True))


def contract_rows(left, right):
    return lax.dot_general(
        left, right, (((1,), (1,)), ((), ())), preferred_element_type=jnp.float32
    )


def contract_cols(left, right):
    return lax.dot_general(
        left, right, (((0,), (0,)), ((), ())), preferred_element_type=jnp.float32
    )


def visibility(query_positions, query_docs, key_positions, key_docs):
    same_doc = query_docs[:, None] == key_docs[None, :]
    earlier = key_positions[None, :] <= query_positions[:, None]
    return jnp.where(same_doc & earlier, 1.0, 0.0).astype(jnp.float32)


def merge_heads(stacked):
    return jnp.transpose(stacked, (1, 0, 2)).reshape(stacked.shape[1], -1)


def head_slice(matrix, offset):
    return lax.dynamic_slice_in_dim(matrix, offset, HEAD_DIM, 1)


def attend_forward(queries, key_rows, value_rows, visible):
    score_scale = HEAD_DIM ** (-0.5)

    def one_head(head_index):
        offset = head_index * HEAD_DIM
        scores = (
            contract_rows(head_slice(queries, offset), head_slice(key_rows, offset)) * score_scale
        )
        weights = (jax.nn.sigmoid(scores - SHIFT) * visible).astype(jnp.bfloat16)
        return jnp.dot(weights, head_slice(value_rows, offset), preferred_element_type=jnp.float32)

    stacked = lax.map(one_head, jnp.arange(queries.shape[1] // HEAD_DIM))
    return merge_heads(stacked)


def attend_back(queries, key_rows, value_rows, grad_attended, visible):
    score_scale = HEAD_DIM ** (-0.5)

    def one_head(head_index):
        offset = head_index * HEAD_DIM
        head_query = head_slice(queries, offset)
        head_key = head_slice(key_rows, offset)
        head_grad = head_slice(grad_attended, offset)
        scores = contract_rows(head_query, head_key) * score_scale
        sigma = jax.nn.sigmoid(scores - SHIFT)
        grad_weights = contract_rows(head_grad, head_slice(value_rows, offset))
        grad_scores = (grad_weights * visible * sigma * (1.0 - sigma)).astype(jnp.bfloat16)
        pieces = []
        pieces.append(
            jnp.dot(grad_scores, head_key, preferred_element_type=jnp.float32) * score_scale
        )
        weights = (sigma * visible).astype(jnp.bfloat16)
        pieces.append(contract_cols(grad_scores, head_query) * score_scale)
        pieces.append(contract_cols(weights, head_grad))
        return tuple(pieces)

    stacked = lax.map(one_head, jnp.arange(queries.shape[1] // HEAD_DIM))
    return tuple((merge_heads(piece) for piece in stacked))


def rows_shards(
    activations,
    document_ids,
    attn_gain,
    w_query,
    w_key,
    w_value,
    w_out,
    mlp_gain,
    w_gate,
    w_up,
    w_down,
    cotangent,
):
    groups = lax.axis_size("cp")
    rank = lax.axis_index("cp")
    stretch_len = activations.shape[3]
    width = activations.shape[4]
    row_count = 2 * stretch_len
    offsets = jnp.arange(stretch_len, dtype=jnp.int32)
    my_positions = jnp.concatenate(
        [rank * stretch_len + offsets, (2 * groups - 1 - rank) * stretch_len + offsets]
    )
    all_docs = document_ids[0]
    my_docs = jnp.take(all_docs, my_positions)
    slots = jnp.arange(groups * row_count, dtype=jnp.int32)
    owners = slots // row_count
    halves = slots // stretch_len % 2
    key_positions = (
        jnp.where(halves == 0, owners, 2 * groups - 1 - owners) * stretch_len + slots % stretch_len
    )
    key_docs = jnp.take(all_docs, key_positions)
    visible = visibility(my_positions, my_docs, key_positions, key_docs)
    gathered = (
        lax.all_gather(w_query, "cp", axis=0, tiled=True),
        lax.all_gather(w_key, "cp", axis=0, tiled=True),
        lax.all_gather(w_value, "cp", axis=0, tiled=True),
        lax.all_gather(w_out, "cp", axis=1, tiled=True),
        lax.all_gather(w_gate, "cp", axis=0, tiled=True),
        lax.all_gather(w_up, "cp", axis=0, tiled=True),
        lax.all_gather(w_down, "cp", axis=1, tiled=True),
        lax.all_gather(attn_gain, "cp", axis=0, tiled=True),
        lax.all_gather(mlp_gain, "cp", axis=0, tiled=True),
    )
    (
        query_full,
        key_full,
        value_full,
        out_full,
        gate_full,
        up_full,
        down_full,
        gain_one,
        gain_two,
    ) = gathered
    gain_one = gain_one.astype(jnp.float32)
    gain_two = gain_two.astype(jnp.float32)
    inputs = activations.reshape(row_count, width).astype(jnp.float32)
    normed_one, inverse_one = normalize(inputs)
    hidden_one = (normed_one * gain_one).astype(jnp.bfloat16)
    queries = rotate(
        jnp.dot(hidden_one, query_full, preferred_element_type=jnp.float32), my_positions
    ).astype(jnp.bfloat16)
    keys_local = rotate(
        jnp.dot(hidden_one, key_full, preferred_element_type=jnp.float32), my_positions
    ).astype(jnp.bfloat16)
    values_local = jnp.dot(hidden_one, value_full, preferred_element_type=jnp.float32).astype(
        jnp.bfloat16
    )
    keys_all, values_all = (
        lax.all_gather(keys_local, "cp", axis=0, tiled=True),
        lax.all_gather(values_local, "cp", axis=0, tiled=True),
    )
    attended = attend_forward(queries, keys_all, values_all, visible).astype(jnp.bfloat16)
    branch = lax.psum(jnp.dot(attended, out_full, preferred_element_type=jnp.float32), "tp")
    middle = inputs + branch
    normed_two, inverse_two = normalize(middle)
    hidden_two = (normed_two * gain_two).astype(jnp.bfloat16)
    gate = jnp.dot(hidden_two, gate_full, preferred_element_type=jnp.float32)
    upward = jnp.dot(hidden_two, up_full, preferred_element_type=jnp.float32)
    sigma_gate = jax.nn.sigmoid(gate)
    silu_gate = gate * sigma_gate
    product = (silu_gate * upward).astype(jnp.bfloat16)
    feed = lax.psum(jnp.dot(product, down_full, preferred_element_type=jnp.float32), "tp")
    result = middle + feed
    layer_out = result.astype(jnp.bfloat16).reshape(activations.shape)
    grad_result = cotangent.reshape(row_count, width).astype(jnp.float32)
    grad_feed = grad_result.astype(jnp.bfloat16)
    grad_product = contract_rows(grad_feed, down_full)
    grad_gate = (grad_product * upward * sigma_gate * (1.0 + gate * (1.0 - sigma_gate))).astype(
        jnp.bfloat16
    )
    grad_up = (grad_product * silu_gate).astype(jnp.bfloat16)
    grad_hidden_two = lax.psum(
        contract_rows(grad_gate, gate_full) + contract_rows(grad_up, up_full), "tp"
    )
    grad_gain_two = jnp.sum(grad_hidden_two * normed_two, axis=0)
    grad_middle = grad_result + norm_back(grad_hidden_two, normed_two, inverse_two, gain_two)
    grad_down = contract_cols(product, grad_feed)
    grad_gate_w = contract_cols(hidden_two, grad_gate)
    grad_up_w = contract_cols(hidden_two, grad_up)
    share_gate, share_up, share_down, share_gain_two = (
        lax.psum_scatter(grad_gate_w, "cp", scatter_dimension=0, tiled=True),
        lax.psum_scatter(grad_up_w, "cp", scatter_dimension=0, tiled=True),
        lax.psum_scatter(grad_down, "cp", scatter_dimension=1, tiled=True),
        lax.psum_scatter(grad_gain_two, "cp", scatter_dimension=0, tiled=True),
    )
    grad_branch = grad_middle.astype(jnp.bfloat16)
    grad_attended = contract_rows(grad_branch, out_full).astype(jnp.bfloat16)
    grad_queries, key_terms, value_terms = attend_back(
        queries, keys_all, values_all, grad_attended, visible
    )
    grad_keys, grad_values = (
        lax.psum_scatter(key_terms, "cp", scatter_dimension=0, tiled=True),
        lax.psum_scatter(value_terms, "cp", scatter_dimension=0, tiled=True),
    )
    grad_query_pre = unrotate(grad_queries, my_positions).astype(jnp.bfloat16)
    grad_key_pre = unrotate(grad_keys, my_positions).astype(jnp.bfloat16)
    grad_value_pre = grad_values.astype(jnp.bfloat16)
    local_hidden = (
        contract_rows(grad_query_pre, query_full)
        + contract_rows(grad_key_pre, key_full)
        + contract_rows(grad_value_pre, value_full)
    )
    grad_hidden_one = lax.psum(local_hidden, "tp")
    grad_gain_one = jnp.sum(grad_hidden_one * normed_one, axis=0)
    grad_inputs = grad_middle + norm_back(grad_hidden_one, normed_one, inverse_one, gain_one)
    grad_query_w = contract_cols(hidden_one, grad_query_pre)
    grad_key_w = contract_cols(hidden_one, grad_key_pre)
    grad_value_w = contract_cols(hidden_one, grad_value_pre)
    grad_out_w = contract_cols(attended, grad_branch)
    share_query, share_key, share_value, share_out, share_gain_one = (
        lax.psum_scatter(grad_query_w, "cp", scatter_dimension=0, tiled=True),
        lax.psum_scatter(grad_key_w, "cp", scatter_dimension=0, tiled=True),
        lax.psum_scatter(grad_value_w, "cp", scatter_dimension=0, tiled=True),
        lax.psum_scatter(grad_out_w, "cp", scatter_dimension=1, tiled=True),
        lax.psum_scatter(grad_gain_one, "cp", scatter_dimension=0, tiled=True),
    )
    summed = lax.psum(
        (
            share_gain_one,
            share_query,
            share_key,
            share_value,
            share_out,
            share_gain_two,
            share_gate,
            share_up,
            share_down,
        ),
        "dp",
    )
    input_grad = grad_inputs.astype(jnp.bfloat16).reshape(activations.shape)
    return (
        layer_out,
        input_grad,
        summed[0],
        summed[1],
        summed[2],
        summed[3],
        summed[4],
        summed[5],
        summed[6],
        summed[7],
        summed[8],
    )


def layer(sizes, *args):
    heads = args[3].shape[1] // HEAD_DIM
    zs = sizes["cp"]
    fits = sizes["dp"] == 4 and sizes["tp"] == 2 and zs == 4 and heads == 2 * zs
    fits = fits and args[0].shape[3] % 32 == 0 and args[8].shape[1] % (2 * zs * HEAD_DIM) == 0
    fits = fits and args[3].shape[0] % HEAD_DIM == 0 and args[1].shape[1] % args[3].shape[0] == 0
    fits = fits and args[1].shape[1] <= 6 * args[3].shape[0]
    if fits:
        return heads_shards(zs, *args)
    return rows_shards(*args)


def solution(mesh):
    return jax.shard_map(
        functools.partial(layer, dict(mesh.shape)),
        mesh=mesh,
        in_specs=(
            P("dp", "cp", None, None, None),
            P("dp", None),
            P("cp"),
            P("cp", "tp"),
            P("cp", "tp"),
            P("cp", "tp"),
            P("tp", "cp"),
            P("cp"),
            P("cp", "tp"),
            P("cp", "tp"),
            P("tp", "cp"),
            P("dp", "cp", None, None, None),
        ),
        out_specs=(
            P("dp", "cp", None, None, None),
            P("dp", "cp", None, None, None),
            P("cp"),
            P("cp", "tp"),
            P("cp", "tp"),
            P("cp", "tp"),
            P("tp", "cp"),
            P("cp"),
            P("cp", "tp"),
            P("cp", "tp"),
            P("tp", "cp"),
        ),
        check_vma=False,
    )
```

```python
import functools
import math

import jax
import jax.numpy as jnp
import numpy as np
from jax import lax
from jax.experimental import pallas as pl
from jax.experimental.pallas import tpu as pltpu
from jax.sharding import PartitionSpec as P

HEAD_DIM = 128
EPS = 1e-05
SHIFT = math.log(4096.0)
ROPE_BASE = 10000.0
BF = jnp.bfloat16
F32 = jnp.float32
MESH = pl.DeviceIdType.MESH
ANY = pl.ANY
VMEM = pltpu.VMEM
MIB = 2**20


class Net:
    def __init__(self, zs, send_sems, recv_sems, local_sems):
        self.zs = zs
        self.dp, self.z, self.t = (lax.axis_index(a) for a in ("dp", "cp", "tp"))
        self.a, self.b = lax.div(self.dp, 2), lax.rem(self.dp, 2)
        self.send_sems, self.recv_sems, self.local_sems = send_sems, recv_sems, local_sems
        self.arrivals = 0
        self.free_locals = list(range(local_sems.shape[0]))
        self.open = []

    def along_z(self, s):
        return (self.dp, lax.rem(self.z + s, self.zs), self.t)

    def source_z(self, s):
        return lax.rem(self.z + self.zs - s, self.zs)

    @property
    def over_x(self):
        return (2 * self.a + 1 - self.b, self.z, self.t)

    @property
    def over_y(self):
        return (2 * (1 - self.a) + self.b, self.z, self.t)

    @property
    def sibling(self):
        return (self.dp, self.z, 1 - self.t)

    @property
    def across(self):
        return (2 * (1 - self.a) + 1 - self.b, self.z, self.t)

    def meet(self):
        ways = [self.along_z(s) for s in range(1, self.zs)] + [self.over_x, self.over_y, self.across, self.sibling]
        barrier = pltpu.get_barrier_semaphore()
        for way in ways:
            pl.semaphore_signal(barrier, inc=1, device_id=way, device_id_type=MESH)
        pl.semaphore_wait(barrier, len(ways))

    def slot(self):
        self.arrivals += 1
        return self.arrivals - 1

    def send(self, src, dst, way, arrive=None, when=None):
        arrive = self.slot() if arrive is None else arrive
        sem = self.send_sems.at[len(self.open)]
        copy = pltpu.make_async_remote_copy(
            src, dst, sem, self.recv_sems.at[arrive], device_id=way, device_id_type=MESH
        )
        if when is None:
            copy.start()
        else:
            pl.when(when)(copy.start)
        self.open.append((copy, when))
        return copy

    def arrival(self, ref, slot):
        return pltpu.make_async_remote_copy(
            ref, ref, self.send_sems.at[0], self.recv_sems.at[slot], device_id=self.sibling, device_id_type=MESH
        )

    def keep(self, src, dst):
        return Kept(self, src, dst)

    def finish(self):
        for copy, when in self.open:
            if when is None:
                copy.wait_send()
            else:
                pl.when(when)(copy.wait_send)


class Kept:
    def __init__(self, net, src, dst):
        self.net, self.slot = net, net.free_locals.pop(0)
        self.copy = pltpu.make_async_copy(src, dst, net.local_sems.at[self.slot])
        self.copy.start()

    def wait(self):
        self.copy.wait()
        self.net.free_locals.append(self.slot)


class LineGather:
    def __init__(self, net, src, place):
        self.net, self.src, self.place = net, src, place
        self.h, self.low = lax.div(net.z, 2), lax.rem(net.z, 2)
        self.mate = (net.dp, net.z + 1 - 2 * self.low, net.t)
        self.gate = (net.dp, 2 - self.h, net.t)
        self.hands_on = self.h != self.low

    def start(self):
        net = self.net
        mine = self.place(net.z)
        self.near = net.send(self.src, mine, self.mate)
        self.slots = [net.slot(), net.slot()]
        net.send(self.src, mine, self.gate, arrive=self.slots[0] + self.low)

    def take(self, s):
        net = self.net
        if s == 1:
            self.near.wait_recv()
            return net.z + 1 - 2 * self.low
        z = 2 * (1 - self.h) + s - 2
        ref = self.place(z)
        net.arrival(ref, self.slots[s - 2]).wait_recv()
        net.send(ref, ref, self.mate, arrive=self.slots[s - 2], when=self.hands_on)
        return z


def plane_relay(net, place, halves, over_x, over_y, ways="xy", sibling=None):
    dx, dy = 2 * net.a + 1 - net.b, 2 * (1 - net.a) + net.b
    relays = []

    def by_y():
        over_x.wait_recv()
        piece = halves(place(dx), 0) if "x" in ways else place(dx)
        if "y" in ways:
            relays.append(net.send(piece, piece, net.over_y))
        if sibling:
            sibling(dx)

    def by_x():
        over_y.wait_recv()
        piece = halves(place(dy), 1) if "y" in ways else place(dy)
        if "x" in ways:
            relays.append(net.send(piece, piece, net.over_x))
        if sibling:
            sibling(dy)

    for step in (by_x, by_y) if ways == "x" else (by_y, by_x):
        step()
    return relays


def plane_end(net, relays, sibling=None):
    for copy in relays:
        copy.wait_recv()
    if sibling:
        sibling(2 * (1 - net.a) + 1 - net.b)


def rows_loop(count, step, body):
    def one(i, carry):
        body(pl.ds(pl.multiple_of(i * step, step), step))
        return carry

    lax.fori_loop(0, count // step, one, 0)


def add_rows(out, terms, rows):
    def body(at):
        total = terms[0][at, :].astype(F32)
        for term in terms[1:]:
            total += term[at, :].astype(F32)
        out[at, :] = total.astype(out.dtype)

    rows_loop(rows, 16, body)


class GatherAll:
    def __init__(self, net, src, dst):
        self.net, self.src, self.dst = net, src, dst
        rows = src.shape[0] // 2
        self.halves = lambda ref, k: ref.at[pl.ds(k * rows, rows)]

    def place(self, dp, z):
        return self.dst.at[dp, z, self.net.t]

    def start(self):
        net = self.net
        mine = self.place(net.dp, net.z)
        self.line = LineGather(net, self.src, lambda z: self.place(net.dp, z))
        self.line.start()
        self.local = net.keep(self.src, mine)
        self.plane = [(net.z, net.send(self.src, mine, net.over_x), net.send(self.src, mine, net.over_y))]
        self.twin = [net.send(self.src, mine, net.sibling)]
        self.states = []

    def to_twin(self, dp, z):
        ref = self.place(dp, z)
        self.twin.append(self.net.send(ref, ref, self.net.sibling))

    def spread(self, s):
        net = self.net
        z = self.line.take(s)
        ref = self.place(net.dp, z)
        self.plane.append((z, net.send(ref, ref, net.over_x), net.send(ref, ref, net.over_y)))
        self.to_twin(net.dp, z)

    def relay(self, s):
        z, over_x, over_y = self.plane[s]
        place = functools.partial(self.place, z=z)
        self.states.append((z, plane_relay(self.net, place, self.halves, over_x, over_y, sibling=lambda dp: self.to_twin(dp, z))))

    def end(self):
        for z, relays in self.states:
            plane_end(self.net, relays, lambda dp, z=z: self.to_twin(dp, z))
        for copy in self.twin:
            copy.wait_recv()
        self.local.wait()


class GatherGroup:
    def __init__(self, net, src, dst, own_lanes=None):
        self.net, self.src, self.dst, self.own_lanes = net, src, dst, own_lanes
        self.rows = src.shape[0]

    def place(self, b, z, t=None):
        t = self.net.t if t is None else t
        last = 2 * self.net.zs - 1
        at = ((last + 1) * b + z + t * (last - 2 * z)) * self.rows
        return self.dst.at[pl.ds(pl.multiple_of(at, self.rows), self.rows)]

    def start(self):
        net = self.net
        mine = self.place(net.b, net.z)
        self.line = LineGather(net, self.src, lambda z: self.place(net.b, z))
        self.line.start()
        self.over = [(net.z, net.send(self.src, mine, net.over_x))]
        self.twin, self.local = [], []
        if self.own_lanes is None:
            self.local.append(net.keep(self.src, mine))
            self.twin.append((net.b, net.z, net.send(self.src, mine, net.sibling)))
        else:
            for t in (0, 1):
                self.local.append(net.keep(self.own_lanes.at[t], self.place(net.b, net.z, t)))

    def to_twin(self, b, z):
        ref = self.place(b, z)
        self.twin.append((b, z, self.net.send(ref, ref, self.net.sibling)))

    def spread(self, s):
        net = self.net
        z = self.line.take(s)
        ref = self.place(net.b, z)
        self.over.append((z, net.send(ref, ref, net.over_x)))
        self.to_twin(net.b, z)
        return z

    def far(self, s):
        z, copy = self.over[s]
        copy.wait_recv()
        self.to_twin(1 - self.net.b, z)
        return z

    def end(self):
        for _, _, copy in self.twin:
            copy.wait_recv()
        for copy in self.local:
            copy.wait()


class SumGroup:
    def __init__(self, net, part, sib, far, landed):
        self.net, self.part, self.sib, self.far, self.landed = net, part, sib, far, landed
        self.rows = part.shape[3]
        self.twin, self.over, self.z_sends = {}, [], []

    def order(self):
        return [lax.rem(self.net.z + s + 1, self.net.zs) for s in range(self.net.zs)]

    def give(self, k):
        net = self.net
        b = net.b if k else 1 - net.b
        for s, z in enumerate(self.order()):
            self.twin[k, s] = net.send(self.part.at[b, 1 - net.t, z], self.sib.at[b, z], net.sibling)

    def take(self, k):
        net = self.net
        b = net.b if k else 1 - net.b
        for s, z in enumerate(self.order()):
            self.twin[k, s].wait_recv()
            own = self.part.at[b, net.t, z]
            add_rows(own, [own, self.sib.at[b, z]], self.rows)
            if k == 0:
                self.over.append(net.send(own, self.far.at[z], net.over_x))

    def along(self):
        net = self.net
        for s, z in enumerate(self.order()):
            self.over[s].wait_recv()
            last = s == net.zs - 1
            own = self.part.at[net.b, net.t, z]
            out = self.landed.at[net.z] if last else own
            add_rows(out, [own, self.far.at[z]], self.rows)
            if not last:
                self.z_sends.append(net.send(out, self.landed.at[net.z], net.along_z(s + 1)))

    def end(self):
        for copy in self.z_sends:
            copy.wait_recv()


class SumLine(SumGroup):
    def take(self, k):
        net = self.net
        b = net.b if k else 1 - net.b
        for s, z in enumerate(self.order()):
            self.twin[k, s].wait_recv()
            own, last = self.part.at[b, net.t, z], s == net.zs - 1
            out = self.landed.at[b, net.z] if last else own
            add_rows(out, [own, self.sib.at[b, z]], self.rows)
            if not last:
                self.z_sends.append(net.send(own, self.landed.at[b, net.z], net.along_z(s + 1)))

    def across(self):
        net = self.net
        b = 1 - net.b
        for copy in self.z_sends[: net.zs - 1]:
            copy.wait_recv()
        out = self.part.at[b, net.t, net.z]
        add_rows(out, [self.landed.at[b, z] for z in range(net.zs)], self.rows)
        self.over = net.send(out, self.far, net.over_x)

    def end(self):
        for copy in self.z_sends[self.net.zs - 1 :]:
            copy.wait_recv()
        self.over.wait_recv()


class SumAll:
    def __init__(self, net, part, own, sib, one, two, landed):
        self.net, self.part, self.own, self.sib = net, part, own, sib
        self.one, self.two, self.landed = one, two, landed
        self.half = part.shape[3] // 2

    def order(self):
        net = self.net
        return [lax.rem(net.z + s + 1, net.zs) for s in range(net.zs)]

    def places(self):
        a, b = self.net.a, self.net.b
        return [2 * (1 - a) + 1 - b, 2 * a + 1 - b, 2 * (1 - a) + b, 2 * a + b]

    def start(self):
        net = self.net
        self.twin, self.mine = [], []
        for z in self.order():
            self.twin.append(net.send(self.part.at[:, z, 1 - net.t], self.sib.at[:, z], net.sibling))
            self.mine.append(net.keep(self.part.at[:, z, net.t], self.own.at[:, z]))

    def upper(self, ref):
        return ref.at[pl.ds(0, self.half)]

    def lower(self, ref):
        return ref.at[pl.ds(self.half, self.half)]

    def first(self, s):
        net = self.net
        z = self.order()[s]
        dd, dx, dy, me = self.places()
        self.twin[s].wait_recv()
        self.mine[s].wait()
        for dp in (dd, dx, dy, me):
            add_rows(self.own.at[dp, z], [self.own.at[dp, z], self.sib.at[dp, z]], 2 * self.half)
        self.ones = getattr(self, "ones", [])
        self.ones.append(
            (
                net.send(self.upper(self.own.at[dd, z]), self.one.at[0, 0, z], net.over_x),
                net.send(self.upper(self.own.at[dx, z]), self.one.at[0, 1, z], net.over_x),
                net.send(self.lower(self.own.at[dd, z]), self.one.at[1, 0, z], net.over_y),
                net.send(self.lower(self.own.at[dy, z]), self.one.at[1, 1, z], net.over_y),
            )
        )

    def second(self, s):
        net = self.net
        z = self.order()[s]
        dd, dx, dy, me = self.places()
        x_dd, x_me, y_dd, y_me = self.ones[s]
        self.twos = getattr(self, "twos", [])
        x_dd.wait_recv()
        out = self.upper(self.own.at[dy, z])
        add_rows(out, [out, self.one.at[0, 0, z]], self.half)
        up = net.send(out, self.two.at[0, z], net.over_y)
        y_dd.wait_recv()
        out = self.lower(self.own.at[dx, z])
        add_rows(out, [out, self.one.at[1, 0, z]], self.half)
        side = net.send(out, self.two.at[1, z], net.over_x)
        self.twos.append((up, side))

    def third(self, s):
        net = self.net
        z = self.order()[s]
        dd, dx, dy, me = self.places()
        _, x_me, _, y_me = self.ones[s]
        up, side = self.twos[s]
        last = s == net.zs - 1
        out = self.landed.at[net.z] if last else self.own.at[me, z]
        x_me.wait_recv()
        up.wait_recv()
        mine = self.own.at[me, z]
        add_rows(self.upper(out), [self.upper(mine), self.one.at[0, 1, z], self.two.at[0, z]], self.half)
        y_me.wait_recv()
        side.wait_recv()
        add_rows(self.lower(out), [self.lower(mine), self.one.at[1, 1, z], self.two.at[1, z]], self.half)
        self.z_sends = getattr(self, "z_sends", [])
        if not last:
            self.z_sends.append(net.send(out, self.landed.at[net.z], net.along_z(s + 1)))

    def end(self):
        for copy in self.z_sends:
            copy.wait_recv()


class SpreadGrads:
    def __init__(self, net, src, dst, ways):
        self.net, self.src, self.dst, self.ways = net, src, dst, ways
        self.z_sends, self.plane, self.states = {}, {}, []

    def mine(self):
        return self.dst(self.net.dp, self.net.z)

    def start(self):
        self.own()
        for s in range(1, self.net.zs):
            self.go(s)

    def own(self):
        self.local = self.net.keep(self.src(self.net.z), self.mine())

    def go(self, s):
        net = self.net
        self.z_sends[s] = net.send(self.src(lax.rem(net.z + s, net.zs)), self.mine(), net.along_z(s))

    def spread(self, s):
        net = self.net
        z = net.source_z(s)
        ref = self.dst(net.dp, z)
        if s:
            self.z_sends[s].wait_recv()
            src = ref
        else:
            src = self.src(net.z)
        self.plane[s] = (z, net.send(src, ref, net.over_x), net.send(src, ref, net.over_y))

    def relay(self, s):
        z, over_x, over_y = self.plane[s]
        self.states.append(plane_relay(self.net, lambda dp: self.dst(dp, z), half_rows, over_x, over_y, self.ways))

    def end(self):
        for relays in self.states:
            plane_end(self.net, relays)
        self.local.wait()


def half_rows(ref, k):
    n = ref.shape[0] // 2
    return ref.at[pl.ds(k * n, n)]


def aligned(i, size):
    return pl.ds(pl.multiple_of(i * size, size), size)


def loop(count, body):
    def one(i, carry):
        body(i)
        return carry

    lax.fori_loop(0, count, one, 0)


def dot(left, right, dims=((1,), (0,)), kind=F32):
    return lax.dot_general(left, right, (dims, ((), ())), preferred_element_type=F32).astype(kind)


def turn(u, cosine, sine):
    return u * cosine + pltpu.roll(u, HEAD_DIM // 2, 1) * sine


def column(row, start, count):
    n = row.shape[1]
    here = lax.broadcasted_iota(jnp.int32, (count, n), 1) == start + lax.broadcasted_iota(jnp.int32, (count, n), 0)
    return jnp.sum(jnp.where(here, row, 0.0), axis=1, keepdims=True)


def seen(row, start, count, flip=False):
    n = row.shape[1]
    same = column(row, start, count) == row
    mine = start + lax.broadcasted_iota(jnp.int32, (count, n), 0)
    other = lax.broadcasted_iota(jnp.int32, (count, n), 1)
    return same & ((mine <= other) if flip else (other <= mine))


def sigma_of(left, right):
    return jax.nn.sigmoid(dot(left, right, ((1,), (1,))) * HEAD_DIM**-0.5 - SHIFT)


def call(kernel, name, outs, scratch, counts, args, vmem):
    return pl.pallas_call(
        kernel,
        out_shape=[jax.ShapeDtypeStruct(shape, kind) for shape, kind, _ in outs],
        in_specs=[pl.BlockSpec(memory_space=ANY)] * len(args),
        out_specs=[pl.BlockSpec(memory_space=space) for _, _, space in outs],
        scratch_shapes=list(scratch) + [pltpu.SemaphoreType.DMA(shape) for shape in counts],
        compiler_params=pltpu.CompilerParams(
            collective_id=name, has_side_effects=True, vmem_limit_bytes=vmem * MIB
        ),
    )(*args)


def forward_kernel(
    zs, x, wq, wk, wv, wo, small, cosine, sine, wg, wu, wd, cot,
    hidden_out, qkv_out, attended_out, qkv_w_out, out_w_out, gains_out, docs_out, middle, h2_out, cot_out, gh_out, feed_out, grad_gu_out, product_out,
    x_all, h1, qkv_w, out_w, small_z, small_x, gains, docs, cos_v, sin_v, qkv, attended, part, sib, far, landed,
    x_lane, h2, mid_v, h2_all, cot_all, gu_w, down_w, gate_v, gp_v,
    grad_gu, product, gh_v, feed_v, send_sems, recv_sems, local_sems, stage_sems,
):
    net = Net(zs, send_sems, recv_sems, local_sems)
    net.meet()
    deep, wide = wg.shape[0], gu_w.shape[1] // 2
    seq = docs.shape[1]
    half, side = deep // 2, HEAD_DIM // 2
    gather = GatherGroup(net, x.at[net.t], x_all, own_lanes=x)
    gather.start()
    small_waits = [net.send(small, small_z.at[net.z], net.along_z(s)) for s in range(1, zs)]
    small_waits.append(net.send(small, small_x.at[net.b], net.over_x))
    local = [net.keep(small, small_z.at[net.z]), net.keep(small, small_x.at[net.b])]
    local += [net.keep(cosine, cos_v), net.keep(sine, sin_v)]
    lane = net.keep(x.at[net.t], x_lane)

    def head(z):
        return aligned(net.b * zs + z, HEAD_DIM)

    mine = aligned(net.z, deep)
    my_half = pl.ds(pl.multiple_of(net.a * half, half), half)
    qkv_sends, out_sends, w_local = [], [], []
    for m, w in enumerate((wq, wk, wv)):
        col = pl.ds(m * HEAD_DIM, HEAD_DIM)
        w_local.append(net.keep(w.at[:, head(net.z)], qkv_w.at[mine, col]))
    for s in range(1, zs):
        z = lax.rem(net.z + s, zs)
        rows = pl.ds(pl.multiple_of(net.z * deep + net.a * half, half), half)
        qkv_sends.append(
            [
                net.send(w.at[my_half, head(z)], qkv_w.at[rows, pl.ds(m * HEAD_DIM, HEAD_DIM)], net.along_z(s))
                for m, w in enumerate((wq, wk, wv))
            ]
        )
    out_rows = pl.ds(pl.multiple_of(net.a * side, side), side)
    w_local.append(net.keep(wo.at[head(net.z)], out_w.at[:, mine]))
    for s in range(1, zs):
        z = lax.rem(net.z + s, zs)
        at = pl.ds(pl.multiple_of((net.b * zs + z) * HEAD_DIM + net.a * side, side), side)
        out_sends.append(net.send(wo.at[at], out_w.at[out_rows, mine], net.along_z(s)))

    cotan = GatherAll(net, cot.at[net.t], cot_all)
    mlp_waits, mlp_local = {}, {}

    def block(z):
        return aligned(net.dp * zs + z, wide)

    mlp = (
        (lambda z: wg.at[:, block(z)], gu_w.at[mine, pl.ds(0, wide)]),
        (lambda z: wu.at[:, block(z)], gu_w.at[mine, pl.ds(wide, wide)]),
        (lambda z: wd.at[block(z)], down_w.at[:, mine]),
    )
    for k, (src, dst) in enumerate(mlp):
        mlp_local[k] = net.keep(src(net.z), dst)

    def fetch(k):
        src, dst = mlp[k]
        mlp_waits[k] = [net.send(src(lax.rem(net.z + s, zs)), dst, net.along_z(s)) for s in range(zs - 1, 0, -1)]

    def fetched(k):
        for copy in mlp_waits[k]:
            copy.wait_recv()
        mlp_local[k].wait()

    for copy in small_waits:
        copy.wait_recv()
    for copy in local:
        copy.wait()
    for z in range(zs):
        gains[0:1, z * deep : (z + 1) * deep] = small_z[z, 0:1, :]
        gains[1:2, z * deep : (z + 1) * deep] = small_z[z, 1:2, :]
    for b in range(2):
        for k in range(seq // deep):
            docs[b : b + 1, k * deep : (k + 1) * deep] = small_x[b, 2 + k : 3 + k, :]

    def norm_block(ref_at):
        def body(i):
            at = pl.ds(pl.multiple_of(ref_at + i * 16, 16), 16)
            rows = x_all[at, :].astype(F32)
            inverse = lax.rsqrt(jnp.mean(rows * rows, axis=-1, keepdims=True) + EPS)
            h1[at, :] = (rows * inverse * gains[0:1, :]).astype(BF)

        loop(x.shape[1] // 16, body)

    rows = x.shape[1]
    last = 2 * zs - 1

    def offset(b, z, t):
        return ((last + 1) * b + z + t * (last - 2 * z)) * rows

    for copy in gather.local:
        copy.wait()
    gather.local = []
    for t in (0, 1):
        norm_block(offset(net.b, net.z, t))
    for s in range(1, zs):
        norm_block(offset(net.b, gather.spread(s), net.t))
    cotan.start()
    fetch(2)
    qkv_y = []
    for s in range(1, zs):
        norm_block(offset(1 - net.b, gather.far(s - 1), net.t))
        for copy in qkv_sends[s - 1]:
            copy.wait_recv()
        at = qkv_w.at[pl.ds(pl.multiple_of(net.source_z(s) * deep + net.a * half, half), half)]
        qkv_y.append(net.send(at, at, net.over_y))
    norm_block(offset(1 - net.b, gather.far(zs - 1), net.t))
    out_y = []
    for s in range(1, zs):
        out_sends[s - 1].wait_recv()
        at = out_w.at[out_rows, aligned(net.source_z(s), deep)]
        out_y.append(net.send(at, at, net.over_y))
    for b, z, copy in gather.twin:
        copy.wait_recv()
        norm_block(offset(b, z, 1 - net.t))
    for copy in qkv_y:
        copy.wait_recv()
    for copy in w_local:
        copy.wait()
    for s in range(1, zs):
        cotan.spread(s)
    for copy in out_y:
        copy.wait_recv()

    branch = SumGroup(net, part, sib, far, landed)
    tile = 128
    for k in range(2):
        b = net.b if k else 1 - net.b
        base = b * seq

        def project(i):
            at = pl.ds(pl.multiple_of(base + i * 256, 256), 256)
            pos = aligned(i, 256)
            pre = dot(h1[at, :], qkv_w[...])
            c, s = cos_v[pos, :], sin_v[pos, :]
            qkv[at, 0:HEAD_DIM] = turn(pre[:, 0:HEAD_DIM], c, s).astype(BF)
            qkv[at, HEAD_DIM : 2 * HEAD_DIM] = turn(pre[:, HEAD_DIM : 2 * HEAD_DIM], c, s).astype(BF)
            qkv[at, 2 * HEAD_DIM : 3 * HEAD_DIM] = pre[:, 2 * HEAD_DIM : 3 * HEAD_DIM].astype(BF)

        loop(seq // 256, project)
        every = pl.ds(pl.multiple_of(base, seq), seq)
        row = docs[pl.ds(b, 1), :]

        def attend(i):
            at = pl.ds(pl.multiple_of(base + i * tile, tile), tile)
            sigma = sigma_of(qkv[at, 0:HEAD_DIM], qkv[every, HEAD_DIM : 2 * HEAD_DIM])
            weights = jnp.where(seen(row, i * tile, tile), sigma, 0.0).astype(BF)
            found = dot(weights, qkv[every, 2 * HEAD_DIM : 3 * HEAD_DIM], kind=BF)
            attended[at, :] = found
            out = dot(found, out_w[...], kind=BF)
            for j in range(tile // rows):
                blk = i * (tile // rows) + j
                t = lax.div(blk, zs)
                z = (1 - t) * blk + t * (last - blk)
                part[b, t, z] = out[j * rows : (j + 1) * rows, :]

        loop(seq // tile, attend)
        branch.give(k)
    saved = [
        net.keep(h1, hidden_out), net.keep(qkv, qkv_out), net.keep(attended, attended_out),
        net.keep(qkv_w, qkv_w_out), net.keep(out_w, out_w_out), net.keep(gains, gains_out), net.keep(docs, docs_out),
    ]
    branch.take(0)
    branch.take(1)
    branch.along()
    for s in range(zs):
        cotan.relay(s)
    lane.wait()
    branch.end()

    def body(i):
        at = aligned(i, 16)
        total = x_lane[at, :].astype(F32)
        for z in range(zs):
            total += landed[z, at, :].astype(F32)
        mid_v[at, :] = total
        inverse = lax.rsqrt(jnp.mean(total * total, axis=-1, keepdims=True) + EPS)
        h2[at, :] = (total * inverse * gains[1:2, :]).astype(BF)

    loop(rows // 16, body)
    saved.append(net.keep(mid_v, middle))
    hidden = GatherAll(net, h2, h2_all)
    hidden.start()
    hidden.spread(1)
    hidden.spread(2)
    hidden.spread(3)
    fetch(0)
    fetch(1)
    cotan.end()
    saved.append(net.keep(cot_all, cot_out))

    few = 256 // (2 * rows)

    def tiles(body):
        def one(i):
            dp, z = lax.div(i, zs // few), pl.ds(lax.rem(i, zs // few) * few, few)
            body(dp, z, aligned(i, 256))

        loop(4 * zs // few, one)

    def gates(dp, z, at):
        gate_v[at, :] = dot(h2_all[dp, z].reshape(256, -1), gu_w[:, 0:wide])

    def products(dp, z, at):
        gp_v[at, :] = dot(cot_all[dp, z].reshape(256, -1), down_w[...], ((1,), (1,)))

    hidden.relay(0)
    fetched(2)
    tiles(products)
    for s in range(1, zs):
        hidden.relay(s)
    hidden.end()
    saved.append(net.keep(h2_all, h2_out))
    fetched(0)
    tiles(gates)
    fetched(1)

    def leave(slot, at):
        return (
            pltpu.make_async_copy(gh_v.at[slot], gh_out.at[at], stage_sems.at[0, slot]),
            pltpu.make_async_copy(feed_v.at[slot], feed_out.at[at], stage_sems.at[1, slot]),
        )

    def both(pair):
        for slot in range(2):
            i = 2 * pair + slot
            dp, z = lax.div(i, zs // few), pl.ds(lax.rem(i, zs // few) * few, few)
            at = aligned(i, 256)
            upward = dot(h2_all[dp, z].reshape(256, -1), gu_w[:, wide:])
            gate, grad_product = gate_v[at, :], gp_v[at, :]
            sigma = jax.nn.sigmoid(gate)
            silu = gate * sigma
            product[at, :] = (silu * upward).astype(BF)
            grad_gu[at, 0:wide] = (grad_product * upward * sigma * (1.0 + gate * (1.0 - sigma))).astype(BF)
            grad_gu[at, wide:] = (grad_product * silu).astype(BF)

            @pl.when(pair > 0)
            def _():
                for copy in leave(slot, at):
                    copy.wait()

            gh_v[slot] = dot(grad_gu[at, :], gu_w[...], ((1,), (1,)), BF)
            feed_v[slot] = dot(product[at, :], down_w[...], kind=BF)
            for copy in leave(slot, at):
                copy.start()

    loop(2 * zs // few, both)
    saved += [net.keep(grad_gu, grad_gu_out), net.keep(product, product_out)]
    for slot in range(2):
        for copy in leave(slot, aligned(slot, 256)):
            copy.wait()
    for copy in saved:
        copy.wait()
    net.finish()


ORDER = (
    "hstart", "F0", "F1", "MG", "g0s0", "F2", "g0z", "S0", "F3", "S1", "T0", "g1s0", "fstart", "S2",
    "T1", "S3", "g0r0", "T2", "g0s1", "T3", "g0s2", "fF0", "g0r1", "hend", "gstart", "MD", "fF1", "gs1",
    "fF2", "gs2", "g0r2", "g2s0", "gs3", "g2z", "gf0", "g2s1", "fS0", "g1z", "gf1", "g2r0", "g0s3", "gf2",
    "gf3", "fS1", "gend", "fS2", "A0", "g2s2", "fF3", "B0", "A1", "g1s1", "g1s2", "bt0", "g1r0", "B1",
    "g2r1", "W1", "g2r2", "bt1", "g1s3", "g0r3", "bx", "W2", "sw0", "sw1", "fT0", "sw2", "fT1", "fS3",
    "sw3", "g2s3", "g1r1", "Ls0", "bend", "g1r2", "Ls1", "Lr0", "gain2", "Lr1", "fT2", "Ls2", "Ls3", "fT3",
    "g2r3", "Lr2", "g1r3", "Lr3", "gain3", "fend",
)
RELAY_WAYS = ("y", "xy", "x", "xy", "y", "xy", "xy")


def backward_kernel(
    zs, gh_part, feed_part, h2_in, cots_in, grad_gu_in, product_in, middle, cot, x, gains_in, docs_in, cosine, sine,
    hidden_in, qkv_in, attended_in, qkv_w_in, out_w_in,
    layer_out, input_grad, q_out, k_out, v_out, o_out, gate_out, up_out, down_out, gains_out,
    own, sib, one, two, landed, own_f, sib_f, one_f, two_f, landed_f, part, sib_1, far_1, landed_1,
    h1, qkv, attended, qkv_w, out_w, gbr_all, gqkv, gains, docs, cos_v, sin_v, hg, mid_v, cot_v, x_v, gm_v, gbr_v, out_v,
    lo_v, gsum, gall, gsum_z, g_far, g_land, q_give, q_own, q_land, o_part, o_own, o_land,
    grad_gu, product_t, strip, gu_grad, down_grad, send_sems, recv_sems, local_sems, strip_sems,
):
    net = Net(zs, send_sems, recv_sems, local_sems)
    net.meet()
    deep, wide = gate_out.shape[0], gu_grad.shape[1] // 2
    seq = docs.shape[1]
    half, side = deep // 2, HEAD_DIM // 2
    rows = x.shape[1]
    last = 2 * zs - 1
    scale = HEAD_DIM**-0.5
    hidden = SumAll(net, gh_part, own, sib, one, two, landed)
    feed = SumAll(net, feed_part, own_f, sib_f, one_f, two_f, landed_f)
    mlp_local = [net.keep(grad_gu_in, grad_gu)]
    local = [net.keep(middle, mid_v), net.keep(cot.at[net.t], cot_v), net.keep(gains_in, gains)]
    local += [net.keep(x.at[net.t], x_v), net.keep(docs_in, docs), net.keep(cosine, cos_v), net.keep(sine, sin_v)]
    local += [net.keep(qkv_in, qkv), net.keep(attended_in, attended), net.keep(qkv_w_in, qkv_w)]
    local += [net.keep(out_w_in, out_w), net.keep(hidden_in, h1)]

    def block(dp, z):
        return aligned(dp * zs + z, wide)

    ways = iter(RELAY_WAYS)
    grads = [
        SpreadGrads(
            net,
            lambda z: gu_grad.at[aligned(z, deep), pl.ds(0, wide)],
            lambda dp, z: gate_out.at[:, block(dp, z)],
            next(ways),
        ),
        SpreadGrads(
            net,
            lambda z: gu_grad.at[aligned(z, deep), pl.ds(wide, wide)],
            lambda dp, z: up_out.at[:, block(dp, z)],
            next(ways),
        ),
        SpreadGrads(
            net,
            lambda z: down_grad.at[:, aligned(z, deep)],
            lambda dp, z: down_out.at[block(dp, z)],
            next(ways),
        ),
    ]

    def q_place(ref):
        def place(dp, z):
            a, b = lax.div(dp, 2), lax.rem(dp, 2)
            return ref.at[pl.ds(pl.multiple_of(a * half, half), half), aligned(b * zs + z, HEAD_DIM)]

        return place

    def o_place(dp, z):
        a, b = lax.div(dp, 2), lax.rem(dp, 2)
        return o_out.at[pl.ds(pl.multiple_of((b * zs + z) * HEAD_DIM + a * side, side), side)]

    late = [
        SpreadGrads(net, lambda z, m=m: q_own.at[z, :, pl.ds(m * HEAD_DIM, HEAD_DIM)], q_place(ref), next(ways))
        for m, ref in enumerate((q_out, k_out, v_out))
    ]
    late.append(SpreadGrads(net, lambda z: o_own.at[z], o_place, next(ways)))
    branch = SumLine(net, part, sib_1, far_1, landed_1)
    gather = GatherGroup(net, gbr_v, gbr_all)
    tile = 128
    outs, pairs, swaps, plane, z_gain = [], [], [], [], []

    def total_of(ref, at):
        total = ref[0, at, :].astype(F32)
        for z in range(1, zs):
            total += ref[z, at, :].astype(F32)
        return total

    def norm_back(inputs, total, gain, k):
        inverse = lax.rsqrt(jnp.mean(inputs * inputs, axis=-1, keepdims=True) + EPS)
        normed = inputs * inverse
        prod = total * normed
        gsum[k] += prod[0:8, :] + prod[8:16, :]
        scaled = total * gain
        return inverse * (scaled - normed * jnp.mean(scaled * normed, axis=-1, keepdims=True))

    def hidden_end():
        for copy in local:
            copy.wait()
        hidden.end()
        gsum[...] = jnp.zeros_like(gsum)

        def back_two(i):
            at = aligned(i, 16)
            grad = cot_v[at, :].astype(F32) + norm_back(mid_v[at, :], total_of(landed, at), gains[1:2, :], 1)
            gm_v[at, :] = grad
            gbr_v[at, :] = grad.astype(BF)

        loop(rows // 16, back_two)

    def place_of(k):
        b = net.b if k else 1 - net.b
        return b, b * seq, pl.ds(pl.multiple_of(b * seq, seq), seq), docs[pl.ds(b, 1), :]

    def queries_back(k):
        b, base, every, row = place_of(k)

        def heads_grad(i):
            at = pl.ds(pl.multiple_of(base + i * 256, 256), 256)
            hg[aligned(i, 256), :] = dot(gbr_all[at, :], out_w[...], ((1,), (1,)), BF)

        loop(seq // 256, heads_grad)

        def by_query(i):
            at = pl.ds(pl.multiple_of(base + i * tile, tile), tile)
            pos = aligned(i, tile)
            keys = qkv[every, HEAD_DIM : 2 * HEAD_DIM]
            sigma = sigma_of(qkv[at, 0:HEAD_DIM], keys)
            gw = dot(hg[pos, :], qkv[every, 2 * HEAD_DIM : 3 * HEAD_DIM], ((1,), (1,)))
            gs = jnp.where(seen(row, i * tile, tile), gw * sigma * (1.0 - sigma), 0.0).astype(BF)
            gq = dot(gs, keys) * scale
            gqkv[at, 0:HEAD_DIM] = turn(gq, cos_v[pos, :], -sin_v[pos, :]).astype(BF)

        loop(seq // tile, by_query)

    def keys_back(k):
        b, base, every, row = place_of(k)

        def by_key(i):
            at = pl.ds(pl.multiple_of(base + i * tile, tile), tile)
            pos = aligned(i, tile)
            queries = qkv[every, 0:HEAD_DIM]
            sigma = sigma_of(qkv[at, HEAD_DIM : 2 * HEAD_DIM], queries)
            gw = dot(qkv[at, 2 * HEAD_DIM : 3 * HEAD_DIM], hg[...], ((1,), (1,)))
            mask = seen(row, i * tile, tile, flip=True)
            gs = jnp.where(mask, gw * sigma * (1.0 - sigma), 0.0).astype(BF)
            weights = jnp.where(mask, sigma, 0.0).astype(BF)
            gk = dot(gs, queries) * scale
            gqkv[at, HEAD_DIM : 2 * HEAD_DIM] = turn(gk, cos_v[pos, :], -sin_v[pos, :]).astype(BF)
            gqkv[at, 2 * HEAD_DIM : 3 * HEAD_DIM] = dot(weights, hg[...], kind=BF)

        loop(seq // tile, by_key)

        def back_one(i):
            at = pl.ds(pl.multiple_of(base + i * tile, tile), tile)
            out = dot(gqkv[at, :], qkv_w[...], ((1,), (1,)), BF)
            for j in range(tile // rows):
                blk = i * (tile // rows) + j
                t = lax.div(blk, zs)
                z = (1 - t) * blk + t * (last - blk)
                part[b, t, z] = out[j * rows : (j + 1) * rows, :]

        loop(seq // tile, back_one)
        branch.give(k)

    def qkv_grad(z, a):
        at = pl.ds(pl.multiple_of(z * deep + a * half, half), half)
        return dot(h1[:, at], gqkv[...], ((0,), (0,)), BF)

    def side_rows(a):
        return pl.ds(pl.multiple_of(a * side, side), side)

    def weights_give():
        def out_grad(z):
            o_part[z] = dot(attended[...], gbr_all[:, aligned(z, deep)], ((0,), (0,)), BF)

        def theirs(z):
            q_give[z] = qkv_grad(z, 1 - net.a)

        loop(zs, out_grad)
        loop(zs, theirs)
        for s in range(zs):
            z = lax.rem(net.z + s + 1, zs)
            swaps.append(
                (
                    z,
                    net.send(q_give.at[z], q_land.at[z], net.over_y),
                    net.send(o_part.at[z, side_rows(1 - net.a)], o_land.at[z], net.over_y),
                )
            )

    def weights_own():
        def ours(z):
            q_own[z] = qkv_grad(z, net.a)

        loop(zs, ours)

    def weights_sum(s):
        z, q_in, o_in = swaps[s]
        q_in.wait_recv()
        add_rows(q_own.at[z], [q_own.at[z], q_land.at[z]], half)
        o_in.wait_recv()
        add_rows(o_own.at[z], [o_part.at[z, side_rows(net.a)], o_land.at[z]], side)
        for grad in late:
            grad.go(s + 1) if s < zs - 1 else grad.own()

    def branch_end():
        branch.end()

        def back_last(i):
            at = aligned(i, 16)
            total = total_of(landed_1.at[net.b], at) + far_1[at, :].astype(F32)
            grad = gm_v[at, :] + norm_back(x_v[at, :].astype(F32), total, gains[0:1, :], 0)
            out_v[at, :] = grad.astype(BF)

        loop(rows // 16, back_last)
        outs.append(net.keep(out_v, input_grad.at[net.t]))
        pairs.append(net.send(out_v, input_grad.at[net.t], net.sibling))
        plane.append(net.send(gsum, g_far.at[0], net.sibling))

    def gains_plane():
        plane[0].wait_recv()
        gall[...] = gsum[...] + g_far[0]
        for k, way in ((1, net.over_x), (2, net.over_y), (3, net.across)):
            plane.append(net.send(gall, g_far.at[k], way))

    def gains_line():
        for copy in plane[1:]:
            copy.wait_recv()
        gsum_z[...] = gall[...] + g_far[1] + g_far[2] + g_far[3]

        def cut(z):
            return gsum_z.at[:, :, aligned(z, deep)]

        z_gain.extend(net.send(cut(lax.rem(net.z + s, zs)), g_land.at[net.z], net.along_z(s)) for s in range(1, zs))
        outs.append(net.keep(cut(net.z), g_land.at[net.z]))

    def feed_end():
        feed.end()

        def close(i):
            at = aligned(i, 16)
            lo_v[at, :] = (mid_v[at, :] + total_of(landed_f, at)).astype(BF)

        loop(rows // 16, close)
        outs.append(net.keep(lo_v, layer_out.at[net.t]))
        pairs.append(net.send(lo_v, layer_out.at[net.t], net.sibling))

    def each(method):
        def step(s):
            for grad in late:
                getattr(grad, method)(s)

        return step

    thin = strip.shape[2]

    def strips(ref, body, first=None):
        def load(i):
            return pltpu.make_async_copy(ref.at[:, aligned(i, thin)], strip.at[lax.rem(i, 2)], strip_sems.at[lax.rem(i, 2)])

        count = ref.shape[1] // thin
        load(0).start()
        if first:
            first()

        def one(i):
            @pl.when(i + 1 < count)
            def _():
                load(i + 1).start()

            load(i).wait()
            body(i, strip.at[lax.rem(i, 2)])

        loop(count, one)

    def gate_up_grads():
        mlp_local[0].wait()

        def one(i, part):
            gu_grad[aligned(i, thin), :] = dot(part[...], grad_gu[...], ((0,), (0,)), BF)

        strips(h2_in, one)

    def down_grads():
        def turn_product():
            net.keep(product_in, strip.at[1]).wait()
            product_t[...] = strip[1].T

        def one(i, part):
            down_grad[:, aligned(i, thin)] = dot(product_t[...], part[...], kind=BF)

        strips(cots_in, one, turn_product)

    steps = {
        "MG": gate_up_grads, "MD": down_grads, "hstart": hidden.start, "hend": hidden_end, "gstart": gather.start, "gend": gather.end, "fstart": feed.start,
        "fend": feed_end, "W1": weights_give, "W2": weights_own, "bx": branch.across, "bend": branch_end,
        "gain2": gains_plane, "gain3": gains_line,
    }
    counted = {
        "F": hidden.first, "S": hidden.second, "T": hidden.third, "fF": feed.first, "fS": feed.second,
        "fT": feed.third, "gs": gather.spread, "gf": gather.far, "A": queries_back, "B": keys_back, "sw": weights_sum,
        "bt": branch.take, "Ls": each("spread"), "Lr": each("relay"),
    }
    for k, grad in enumerate(grads):
        steps["g%dz" % k] = grad.start
        counted["g%ds" % k], counted["g%dr" % k] = grad.spread, grad.relay
    for name in ORDER:
        if name in steps:
            steps[name]()
        else:
            counted[name[:-1]](int(name[-1]))
    for grad in grads + late:
        grad.end()
    for copy in outs:
        copy.wait()
    for copy in z_gain + pairs:
        copy.wait_recv()
    total = g_land[0]
    for z in range(1, zs):
        total += g_land[z]
    gains_out[...] = jnp.sum(total, axis=1)
    net.finish()


def widen(*arrays):
    steps = 16

    def kernel(*refs):
        for src, dst in zip(refs[: len(arrays)], refs[len(arrays) :], strict=True):
            dst[...] = src[...].astype(F32)

    specs = [pl.BlockSpec((a.shape[0] // steps, a.shape[1]), lambda i: (i, 0)) for a in arrays]
    return pl.pallas_call(
        kernel,
        grid=(steps,),
        in_specs=specs,
        out_specs=specs,
        out_shape=[jax.ShapeDtypeStruct(a.shape, F32) for a in arrays],
        compiler_params=pltpu.CompilerParams(vmem_limit_bytes=60 * MIB),
    )(*arrays)


def rope_tables(seq):
    half_dim = HEAD_DIM // 2
    frequency = ROPE_BASE ** (-np.arange(half_dim, dtype=np.float32) / half_dim)
    angle = np.arange(seq, dtype=np.float32)[:, None] * frequency.astype(np.float32)[None, :]
    cosine, sine = np.cos(angle), np.sin(angle)
    return (
        np.concatenate([cosine, cosine], axis=1).astype(np.float32),
        np.concatenate([-sine, sine], axis=1).astype(np.float32),
    )


def heads_shards(
    zs, activations, document_ids, attn_gain, w_query, w_key, w_value, w_out, mlp_gain, w_gate, w_up, w_down, cotangent
):
    stretch, width = activations.shape[3:]
    deep = w_query.shape[0]
    seq = document_ids.shape[1]
    pair = 2 * seq
    wide = w_gate.shape[1] // (4 * zs)
    x = activations.reshape(2, stretch, width)
    cot = cotangent.reshape(2, stretch, width)
    small = jnp.stack([attn_gain.astype(F32), mlp_gain.astype(F32)])
    docs_rows = document_ids.astype(F32).reshape(seq // deep, deep)
    small = jnp.concatenate([small, docs_rows, jnp.zeros((6 - seq // deep, deep), F32)])
    cosine, sine = (jnp.asarray(table) for table in rope_tables(seq))
    half = stretch // 2
    hidden, qkv, attended, qkv_w, out_w, gains, docs, middle, h2_all, cot_all, gh_part, feed_part, grad_gu, product = call(
        functools.partial(forward_kernel, zs),
        1,
        [
            ((pair, width), BF, ANY),
            ((pair, 3 * HEAD_DIM), BF, ANY),
            ((pair, HEAD_DIM), BF, ANY),
            ((width, 3 * HEAD_DIM), BF, ANY),
            ((HEAD_DIM, width), BF, ANY),
            ((8, width), F32, ANY),
            ((8, seq), F32, ANY),
            ((stretch, width), F32, ANY),
            ((4, zs, 2, stretch, width), BF, ANY),
            ((4, zs, 2, stretch, width), BF, ANY),
            ((4 * seq, width), BF, ANY),
            ((4 * seq, width), BF, ANY),
            ((4 * seq, 2 * wide), BF, ANY),
            ((4 * seq, wide), BF, ANY),
        ],
        [
            VMEM((pair, width), BF),
            VMEM((pair, width), BF),
            VMEM((width, 3 * HEAD_DIM), BF),
            VMEM((HEAD_DIM, width), BF),
            VMEM((zs, 8, deep), F32),
            VMEM((2, 8, deep), F32),
            VMEM((8, width), F32),
            VMEM((8, seq), F32),
            VMEM((seq, HEAD_DIM), F32),
            VMEM((seq, HEAD_DIM), F32),
            VMEM((pair, 3 * HEAD_DIM), BF),
            VMEM((pair, HEAD_DIM), BF),
            VMEM((2, 2, zs, stretch, width), BF),
            VMEM((2, zs, stretch, width), BF),
            VMEM((zs, stretch, width), BF),
            VMEM((zs, stretch, width), BF),
            VMEM((stretch, width), BF),
            VMEM((stretch, width), BF),
            VMEM((stretch, width), F32),
            VMEM((4, zs, 2, stretch, width), BF),
            VMEM((4, zs, 2, stretch, width), BF),
            VMEM((width, 2 * wide), BF),
            VMEM((wide, width), BF),
            VMEM((4 * seq, wide), F32),
            VMEM((4 * seq, wide), F32),
            VMEM((4 * seq, 2 * wide), BF),
            VMEM((4 * seq, wide), BF),
            VMEM((2, 256, width), BF),
            VMEM((2, 256, width), BF),
        ],
        ((134,), (131,), (34,), (2, 2)),
        (x, w_query, w_key, w_value, w_out, small, cosine, sine, w_gate, w_up, w_down, cot),
        60,
    )

    h2 = h2_all.reshape(4 * seq, width)
    cots = cot_all.reshape(4 * seq, width)
    gh_part = gh_part.reshape(4, zs, 2, stretch, width)
    feed_part = feed_part.reshape(4, zs, 2, stretch, width)

    sum_scratch = [
        VMEM((4, zs, stretch, width), BF),
        VMEM((4, zs, stretch, width), BF),
        VMEM((2, 2, zs, half, width), BF),
        VMEM((2, zs, half, width), BF),
        VMEM((zs, stretch, width), BF),
    ]
    layer_out, input_grad, q_g, k_g, v_g, o_g, gate_g, up_g, down_g, gains_g = call(
        functools.partial(backward_kernel, zs),
        2,
        [
            ((2, stretch, width), BF, ANY),
            ((2, stretch, width), BF, ANY),
            (w_query.shape, BF, ANY),
            (w_key.shape, BF, ANY),
            (w_value.shape, BF, ANY),
            (w_out.shape, BF, ANY),
            (w_gate.shape, BF, ANY),
            (w_up.shape, BF, ANY),
            (w_down.shape, BF, ANY),
            ((2, deep), F32, VMEM),
        ],
        sum_scratch
        + sum_scratch
        + [
            VMEM((2, 2, zs, stretch, width), BF),
            VMEM((2, zs, stretch, width), BF),
            VMEM((stretch, width), BF),
            VMEM((2, zs, stretch, width), BF),
            VMEM((pair, width), BF),
            VMEM((pair, 3 * HEAD_DIM), BF),
            VMEM((pair, HEAD_DIM), BF),
            VMEM((width, 3 * HEAD_DIM), BF),
            VMEM((HEAD_DIM, width), BF),
            VMEM((pair, width), BF),
            VMEM((pair, 3 * HEAD_DIM), BF),
            VMEM((8, width), F32),
            VMEM((8, seq), F32),
            VMEM((seq, HEAD_DIM), F32),
            VMEM((seq, HEAD_DIM), F32),
            VMEM((seq, HEAD_DIM), BF),
            VMEM((stretch, width), F32),
            VMEM((stretch, width), BF),
            VMEM((stretch, width), BF),
            VMEM((stretch, width), F32),
            VMEM((stretch, width), BF),
            VMEM((stretch, width), BF),
            VMEM((stretch, width), BF),
            VMEM((2, 8, width), F32),
            VMEM((2, 8, width), F32),
            VMEM((2, 8, width), F32),
            VMEM((4, 2, 8, width), F32),
            VMEM((zs, 2, 8, deep), F32),
            VMEM((zs, deep // 2, 3 * HEAD_DIM), BF),
            VMEM((zs, deep // 2, 3 * HEAD_DIM), BF),
            VMEM((zs, deep // 2, 3 * HEAD_DIM), BF),
            VMEM((zs, HEAD_DIM, deep), BF),
            VMEM((zs, HEAD_DIM // 2, deep), BF),
            VMEM((zs, HEAD_DIM // 2, deep), BF),
            VMEM((4 * seq, 2 * wide), BF),
            VMEM((wide, 4 * seq), BF),
            VMEM((2, 4 * seq, 256), BF),
            VMEM((width, 2 * wide), BF),
            VMEM((wide, width), BF),
        ],
        ((232,), (231,), (36,), (2,)),
        (
            gh_part, feed_part, h2, cots, grad_gu, product, middle, cot, x, gains, docs, cosine, sine,
            hidden, qkv, attended, qkv_w, out_w,
        ),
        60,
    )
    q_g, k_g, v_g, o_g, gate_g, up_g, down_g = widen(q_g, k_g, v_g, o_g, gate_g, up_g, down_g)
    return (
        layer_out.reshape(activations.shape),
        input_grad.reshape(activations.shape),
        gains_g[0],
        q_g,
        k_g,
        v_g,
        o_g,
        gains_g[1],
        gate_g,
        up_g,
        down_g,
    )


def angles(positions):
    half_dim = HEAD_DIM // 2
    frequency = ROPE_BASE ** (-jnp.arange(half_dim, dtype=jnp.float32) / half_dim)
    angle = positions.astype(jnp.float32)[:, None] * frequency[None, :]
    return (jnp.cos(angle)[:, None, :], jnp.sin(angle)[:, None, :])


def rotate(flat, positions):
    row_count = flat.shape[0]
    heads = flat.reshape(row_count, -1, HEAD_DIM)
    cosine, sine = angles(positions)
    first = heads[..., : HEAD_DIM // 2]
    second = heads[..., HEAD_DIM // 2 :]
    turned = jnp.concatenate(
        [first * cosine - second * sine, second * cosine + first * sine], axis=-1
    )
    return turned.reshape(row_count, -1)


def unrotate(flat, positions):
    row_count = flat.shape[0]
    heads = flat.reshape(row_count, -1, HEAD_DIM)
    cosine, sine = angles(positions)
    first = heads[..., : HEAD_DIM // 2]
    second = heads[..., HEAD_DIM // 2 :]
    turned = jnp.concatenate(
        [first * cosine + second * sine, second * cosine - first * sine], axis=-1
    )
    return turned.reshape(row_count, -1)


def normalize(values):
    inverse = lax.rsqrt(jnp.mean(values * values, axis=-1, keepdims=True) + EPS)
    return (values * inverse, inverse)


def norm_back(grad_normed_out, normed, inverse, gain):
    scaled = grad_normed_out * gain
    return inverse * (scaled - normed * jnp.mean(scaled * normed, axis=-1, keepdims=True))


def contract_rows(left, right):
    return lax.dot_general(
        left, right, (((1,), (1,)), ((), ())), preferred_element_type=jnp.float32
    )


def contract_cols(left, right):
    return lax.dot_general(
        left, right, (((0,), (0,)), ((), ())), preferred_element_type=jnp.float32
    )


def visibility(query_positions, query_docs, key_positions, key_docs):
    same_doc = query_docs[:, None] == key_docs[None, :]
    earlier = key_positions[None, :] <= query_positions[:, None]
    return jnp.where(same_doc & earlier, 1.0, 0.0).astype(jnp.float32)


def merge_heads(stacked):
    return jnp.transpose(stacked, (1, 0, 2)).reshape(stacked.shape[1], -1)


def head_slice(matrix, offset):
    return lax.dynamic_slice_in_dim(matrix, offset, HEAD_DIM, 1)


def attend_forward(queries, key_rows, value_rows, visible):
    score_scale = HEAD_DIM ** (-0.5)

    def one_head(head_index):
        offset = head_index * HEAD_DIM
        scores = (
            contract_rows(head_slice(queries, offset), head_slice(key_rows, offset)) * score_scale
        )
        weights = (jax.nn.sigmoid(scores - SHIFT) * visible).astype(jnp.bfloat16)
        return jnp.dot(weights, head_slice(value_rows, offset), preferred_element_type=jnp.float32)

    stacked = lax.map(one_head, jnp.arange(queries.shape[1] // HEAD_DIM))
    return merge_heads(stacked)


def attend_back(queries, key_rows, value_rows, grad_attended, visible):
    score_scale = HEAD_DIM ** (-0.5)

    def one_head(head_index):
        offset = head_index * HEAD_DIM
        head_query = head_slice(queries, offset)
        head_key = head_slice(key_rows, offset)
        head_grad = head_slice(grad_attended, offset)
        scores = contract_rows(head_query, head_key) * score_scale
        sigma = jax.nn.sigmoid(scores - SHIFT)
        grad_weights = contract_rows(head_grad, head_slice(value_rows, offset))
        grad_scores = (grad_weights * visible * sigma * (1.0 - sigma)).astype(jnp.bfloat16)
        pieces = []
        pieces.append(
            jnp.dot(grad_scores, head_key, preferred_element_type=jnp.float32) * score_scale
        )
        weights = (sigma * visible).astype(jnp.bfloat16)
        pieces.append(contract_cols(grad_scores, head_query) * score_scale)
        pieces.append(contract_cols(weights, head_grad))
        return tuple(pieces)

    stacked = lax.map(one_head, jnp.arange(queries.shape[1] // HEAD_DIM))
    return tuple((merge_heads(piece) for piece in stacked))


def rows_shards(
    activations,
    document_ids,
    attn_gain,
    w_query,
    w_key,
    w_value,
    w_out,
    mlp_gain,
    w_gate,
    w_up,
    w_down,
    cotangent,
):
    groups = lax.axis_size("cp")
    rank = lax.axis_index("cp")
    stretch_len = activations.shape[3]
    width = activations.shape[4]
    row_count = 2 * stretch_len
    offsets = jnp.arange(stretch_len, dtype=jnp.int32)
    my_positions = jnp.concatenate(
        [rank * stretch_len + offsets, (2 * groups - 1 - rank) * stretch_len + offsets]
    )
    all_docs = document_ids[0]
    my_docs = jnp.take(all_docs, my_positions)
    slots = jnp.arange(groups * row_count, dtype=jnp.int32)
    owners = slots // row_count
    halves = slots // stretch_len % 2
    key_positions = (
        jnp.where(halves == 0, owners, 2 * groups - 1 - owners) * stretch_len + slots % stretch_len
    )
    key_docs = jnp.take(all_docs, key_positions)
    visible = visibility(my_positions, my_docs, key_positions, key_docs)
    gathered = (
        lax.all_gather(w_query, "cp", axis=0, tiled=True),
        lax.all_gather(w_key, "cp", axis=0, tiled=True),
        lax.all_gather(w_value, "cp", axis=0, tiled=True),
        lax.all_gather(w_out, "cp", axis=1, tiled=True),
        lax.all_gather(w_gate, "cp", axis=0, tiled=True),
        lax.all_gather(w_up, "cp", axis=0, tiled=True),
        lax.all_gather(w_down, "cp", axis=1, tiled=True),
        lax.all_gather(attn_gain, "cp", axis=0, tiled=True),
        lax.all_gather(mlp_gain, "cp", axis=0, tiled=True),
    )
    (
        query_full,
        key_full,
        value_full,
        out_full,
        gate_full,
        up_full,
        down_full,
        gain_one,
        gain_two,
    ) = gathered
    gain_one = gain_one.astype(jnp.float32)
    gain_two = gain_two.astype(jnp.float32)
    inputs = activations.reshape(row_count, width).astype(jnp.float32)
    normed_one, inverse_one = normalize(inputs)
    hidden_one = (normed_one * gain_one).astype(jnp.bfloat16)
    queries = rotate(
        jnp.dot(hidden_one, query_full, preferred_element_type=jnp.float32), my_positions
    ).astype(jnp.bfloat16)
    keys_local = rotate(
        jnp.dot(hidden_one, key_full, preferred_element_type=jnp.float32), my_positions
    ).astype(jnp.bfloat16)
    values_local = jnp.dot(hidden_one, value_full, preferred_element_type=jnp.float32).astype(
        jnp.bfloat16
    )
    keys_all, values_all = (
        lax.all_gather(keys_local, "cp", axis=0, tiled=True),
        lax.all_gather(values_local, "cp", axis=0, tiled=True),
    )
    attended = attend_forward(queries, keys_all, values_all, visible).astype(jnp.bfloat16)
    branch = lax.psum(jnp.dot(attended, out_full, preferred_element_type=jnp.float32), "tp")
    middle = inputs + branch
    normed_two, inverse_two = normalize(middle)
    hidden_two = (normed_two * gain_two).astype(jnp.bfloat16)
    gate = jnp.dot(hidden_two, gate_full, preferred_element_type=jnp.float32)
    upward = jnp.dot(hidden_two, up_full, preferred_element_type=jnp.float32)
    sigma_gate = jax.nn.sigmoid(gate)
    silu_gate = gate * sigma_gate
    product = (silu_gate * upward).astype(jnp.bfloat16)
    feed = lax.psum(jnp.dot(product, down_full, preferred_element_type=jnp.float32), "tp")
    result = middle + feed
    layer_out = result.astype(jnp.bfloat16).reshape(activations.shape)
    grad_result = cotangent.reshape(row_count, width).astype(jnp.float32)
    grad_feed = grad_result.astype(jnp.bfloat16)
    grad_product = contract_rows(grad_feed, down_full)
    grad_gate = (grad_product * upward * sigma_gate * (1.0 + gate * (1.0 - sigma_gate))).astype(
        jnp.bfloat16
    )
    grad_up = (grad_product * silu_gate).astype(jnp.bfloat16)
    grad_hidden_two = lax.psum(
        contract_rows(grad_gate, gate_full) + contract_rows(grad_up, up_full), "tp"
    )
    grad_gain_two = jnp.sum(grad_hidden_two * normed_two, axis=0)
    grad_middle = grad_result + norm_back(grad_hidden_two, normed_two, inverse_two, gain_two)
    grad_down = contract_cols(product, grad_feed)
    grad_gate_w = contract_cols(hidden_two, grad_gate)
    grad_up_w = contract_cols(hidden_two, grad_up)
    share_gate, share_up, share_down, share_gain_two = (
        lax.psum_scatter(grad_gate_w, "cp", scatter_dimension=0, tiled=True),
        lax.psum_scatter(grad_up_w, "cp", scatter_dimension=0, tiled=True),
        lax.psum_scatter(grad_down, "cp", scatter_dimension=1, tiled=True),
        lax.psum_scatter(grad_gain_two, "cp", scatter_dimension=0, tiled=True),
    )
    grad_branch = grad_middle.astype(jnp.bfloat16)
    grad_attended = contract_rows(grad_branch, out_full).astype(jnp.bfloat16)
    grad_queries, key_terms, value_terms = attend_back(
        queries, keys_all, values_all, grad_attended, visible
    )
    grad_keys, grad_values = (
        lax.psum_scatter(key_terms, "cp", scatter_dimension=0, tiled=True),
        lax.psum_scatter(value_terms, "cp", scatter_dimension=0, tiled=True),
    )
    grad_query_pre = unrotate(grad_queries, my_positions).astype(jnp.bfloat16)
    grad_key_pre = unrotate(grad_keys, my_positions).astype(jnp.bfloat16)
    grad_value_pre = grad_values.astype(jnp.bfloat16)
    local_hidden = (
        contract_rows(grad_query_pre, query_full)
        + contract_rows(grad_key_pre, key_full)
        + contract_rows(grad_value_pre, value_full)
    )
    grad_hidden_one = lax.psum(local_hidden, "tp")
    grad_gain_one = jnp.sum(grad_hidden_one * normed_one, axis=0)
    grad_inputs = grad_middle + norm_back(grad_hidden_one, normed_one, inverse_one, gain_one)
    grad_query_w = contract_cols(hidden_one, grad_query_pre)
    grad_key_w = contract_cols(hidden_one, grad_key_pre)
    grad_value_w = contract_cols(hidden_one, grad_value_pre)
    grad_out_w = contract_cols(attended, grad_branch)
    share_query, share_key, share_value, share_out, share_gain_one = (
        lax.psum_scatter(grad_query_w, "cp", scatter_dimension=0, tiled=True),
        lax.psum_scatter(grad_key_w, "cp", scatter_dimension=0, tiled=True),
        lax.psum_scatter(grad_value_w, "cp", scatter_dimension=0, tiled=True),
        lax.psum_scatter(grad_out_w, "cp", scatter_dimension=1, tiled=True),
        lax.psum_scatter(grad_gain_one, "cp", scatter_dimension=0, tiled=True),
    )
    summed = lax.psum(
        (
            share_gain_one,
            share_query,
            share_key,
            share_value,
            share_out,
            share_gain_two,
            share_gate,
            share_up,
            share_down,
        ),
        "dp",
    )
    input_grad = grad_inputs.astype(jnp.bfloat16).reshape(activations.shape)
    return (
        layer_out,
        input_grad,
        summed[0],
        summed[1],
        summed[2],
        summed[3],
        summed[4],
        summed[5],
        summed[6],
        summed[7],
        summed[8],
    )


def layer(sizes, *args):
    heads = args[3].shape[1] // HEAD_DIM
    zs = sizes["cp"]
    fits = sizes["dp"] == 4 and sizes["tp"] == 2 and zs == 4 and heads == 2 * zs
    fits = fits and args[0].shape[3] % 32 == 0 and args[8].shape[1] % (2 * zs * HEAD_DIM) == 0
    fits = fits and args[3].shape[0] % HEAD_DIM == 0 and args[1].shape[1] % args[3].shape[0] == 0
    fits = fits and args[1].shape[1] <= 6 * args[3].shape[0]
    if fits:
        return heads_shards(zs, *args)
    return rows_shards(*args)


def solution(mesh):
    return jax.shard_map(
        functools.partial(layer, dict(mesh.shape)),
        mesh=mesh,
        in_specs=(
            P("dp", "cp", None, None, None),
            P("dp", None),
            P("cp"),
            P("cp", "tp"),
            P("cp", "tp"),
            P("cp", "tp"),
            P("tp", "cp"),
            P("cp"),
            P("cp", "tp"),
            P("cp", "tp"),
            P("tp", "cp"),
            P("dp", "cp", None, None, None),
        ),
        out_specs=(
            P("dp", "cp", None, None, None),
            P("dp", "cp", None, None, None),
            P("cp"),
            P("cp", "tp"),
            P("cp", "tp"),
            P("cp", "tp"),
            P("tp", "cp"),
            P("cp"),
            P("cp", "tp"),
            P("cp", "tp"),
            P("tp", "cp"),
        ),
        check_vma=False,
    )
```

```python
import functools
import math

import jax
import jax.numpy as jnp
import numpy as np
from jax import lax
from jax.experimental import pallas as pl
from jax.experimental.pallas import tpu as pltpu
from jax.sharding import PartitionSpec as P

HEAD_DIM = 128
EPS = 1e-05
SHIFT = math.log(4096.0)
ROPE_BASE = 10000.0
BF = jnp.bfloat16
F32 = jnp.float32
MESH = pl.DeviceIdType.MESH
ANY = pl.ANY
VMEM = pltpu.VMEM
MIB = 2**20


class Net:
    def __init__(self, zs, send_sems, recv_sems, local_sems):
        self.zs = zs
        self.dp, self.z, self.t = (lax.axis_index(a) for a in ("dp", "cp", "tp"))
        self.a, self.b = lax.div(self.dp, 2), lax.rem(self.dp, 2)
        self.send_sems, self.recv_sems, self.local_sems = send_sems, recv_sems, local_sems
        self.arrivals = 0
        self.free_locals = list(range(local_sems.shape[0]))
        self.open = []

    def along_z(self, s):
        return (self.dp, lax.rem(self.z + s, self.zs), self.t)

    def source_z(self, s):
        return lax.rem(self.z + self.zs - s, self.zs)

    @property
    def over_x(self):
        return (2 * self.a + 1 - self.b, self.z, self.t)

    @property
    def over_y(self):
        return (2 * (1 - self.a) + self.b, self.z, self.t)

    @property
    def sibling(self):
        return (self.dp, self.z, 1 - self.t)

    @property
    def across(self):
        return (2 * (1 - self.a) + 1 - self.b, self.z, self.t)

    def meet(self):
        ways = [self.along_z(s) for s in range(1, self.zs)] + [self.over_x, self.over_y, self.across, self.sibling]
        barrier = pltpu.get_barrier_semaphore()
        for way in ways:
            pl.semaphore_signal(barrier, inc=1, device_id=way, device_id_type=MESH)
        pl.semaphore_wait(barrier, len(ways))

    def slot(self):
        self.arrivals += 1
        return self.arrivals - 1

    def send(self, src, dst, way, arrive=None, when=None):
        arrive = self.slot() if arrive is None else arrive
        sem = self.send_sems.at[len(self.open)]
        copy = pltpu.make_async_remote_copy(
            src, dst, sem, self.recv_sems.at[arrive], device_id=way, device_id_type=MESH
        )
        if when is None:
            copy.start()
        else:
            pl.when(when)(copy.start)
        self.open.append((copy, when))
        return copy

    def arrival(self, ref, slot):
        return pltpu.make_async_remote_copy(
            ref, ref, self.send_sems.at[0], self.recv_sems.at[slot], device_id=self.sibling, device_id_type=MESH
        )

    def keep(self, src, dst):
        return Kept(self, src, dst)

    def finish(self):
        for copy, when in self.open:
            if when is None:
                copy.wait_send()
            else:
                pl.when(when)(copy.wait_send)


class Kept:
    def __init__(self, net, src, dst):
        self.net, self.slot = net, net.free_locals.pop(0)
        self.copy = pltpu.make_async_copy(src, dst, net.local_sems.at[self.slot])
        self.copy.start()

    def wait(self):
        self.copy.wait()
        self.net.free_locals.append(self.slot)


class LineGather:
    def __init__(self, net, src, place):
        self.net, self.src, self.place = net, src, place
        self.h, self.low = lax.div(net.z, 2), lax.rem(net.z, 2)
        self.mate = (net.dp, net.z + 1 - 2 * self.low, net.t)
        self.gate = (net.dp, 2 - self.h, net.t)
        self.hands_on = self.h != self.low

    def start(self):
        net = self.net
        mine = self.place(net.z)
        self.near = net.send(self.src, mine, self.mate)
        self.slots = [net.slot(), net.slot()]
        net.send(self.src, mine, self.gate, arrive=self.slots[0] + self.low)

    def take(self, s):
        net = self.net
        if s == 1:
            self.near.wait_recv()
            return net.z + 1 - 2 * self.low
        z = 2 * (1 - self.h) + s - 2
        ref = self.place(z)
        net.arrival(ref, self.slots[s - 2]).wait_recv()
        net.send(ref, ref, self.mate, arrive=self.slots[s - 2], when=self.hands_on)
        return z


def plane_relay(net, place, halves, over_x, over_y, ways="xy", sibling=None):
    dx, dy = 2 * net.a + 1 - net.b, 2 * (1 - net.a) + net.b
    relays = []

    def by_y():
        over_x.wait_recv()
        piece = halves(place(dx), 0) if "x" in ways else place(dx)
        if "y" in ways:
            relays.append(net.send(piece, piece, net.over_y))
        if sibling:
            sibling(dx)

    def by_x():
        over_y.wait_recv()
        piece = halves(place(dy), 1) if "y" in ways else place(dy)
        if "x" in ways:
            relays.append(net.send(piece, piece, net.over_x))
        if sibling:
            sibling(dy)

    for step in (by_x, by_y) if ways == "x" else (by_y, by_x):
        step()
    return relays


def plane_end(net, relays, sibling=None):
    for copy in relays:
        copy.wait_recv()
    if sibling:
        sibling(2 * (1 - net.a) + 1 - net.b)


def rows_loop(count, step, body):
    def one(i, carry):
        body(pl.ds(pl.multiple_of(i * step, step), step))
        return carry

    lax.fori_loop(0, count // step, one, 0)


def add_rows(out, terms, rows):
    def body(at):
        total = terms[0][at, :].astype(F32)
        for term in terms[1:]:
            total += term[at, :].astype(F32)
        out[at, :] = total.astype(out.dtype)

    rows_loop(rows, 16, body)


class GatherAll:
    def __init__(self, net, src, dst):
        self.net, self.src, self.dst = net, src, dst
        rows = src.shape[0] // 2
        self.halves = lambda ref, k: ref.at[pl.ds(k * rows, rows)]

    def place(self, dp, z):
        return self.dst.at[dp, z, self.net.t]

    def start(self):
        net = self.net
        mine = self.place(net.dp, net.z)
        self.line = LineGather(net, self.src, lambda z: self.place(net.dp, z))
        self.line.start()
        self.local = net.keep(self.src, mine)
        self.plane = [(net.z, net.send(self.src, mine, net.over_x), net.send(self.src, mine, net.over_y))]
        self.twin = [net.send(self.src, mine, net.sibling)]
        self.states = []

    def to_twin(self, dp, z):
        ref = self.place(dp, z)
        self.twin.append(self.net.send(ref, ref, self.net.sibling))

    def spread(self, s):
        net = self.net
        z = self.line.take(s)
        ref = self.place(net.dp, z)
        self.plane.append((z, net.send(ref, ref, net.over_x), net.send(ref, ref, net.over_y)))
        self.to_twin(net.dp, z)

    def relay(self, s):
        z, over_x, over_y = self.plane[s]
        place = functools.partial(self.place, z=z)
        self.states.append((z, plane_relay(self.net, place, self.halves, over_x, over_y, sibling=lambda dp: self.to_twin(dp, z))))

    def end(self):
        for z, relays in self.states:
            plane_end(self.net, relays, lambda dp, z=z: self.to_twin(dp, z))
        for copy in self.twin:
            copy.wait_recv()
        self.local.wait()


class GatherGroup:
    def __init__(self, net, src, dst, own_lanes=None):
        self.net, self.src, self.dst, self.own_lanes = net, src, dst, own_lanes
        self.rows = src.shape[0]

    def place(self, b, z, t=None):
        t = self.net.t if t is None else t
        last = 2 * self.net.zs - 1
        at = ((last + 1) * b + z + t * (last - 2 * z)) * self.rows
        return self.dst.at[pl.ds(pl.multiple_of(at, self.rows), self.rows)]

    def start(self):
        net = self.net
        mine = self.place(net.b, net.z)
        self.line = LineGather(net, self.src, lambda z: self.place(net.b, z))
        self.line.start()
        self.over = [(net.z, net.send(self.src, mine, net.over_x))]
        self.twin, self.local = [], []
        if self.own_lanes is None:
            self.local.append(net.keep(self.src, mine))
            self.twin.append((net.b, net.z, net.send(self.src, mine, net.sibling)))
        else:
            for t in (0, 1):
                self.local.append(net.keep(self.own_lanes.at[t], self.place(net.b, net.z, t)))

    def to_twin(self, b, z):
        ref = self.place(b, z)
        self.twin.append((b, z, self.net.send(ref, ref, self.net.sibling)))

    def spread(self, s):
        net = self.net
        z = self.line.take(s)
        ref = self.place(net.b, z)
        self.over.append((z, net.send(ref, ref, net.over_x)))
        self.to_twin(net.b, z)
        return z

    def far(self, s):
        z, copy = self.over[s]
        copy.wait_recv()
        self.to_twin(1 - self.net.b, z)
        return z

    def end(self):
        for _, _, copy in self.twin:
            copy.wait_recv()
        for copy in self.local:
            copy.wait()


class SumGroup:
    def __init__(self, net, part, sib, far, landed):
        self.net, self.part, self.sib, self.far, self.landed = net, part, sib, far, landed
        self.rows = part.shape[3]
        self.twin, self.over, self.z_sends = {}, [], []

    def order(self):
        return [lax.rem(self.net.z + s + 1, self.net.zs) for s in range(self.net.zs)]

    def give(self, k):
        net = self.net
        b = net.b if k else 1 - net.b
        for s, z in enumerate(self.order()):
            self.twin[k, s] = net.send(self.part.at[b, 1 - net.t, z], self.sib.at[b, z], net.sibling)

    def take(self, k):
        net = self.net
        b = net.b if k else 1 - net.b
        for s, z in enumerate(self.order()):
            self.twin[k, s].wait_recv()
            own = self.part.at[b, net.t, z]
            add_rows(own, [own, self.sib.at[b, z]], self.rows)
            if k == 0:
                self.over.append(net.send(own, self.far.at[z], net.over_x))

    def along(self):
        net = self.net
        for s, z in enumerate(self.order()):
            self.over[s].wait_recv()
            last = s == net.zs - 1
            own = self.part.at[net.b, net.t, z]
            out = self.landed.at[net.z] if last else own
            add_rows(out, [own, self.far.at[z]], self.rows)
            if not last:
                self.z_sends.append(net.send(out, self.landed.at[net.z], net.along_z(s + 1)))

    def end(self):
        for copy in self.z_sends:
            copy.wait_recv()


class SumLine(SumGroup):
    def take(self, k):
        net = self.net
        b = net.b if k else 1 - net.b
        for s, z in enumerate(self.order()):
            self.twin[k, s].wait_recv()
            own, last = self.part.at[b, net.t, z], s == net.zs - 1
            out = self.landed.at[b, net.z] if last else own
            add_rows(out, [own, self.sib.at[b, z]], self.rows)
            if not last:
                self.z_sends.append(net.send(own, self.landed.at[b, net.z], net.along_z(s + 1)))

    def across(self):
        net = self.net
        b = 1 - net.b
        for copy in self.z_sends[: net.zs - 1]:
            copy.wait_recv()
        out = self.part.at[b, net.t, net.z]
        add_rows(out, [self.landed.at[b, z] for z in range(net.zs)], self.rows)
        self.over = net.send(out, self.far, net.over_x)

    def end(self):
        for copy in self.z_sends[self.net.zs - 1 :]:
            copy.wait_recv()
        self.over.wait_recv()


class SumAll:
    def __init__(self, net, part, own, sib, one, two, landed):
        self.net, self.part, self.own, self.sib = net, part, own, sib
        self.one, self.two, self.landed = one, two, landed
        self.half = part.shape[3] // 2

    def order(self):
        net = self.net
        return [lax.rem(net.z + s + 1, net.zs) for s in range(net.zs)]

    def places(self):
        a, b = self.net.a, self.net.b
        return [2 * (1 - a) + 1 - b, 2 * a + 1 - b, 2 * (1 - a) + b, 2 * a + b]

    def start(self):
        net = self.net
        self.twin, self.mine = [], []
        for z in self.order():
            self.twin.append(net.send(self.part.at[:, z, 1 - net.t], self.sib.at[:, z], net.sibling))
            self.mine.append(net.keep(self.part.at[:, z, net.t], self.own.at[:, z]))

    def upper(self, ref):
        return ref.at[pl.ds(0, self.half)]

    def lower(self, ref):
        return ref.at[pl.ds(self.half, self.half)]

    def first(self, s):
        net = self.net
        z = self.order()[s]
        dd, dx, dy, me = self.places()
        self.twin[s].wait_recv()
        self.mine[s].wait()
        for dp in (dd, dx, dy, me):
            add_rows(self.own.at[dp, z], [self.own.at[dp, z], self.sib.at[dp, z]], 2 * self.half)
        self.ones = getattr(self, "ones", [])
        self.ones.append(
            (
                net.send(self.upper(self.own.at[dd, z]), self.one.at[0, 0, z], net.over_x),
                net.send(self.upper(self.own.at[dx, z]), self.one.at[0, 1, z], net.over_x),
                net.send(self.lower(self.own.at[dd, z]), self.one.at[1, 0, z], net.over_y),
                net.send(self.lower(self.own.at[dy, z]), self.one.at[1, 1, z], net.over_y),
            )
        )

    def second(self, s):
        net = self.net
        z = self.order()[s]
        dd, dx, dy, me = self.places()
        x_dd, x_me, y_dd, y_me = self.ones[s]
        self.twos = getattr(self, "twos", [])
        x_dd.wait_recv()
        out = self.upper(self.own.at[dy, z])
        add_rows(out, [out, self.one.at[0, 0, z]], self.half)
        up = net.send(out, self.two.at[0, z], net.over_y)
        y_dd.wait_recv()
        out = self.lower(self.own.at[dx, z])
        add_rows(out, [out, self.one.at[1, 0, z]], self.half)
        side = net.send(out, self.two.at[1, z], net.over_x)
        self.twos.append((up, side))

    def third(self, s):
        net = self.net
        z = self.order()[s]
        dd, dx, dy, me = self.places()
        _, x_me, _, y_me = self.ones[s]
        up, side = self.twos[s]
        last = s == net.zs - 1
        out = self.landed.at[net.z] if last else self.own.at[me, z]
        x_me.wait_recv()
        up.wait_recv()
        mine = self.own.at[me, z]
        add_rows(self.upper(out), [self.upper(mine), self.one.at[0, 1, z], self.two.at[0, z]], self.half)
        y_me.wait_recv()
        side.wait_recv()
        add_rows(self.lower(out), [self.lower(mine), self.one.at[1, 1, z], self.two.at[1, z]], self.half)
        self.z_sends = getattr(self, "z_sends", [])
        if not last:
            self.z_sends.append(net.send(out, self.landed.at[net.z], net.along_z(s + 1)))

    def end(self):
        for copy in self.z_sends:
            copy.wait_recv()


class SpreadGrads:
    def __init__(self, net, src, dst, ways):
        self.net, self.src, self.dst, self.ways = net, src, dst, ways
        self.z_sends, self.plane, self.states = {}, {}, []

    def mine(self):
        return self.dst(self.net.dp, self.net.z)

    def start(self):
        self.own()
        for s in range(1, self.net.zs):
            self.go(s)

    def own(self):
        self.local = self.net.keep(self.src(self.net.z), self.mine())

    def go(self, s):
        net = self.net
        self.z_sends[s] = net.send(self.src(lax.rem(net.z + s, net.zs)), self.mine(), net.along_z(s))

    def spread(self, s):
        net = self.net
        z = net.source_z(s)
        ref = self.dst(net.dp, z)
        if s:
            self.z_sends[s].wait_recv()
            src = ref
        else:
            src = self.src(net.z)
        self.plane[s] = (z, net.send(src, ref, net.over_x), net.send(src, ref, net.over_y))

    def relay(self, s):
        z, over_x, over_y = self.plane[s]
        self.states.append(plane_relay(self.net, lambda dp: self.dst(dp, z), half_rows, over_x, over_y, self.ways))

    def end(self):
        for relays in self.states:
            plane_end(self.net, relays)
        self.local.wait()


def half_rows(ref, k):
    n = ref.shape[0] // 2
    return ref.at[pl.ds(k * n, n)]


def aligned(i, size):
    return pl.ds(pl.multiple_of(i * size, size), size)


def loop(count, body):
    def one(i, carry):
        body(i)
        return carry

    lax.fori_loop(0, count, one, 0)


def dot(left, right, dims=((1,), (0,)), kind=F32):
    return lax.dot_general(left, right, (dims, ((), ())), preferred_element_type=F32).astype(kind)


def turn(u, cosine, sine):
    return u * cosine + pltpu.roll(u, HEAD_DIM // 2, 1) * sine


def column(row, start, count):
    n = row.shape[1]
    here = lax.broadcasted_iota(jnp.int32, (count, n), 1) == start + lax.broadcasted_iota(jnp.int32, (count, n), 0)
    return jnp.sum(jnp.where(here, row, 0.0), axis=1, keepdims=True)


def seen(row, start, count, flip=False):
    n = row.shape[1]
    same = column(row, start, count) == row
    mine = start + lax.broadcasted_iota(jnp.int32, (count, n), 0)
    other = lax.broadcasted_iota(jnp.int32, (count, n), 1)
    return same & ((mine <= other) if flip else (other <= mine))


def sigma_of(left, right):
    return jax.nn.sigmoid(dot(left, right, ((1,), (1,))) * HEAD_DIM**-0.5 - SHIFT)


def call(kernel, name, outs, scratch, counts, args, vmem):
    return pl.pallas_call(
        kernel,
        out_shape=[jax.ShapeDtypeStruct(shape, kind) for shape, kind, _ in outs],
        in_specs=[pl.BlockSpec(memory_space=ANY)] * len(args),
        out_specs=[pl.BlockSpec(memory_space=space) for _, _, space in outs],
        scratch_shapes=list(scratch) + [pltpu.SemaphoreType.DMA(shape) for shape in counts],
        compiler_params=pltpu.CompilerParams(
            collective_id=name, has_side_effects=True, vmem_limit_bytes=vmem * MIB
        ),
    )(*args)


def forward_kernel(
    zs, x, wq, wk, wv, wo, small, cosine, sine, wg, wu, wd, cot,
    hidden_out, qkv_out, attended_out, qkv_w_out, out_w_out, gains_out, docs_out, middle, h2_out, cot_out, gh_out, feed_out, grad_gu_out, product_out,
    x_all, h1, qkv_w, out_w, small_z, small_x, gains, docs, cos_v, sin_v, qkv, attended, part, sib, far, landed,
    x_lane, h2, mid_v, h2_all, cot_all, gu_w, down_w, gate_v, gp_v,
    grad_gu, product, gh_v, feed_v, send_sems, recv_sems, local_sems, stage_sems,
):
    net = Net(zs, send_sems, recv_sems, local_sems)
    net.meet()
    deep, wide = wg.shape[0], gu_w.shape[1] // 2
    seq = docs.shape[1]
    half, side = deep // 2, HEAD_DIM // 2
    gather = GatherGroup(net, x.at[net.t], x_all, own_lanes=x)
    gather.start()
    small_waits = [net.send(small, small_z.at[net.z], net.along_z(s)) for s in range(1, zs)]
    small_waits.append(net.send(small, small_x.at[net.b], net.over_x))
    local = [net.keep(small, small_z.at[net.z]), net.keep(small, small_x.at[net.b])]
    local += [net.keep(cosine, cos_v), net.keep(sine, sin_v)]
    lane = net.keep(x.at[net.t], x_lane)

    def head(z):
        return aligned(net.b * zs + z, HEAD_DIM)

    mine = aligned(net.z, deep)
    my_half = pl.ds(pl.multiple_of(net.a * half, half), half)
    qkv_sends, out_sends, w_local = [], [], []
    for m, w in enumerate((wq, wk, wv)):
        col = pl.ds(m * HEAD_DIM, HEAD_DIM)
        w_local.append(net.keep(w.at[:, head(net.z)], qkv_w.at[mine, col]))
    for s in range(zs - 1, 0, -1):
        z = lax.rem(net.z + s, zs)
        rows = pl.ds(pl.multiple_of(net.z * deep + net.a * half, half), half)
        qkv_sends.append(
            [
                net.send(w.at[my_half, head(z)], qkv_w.at[rows, pl.ds(m * HEAD_DIM, HEAD_DIM)], net.along_z(s))
                for m, w in enumerate((wq, wk, wv))
            ]
        )
    out_rows = pl.ds(pl.multiple_of(net.a * side, side), side)
    w_local.append(net.keep(wo.at[head(net.z)], out_w.at[:, mine]))
    for s in range(zs - 1, 0, -1):
        z = lax.rem(net.z + s, zs)
        at = pl.ds(pl.multiple_of((net.b * zs + z) * HEAD_DIM + net.a * side, side), side)
        out_sends.append(net.send(wo.at[at], out_w.at[out_rows, mine], net.along_z(s)))
    qkv_sends.reverse()
    out_sends.reverse()

    cotan = GatherAll(net, cot.at[net.t], cot_all)
    mlp_waits, mlp_local = {}, {}

    def block(z):
        return aligned(net.dp * zs + z, wide)

    mlp = (
        (lambda z: wg.at[:, block(z)], gu_w.at[mine, pl.ds(0, wide)]),
        (lambda z: wu.at[:, block(z)], gu_w.at[mine, pl.ds(wide, wide)]),
        (lambda z: wd.at[block(z)], down_w.at[:, mine]),
    )
    for k, (src, dst) in enumerate(mlp):
        mlp_local[k] = net.keep(src(net.z), dst)

    def fetch(k):
        src, dst = mlp[k]
        mlp_waits[k] = [net.send(src(lax.rem(net.z + s, zs)), dst, net.along_z(s)) for s in range(zs - 1, 0, -1)]

    def fetched(k):
        for copy in mlp_waits[k]:
            copy.wait_recv()
        mlp_local[k].wait()

    for copy in small_waits:
        copy.wait_recv()
    for copy in local:
        copy.wait()
    for z in range(zs):
        gains[0:1, z * deep : (z + 1) * deep] = small_z[z, 0:1, :]
        gains[1:2, z * deep : (z + 1) * deep] = small_z[z, 1:2, :]
    for b in range(2):
        for k in range(seq // deep):
            docs[b : b + 1, k * deep : (k + 1) * deep] = small_x[b, 2 + k : 3 + k, :]

    def norm_block(ref_at):
        def body(i):
            at = pl.ds(pl.multiple_of(ref_at + i * 16, 16), 16)
            rows = x_all[at, :].astype(F32)
            inverse = lax.rsqrt(jnp.mean(rows * rows, axis=-1, keepdims=True) + EPS)
            h1[at, :] = (rows * inverse * gains[0:1, :]).astype(BF)

        loop(x.shape[1] // 16, body)

    rows = x.shape[1]
    last = 2 * zs - 1

    def offset(b, z, t):
        return ((last + 1) * b + z + t * (last - 2 * z)) * rows

    for copy in gather.local:
        copy.wait()
    gather.local = []
    for t in (0, 1):
        norm_block(offset(net.b, net.z, t))
    for s in range(1, zs):
        norm_block(offset(net.b, gather.spread(s), net.t))
    cotan.start()
    fetch(2)
    qkv_y = []
    for s in range(1, zs):
        norm_block(offset(1 - net.b, gather.far(s - 1), net.t))
        for copy in qkv_sends[s - 1]:
            copy.wait_recv()
        at = qkv_w.at[pl.ds(pl.multiple_of(net.source_z(s) * deep + net.a * half, half), half)]
        qkv_y.append(net.send(at, at, net.over_y))
    norm_block(offset(1 - net.b, gather.far(zs - 1), net.t))
    out_y = []
    for s in range(1, zs):
        out_sends[s - 1].wait_recv()
        at = out_w.at[out_rows, aligned(net.source_z(s), deep)]
        out_y.append(net.send(at, at, net.over_y))
    for b, z, copy in gather.twin:
        copy.wait_recv()
        norm_block(offset(b, z, 1 - net.t))
    for copy in qkv_y:
        copy.wait_recv()
    for copy in w_local:
        copy.wait()
    for s in range(1, zs):
        cotan.spread(s)
    for copy in out_y:
        copy.wait_recv()

    branch = SumGroup(net, part, sib, far, landed)
    tile = 128
    for k in range(2):
        b = net.b if k else 1 - net.b
        base = b * seq

        def project(i):
            at = pl.ds(pl.multiple_of(base + i * 256, 256), 256)
            pos = aligned(i, 256)
            pre = dot(h1[at, :], qkv_w[...])
            c, s = cos_v[pos, :], sin_v[pos, :]
            qkv[at, 0:HEAD_DIM] = turn(pre[:, 0:HEAD_DIM], c, s).astype(BF)
            qkv[at, HEAD_DIM : 2 * HEAD_DIM] = turn(pre[:, HEAD_DIM : 2 * HEAD_DIM], c, s).astype(BF)
            qkv[at, 2 * HEAD_DIM : 3 * HEAD_DIM] = pre[:, 2 * HEAD_DIM : 3 * HEAD_DIM].astype(BF)

        loop(seq // 256, project)
        every = pl.ds(pl.multiple_of(base, seq), seq)
        row = docs[pl.ds(b, 1), :]

        def attend(i):
            at = pl.ds(pl.multiple_of(base + i * tile, tile), tile)
            sigma = sigma_of(qkv[at, 0:HEAD_DIM], qkv[every, HEAD_DIM : 2 * HEAD_DIM])
            weights = jnp.where(seen(row, i * tile, tile), sigma, 0.0).astype(BF)
            found = dot(weights, qkv[every, 2 * HEAD_DIM : 3 * HEAD_DIM], kind=BF)
            attended[at, :] = found
            out = dot(found, out_w[...], kind=BF)
            for j in range(tile // rows):
                blk = i * (tile // rows) + j
                t = lax.div(blk, zs)
                z = (1 - t) * blk + t * (last - blk)
                part[b, t, z] = out[j * rows : (j + 1) * rows, :]

        loop(seq // tile, attend)
        branch.give(k)
    saved = [
        net.keep(h1, hidden_out), net.keep(qkv, qkv_out), net.keep(attended, attended_out),
        net.keep(qkv_w, qkv_w_out), net.keep(out_w, out_w_out), net.keep(gains, gains_out), net.keep(docs, docs_out),
    ]
    branch.take(0)
    branch.take(1)
    branch.along()
    for s in range(zs):
        cotan.relay(s)
    lane.wait()
    branch.end()

    def body(i):
        at = aligned(i, 16)
        total = x_lane[at, :].astype(F32)
        for z in range(zs):
            total += landed[z, at, :].astype(F32)
        mid_v[at, :] = total
        inverse = lax.rsqrt(jnp.mean(total * total, axis=-1, keepdims=True) + EPS)
        h2[at, :] = (total * inverse * gains[1:2, :]).astype(BF)

    loop(rows // 16, body)
    saved.append(net.keep(mid_v, middle))
    hidden = GatherAll(net, h2, h2_all)
    hidden.start()
    hidden.spread(1)
    hidden.spread(2)
    hidden.spread(3)
    fetch(0)
    fetch(1)
    cotan.end()
    saved.append(net.keep(cot_all, cot_out))

    few = 256 // (2 * rows)

    def tiles(body):
        def one(i):
            dp, z = lax.div(i, zs // few), pl.ds(lax.rem(i, zs // few) * few, few)
            body(dp, z, aligned(i, 256))

        loop(4 * zs // few, one)

    def gates(dp, z, at):
        gate_v[at, :] = dot(h2_all[dp, z].reshape(256, -1), gu_w[:, 0:wide])

    def products(dp, z, at):
        gp_v[at, :] = dot(cot_all[dp, z].reshape(256, -1), down_w[...], ((1,), (1,)))

    hidden.relay(0)
    fetched(2)
    tiles(products)
    for s in range(1, zs):
        hidden.relay(s)
    hidden.end()
    saved.append(net.keep(h2_all, h2_out))
    fetched(0)
    tiles(gates)
    fetched(1)

    def leave(slot, at):
        return (
            pltpu.make_async_copy(gh_v.at[slot], gh_out.at[at], stage_sems.at[0, slot]),
            pltpu.make_async_copy(feed_v.at[slot], feed_out.at[at], stage_sems.at[1, slot]),
        )

    def both(pair):
        for slot in range(2):
            i = 2 * pair + slot
            dp, z = lax.div(i, zs // few), pl.ds(lax.rem(i, zs // few) * few, few)
            at = aligned(i, 256)
            upward = dot(h2_all[dp, z].reshape(256, -1), gu_w[:, wide:])
            gate, grad_product = gate_v[at, :], gp_v[at, :]
            sigma = jax.nn.sigmoid(gate)
            silu = gate * sigma
            product[at, :] = (silu * upward).astype(BF)
            grad_gu[at, 0:wide] = (grad_product * upward * sigma * (1.0 + gate * (1.0 - sigma))).astype(BF)
            grad_gu[at, wide:] = (grad_product * silu).astype(BF)

            @pl.when(pair > 0)
            def _():
                for copy in leave(slot, at):
                    copy.wait()

            gh_v[slot] = dot(grad_gu[at, :], gu_w[...], ((1,), (1,)), BF)
            feed_v[slot] = dot(product[at, :], down_w[...], kind=BF)
            for copy in leave(slot, at):
                copy.start()

    loop(2 * zs // few, both)
    saved += [net.keep(grad_gu, grad_gu_out), net.keep(product, product_out)]
    for slot in range(2):
        for copy in leave(slot, aligned(slot, 256)):
            copy.wait()
    for copy in saved:
        copy.wait()
    net.finish()


ORDER = (
    "hstart", "F0", "F1", "MG", "g0s0", "F2", "g0z", "S0", "F3", "S1", "T0", "g1s0", "fstart", "S2",
    "T1", "S3", "g0r0", "T2", "g0s1", "T3", "g0s2", "fF0", "g0r1", "hend", "gstart", "MD", "fF1", "gs1",
    "fF2", "gs2", "g0r2", "g2s0", "gs3", "g2z", "gf0", "g2s1", "fS0", "g1z", "gf1", "g2r0", "g0s3", "gf2",
    "gf3", "fS1", "gend", "fS2", "A0", "g2s2", "fF3", "B0", "A1", "g1s1", "g1s2", "bt0", "g1r0", "B1",
    "g2r1", "W1", "g2r2", "bt1", "g1s3", "g0r3", "bx", "W2", "sw0", "sw1", "fT0", "sw2", "fT1", "fS3",
    "sw3", "g2s3", "g1r1", "Ls0", "bend", "g1r2", "Ls1", "Lr0", "gain2", "Lr1", "fT2", "Ls2", "Ls3", "fT3",
    "g2r3", "Lr2", "g1r3", "Lr3", "gain3", "fend",
)
RELAY_WAYS = ("y", "xy", "x", "xy", "y", "xy", "xy")


def backward_kernel(
    zs, gh_part, feed_part, h2_in, cots_in, grad_gu_in, product_in, middle, cot, x, gains_in, docs_in, cosine, sine,
    hidden_in, qkv_in, attended_in, qkv_w_in, out_w_in,
    layer_out, input_grad, q_out, k_out, v_out, o_out, gate_out, up_out, down_out, gains_out,
    own, sib, one, two, landed, own_f, sib_f, one_f, two_f, landed_f, part, sib_1, far_1, landed_1,
    h1, qkv, attended, qkv_w, out_w, gbr_all, gqkv, gains, docs, cos_v, sin_v, hg, mid_v, cot_v, x_v, gm_v, gbr_v, out_v,
    lo_v, gsum, gall, gsum_z, g_far, g_land, q_give, q_own, q_land, o_part, o_own, o_land,
    grad_gu, product_t, strip, gu_grad, down_grad, send_sems, recv_sems, local_sems, strip_sems,
):
    net = Net(zs, send_sems, recv_sems, local_sems)
    net.meet()
    deep, wide = gate_out.shape[0], gu_grad.shape[1] // 2
    seq = docs.shape[1]
    half, side = deep // 2, HEAD_DIM // 2
    rows = x.shape[1]
    last = 2 * zs - 1
    scale = HEAD_DIM**-0.5
    hidden = SumAll(net, gh_part, own, sib, one, two, landed)
    feed = SumAll(net, feed_part, own_f, sib_f, one_f, two_f, landed_f)
    mlp_local = [net.keep(grad_gu_in, grad_gu)]
    local = [net.keep(middle, mid_v), net.keep(cot.at[net.t], cot_v), net.keep(gains_in, gains)]
    local += [net.keep(x.at[net.t], x_v), net.keep(docs_in, docs), net.keep(cosine, cos_v), net.keep(sine, sin_v)]
    local += [net.keep(qkv_in, qkv), net.keep(attended_in, attended), net.keep(qkv_w_in, qkv_w)]
    local += [net.keep(out_w_in, out_w), net.keep(hidden_in, h1)]

    def block(dp, z):
        return aligned(dp * zs + z, wide)

    ways = iter(RELAY_WAYS)
    grads = [
        SpreadGrads(
            net,
            lambda z: gu_grad.at[aligned(z, deep), pl.ds(0, wide)],
            lambda dp, z: gate_out.at[:, block(dp, z)],
            next(ways),
        ),
        SpreadGrads(
            net,
            lambda z: gu_grad.at[aligned(z, deep), pl.ds(wide, wide)],
            lambda dp, z: up_out.at[:, block(dp, z)],
            next(ways),
        ),
        SpreadGrads(
            net,
            lambda z: down_grad.at[:, aligned(z, deep)],
            lambda dp, z: down_out.at[block(dp, z)],
            next(ways),
        ),
    ]

    def q_place(ref):
        def place(dp, z):
            a, b = lax.div(dp, 2), lax.rem(dp, 2)
            return ref.at[pl.ds(pl.multiple_of(a * half, half), half), aligned(b * zs + z, HEAD_DIM)]

        return place

    def o_place(dp, z):
        a, b = lax.div(dp, 2), lax.rem(dp, 2)
        return o_out.at[pl.ds(pl.multiple_of((b * zs + z) * HEAD_DIM + a * side, side), side)]

    late = [
        SpreadGrads(net, lambda z, m=m: q_own.at[z, :, pl.ds(m * HEAD_DIM, HEAD_DIM)], q_place(ref), next(ways))
        for m, ref in enumerate((q_out, k_out, v_out))
    ]
    late.append(SpreadGrads(net, lambda z: o_own.at[z], o_place, next(ways)))
    branch = SumLine(net, part, sib_1, far_1, landed_1)
    gather = GatherGroup(net, gbr_v, gbr_all)
    tile = 128
    outs, pairs, swaps, plane, z_gain = [], [], [], [], []

    def total_of(ref, at):
        total = ref[0, at, :].astype(F32)
        for z in range(1, zs):
            total += ref[z, at, :].astype(F32)
        return total

    def norm_back(inputs, total, gain, k):
        inverse = lax.rsqrt(jnp.mean(inputs * inputs, axis=-1, keepdims=True) + EPS)
        normed = inputs * inverse
        prod = total * normed
        gsum[k] += prod[0:8, :] + prod[8:16, :]
        scaled = total * gain
        return inverse * (scaled - normed * jnp.mean(scaled * normed, axis=-1, keepdims=True))

    def hidden_end():
        for copy in local:
            copy.wait()
        hidden.end()
        gsum[...] = jnp.zeros_like(gsum)

        def back_two(i):
            at = aligned(i, 16)
            grad = cot_v[at, :].astype(F32) + norm_back(mid_v[at, :], total_of(landed, at), gains[1:2, :], 1)
            gm_v[at, :] = grad
            gbr_v[at, :] = grad.astype(BF)

        loop(rows // 16, back_two)

    def place_of(k):
        b = net.b if k else 1 - net.b
        return b, b * seq, pl.ds(pl.multiple_of(b * seq, seq), seq), docs[pl.ds(b, 1), :]

    def queries_back(k):
        b, base, every, row = place_of(k)

        def heads_grad(i):
            at = pl.ds(pl.multiple_of(base + i * 256, 256), 256)
            hg[aligned(i, 256), :] = dot(gbr_all[at, :], out_w[...], ((1,), (1,)), BF)

        loop(seq // 256, heads_grad)

        def by_query(i):
            at = pl.ds(pl.multiple_of(base + i * tile, tile), tile)
            pos = aligned(i, tile)
            keys = qkv[every, HEAD_DIM : 2 * HEAD_DIM]
            sigma = sigma_of(qkv[at, 0:HEAD_DIM], keys)
            gw = dot(hg[pos, :], qkv[every, 2 * HEAD_DIM : 3 * HEAD_DIM], ((1,), (1,)))
            gs = jnp.where(seen(row, i * tile, tile), gw * sigma * (1.0 - sigma), 0.0).astype(BF)
            gq = dot(gs, keys) * scale
            gqkv[at, 0:HEAD_DIM] = turn(gq, cos_v[pos, :], -sin_v[pos, :]).astype(BF)

        loop(seq // tile, by_query)

    def keys_back(k):
        b, base, every, row = place_of(k)

        def by_key(i):
            at = pl.ds(pl.multiple_of(base + i * tile, tile), tile)
            pos = aligned(i, tile)
            queries = qkv[every, 0:HEAD_DIM]
            sigma = sigma_of(qkv[at, HEAD_DIM : 2 * HEAD_DIM], queries)
            gw = dot(qkv[at, 2 * HEAD_DIM : 3 * HEAD_DIM], hg[...], ((1,), (1,)))
            mask = seen(row, i * tile, tile, flip=True)
            gs = jnp.where(mask, gw * sigma * (1.0 - sigma), 0.0).astype(BF)
            weights = jnp.where(mask, sigma, 0.0).astype(BF)
            gk = dot(gs, queries) * scale
            gqkv[at, HEAD_DIM : 2 * HEAD_DIM] = turn(gk, cos_v[pos, :], -sin_v[pos, :]).astype(BF)
            gqkv[at, 2 * HEAD_DIM : 3 * HEAD_DIM] = dot(weights, hg[...], kind=BF)

        loop(seq // tile, by_key)

        def back_one(i):
            at = pl.ds(pl.multiple_of(base + i * tile, tile), tile)
            out = dot(gqkv[at, :], qkv_w[...], ((1,), (1,)), BF)
            for j in range(tile // rows):
                blk = i * (tile // rows) + j
                t = lax.div(blk, zs)
                z = (1 - t) * blk + t * (last - blk)
                part[b, t, z] = out[j * rows : (j + 1) * rows, :]

        loop(seq // tile, back_one)
        branch.give(k)

    def qkv_grad(z, a):
        at = pl.ds(pl.multiple_of(z * deep + a * half, half), half)
        return dot(h1[:, at], gqkv[...], ((0,), (0,)), BF)

    def side_rows(a):
        return pl.ds(pl.multiple_of(a * side, side), side)

    def weights_give():
        def out_grad(z):
            o_part[z] = dot(attended[...], gbr_all[:, aligned(z, deep)], ((0,), (0,)), BF)

        def theirs(z):
            q_give[z] = qkv_grad(z, 1 - net.a)

        loop(zs, out_grad)
        loop(zs, theirs)
        for s in range(zs):
            z = lax.rem(net.z + s + 1, zs)
            swaps.append(
                (
                    z,
                    net.send(q_give.at[z], q_land.at[z], net.over_y),
                    net.send(o_part.at[z, side_rows(1 - net.a)], o_land.at[z], net.over_y),
                )
            )

    def weights_own():
        def ours(z):
            q_own[z] = qkv_grad(z, net.a)

        loop(zs, ours)

    def weights_sum(s):
        z, q_in, o_in = swaps[s]
        q_in.wait_recv()
        add_rows(q_own.at[z], [q_own.at[z], q_land.at[z]], half)
        o_in.wait_recv()
        add_rows(o_own.at[z], [o_part.at[z, side_rows(net.a)], o_land.at[z]], side)
        for grad in late:
            grad.go(s + 1) if s < zs - 1 else grad.own()

    def branch_end():
        branch.end()

        def back_last(i):
            at = aligned(i, 16)
            total = total_of(landed_1.at[net.b], at) + far_1[at, :].astype(F32)
            grad = gm_v[at, :] + norm_back(x_v[at, :].astype(F32), total, gains[0:1, :], 0)
            out_v[at, :] = grad.astype(BF)

        loop(rows // 16, back_last)
        outs.append(net.keep(out_v, input_grad.at[net.t]))
        pairs.append(net.send(out_v, input_grad.at[net.t], net.sibling))
        plane.append(net.send(gsum, g_far.at[0], net.sibling))

    def gains_plane():
        plane[0].wait_recv()
        gall[...] = gsum[...] + g_far[0]
        for k, way in ((1, net.over_x), (2, net.over_y), (3, net.across)):
            plane.append(net.send(gall, g_far.at[k], way))

    def gains_line():
        for copy in plane[1:]:
            copy.wait_recv()
        gsum_z[...] = gall[...] + g_far[1] + g_far[2] + g_far[3]

        def cut(z):
            return gsum_z.at[:, :, aligned(z, deep)]

        z_gain.extend(net.send(cut(lax.rem(net.z + s, zs)), g_land.at[net.z], net.along_z(s)) for s in range(1, zs))
        outs.append(net.keep(cut(net.z), g_land.at[net.z]))

    def feed_end():
        feed.end()

        def close(i):
            at = aligned(i, 16)
            lo_v[at, :] = (mid_v[at, :] + total_of(landed_f, at)).astype(BF)

        loop(rows // 16, close)
        outs.append(net.keep(lo_v, layer_out.at[net.t]))
        pairs.append(net.send(lo_v, layer_out.at[net.t], net.sibling))

    def each(method):
        def step(s):
            for grad in late:
                getattr(grad, method)(s)

        return step

    thin = strip.shape[2]

    def strips(ref, body, first=None):
        def load(i):
            return pltpu.make_async_copy(ref.at[:, aligned(i, thin)], strip.at[lax.rem(i, 2)], strip_sems.at[lax.rem(i, 2)])

        count = ref.shape[1] // thin
        load(0).start()
        if first:
            first()

        def one(i):
            @pl.when(i + 1 < count)
            def _():
                load(i + 1).start()

            load(i).wait()
            body(i, strip.at[lax.rem(i, 2)])

        loop(count, one)

    def gate_up_grads():
        mlp_local[0].wait()

        def one(i, part):
            gu_grad[aligned(i, thin), :] = dot(part[...], grad_gu[...], ((0,), (0,)), BF)

        strips(h2_in, one)

    def down_grads():
        def turn_product():
            net.keep(product_in, strip.at[1]).wait()
            product_t[...] = strip[1].T

        def one(i, part):
            down_grad[:, aligned(i, thin)] = dot(product_t[...], part[...], kind=BF)

        strips(cots_in, one, turn_product)

    steps = {
        "MG": gate_up_grads, "MD": down_grads, "hstart": hidden.start, "hend": hidden_end, "gstart": gather.start, "gend": gather.end, "fstart": feed.start,
        "fend": feed_end, "W1": weights_give, "W2": weights_own, "bx": branch.across, "bend": branch_end,
        "gain2": gains_plane, "gain3": gains_line,
    }
    counted = {
        "F": hidden.first, "S": hidden.second, "T": hidden.third, "fF": feed.first, "fS": feed.second,
        "fT": feed.third, "gs": gather.spread, "gf": gather.far, "A": queries_back, "B": keys_back, "sw": weights_sum,
        "bt": branch.take, "Ls": each("spread"), "Lr": each("relay"),
    }
    for k, grad in enumerate(grads):
        steps["g%dz" % k] = grad.start
        counted["g%ds" % k], counted["g%dr" % k] = grad.spread, grad.relay
    for name in ORDER:
        if name in steps:
            steps[name]()
        else:
            counted[name[:-1]](int(name[-1]))
    for grad in grads + late:
        grad.end()
    for copy in outs:
        copy.wait()
    for copy in z_gain + pairs:
        copy.wait_recv()
    total = g_land[0]
    for z in range(1, zs):
        total += g_land[z]
    gains_out[...] = jnp.sum(total, axis=1)
    net.finish()


def widen(*arrays):
    steps = 16

    def kernel(*refs):
        for src, dst in zip(refs[: len(arrays)], refs[len(arrays) :], strict=True):
            dst[...] = src[...].astype(F32)

    specs = [pl.BlockSpec((a.shape[0] // steps, a.shape[1]), lambda i: (i, 0)) for a in arrays]
    return pl.pallas_call(
        kernel,
        grid=(steps,),
        in_specs=specs,
        out_specs=specs,
        out_shape=[jax.ShapeDtypeStruct(a.shape, F32) for a in arrays],
        compiler_params=pltpu.CompilerParams(vmem_limit_bytes=60 * MIB),
    )(*arrays)


def rope_tables(seq):
    half_dim = HEAD_DIM // 2
    frequency = ROPE_BASE ** (-np.arange(half_dim, dtype=np.float32) / half_dim)
    angle = np.arange(seq, dtype=np.float32)[:, None] * frequency.astype(np.float32)[None, :]
    cosine, sine = np.cos(angle), np.sin(angle)
    return (
        np.concatenate([cosine, cosine], axis=1).astype(np.float32),
        np.concatenate([-sine, sine], axis=1).astype(np.float32),
    )


def heads_shards(
    zs, activations, document_ids, attn_gain, w_query, w_key, w_value, w_out, mlp_gain, w_gate, w_up, w_down, cotangent
):
    stretch, width = activations.shape[3:]
    deep = w_query.shape[0]
    seq = document_ids.shape[1]
    pair = 2 * seq
    wide = w_gate.shape[1] // (4 * zs)
    x = activations.reshape(2, stretch, width)
    cot = cotangent.reshape(2, stretch, width)
    small = jnp.stack([attn_gain.astype(F32), mlp_gain.astype(F32)])
    docs_rows = document_ids.astype(F32).reshape(seq // deep, deep)
    small = jnp.concatenate([small, docs_rows, jnp.zeros((6 - seq // deep, deep), F32)])
    cosine, sine = (jnp.asarray(table) for table in rope_tables(seq))
    half = stretch // 2
    hidden, qkv, attended, qkv_w, out_w, gains, docs, middle, h2_all, cot_all, gh_part, feed_part, grad_gu, product = call(
        functools.partial(forward_kernel, zs),
        1,
        [
            ((pair, width), BF, ANY),
            ((pair, 3 * HEAD_DIM), BF, ANY),
            ((pair, HEAD_DIM), BF, ANY),
            ((width, 3 * HEAD_DIM), BF, ANY),
            ((HEAD_DIM, width), BF, ANY),
            ((8, width), F32, ANY),
            ((8, seq), F32, ANY),
            ((stretch, width), F32, ANY),
            ((4, zs, 2, stretch, width), BF, ANY),
            ((4, zs, 2, stretch, width), BF, ANY),
            ((4 * seq, width), BF, ANY),
            ((4 * seq, width), BF, ANY),
            ((4 * seq, 2 * wide), BF, ANY),
            ((4 * seq, wide), BF, ANY),
        ],
        [
            VMEM((pair, width), BF),
            VMEM((pair, width), BF),
            VMEM((width, 3 * HEAD_DIM), BF),
            VMEM((HEAD_DIM, width), BF),
            VMEM((zs, 8, deep), F32),
            VMEM((2, 8, deep), F32),
            VMEM((8, width), F32),
            VMEM((8, seq), F32),
            VMEM((seq, HEAD_DIM), F32),
            VMEM((seq, HEAD_DIM), F32),
            VMEM((pair, 3 * HEAD_DIM), BF),
            VMEM((pair, HEAD_DIM), BF),
            VMEM((2, 2, zs, stretch, width), BF),
            VMEM((2, zs, stretch, width), BF),
            VMEM((zs, stretch, width), BF),
            VMEM((zs, stretch, width), BF),
            VMEM((stretch, width), BF),
            VMEM((stretch, width), BF),
            VMEM((stretch, width), F32),
            VMEM((4, zs, 2, stretch, width), BF),
            VMEM((4, zs, 2, stretch, width), BF),
            VMEM((width, 2 * wide), BF),
            VMEM((wide, width), BF),
            VMEM((4 * seq, wide), F32),
            VMEM((4 * seq, wide), F32),
            VMEM((4 * seq, 2 * wide), BF),
            VMEM((4 * seq, wide), BF),
            VMEM((2, 256, width), BF),
            VMEM((2, 256, width), BF),
        ],
        ((134,), (131,), (34,), (2, 2)),
        (x, w_query, w_key, w_value, w_out, small, cosine, sine, w_gate, w_up, w_down, cot),
        60,
    )

    h2 = h2_all.reshape(4 * seq, width)
    cots = cot_all.reshape(4 * seq, width)
    gh_part = gh_part.reshape(4, zs, 2, stretch, width)
    feed_part = feed_part.reshape(4, zs, 2, stretch, width)

    sum_scratch = [
        VMEM((4, zs, stretch, width), BF),
        VMEM((4, zs, stretch, width), BF),
        VMEM((2, 2, zs, half, width), BF),
        VMEM((2, zs, half, width), BF),
        VMEM((zs, stretch, width), BF),
    ]
    layer_out, input_grad, q_g, k_g, v_g, o_g, gate_g, up_g, down_g, gains_g = call(
        functools.partial(backward_kernel, zs),
        2,
        [
            ((2, stretch, width), BF, ANY),
            ((2, stretch, width), BF, ANY),
            (w_query.shape, BF, ANY),
            (w_key.shape, BF, ANY),
            (w_value.shape, BF, ANY),
            (w_out.shape, BF, ANY),
            (w_gate.shape, BF, ANY),
            (w_up.shape, BF, ANY),
            (w_down.shape, BF, ANY),
            ((2, deep), F32, VMEM),
        ],
        sum_scratch
        + sum_scratch
        + [
            VMEM((2, 2, zs, stretch, width), BF),
            VMEM((2, zs, stretch, width), BF),
            VMEM((stretch, width), BF),
            VMEM((2, zs, stretch, width), BF),
            VMEM((pair, width), BF),
            VMEM((pair, 3 * HEAD_DIM), BF),
            VMEM((pair, HEAD_DIM), BF),
            VMEM((width, 3 * HEAD_DIM), BF),
            VMEM((HEAD_DIM, width), BF),
            VMEM((pair, width), BF),
            VMEM((pair, 3 * HEAD_DIM), BF),
            VMEM((8, width), F32),
            VMEM((8, seq), F32),
            VMEM((seq, HEAD_DIM), F32),
            VMEM((seq, HEAD_DIM), F32),
            VMEM((seq, HEAD_DIM), BF),
            VMEM((stretch, width), F32),
            VMEM((stretch, width), BF),
            VMEM((stretch, width), BF),
            VMEM((stretch, width), F32),
            VMEM((stretch, width), BF),
            VMEM((stretch, width), BF),
            VMEM((stretch, width), BF),
            VMEM((2, 8, width), F32),
            VMEM((2, 8, width), F32),
            VMEM((2, 8, width), F32),
            VMEM((4, 2, 8, width), F32),
            VMEM((zs, 2, 8, deep), F32),
            VMEM((zs, deep // 2, 3 * HEAD_DIM), BF),
            VMEM((zs, deep // 2, 3 * HEAD_DIM), BF),
            VMEM((zs, deep // 2, 3 * HEAD_DIM), BF),
            VMEM((zs, HEAD_DIM, deep), BF),
            VMEM((zs, HEAD_DIM // 2, deep), BF),
            VMEM((zs, HEAD_DIM // 2, deep), BF),
            VMEM((4 * seq, 2 * wide), BF),
            VMEM((wide, 4 * seq), BF),
            VMEM((2, 4 * seq, 256), BF),
            VMEM((width, 2 * wide), BF),
            VMEM((wide, width), BF),
        ],
        ((232,), (231,), (36,), (2,)),
        (
            gh_part, feed_part, h2, cots, grad_gu, product, middle, cot, x, gains, docs, cosine, sine,
            hidden, qkv, attended, qkv_w, out_w,
        ),
        60,
    )
    q_g, k_g, v_g, o_g, gate_g, up_g, down_g = widen(q_g, k_g, v_g, o_g, gate_g, up_g, down_g)
    return (
        layer_out.reshape(activations.shape),
        input_grad.reshape(activations.shape),
        gains_g[0],
        q_g,
        k_g,
        v_g,
        o_g,
        gains_g[1],
        gate_g,
        up_g,
        down_g,
    )


def angles(positions):
    half_dim = HEAD_DIM // 2
    frequency = ROPE_BASE ** (-jnp.arange(half_dim, dtype=jnp.float32) / half_dim)
    angle = positions.astype(jnp.float32)[:, None] * frequency[None, :]
    return (jnp.cos(angle)[:, None, :], jnp.sin(angle)[:, None, :])


def rotate(flat, positions):
    row_count = flat.shape[0]
    heads = flat.reshape(row_count, -1, HEAD_DIM)
    cosine, sine = angles(positions)
    first = heads[..., : HEAD_DIM // 2]
    second = heads[..., HEAD_DIM // 2 :]
    turned = jnp.concatenate(
        [first * cosine - second * sine, second * cosine + first * sine], axis=-1
    )
    return turned.reshape(row_count, -1)


def unrotate(flat, positions):
    row_count = flat.shape[0]
    heads = flat.reshape(row_count, -1, HEAD_DIM)
    cosine, sine = angles(positions)
    first = heads[..., : HEAD_DIM // 2]
    second = heads[..., HEAD_DIM // 2 :]
    turned = jnp.concatenate(
        [first * cosine + second * sine, second * cosine - first * sine], axis=-1
    )
    return turned.reshape(row_count, -1)


def normalize(values):
    inverse = lax.rsqrt(jnp.mean(values * values, axis=-1, keepdims=True) + EPS)
    return (values * inverse, inverse)


def norm_back(grad_normed_out, normed, inverse, gain):
    scaled = grad_normed_out * gain
    return inverse * (scaled - normed * jnp.mean(scaled * normed, axis=-1, keepdims=True))


def contract_rows(left, right):
    return lax.dot_general(
        left, right, (((1,), (1,)), ((), ())), preferred_element_type=jnp.float32
    )


def contract_cols(left, right):
    return lax.dot_general(
        left, right, (((0,), (0,)), ((), ())), preferred_element_type=jnp.float32
    )


def visibility(query_positions, query_docs, key_positions, key_docs):
    same_doc = query_docs[:, None] == key_docs[None, :]
    earlier = key_positions[None, :] <= query_positions[:, None]
    return jnp.where(same_doc & earlier, 1.0, 0.0).astype(jnp.float32)


def merge_heads(stacked):
    return jnp.transpose(stacked, (1, 0, 2)).reshape(stacked.shape[1], -1)


def head_slice(matrix, offset):
    return lax.dynamic_slice_in_dim(matrix, offset, HEAD_DIM, 1)


def attend_forward(queries, key_rows, value_rows, visible):
    score_scale = HEAD_DIM ** (-0.5)

    def one_head(head_index):
        offset = head_index * HEAD_DIM
        scores = (
            contract_rows(head_slice(queries, offset), head_slice(key_rows, offset)) * score_scale
        )
        weights = (jax.nn.sigmoid(scores - SHIFT) * visible).astype(jnp.bfloat16)
        return jnp.dot(weights, head_slice(value_rows, offset), preferred_element_type=jnp.float32)

    stacked = lax.map(one_head, jnp.arange(queries.shape[1] // HEAD_DIM))
    return merge_heads(stacked)


def attend_back(queries, key_rows, value_rows, grad_attended, visible):
    score_scale = HEAD_DIM ** (-0.5)

    def one_head(head_index):
        offset = head_index * HEAD_DIM
        head_query = head_slice(queries, offset)
        head_key = head_slice(key_rows, offset)
        head_grad = head_slice(grad_attended, offset)
        scores = contract_rows(head_query, head_key) * score_scale
        sigma = jax.nn.sigmoid(scores - SHIFT)
        grad_weights = contract_rows(head_grad, head_slice(value_rows, offset))
        grad_scores = (grad_weights * visible * sigma * (1.0 - sigma)).astype(jnp.bfloat16)
        pieces = []
        pieces.append(
            jnp.dot(grad_scores, head_key, preferred_element_type=jnp.float32) * score_scale
        )
        weights = (sigma * visible).astype(jnp.bfloat16)
        pieces.append(contract_cols(grad_scores, head_query) * score_scale)
        pieces.append(contract_cols(weights, head_grad))
        return tuple(pieces)

    stacked = lax.map(one_head, jnp.arange(queries.shape[1] // HEAD_DIM))
    return tuple((merge_heads(piece) for piece in stacked))


def rows_shards(
    activations,
    document_ids,
    attn_gain,
    w_query,
    w_key,
    w_value,
    w_out,
    mlp_gain,
    w_gate,
    w_up,
    w_down,
    cotangent,
):
    groups = lax.axis_size("cp")
    rank = lax.axis_index("cp")
    stretch_len = activations.shape[3]
    width = activations.shape[4]
    row_count = 2 * stretch_len
    offsets = jnp.arange(stretch_len, dtype=jnp.int32)
    my_positions = jnp.concatenate(
        [rank * stretch_len + offsets, (2 * groups - 1 - rank) * stretch_len + offsets]
    )
    all_docs = document_ids[0]
    my_docs = jnp.take(all_docs, my_positions)
    slots = jnp.arange(groups * row_count, dtype=jnp.int32)
    owners = slots // row_count
    halves = slots // stretch_len % 2
    key_positions = (
        jnp.where(halves == 0, owners, 2 * groups - 1 - owners) * stretch_len + slots % stretch_len
    )
    key_docs = jnp.take(all_docs, key_positions)
    visible = visibility(my_positions, my_docs, key_positions, key_docs)
    gathered = (
        lax.all_gather(w_query, "cp", axis=0, tiled=True),
        lax.all_gather(w_key, "cp", axis=0, tiled=True),
        lax.all_gather(w_value, "cp", axis=0, tiled=True),
        lax.all_gather(w_out, "cp", axis=1, tiled=True),
        lax.all_gather(w_gate, "cp", axis=0, tiled=True),
        lax.all_gather(w_up, "cp", axis=0, tiled=True),
        lax.all_gather(w_down, "cp", axis=1, tiled=True),
        lax.all_gather(attn_gain, "cp", axis=0, tiled=True),
        lax.all_gather(mlp_gain, "cp", axis=0, tiled=True),
    )
    (
        query_full,
        key_full,
        value_full,
        out_full,
        gate_full,
        up_full,
        down_full,
        gain_one,
        gain_two,
    ) = gathered
    gain_one = gain_one.astype(jnp.float32)
    gain_two = gain_two.astype(jnp.float32)
    inputs = activations.reshape(row_count, width).astype(jnp.float32)
    normed_one, inverse_one = normalize(inputs)
    hidden_one = (normed_one * gain_one).astype(jnp.bfloat16)
    queries = rotate(
        jnp.dot(hidden_one, query_full, preferred_element_type=jnp.float32), my_positions
    ).astype(jnp.bfloat16)
    keys_local = rotate(
        jnp.dot(hidden_one, key_full, preferred_element_type=jnp.float32), my_positions
    ).astype(jnp.bfloat16)
    values_local = jnp.dot(hidden_one, value_full, preferred_element_type=jnp.float32).astype(
        jnp.bfloat16
    )
    keys_all, values_all = (
        lax.all_gather(keys_local, "cp", axis=0, tiled=True),
        lax.all_gather(values_local, "cp", axis=0, tiled=True),
    )
    attended = attend_forward(queries, keys_all, values_all, visible).astype(jnp.bfloat16)
    branch = lax.psum(jnp.dot(attended, out_full, preferred_element_type=jnp.float32), "tp")
    middle = inputs + branch
    normed_two, inverse_two = normalize(middle)
    hidden_two = (normed_two * gain_two).astype(jnp.bfloat16)
    gate = jnp.dot(hidden_two, gate_full, preferred_element_type=jnp.float32)
    upward = jnp.dot(hidden_two, up_full, preferred_element_type=jnp.float32)
    sigma_gate = jax.nn.sigmoid(gate)
    silu_gate = gate * sigma_gate
    product = (silu_gate * upward).astype(jnp.bfloat16)
    feed = lax.psum(jnp.dot(product, down_full, preferred_element_type=jnp.float32), "tp")
    result = middle + feed
    layer_out = result.astype(jnp.bfloat16).reshape(activations.shape)
    grad_result = cotangent.reshape(row_count, width).astype(jnp.float32)
    grad_feed = grad_result.astype(jnp.bfloat16)
    grad_product = contract_rows(grad_feed, down_full)
    grad_gate = (grad_product * upward * sigma_gate * (1.0 + gate * (1.0 - sigma_gate))).astype(
        jnp.bfloat16
    )
    grad_up = (grad_product * silu_gate).astype(jnp.bfloat16)
    grad_hidden_two = lax.psum(
        contract_rows(grad_gate, gate_full) + contract_rows(grad_up, up_full), "tp"
    )
    grad_gain_two = jnp.sum(grad_hidden_two * normed_two, axis=0)
    grad_middle = grad_result + norm_back(grad_hidden_two, normed_two, inverse_two, gain_two)
    grad_down = contract_cols(product, grad_feed)
    grad_gate_w = contract_cols(hidden_two, grad_gate)
    grad_up_w = contract_cols(hidden_two, grad_up)
    share_gate, share_up, share_down, share_gain_two = (
        lax.psum_scatter(grad_gate_w, "cp", scatter_dimension=0, tiled=True),
        lax.psum_scatter(grad_up_w, "cp", scatter_dimension=0, tiled=True),
        lax.psum_scatter(grad_down, "cp", scatter_dimension=1, tiled=True),
        lax.psum_scatter(grad_gain_two, "cp", scatter_dimension=0, tiled=True),
    )
    grad_branch = grad_middle.astype(jnp.bfloat16)
    grad_attended = contract_rows(grad_branch, out_full).astype(jnp.bfloat16)
    grad_queries, key_terms, value_terms = attend_back(
        queries, keys_all, values_all, grad_attended, visible
    )
    grad_keys, grad_values = (
        lax.psum_scatter(key_terms, "cp", scatter_dimension=0, tiled=True),
        lax.psum_scatter(value_terms, "cp", scatter_dimension=0, tiled=True),
    )
    grad_query_pre = unrotate(grad_queries, my_positions).astype(jnp.bfloat16)
    grad_key_pre = unrotate(grad_keys, my_positions).astype(jnp.bfloat16)
    grad_value_pre = grad_values.astype(jnp.bfloat16)
    local_hidden = (
        contract_rows(grad_query_pre, query_full)
        + contract_rows(grad_key_pre, key_full)
        + contract_rows(grad_value_pre, value_full)
    )
    grad_hidden_one = lax.psum(local_hidden, "tp")
    grad_gain_one = jnp.sum(grad_hidden_one * normed_one, axis=0)
    grad_inputs = grad_middle + norm_back(grad_hidden_one, normed_one, inverse_one, gain_one)
    grad_query_w = contract_cols(hidden_one, grad_query_pre)
    grad_key_w = contract_cols(hidden_one, grad_key_pre)
    grad_value_w = contract_cols(hidden_one, grad_value_pre)
    grad_out_w = contract_cols(attended, grad_branch)
    share_query, share_key, share_value, share_out, share_gain_one = (
        lax.psum_scatter(grad_query_w, "cp", scatter_dimension=0, tiled=True),
        lax.psum_scatter(grad_key_w, "cp", scatter_dimension=0, tiled=True),
        lax.psum_scatter(grad_value_w, "cp", scatter_dimension=0, tiled=True),
        lax.psum_scatter(grad_out_w, "cp", scatter_dimension=1, tiled=True),
        lax.psum_scatter(grad_gain_one, "cp", scatter_dimension=0, tiled=True),
    )
    summed = lax.psum(
        (
            share_gain_one,
            share_query,
            share_key,
            share_value,
            share_out,
            share_gain_two,
            share_gate,
            share_up,
            share_down,
        ),
        "dp",
    )
    input_grad = grad_inputs.astype(jnp.bfloat16).reshape(activations.shape)
    return (
        layer_out,
        input_grad,
        summed[0],
        summed[1],
        summed[2],
        summed[3],
        summed[4],
        summed[5],
        summed[6],
        summed[7],
        summed[8],
    )


def layer(sizes, *args):
    heads = args[3].shape[1] // HEAD_DIM
    zs = sizes["cp"]
    fits = sizes["dp"] == 4 and sizes["tp"] == 2 and zs == 4 and heads == 2 * zs
    fits = fits and args[0].shape[3] % 32 == 0 and args[8].shape[1] % (2 * zs * HEAD_DIM) == 0
    fits = fits and args[3].shape[0] % HEAD_DIM == 0 and args[1].shape[1] % args[3].shape[0] == 0
    fits = fits and args[1].shape[1] <= 6 * args[3].shape[0]
    if fits:
        return heads_shards(zs, *args)
    return rows_shards(*args)


def solution(mesh):
    return jax.shard_map(
        functools.partial(layer, dict(mesh.shape)),
        mesh=mesh,
        in_specs=(
            P("dp", "cp", None, None, None),
            P("dp", None),
            P("cp"),
            P("cp", "tp"),
            P("cp", "tp"),
            P("cp", "tp"),
            P("tp", "cp"),
            P("cp"),
            P("cp", "tp"),
            P("cp", "tp"),
            P("tp", "cp"),
            P("dp", "cp", None, None, None),
        ),
        out_specs=(
            P("dp", "cp", None, None, None),
            P("dp", "cp", None, None, None),
            P("cp"),
            P("cp", "tp"),
            P("cp", "tp"),
            P("cp", "tp"),
            P("tp", "cp"),
            P("cp"),
            P("cp", "tp"),
            P("cp", "tp"),
            P("tp", "cp"),
        ),
        check_vma=False,
    )
```
